32 devices in a mesh: dp: 4 (over x, core), row: 4 (over z), col: 2 (over y).
Axes of the slice: x: 2, y: 2, z: 4, core: 2. Of those that a mesh axis runs over, the one named last changes fastest.
Arguments:
- tokens: bfloat16 [4096, 2048], P(('dp', 'col'), 'row'), may hold values from -6 to 6
- cotangent: bfloat16 [4096, 2048], P(('dp', 'col'), 'row'), may hold values from -9.5 to 9.5
- seq_lens: int32 [4, 4], P('dp'), may hold values from 0 to 1024, as said below
- query_weight: float32 [2048, 2048], P(('row', 'dp'), 'col'), may hold values from -0.125 to 0.125
- query_moment: float32 [2048, 2048], P(('row', 'dp'), 'col'), may hold values from -40 to 40
- query_second: float32 [2048, 2048], P(('row', 'dp'), 'col'), may hold values from 204.8 to 819.2
- key_value_master_weight: float32 [2048, 2, 1024], P(('row', 'dp'), None, 'col'), may hold values from -0.125 to 0.125
- key_value_first_moment: float32 [2048, 2, 1024], P(('row', 'dp'), None, 'col'), may hold values from -40 to 40
- key_value_second_moment: float32 [2048, 2, 1024], P(('row', 'dp'), None, 'col'), may hold values from 204.8 to 819.2
- output_weight: float32 [2048, 2048], P(('col', 'dp'), 'row'), may hold values from -1 to 1
- output_moment: float32 [2048, 2048], P(('col', 'dp'), 'row'), may hold values from -6 to 6
- output_second: float32 [2048, 2048], P(('col', 'dp'), 'row'), may hold values from 4.096 to 16.384
- gateup_weight: float32 [2048, 2, 6144], P(('row', 'dp'), None, 'col'), may hold values from -0.125 to 0.125
- gateup_moment: float32 [2048, 2, 6144], P(('row', 'dp'), None, 'col'), may hold values from -16 to 16
- gateup_second: float32 [2048, 2, 6144], P(('row', 'dp'), None, 'col'), may hold values from 30.72 to 122.88
- down_weight: float32 [6144, 2048], P(('col', 'dp'), 'row'), may hold values from -0.078125 to 0.078125
- down_moment: float32 [6144, 2048], P(('col', 'dp'), 'row'), may hold values from -32 to 32
- down_second: float32 [6144, 2048], P(('col', 'dp'), 'row'), may hold values from 102.4 to 409.6
- norm_gains: float32 [2, 2048], replicated, may hold values from 0.3 to 2.3
- norm_moment: float32 [2, 2048], replicated, may hold values from -40 to 40
- norm_second: float32 [2, 2048], replicated, may hold values from 204.8 to 819.2
- head_gains: float32 [2, 128], replicated, may hold values from 0.9 to 1.6
- head_moment: float32 [2, 128], replicated, may hold values from -128 to 128
- head_second: float32 [2, 128], replicated, may hold values from 2457.6 to 9830.4
Outputs:
- layer_output: float32 [4096, 2048], P(('dp', 'col'), 'row')
- input_grad: float32 [4096, 2048], P(('dp', 'col'), 'row')
- query_moment_new: float32 [2048, 2048], P(('row', 'dp'), 'col')
- query_second_new: float32 [2048, 2048], P(('row', 'dp'), 'col')
- query_weight_new: float32 [2048, 2048], P(('row', 'dp'), 'col')
- keyval_moment_new: float32 [2048, 2, 1024], P(('row', 'dp'), None, 'col')
- keyval_second_new: float32 [2048, 2, 1024], P(('row', 'dp'), None, 'col')
- keyval_weight_new: float32 [2048, 2, 1024], P(('row', 'dp'), None, 'col')
- output_moment_new: float32 [2048, 2048], P(('col', 'dp'), 'row')
- output_second_new: float32 [2048, 2048], P(('col', 'dp'), 'row')
- output_weight_new: float32 [2048, 2048], P(('col', 'dp'), 'row')
- gateup_moment_new: float32 [2048, 2, 6144], P(('row', 'dp'), None, 'col')
- gateup_second_new: float32 [2048, 2, 6144], P(('row', 'dp'), None, 'col')
- gateup_weight_new: float32 [2048, 2, 6144], P(('row', 'dp'), None, 'col')
- down_moment_new: float32 [6144, 2048], P(('col', 'dp'), 'row')
- down_second_new: float32 [6144, 2048], P(('col', 'dp'), 'row')
- down_weight_new: float32 [6144, 2048], P(('col', 'dp'), 'row')
- norm_moment_new: float32 [2, 2048], replicated
- norm_second_new: float32 [2, 2048], replicated
- norm_gains_new: float32 [2, 2048], replicated
- head_moment_new: float32 [2, 128], replicated
- head_second_new: float32 [2, 128], replicated
- head_gains_new: float32 [2, 128], replicated
The draws below stay inside these ranges and needn't reach their ends.
Inputs may be any that keep to these rules, and one draw needn't show every extreme that they name: `seq_lens`: each row lists the lengths of the sequences packed in order from the first slot of a group of 1024 slots, zero for an unused entry; a row sums to at most 1024 and its longest entry exceeds 3 * 256; the last group holds one sequence of exactly 1024; slots after the sum are padding.
All inputs are finite; a program needn't handle non-finite values.
Results may differ from the reference program's by a relative error of at most 0.018.
Values may be sent and summed in bfloat16 or wider, within the bound.
No kernel may reach another device: no remote copies, remote signals or barrier semaphores. Data moves between devices by JAX's collectives and lax.ppermute only.
A program may use at most 192 MiB of HBM per device.

```python
import math
import jax
import jax.numpy as jnp
from jax import lax

MODEL_WIDTH = 2048
HQ = 16
KEY_VALUE_HEADS = 8
HEAD_SIZE = 128
FF = 6144
TOK_GRP = 1024
SEQS = 4
STEP = 10
GROUPS = 4
TOKEN_SLOTS = 4096


def draw_tokens(key, part):
    key = jax.random.fold_in(key, 37)
    rank = jnp.arange(MODEL_WIDTH, dtype=jnp.float32) / (MODEL_WIDTH - 1)
    base = jnp.clip(jax.random.normal(key, (TOKEN_SLOTS, MODEL_WIDTH), jnp.float32), -5.0, 5.0)
    scale = 0.7 + 0.5 * rank
    return (base * scale[None, :]).astype(jnp.bfloat16)


def draw_cotangent(key, part):
    key = jax.random.fold_in(key, 23)
    rank = (jnp.arange(TOKEN_SLOTS) // TOK_GRP).astype(jnp.float32) / max(GROUPS - 1, 1)
    base = jnp.clip(jax.random.normal(key, (TOKEN_SLOTS, MODEL_WIDTH), jnp.float32), -5.0, 5.0)
    scale = 0.6 + 1.2 * rank
    return (base * scale[:, None]).astype(jnp.bfloat16)


def draw_seq_lens(key, part):
    key = jax.random.fold_in(key, 11)
    short_key, order_key = jax.random.split(key)
    short_top = TOK_GRP // (8 * (SEQS - 1)) - 1
    shorts = jax.random.randint(short_key, (GROUPS, SEQS - 1), 1, short_top + 1)
    index = jnp.arange(GROUPS)
    used = TOK_GRP - TOK_GRP // 8 * (GROUPS - 1 - index) // max(GROUPS - 1, 1)
    final = index == GROUPS - 1
    shorts = jnp.where(final[:, None], 0, shorts)
    longest = used - jnp.sum(shorts, axis=1)
    lengths = jnp.concatenate([longest[:, None], shorts], axis=1)
    scores = jax.random.randint(order_key, (GROUPS, SEQS), 0, 1 << 20) * SEQS + jnp.arange(SEQS)[None, :]
    order = jnp.argsort(scores, axis=1)
    return jnp.take_along_axis(lengths, order, axis=1).astype(jnp.int32)


def draw_norm_gains(key, part):
    key = jax.random.fold_in(key, 53)
    rank = jnp.arange(MODEL_WIDTH, dtype=jnp.float32) / (MODEL_WIDTH - 1)
    spread = jax.random.uniform(key, (2, MODEL_WIDTH), jnp.float32, 0.85, 1.15)
    return (0.5 + rank)[None, :] * spread


def level_of(stream_key, extent, cuts, low, largest):
    factor_of = 1.0
    for dim, blocks in cuts:
        draws = jax.random.uniform(jax.random.fold_in(jax.random.fold_in(stream_key, 6), dim), (blocks,), jnp.float32, low / len(cuts), largest / len(cuts))
        factor_of = factor_of * jnp.repeat(jnp.exp(draws), extent[dim] // blocks).reshape((-1,) + (1,) * (len(extent) - 1 - dim))
    return factor_of


def normal_values(key, extent, scale, most, shards=(), held_as=jnp.bfloat16):
    level = level_of(key, extent, shards, -0.22, 0.18) if shards else 1.0
    result = jax.random.normal(key, extent, jnp.float32) * scale * level
    return jnp.minimum(jnp.maximum(result, -most), most).astype(held_as)


def setup_inputs(seed: int = 0) -> dict:
    seeds = jax.random.split(jax.random.key(seed), 25)
    return {
        "tokens": draw_tokens(jax.random.fold_in(seeds[24], 71), 0),
        "cotangent": draw_cotangent(jax.random.fold_in(seeds[24], 71), 0),
        "seq_lens": draw_seq_lens(jax.random.fold_in(seeds[24], 71), 0),
        "query_weight": normal_values(seeds[3], (MODEL_WIDTH, HQ * HEAD_SIZE), MODEL_WIDTH ** -0.5, 0.125, ((0, 16), (1, 2)), jnp.float32),
        "query_moment": normal_values(seeds[4], (MODEL_WIDTH, HQ * HEAD_SIZE), (0.11 * TOKEN_SLOTS ** 0.5), 40.0, ((0, 16), (1, 2)), jnp.float32),
        "query_second": jnp.clip(jnp.exp(math.log(819.2) - 1.3862944 * jax.random.uniform(seeds[5], (MODEL_WIDTH, HQ * HEAD_SIZE), jnp.float32) ** level_of(seeds[5], (MODEL_WIDTH, HQ * HEAD_SIZE), ((0, 16), (1, 2)), -0.2, 0.2)), 204.8, 819.2),
        "key_value_master_weight": normal_values(seeds[6], (MODEL_WIDTH, 2, KEY_VALUE_HEADS * HEAD_SIZE), MODEL_WIDTH ** -0.5, 0.125, ((0, 16), (2, 2)), jnp.float32),
        "key_value_first_moment": normal_values(seeds[7], (MODEL_WIDTH, 2, KEY_VALUE_HEADS * HEAD_SIZE), (0.11 * TOKEN_SLOTS ** 0.5), 40.0, ((0, 16), (2, 2)), jnp.float32),
        "key_value_second_moment": jnp.clip(jnp.exp(math.log(819.2) - 1.3862944 * jax.random.uniform(seeds[8], (MODEL_WIDTH, 2, KEY_VALUE_HEADS * HEAD_SIZE), jnp.float32) ** level_of(seeds[8], (MODEL_WIDTH, 2, KEY_VALUE_HEADS * HEAD_SIZE), ((0, 16), (2, 2)), -0.2, 0.2)), 204.8, 819.2),
        "output_weight": normal_values(seeds[9], (HQ * HEAD_SIZE, MODEL_WIDTH), (HQ * HEAD_SIZE // 64) ** -0.5, 1.0, ((0, 8), (1, 4)), jnp.float32),
        "output_moment": normal_values(seeds[10], (HQ * HEAD_SIZE, MODEL_WIDTH), (0.11 * (0.02 * TOKEN_SLOTS) ** 0.5), 6.0, ((0, 8), (1, 4)), jnp.float32),
        "output_second": jnp.clip(jnp.exp(math.log(16.384) - 1.3862944 * jax.random.uniform(seeds[11], (HQ * HEAD_SIZE, MODEL_WIDTH), jnp.float32) ** level_of(seeds[11], (HQ * HEAD_SIZE, MODEL_WIDTH), ((0, 8), (1, 4)), -0.2, 0.2)), 4.096, 16.384),
        "gateup_weight": normal_values(seeds[12], (MODEL_WIDTH, 2, FF), MODEL_WIDTH ** -0.5, 0.125, ((0, 16), (2, 2)), jnp.float32),
        "gateup_moment": normal_values(seeds[13], (MODEL_WIDTH, 2, FF), (0.11 * (0.15 * TOKEN_SLOTS) ** 0.5), 16.0, ((0, 16), (2, 2)), jnp.float32),
        "gateup_second": jnp.clip(jnp.exp(math.log(122.88) - 1.3862944 * jax.random.uniform(seeds[14], (MODEL_WIDTH, 2, FF), jnp.float32) ** level_of(seeds[14], (MODEL_WIDTH, 2, FF), ((0, 16), (2, 2)), -0.2, 0.2)), 30.72, 122.88),
        "down_weight": normal_values(seeds[15], (FF, MODEL_WIDTH), FF ** -0.5, 0.078125, ((0, 8), (1, 4)), jnp.float32),
        "down_moment": normal_values(seeds[16], (FF, MODEL_WIDTH), (0.11 * (0.5 * TOKEN_SLOTS) ** 0.5), 32.0, ((0, 8), (1, 4)), jnp.float32),
        "down_second": jnp.clip(jnp.exp(math.log(409.6) - 1.3862944 * jax.random.uniform(seeds[17], (FF, MODEL_WIDTH), jnp.float32) ** level_of(seeds[17], (FF, MODEL_WIDTH), ((0, 8), (1, 4)), -0.2, 0.2)), 102.4, 409.6),
        "norm_gains": draw_norm_gains(jax.random.fold_in(seeds[24], 71), 0),
        "norm_moment": normal_values(seeds[19], (2, MODEL_WIDTH), (0.11 * TOKEN_SLOTS ** 0.5), 40.0, (), jnp.float32),
        "norm_second": jnp.clip(jnp.exp(jax.random.uniform(seeds[20], (2, MODEL_WIDTH), jnp.float32, math.log(204.8), math.log(819.2))), 204.8, 819.2),
        "head_gains": jnp.clip(jax.random.uniform(seeds[21], (2, HEAD_SIZE), jnp.float32, 0.9, 1.6), 0.9, 1.6),
        "head_moment": normal_values(seeds[22], (2, HEAD_SIZE), (0.11 * (12 * TOKEN_SLOTS) ** 0.5), 128.0, (), jnp.float32),
        "head_second": jnp.clip(jnp.exp(jax.random.uniform(seeds[23], (2, HEAD_SIZE), jnp.float32, math.log(2457.6), math.log(9830.4))), 2457.6, 9830.4),
    }


EPS = 1e-06
THETA = 1000000.0
NEGATIVE = -1e+30
BETA_ONE = 0.9
BETA_TWO = 0.95
ADAM_EPS = 1e-08
DECAY = 0.1
RATES = (0.066, 0.066, 0.5, 0.066, 0.04)
GAIN_RATE = 0.6
HIGH = lax.Precision.HIGHEST

@jax.custom_vjp
def low(v):
    return lax.optimization_barrier(v.astype(jnp.bfloat16)).astype(jnp.float32)

@jax.custom_vjp
def reduced_backward(v):
    return v

def low_keep(v):
    return (low(v), None)

def low_pass(kept, grad):
    return (grad,)

def back_keep(v):
    return (v, None)

def back_low(kept, grad):
    return (low(grad),)
low.defvjp(low_keep, low_pass)
reduced_backward.defvjp(back_keep, back_low)

def token_layout(lengths, item_count):
    ends = jnp.cumsum(lengths).astype(jnp.int32)
    places = jnp.arange(item_count, dtype=jnp.int32)
    segment = lax.optimization_barrier(jnp.sum((places[:, None] >= ends[None, :]).astype(jnp.int32), axis=1)).astype(jnp.int32)
    starts = jnp.concatenate([ends - lengths, ends[-1:]]).astype(jnp.int32)
    labels = jnp.arange(starts.shape[0], dtype=jnp.int32)
    begin = lax.optimization_barrier(jnp.sum(jnp.where(segment[:, None] == labels[None, :], starts[None, :], 0), axis=1)).astype(jnp.int32)
    return (segment, (places - begin).astype(jnp.int32))

def rope_tables(position):
    half = HEAD_SIZE // 2
    freq = jnp.exp(jnp.arange(half, dtype=jnp.float32) * (-2.0 * math.log(THETA) / HEAD_SIZE))
    angle = position.astype(jnp.float32)[:, None] * freq[None, :]
    angle = jnp.concatenate([angle, angle], axis=1)
    return (jnp.cos(angle), jnp.sin(angle))

def rotate(values, cosine, sine):
    half = values.shape[-1] // 2
    turned = jnp.concatenate([-values[..., half:], values[..., :half]], axis=-1)
    return values * cosine[:, None, :] + turned * sine[:, None, :]

def head_norm(values, gain):
    return values * lax.rsqrt(lax.optimization_barrier(jnp.mean(values * values, axis=-1, keepdims=True)) + EPS) * gain

def width_norm(values, gain):
    return values * lax.rsqrt(lax.optimization_barrier(jnp.mean(values * values, axis=1, keepdims=True)) + EPS) * gain

def attention(query, keys, values, segment):
    item_count = query.shape[0]
    block = min(512, item_count)
    groups = query.shape[1] // keys.shape[1]
    scale = 1.0 / math.sqrt(query.shape[2])
    key_places = jnp.arange(item_count, dtype=jnp.int32)
    query_blocks = query.reshape(item_count // block, block, keys.shape[1], groups, query.shape[2])
    first_rows = jnp.arange(item_count // block, dtype=jnp.int32) * block

    def one_block(inputs):
        rows, first = inputs
        places = first + jnp.arange(block, dtype=jnp.int32)
        own = lax.dynamic_slice_in_dim(segment, first, block, 0)
        scores = reduced_backward(scale * jnp.einsum('qhgd,khd->hgqk', rows, keys, precision=HIGH))
        allowed = (key_places[None, :] <= places[:, None]) & (segment[None, :] == own[:, None])
        scores = jnp.where(allowed, scores, NEGATIVE)
        top = lax.optimization_barrier(jnp.max(scores, axis=-1, keepdims=True))
        total = top + jnp.log(lax.optimization_barrier(jnp.sum(jnp.exp(scores - top), axis=-1, keepdims=True)))
        weights = low(jnp.exp(scores - total))
        mixed = jnp.einsum('hgqk,khd->qhgd', weights, values, precision=HIGH)
        return mixed.reshape(block, -1)
    blocks = lax.map(jax.checkpoint(one_block), (query_blocks, first_rows))
    return blocks.reshape(item_count, -1)

def layer(inputs, masters, gains, segment, position):
    query_w, keyval_w, output_w, gateup_w, down_w = [low(weight) for weight in masters]
    norm_g, head_g = gains
    item_count = inputs.shape[0]
    normed = low(width_norm(inputs, norm_g[0]))
    query_raw = reduced_backward(jnp.dot(normed, query_w, precision=HIGH)).reshape(item_count, HQ, HEAD_SIZE)
    key_value_pair = jnp.einsum('td,dsk->tsk', normed, keyval_w, precision=HIGH)
    key_unrotated = reduced_backward(key_value_pair[:, 0]).reshape(item_count, KEY_VALUE_HEADS, HEAD_SIZE)
    value_unprojected = reduced_backward(key_value_pair[:, 1]).reshape(item_count, KEY_VALUE_HEADS, HEAD_SIZE)
    cosine, sine = rope_tables(position)
    query = low(rotate(head_norm(query_raw, head_g[0]), cosine, sine))
    keys = low(rotate(head_norm(key_unrotated, head_g[1]), cosine, sine))
    values = low(value_unprojected)
    mixed = low(reduced_backward(attention(query, keys, values, segment)))
    hidden = inputs + reduced_backward(jnp.dot(mixed, output_w, precision=HIGH))
    normed_two = low(width_norm(hidden, norm_g[1]))
    gateup = jnp.einsum('td,dsf->tsf', normed_two, gateup_w, precision=HIGH)
    gate = reduced_backward(gateup[:, 0])
    up = reduced_backward(gateup[:, 1])
    active = low(jax.nn.silu(gate) * up)
    return hidden + reduced_backward(jnp.dot(active, down_w, precision=HIGH))

def adamw(weight, moment, second, grad, rate, decay):
    moment_new = BETA_ONE * moment + (1.0 - BETA_ONE) * grad
    second_new = BETA_TWO * second + (1.0 - BETA_TWO) * grad * grad
    first_hat = moment_new / (1.0 - BETA_ONE ** STEP)
    second_hat = second_new / (1.0 - BETA_TWO ** STEP)
    weight_new = weight - rate * (first_hat / (jnp.sqrt(second_hat) + ADAM_EPS) + decay * weight)
    return (moment_new, second_new, weight_new)

def add_up(first, second):
    return first + second

def reference(tokens, cotangent, seq_lens, query_weight, query_moment, query_second, key_value_master_weight, key_value_first_moment, key_value_second_moment, output_weight, output_moment, output_second, gateup_weight, gateup_moment, gateup_second, down_weight, down_moment, down_second, norm_gains, norm_moment, norm_second, head_gains, head_moment, head_second):
    groups = seq_lens.shape[0]
    inputs = tokens.astype(jnp.float32).reshape(groups, TOK_GRP, MODEL_WIDTH)
    backs = cotangent.astype(jnp.float32).reshape(groups, TOK_GRP, MODEL_WIDTH)
    masters = (query_weight, key_value_master_weight, output_weight, gateup_weight, down_weight)
    gains = (norm_gains, head_gains)

    def one_group(totals, pieces):
        group_in, group_back, lengths = pieces
        segment, position = token_layout(lengths, TOK_GRP)
        valid = (segment < SEQS).astype(jnp.float32)

        def forward(values, weights, scales):
            return layer(values, weights, scales, segment, position)
        output, pull = jax.vjp(forward, group_in, masters, gains)
        input_grad, weight_grads, gain_grads = pull(group_back * valid[:, None])
        totals = jax.tree.map(add_up, totals, (weight_grads, gain_grads))
        return (totals, (output, input_grad))
    start = jax.tree.map(jnp.zeros_like, (masters, gains))
    (weight_grads, gain_grads), (outputs, input_grads) = lax.scan(one_group, start, (inputs, backs, seq_lens))
    query_new = adamw(query_weight, query_moment, query_second, weight_grads[0], RATES[0], DECAY)
    keyval_new = adamw(key_value_master_weight, key_value_first_moment, key_value_second_moment, weight_grads[1], RATES[1], DECAY)
    output_new = adamw(output_weight, output_moment, output_second, weight_grads[2], RATES[2], DECAY)
    gateup_new = adamw(gateup_weight, gateup_moment, gateup_second, weight_grads[3], RATES[3], DECAY)
    down_new = adamw(down_weight, down_moment, down_second, weight_grads[4], RATES[4], DECAY)
    norm_new = adamw(norm_gains, norm_moment, norm_second, gain_grads[0], GAIN_RATE, 0.0)
    head_new = adamw(head_gains, head_moment, head_second, gain_grads[1], GAIN_RATE, 0.0)
    return (outputs.reshape(TOKEN_SLOTS, MODEL_WIDTH), input_grads.reshape(TOKEN_SLOTS, MODEL_WIDTH), query_new[0], query_new[1], query_new[2], keyval_new[0], keyval_new[1], keyval_new[2], output_new[0], output_new[1], output_new[2], gateup_new[0], gateup_new[1], gateup_new[2], down_new[0], down_new[1], down_new[2], norm_new[0], norm_new[1], norm_new[2], head_new[0], head_new[1], head_new[2])
```

```python
import functools
import math

import jax
import jax.numpy as jnp
from jax import lax
from jax.experimental import pallas as pl
from jax.experimental.pallas import tpu as pltpu
from jax.sharding import PartitionSpec as P

MODEL_WIDTH = 2048
HEAD_SIZE = 128
SEQS = 4
STEP = 10

EPS = 1e-06
THETA = 1000000.0
NEGATIVE = -1e30
BETA_ONE = 0.9
BETA_TWO = 0.95
ADAM_EPS = 1e-08
DECAY = 0.1
RATES = (0.066, 0.066, 0.5, 0.066, 0.04)
GAIN_RATE = 0.6
BF = jnp.bfloat16
F32 = jnp.float32
SCALE = 1.0 / math.sqrt(HEAD_SIZE)


def dot(a, b, kind="nn"):
    dims = {"nn": ((1,), (0,)), "nt": ((1,), (1,)), "tn": ((0,), (0,))}[kind]
    return lax.dot_general(a, b, (dims, ((), ())), preferred_element_type=F32)


def token_layout(lengths, item_count):
    ends = jnp.cumsum(lengths)
    places = jnp.arange(item_count, dtype=jnp.int32)
    segment = jnp.sum((places[:, None] >= ends[None, :]).astype(jnp.int32), axis=1)
    starts = jnp.concatenate([ends - lengths, ends[-1:]])
    labels = jnp.arange(starts.shape[0], dtype=jnp.int32)
    begin = jnp.sum(jnp.where(segment[:, None] == labels[None, :], starts[None, :], 0), axis=1)
    return (segment, places - begin)


def rope_tables(position):
    half = HEAD_SIZE // 2
    freq = jnp.exp(jnp.arange(half, dtype=F32) * (-2.0 * math.log(THETA) / HEAD_SIZE))
    angle = position.astype(F32)[:, None] * freq[None, :]
    angle = jnp.concatenate([angle, angle], axis=1)
    return (jnp.cos(angle), jnp.sin(angle))


def block_masks(own_col, own_row, prev_row, later):
    rows = own_col.shape[0]
    r = lax.broadcasted_iota(jnp.int32, (rows, rows), 0)
    c = lax.broadcasted_iota(jnp.int32, (rows, rows), 1)
    own = (c <= r) & (own_col == own_row)
    prev = (own_col == prev_row) & (later > 0)
    return own, prev


def forward_kernel(later, own_col, own_row, prev_row, q, k, v, kp, vp, o, lse):
    own, prev = block_masks(own_col[...], own_row[...], prev_row[...], later[0])
    s_own = jnp.where(own, dot(q[...], k[...], "nt") * SCALE, NEGATIVE)
    s_prev = jnp.where(prev, dot(q[...], kp[...], "nt") * SCALE, NEGATIVE)
    top = jnp.maximum(
        jnp.max(s_own, axis=1, keepdims=True), jnp.max(s_prev, axis=1, keepdims=True)
    )
    total = jnp.sum(jnp.exp(s_own - top), axis=1, keepdims=True) + jnp.sum(
        jnp.exp(s_prev - top), axis=1, keepdims=True
    )
    logsum = top + jnp.log(total)
    p_own = jnp.exp(s_own - logsum).astype(BF)
    p_prev = jnp.exp(s_prev - logsum).astype(BF)
    o[...] = (dot(p_own, v[...]) + dot(p_prev, vp[...])).astype(BF)
    lse[0] = logsum


def attention_forward(later, own_col, own_row, prev_row, q, kv, before, after):
    rows, width = q.shape
    heads = width // HEAD_SIZE
    groups = 2 * width // kv.shape[1]
    inputs = (later, own_col, own_row, prev_row, q, kv, kv, before, before)

    def kernel(*refs):
        forward_kernel(*refs[: len(inputs)], *refs[len(inputs) + len(after) :])

    mine = pl.BlockSpec((rows, HEAD_SIZE), lambda h: (0, h))
    key = pl.BlockSpec((rows, HEAD_SIZE), lambda h: (0, 2 * (h // groups)))
    value = pl.BlockSpec((rows, HEAD_SIZE), lambda h: (0, 2 * (h // groups) + 1))
    column = pl.BlockSpec((rows, 1), lambda h: (0, 0))
    line = pl.BlockSpec((1, rows), lambda h: (0, 0))
    return pl.pallas_call(
        kernel,
        grid=(heads,),
        in_specs=[pl.BlockSpec(memory_space=pltpu.SMEM), column, line, line, mine]
        + [key, value] * 2
        + [pl.BlockSpec(memory_space=pl.ANY)] * len(after),
        out_specs=[mine, pl.BlockSpec((1, rows, 1), lambda h: (h, 0, 0))],
        out_shape=[
            jax.ShapeDtypeStruct((rows, width), BF),
            jax.ShapeDtypeStruct((heads, rows, 1), F32),
        ],
        compiler_params=pltpu.CompilerParams(vmem_limit_bytes=32 * 2**20),
    )(*inputs, *after)


def backward_kernel(
    later, own_col, own_row, prev_row, q, k, v, kp, vp, do, lse, dq, dk, dv, far, total
):
    own, prev = block_masks(own_col[...], own_row[...], prev_row[...], later[0])
    logsum = lse[0]
    p_own = jnp.exp(jnp.where(own, dot(q[...], k[...], "nt") * SCALE, NEGATIVE) - logsum)
    p_prev = jnp.exp(jnp.where(prev, dot(q[...], kp[...], "nt") * SCALE, NEGATIVE) - logsum)
    d_own = dot(do[...], v[...], "nt")
    d_prev = dot(do[...], vp[...], "nt")
    delta = jnp.sum(p_own * d_own, axis=1, keepdims=True) + jnp.sum(
        p_prev * d_prev, axis=1, keepdims=True
    )
    g_own = (p_own * (d_own - delta)).astype(BF)
    g_prev = (p_prev * (d_prev - delta)).astype(BF)
    dq[...] = (dot(g_own, k[...]) + dot(g_prev, kp[...])) * SCALE
    near = ((dk, dot(g_own, q[...], "tn") * SCALE), (dv, dot(p_own.astype(BF), do[...], "tn")))
    dkp = dot(g_prev, q[...], "tn") * SCALE
    dvp = dot(p_prev.astype(BF), do[...], "tn")
    group = pl.program_id(1)

    @pl.when(group == 0)
    def _():
        for ref, value in near:
            ref[...] = value
        total[:, :HEAD_SIZE] = dkp
        total[:, HEAD_SIZE:] = dvp

    @pl.when(group > 0)
    def _():
        for ref, value in near:
            ref[...] += value
        total[:, :HEAD_SIZE] += dkp
        total[:, HEAD_SIZE:] += dvp

    @pl.when(group == pl.num_programs(1) - 1)
    def _():
        far[...] = total[...].astype(BF)


def attention_backward(later, own_col, own_row, prev_row, q, kv, before, do, lse, after):
    rows, width = q.shape
    kv_heads = kv.shape[1] // (2 * HEAD_SIZE)
    groups = 2 * width // kv.shape[1]
    inputs = (later, own_col, own_row, prev_row, q, kv, kv, before, before, do, lse)

    def kernel(*refs):
        backward_kernel(*refs[: len(inputs)], *refs[len(inputs) + len(after) :])

    mine = pl.BlockSpec((rows, HEAD_SIZE), lambda h, g: (0, h * groups + g))
    shared = pl.BlockSpec((rows, HEAD_SIZE), lambda h, g: (0, h))
    key = pl.BlockSpec((rows, HEAD_SIZE), lambda h, g: (0, 2 * h))
    value = pl.BlockSpec((rows, HEAD_SIZE), lambda h, g: (0, 2 * h + 1))
    column = pl.BlockSpec((rows, 1), lambda h, g: (0, 0))
    line = pl.BlockSpec((1, rows), lambda h, g: (0, 0))
    near = jax.ShapeDtypeStruct((rows, kv_heads * HEAD_SIZE), F32)
    return pl.pallas_call(
        kernel,
        grid=(kv_heads, groups),
        in_specs=[pl.BlockSpec(memory_space=pltpu.SMEM), column, line, line, mine]
        + [key, value] * 2
        + [mine, pl.BlockSpec((1, rows, 1), lambda h, g: (h * groups + g, 0, 0))]
        + [pl.BlockSpec(memory_space=pl.ANY)] * len(after),
        out_specs=[mine, shared, shared, pl.BlockSpec((rows, 2 * HEAD_SIZE), lambda h, g: (0, h))],
        out_shape=[
            jax.ShapeDtypeStruct((rows, width), F32),
            near,
            near,
            jax.ShapeDtypeStruct((rows, kv.shape[1]), BF),
        ],
        scratch_shapes=[pltpu.VMEM((rows, 2 * HEAD_SIZE), F32)],
        compiler_params=pltpu.CompilerParams(vmem_limit_bytes=32 * 2**20),
    )(*inputs, *after)


def call(
    kernel,
    out,
    inputs,
    scalars=(),
    grid=(1,),
    in_specs=None,
    out_specs=None,
    scratch=(),
    vmem=20,
    after=(),
    alias=None,
    hbm=4 * 2**20,
):
    def whole(a):
        return pl.BlockSpec(a.shape, lambda *_: (0,) * len(a.shape))

    in_specs = [s or whole(a) for s, a in zip(in_specs or [None] * len(inputs), inputs)]
    out_specs = [s or whole(a) for s, a in zip(out_specs or [None] * len(out), out)]
    alias = alias or {}

    def held(a, least):
        if a.size * a.dtype.itemsize < least:
            return a
        return pltpu.with_memory_space_constraint(a, pltpu.HBM)

    inputs = [held(a, hbm) for a in inputs]
    after = [held(a, hbm) for a in alias.values()] + [held(a, 2**20) for a in after]
    first = len(scalars) + len(inputs)

    def run(*refs):
        kernel(*refs[:first], *refs[first + len(after) :])

    return pl.pallas_call(
        run,
        grid_spec=pltpu.PrefetchScalarGridSpec(
            num_scalar_prefetch=len(scalars),
            grid=grid,
            in_specs=in_specs + [pl.BlockSpec(memory_space=pl.ANY)] * len(after),
            out_specs=out_specs,
            scratch_shapes=list(scratch),
        ),
        out_shape=list(out),
        compiler_params=pltpu.CompilerParams(vmem_limit_bytes=vmem * 2**20),
        input_output_aliases={first + i: place for i, place in enumerate(alias)},
        cost_estimate=pl.CostEstimate(flops=0, bytes_accessed=0, transcendentals=0),
    )(*[s.astype(jnp.int32).reshape(1) for s in scalars], *inputs, *after)


def in_hbm(dims, dtype):
    return pltpu.HBM(tuple(dims), dtype)


def shape(dims, dtype):
    return jax.ShapeDtypeStruct(tuple(dims), dtype)


def blocked(dims, index):
    return pl.BlockSpec(dims, index)


COLUMNS = 512


def other(index, k):
    return lax.bitwise_xor(index, jnp.int32(k))


def partners(z, size):
    return lax.bitwise_xor(z, jnp.arange(size, dtype=jnp.int32))


def ahead(index, k, size):
    return lax.bitwise_and(index + jnp.int32(k), jnp.int32(size - 1))


def behind(index, k, size):
    return lax.bitwise_and(index + jnp.int32(size) - jnp.int32(k), jnp.int32(size - 1))


def out_rows(ref):
    cols, dp, rows, width = ref.shape
    size = 4
    if dp == size:
        return ref[...].reshape(cols * dp * rows, width)
    per = dp // size
    order = [(c, q * per + r) for c in range(cols) for r in range(per) for q in range(size)]
    return jnp.concatenate([ref[c, d] for c, d in order])


def assemble(pieces, z, rolled, direct, after=()):
    def place_of(z, k):
        return behind(z, k, len(pieces)) if direct else other(z, k)

    size, dp = lax.axis_size("row"), lax.axis_size("dp")
    rows, width = pieces[0].shape
    rest = width // dp
    block = rows // size
    if rest % 128:
        out = jnp.stack([p.reshape(rows, dp, rest) for p in pieces], axis=2)
        order = behind(z, jnp.arange(size), size) if direct else partners(z, size)
        out = jnp.take(out, order, axis=2).reshape(rows, -1)
        if rolled:
            out = jnp.concatenate(
                [
                    lax.dynamic_slice_in_dim(out, other(z, k) * block, block, 0)
                    for k in range(size)
                ]
            )
        return out

    def kernel(z, *refs):
        out = refs[-1]
        for k in range(size):
            piece = refs[k][...]
            for d in range(dp):
                place = pl.multiple_of((d * size + place_of(z[0], k)) * rest, rest)
                out[:, pl.ds(place, rest)] = piece[:, d * rest : (d + 1) * rest]

    def index(i, z):
        return (lax.bitwise_xor(z[0], jnp.int32(i)) if rolled else i, 0)

    return call(
        kernel,
        [shape((rows, size * width), pieces[0].dtype)],
        list(pieces),
        [z],
        (size,),
        [blocked((block, width), index)] * size,
        [blocked((block, size * width), lambda i, z: (i, 0))],
        after=after,
    )[0]


def take_apart(full, z, rolled, after=()):
    size, dp = lax.axis_size("row"), lax.axis_size("dp")
    rows, width = full.shape
    rest = width // (size * dp)
    block = rows // size
    if rest % 128:
        if rolled:
            full = jnp.concatenate(
                [
                    lax.dynamic_slice_in_dim(full, other(z, i) * block, block, 0)
                    for i in range(size)
                ]
            )
        split = full.reshape(rows, dp, size, rest)
        split = jnp.take(split, partners(z, size), axis=2)
        return [split[:, :, k].reshape(rows, dp * rest) for k in range(size)]

    def kernel(z, full, *outs):
        for k in range(size):
            for d in range(dp):
                place = pl.multiple_of((d * size + other(z[0], k)) * rest, rest)
                outs[k][:, d * rest : (d + 1) * rest] = full[:, pl.ds(place, rest)]

    def index(i, z):
        return (lax.bitwise_xor(z[0], jnp.int32(i)) if rolled else i, 0)

    return call(
        kernel,
        [shape((rows, dp * rest), full.dtype)] * size,
        [full],
        [z],
        (size,),
        [blocked((block, width), lambda i, z: (i, 0))],
        [blocked((block, dp * rest), index)] * size,
        after=after,
    )


def project_kernel(x, gain, weight, cosine, sine, head_gain, a, scale, qr, kr, qn, kv):
    rows = x.shape[0]
    heads = qr.shape[1] // HEAD_SIZE
    kv_heads = kr.shape[1] // HEAD_SIZE

    @pl.when(pl.program_id(0) == 0)
    def _():
        for first in range(0, rows, 128):
            s = slice(first, first + 128)
            xf = x[s, :].astype(F32)
            r = lax.rsqrt(jnp.mean(xf * xf, axis=1, keepdims=True) + EPS)
            a[s, :] = (xf * r * gain[...]).astype(BF)
            scale[s, :] = r

    raw = dot(a[...], weight[0].reshape(MODEL_WIDTH, COLUMNS))

    def turn(values, gains):
        normed = (
            values
            * lax.rsqrt(jnp.mean(values * values, axis=-1, keepdims=True) + EPS)
            * gains
        )
        half = HEAD_SIZE // 2
        turned = jnp.concatenate([-normed[:, half:], normed[:, :half]], axis=-1)
        return (normed * cosine[...] + turned * sine[...]).astype(BF)

    for h in range(heads):
        s = slice(h * HEAD_SIZE, (h + 1) * HEAD_SIZE)
        qr[:, s] = raw[:, s]
        qn[:, s] = turn(raw[:, s], head_gain[0:1, :])
    first = heads * HEAD_SIZE
    for h in range(kv_heads):
        s = slice(h * HEAD_SIZE, (h + 1) * HEAD_SIZE)
        values = raw[:, first + h * HEAD_SIZE : first + (h + 1) * HEAD_SIZE]
        kr[:, s] = values
        kv[:, s] = turn(values, head_gain[1:2, :])
    kv[:, kv_heads * HEAD_SIZE :] = raw[:, first + kv_heads * HEAD_SIZE :].astype(BF)


def project(x, gain, weight, cosine, sine, head_gain, head_width, kv_width, after):
    rows = x.shape[0]
    cols, dp, _, width = weight.shape
    q = blocked((rows, head_width), lambda c: (0, c))
    k = blocked((rows, kv_width), lambda c: (0, c))
    return call(
        project_kernel,
        [
            shape(x.shape, BF),
            shape((rows, 1), F32),
            shape((rows, cols * head_width), F32),
            shape((rows, cols * kv_width), F32),
            shape((rows, cols * head_width), BF),
            shape((rows, 2 * cols * kv_width), BF),
        ],
        [x, gain, weight, cosine, sine, head_gain],
        (),
        (cols,),
        [None, None, blocked((1, dp, MODEL_WIDTH // dp, width), lambda c: (c, 0, 0, 0)), None, None, None],
        [None, None, q, k, q, blocked((rows, 2 * kv_width), lambda c: (0, c))],
        after=after,
    )


def mixed_parts(mixed, weight, z, base, after):
    size = lax.axis_size("row")
    cols, dp, total_rows, _ = weight.shape
    rows = mixed.shape[0]
    inner = mixed.shape[1] // (cols * dp)
    part = rows // size
    steps = MODEL_WIDTH // COLUMNS

    def kernel(z, mixed, weight, *refs):
        *outs, total = refs
        total[...] = dot(mixed[...], out_rows(weight))
        for k in range(size):
            first = pl.multiple_of(other(z[0], k) * part, part)
            outs[k][...] = total[pl.ds(first, part), :].astype(outs[k].dtype)

    return call(
        kernel,
        [shape((part, MODEL_WIDTH), BF if k else F32) for k in range(size)],
        [mixed, weight],
        [z],
        (steps,),
        [None, blocked((cols, dp, inner, COLUMNS), lambda c, z: (0, 0, base + c, 0))],
        [blocked((part, COLUMNS), lambda c, z: (0, c))] * size,
        scratch=[pltpu.VMEM((rows, COLUMNS), F32)],
        after=after,
    )


def mixed_back(chunks, weight, z, base, inner, after):
    size = len(chunks)
    cols, dp, _, _ = weight.shape
    part, width = chunks[0].shape
    rows = size * part
    heads = cols * dp * inner
    steps = width // COLUMNS

    def kernel(z, *refs):
        *ins, weight, full, out, total = refs
        for k in range(size):
            first = pl.multiple_of(other(z[0], k) * part, part)
            full[pl.ds(first, part), :] = ins[k][...]
        term = dot(full[...], out_rows(weight), "nt")
        c = pl.program_id(0)

        @pl.when(c == 0)
        def _():
            total[...] = term

        @pl.when(c > 0)
        def _():
            total[...] += term

        @pl.when(c == steps - 1)
        def _():
            out[...] = total[...].astype(BF)

    return call(
        kernel,
        [shape((rows, width), BF), shape((rows, heads), BF)],
        list(chunks) + [weight],
        [z],
        (steps,),
        [blocked((part, COLUMNS), lambda c, z: (0, c))] * size
        + [blocked((cols, dp, inner, COLUMNS), lambda c, z: (0, 0, base + c, 0))],
        [blocked((rows, COLUMNS), lambda c, z: (0, c)), None],
        scratch=[pltpu.VMEM((rows, heads), F32)],
        after=after,
    )


def masked(values, valid, after):
    def kernel(values, valid, out):
        out[...] = jnp.where(valid[...] > 0, values[...], jnp.zeros_like(values))

    return call(kernel, [shape(values.shape, values.dtype)], [values, valid], after=after)[0]


def add_parts(parts, dtype, after=()):
    def kernel(*refs):
        total = refs[0][...].astype(F32)
        for ref in refs[1:-1]:
            total = total + ref[...].astype(F32)
        refs[-1][...] = total.astype(dtype)

    return call(kernel, [shape(parts[0].shape, dtype)], list(parts), after=after)[0]


def hidden_norm(parts, x, gain, z, after=()):
    rows, width = parts[0].shape

    def kernel(z, *refs):
        *ps, x, gain, h, scale, a = refs
        total = x[...].astype(F32)
        for p in ps:
            total = total + p[...].astype(F32)
        r = lax.rsqrt(jnp.mean(total * total, axis=1, keepdims=True) + EPS)
        h[...] = total
        scale[...] = r
        a[...] = (total * r * gain[...]).astype(BF)

    return call(
        kernel,
        [shape((rows, width), F32), shape((rows, 1), F32), shape((rows, width), BF)],
        list(parts) + [x, gain],
        [z],
        (1,),
        [None] * len(parts) + [blocked((rows, width), lambda i, z: (z[0], 0)), None],
        after=after,
    )


def gateup_chunk(parts, weight, grad, index, hidden, news):
    part, width = parts[0].shape
    rows = part * len(parts)
    cols, dp, _, _ = weight.shape
    steps = 2 * hidden // (cols * COLUMNS)
    half = COLUMNS // 2

    def kernel(*refs):
        *ins, weight, grad, act, out, a = refs

        @pl.when((pl.program_id(0) == 0) & (pl.program_id(1) == 0))
        def _():
            for i, ref in enumerate(ins):
                a[i * part : (i + 1) * part, :] = ref[...]

        p = dot(a[...], weight[0].reshape(width, COLUMNS))
        for j in range(half // 128):
            gate, up = p[:, j * 256 : j * 256 + 128], p[:, j * 256 + 128 : j * 256 + 256]
            s = slice(j * 128, (j + 1) * 128)
            spread = 1.0 / (1.0 + jnp.exp(-gate))
            silu = gate * spread
            act[:, s] = (silu * up).astype(BF)
            g = grad[:, s]
            out[:, j * 256 : j * 256 + 128] = (g * up * (spread + silu * (1.0 - spread))).astype(BF)
            out[:, j * 256 + 128 : j * 256 + 256] = (g * silu).astype(BF)

    def place(c, t):
        return (index, c * steps + t)

    total = grad.shape[0]
    return call(
        kernel,
        [shape((total, hidden), BF), shape((total, 2 * hidden), BF)],
        list(parts) + [weight, grad],
        (),
        (cols, steps),
        [None] * len(parts)
        + [
            blocked((1, dp, width // dp, COLUMNS), lambda c, t: (c, 0, t, 0)),
            blocked((rows, half), place),
        ],
        [blocked((rows, half), place), blocked((rows, COLUMNS), place)],
        scratch=[pltpu.VMEM((rows, width), BF)],
        alias=dict(enumerate(news or ())),
    )


def gateup_back(grad, weight, index, kinds):
    cols, dp, _, _ = weight.shape
    both = grad.shape[1]
    block = MODEL_WIDTH // dp
    terms = both // COLUMNS
    per = terms // cols
    part = grad.shape[0] // 4
    rows = part * len(kinds)

    def kernel(grad, weight, *outs):
        total = None
        for t in range(terms):
            right = weight[t // per, 0, (t % per) * block : (t % per + 1) * block, :]
            term = dot(grad[:, t * COLUMNS : (t + 1) * COLUMNS], right, "nt")
            total = term if total is None else total + term
        for i, (out, kind) in enumerate(zip(outs, kinds)):
            out[...] = total[i * part : (i + 1) * part, :].astype(kind)

    return call(
        kernel,
        [shape((part, MODEL_WIDTH), kind) for kind in kinds],
        [grad, weight],
        (),
        (dp,),
        [
            blocked((rows, both), lambda n: (index, 0)),
            blocked((cols, 1, per * block, COLUMNS), lambda n: (0, n, 0, 0)),
        ],
        [blocked((part, block), lambda n: (0, n))] * len(kinds),
    )


def down_back(out_low, weight, base, inner, after):
    cols, dp, _, _ = weight.shape
    rows, width = out_low.shape
    hidden = cols * dp * inner

    def kernel(low, weight, out):
        term = dot(low[...], out_rows(weight), "nt")

        @pl.when(pl.program_id(0) == 0)
        def _():
            out[...] = term

        @pl.when(pl.program_id(0) > 0)
        def _():
            out[...] += term

    return call(
        kernel,
        [shape((rows, hidden), F32)],
        [out_low, weight],
        (),
        (width // COLUMNS,),
        [
            blocked((rows, COLUMNS), lambda c: (0, c)),
            blocked((cols, dp, inner, COLUMNS), lambda c: (0, 0, base + c, 0)),
        ],
        [None],
        vmem=24,
        after=after,
    )[0]


def down_forward(active, hidden, weight, base, inner, after):
    cols, dp, _, _ = weight.shape
    rows, width = active.shape
    part = hidden.shape[0]

    def kernel(active, hidden, weight, out):
        p = dot(active[...], out_rows(weight))
        out[:part, :] = (p[:part, :] + hidden[...]).astype(BF)
        out[part:, :] = p[part:, :].astype(BF)

    return call(
        kernel,
        [shape((rows, MODEL_WIDTH), BF)],
        [active, hidden, weight],
        (),
        (MODEL_WIDTH // COLUMNS,),
        [
            None,
            blocked((part, COLUMNS), lambda c: (0, c)),
            blocked((cols, dp, inner, COLUMNS), lambda c: (0, 0, base + c, 0)),
        ],
        [blocked((rows, COLUMNS), lambda c: (0, c))],
        after=after,
    )[0]


def hidden_back(parts, h, scale, gain, out_low, after):
    rows, width = h.shape

    def kernel(*refs):
        *ps, h, scale, gain, dy, dh, low, gain_grad = refs
        grad = ps[0][...].astype(F32)
        for p in ps[1:]:
            grad = grad + p[...].astype(F32)
        hidden, r = h[...], scale[...]
        weighted = grad * gain[...]
        inner = jnp.sum(weighted * hidden, axis=1, keepdims=True)
        total = dy[...].astype(F32) + r * weighted - (r * r * r * inner / MODEL_WIDTH) * hidden
        dh[...] = total
        low[...] = total.astype(BF)
        gain_grad[...] = jnp.sum(grad * hidden * r, axis=0, keepdims=True)

    return call(
        kernel,
        [shape((rows, width), F32), shape((rows, width), BF), shape((1, width), F32)],
        list(parts) + [h, scale, gain, out_low],
        (),
        (1,),
        [None] * (len(parts) + 3) + [blocked((rows, width), lambda i: (0, 0))],
        after=after,
    )


def heads_back_kernel(
    qr, kr, dqn, dkn, dv, far, cosine, sine, head_gain, out, gain_grad
):
    heads = qr.shape[1] // HEAD_SIZE
    kv_heads = kr.shape[1] // HEAD_SIZE
    half = HEAD_SIZE // 2

    def back(raw, grad, gains):
        turned = grad * sine[...]
        turned = jnp.concatenate([turned[:, half:], -turned[:, :half]], axis=-1)
        g = grad * cosine[...] + turned
        r = lax.rsqrt(jnp.mean(raw * raw, axis=-1, keepdims=True) + EPS)
        weighted = g * gains
        inner = jnp.sum(weighted * raw, axis=-1, keepdims=True)
        low = (r * weighted - (r * r * r * inner / HEAD_SIZE) * raw).astype(BF)
        return low, jnp.sum(g * raw * r, axis=0, keepdims=True)

    @pl.when(pl.program_id(0) == 0)
    def _():
        gain_grad[...] = jnp.zeros_like(gain_grad)

    for h in range(heads):
        s = slice(h * HEAD_SIZE, (h + 1) * HEAD_SIZE)
        low, total = back(qr[:, s], dqn[:, s], head_gain[0:1, :])
        out[:, s] = low
        gain_grad[0:1, :] += total
    first = heads * HEAD_SIZE
    for h in range(kv_heads):
        s = slice(h * HEAD_SIZE, (h + 1) * HEAD_SIZE)
        low, total = back(kr[:, s], dkn[:, s] + far[:, s].astype(F32), head_gain[1:2, :])
        out[:, first + h * HEAD_SIZE : first + (h + 1) * HEAD_SIZE] = low
        gain_grad[1:2, :] += total
    first += kv_heads * HEAD_SIZE
    out[:, first:] = (dv[...] + far[:, kv_heads * HEAD_SIZE :].astype(F32)).astype(BF)


def heads_back(qr, kr, dqn, dkn, dv, far, cosine, sine, head_gain, cols, after):
    rows = qr.shape[0]
    head_width, kv_width = qr.shape[1] // cols, kr.shape[1] // cols
    q = blocked((rows, head_width), lambda c: (0, c))
    k = blocked((rows, kv_width), lambda c: (0, c))
    far_kv = blocked((rows, 2 * kv_width), lambda c: (0, c))
    width = head_width + 2 * kv_width
    return call(
        heads_back_kernel,
        [shape((rows, cols * width), BF), shape((2, HEAD_SIZE), F32)],
        [qr, kr, dqn, dkn, dv, far, cosine, sine, head_gain],
        (),
        (cols,),
        [q, k, q, k, k, far_kv, None, None, None],
        [blocked((rows, width), lambda c: (0, c)), None],
        after=after,
    )


def input_back(grads, weight, x, scale, gain, dh, z, after):
    cols, steps, _, width = weight.shape
    rows = grads.shape[0]
    model = MODEL_WIDTH
    part = dh.shape[0]

    def kernel(z, grads, weight, x, scale, gain, dh, out, c1, gain_grad):
        total = dot(grads[:, :width], weight[0, 0], "nt")
        for c in range(1, cols):
            total = total + dot(grads[:, c * width : (c + 1) * width], weight[c, 0], "nt")
        r = scale[...]
        xf = x[...].astype(F32)
        weighted = total * gain[...]
        moved = weighted * xf
        gain_grad[...] = jnp.sum(total * xf * r, axis=0, keepdims=True)
        out[...] = (r * weighted).astype(BF)
        first = pl.multiple_of(z[0] * part, part)
        own = pl.ds(first, part)
        out[own, :] = (out[own, :].astype(F32) + dh[...]).astype(BF)

        @pl.when(pl.program_id(0) == 0)
        def _():
            c1[...] = jnp.zeros_like(c1)

        c1[...] += jnp.sum(moved, axis=1, keepdims=True)

    block = model // steps
    wide = blocked((rows, block), lambda n, z: (0, n))
    return call(
        kernel,
        [shape((rows, model), BF), shape((rows, 1), F32), shape((1, model), F32)],
        [grads, weight, x, scale, gain, dh],
        [z],
        (steps,),
        [
            None,
            blocked((cols, 1, block, width), lambda n, z: (0, n, 0, 0)),
            wide,
            None,
            blocked((1, block), lambda n, z: (0, n)),
            blocked((part, block), lambda n, z: (0, n)),
        ],
        [wide, None, blocked((1, block), lambda n, z: (0, n))],
        after=after,
    )


def weight_grads(lefts, right, out_left, out_right, cols, after=()):
    size, dp = lax.axis_size("row"), lax.axis_size("dp")
    rows = right.shape[0]
    block = MODEL_WIDTH // dp
    n = right.shape[1] // cols
    part = rows // len(lefts)
    m = out_left.shape[1] // cols
    inner = m // dp
    terms = n // COLUMNS
    total = terms * block + MODEL_WIDTH // COLUMNS * inner

    def kernel(*refs):
        *ins, right, out_left, out_right, out = refs
        left = jnp.concatenate([ref[...] for ref in ins]) if len(ins) > 1 else ins[0][...]
        for t in range(terms):
            term = dot(left, right[:, t * COLUMNS : (t + 1) * COLUMNS], "tn")
            out[0, 0, t * block : (t + 1) * block, :] = term.astype(BF)
        for d in range(dp):
            q, r = d // (dp // size), d % (dp // size)
            first = (r * size + q) * inner

            @pl.when(pl.program_id(1) == d)
            def _():
                term = dot(out_left[:, first : first + inner], out_right[...], "tn").astype(BF)
                for c in range(MODEL_WIDTH // COLUMNS):
                    place = terms * block + c * inner
                    piece = term[:, c * COLUMNS : (c + 1) * COLUMNS]
                    out[0, 0, place : place + inner, :] = piece

    return call(
        kernel,
        [in_hbm((cols, dp, total, COLUMNS), BF)],
        list(lefts) + [right, out_left, out_right],
        (),
        (cols, dp),
        [blocked((part, block), lambda c, d: (0, d))] * len(lefts)
        + [
            blocked((rows, n), lambda c, d: (0, c)),
            blocked((rows, m), lambda c, d: (0, c)),
            None,
        ],
        [blocked((1, 1, total, COLUMNS), lambda c, d: (c, d, 0, 0))],
        after=after,
        vmem=28,
    )[0]


def swap(value, axis, step):
    return lax.ppermute(value, axis, [(i, i ^ step) for i in range(lax.axis_size(axis))])


def gather_pieces(own, beside=None):
    two = swap(own, "row", 2)
    if beside is not None:
        two, beside = lax.optimization_barrier((two, beside))
    pieces = [own, swap(own, "row", 1), two, swap(two, "row", 1)]
    return pieces if beside is None else (pieces, beside)


def gather_direct(own):
    return along_row([own] * lax.axis_size("row"), True)


def scatter_pieces(pieces):
    sent = add_parts([pieces[2], swap(pieces[3], "row", 1)], BF)
    direct, sent = lax.optimization_barrier((pieces[1], sent))
    return [pieces[0], swap(direct, "row", 1), swap(sent, "row", 2)], sent


def add_along(value, axes):
    for axis in axes:
        step = 1
        while step < lax.axis_size(axis):
            value = value + swap(value, axis, step)
            step *= 2
    return value


def along_row(pieces, forward):
    size = len(pieces)
    sign = 1 if forward else -1
    return [pieces[0]] + [
        lax.ppermute(p, "row", [(i, (i + sign * k) % size) for i in range(size)])
        for k, p in enumerate(pieces)
        if k
    ]


def along_quarters(pieces, forward):
    size = len(pieces)
    per = lax.axis_size("dp") // size
    sign = 1 if forward else -1

    def pairs(k):
        places = [(q, r) for q in range(size) for r in range(per)]
        return [(q * per + r, (q + sign * k) % size * per + r) for q, r in places]

    return [pieces[0]] + [lax.ppermute(p, "dp", pairs(k)) for k, p in enumerate(pieces) if k]


def gather_shard(shard):
    full = lax.all_gather(shard, ("col", "dp"), axis=0)
    return full.reshape(lax.axis_size("col"), lax.axis_size("dp"), *shard.shape)


def scatter_shard(full):
    flat_rows = full.reshape(-1, full.shape[-1])
    return lax.psum_scatter(flat_rows, ("col", "dp"), scatter_dimension=0, tiled=True)


def quarter_index():
    return lax.axis_index("dp") // (lax.axis_size("dp") // lax.axis_size("row"))


def pack_attention(query, keyval, z):
    size = lax.axis_size("row")
    rows = query.shape[0]
    hw, kw = query.shape[1] // size, keyval.shape[2] // size

    def kernel(z, query, keyval, *outs):
        for k in range(size):
            at = ahead(z[0], k, size)
            out = outs[k]
            out[:, :hw] = query[:, pl.ds(pl.multiple_of(at * hw, hw), hw)].astype(BF)
            for s in range(2):
                part = keyval[:, s, pl.ds(pl.multiple_of(at * kw, kw), kw)]
                out[:, hw + s * kw : hw + (s + 1) * kw] = part.astype(BF)

    return call(kernel, [shape((rows, hw + 2 * kw), BF)] * size, [query, keyval], [z], hbm=0)


def pack_feed(gateup, downs, z, after):
    size = lax.axis_size("row")
    rows = gateup.shape[0]
    fw = gateup.shape[2] // size
    terms = 2 * fw // COLUMNS
    inner = downs[0].shape[0]

    def kernel(z, gateup, *refs):
        for k in range(size):
            at = ahead(z[0], k, size)
            out = refs[size + k]
            for s in range(2):
                for j in range(fw // 128):
                    first = pl.multiple_of(at * fw + j * 128, 128)
                    place = (2 * j + s) * 128
                    t, lane = place // COLUMNS, place % COLUMNS
                    part = gateup[:, s, pl.ds(first, 128)].astype(BF)
                    out[t * rows : (t + 1) * rows, lane : lane + 128] = part
            out[terms * rows :, :] = refs[k][...]

    return call(
        kernel,
        [shape((terms * rows + inner, COLUMNS), BF)] * size,
        [gateup, *downs],
        [z],
        after=after,
        vmem=32,
    )


def pack_out(blocks, after=()):
    size = lax.axis_size("row")
    rows = [b.shape[0] // size for b in blocks]

    def kernel(q, *refs):
        for k in range(size):
            place = 0
            for ref, n in zip(refs, rows):
                first = pl.multiple_of(ahead(q[0], k, size) * n, n)
                refs[len(rows) + k][place : place + n, :] = ref[pl.ds(first, n), :].astype(BF)
                place += n

    return call(
        kernel,
        [shape((sum(rows), blocks[0].shape[1]), BF)] * size,
        blocks,
        [quarter_index()],
        after=after,
        hbm=0,
    )


def regroup(parts, source, target, cuts, after=()):
    size = len(parts)
    sources = [source(k) for k in range(size)]
    targets = [target(k) for k in range(size)]
    starts = [sum(cuts[:i]) for i in range(len(cuts))]

    def kernel(*refs):
        places, ins = refs[: 2 * size], refs[2 * size : 3 * size]
        outs, held = refs[3 * size : -1], refs[-1]
        for k in range(size):
            held[places[k][0]] = ins[k][...]
        for i, (first, n) in enumerate(zip(starts, cuts)):
            for k in range(size):
                outs[i * size + k][...] = held[places[size + k][0], first : first + n]

    rows, width = parts[0].shape
    outs = call(
        kernel,
        [shape((n, width), BF) for n in cuts for _ in range(size)],
        parts,
        sources + targets,
        scratch=[pltpu.VMEM((size, rows, width), BF)],
        after=after,
    )
    return [outs[i * size : (i + 1) * size] for i in range(len(cuts))]


def make_shard(in_parts, out_parts, z, after=()):
    size, dp = len(in_parts), lax.axis_size("dp")
    rest = MODEL_WIDTH // (size * dp)
    steps = MODEL_WIDTH // COLUMNS
    rows = MODEL_WIDTH // (size * dp)
    if isinstance(out_parts, int):
        inner, joined = out_parts, True
        terms = (in_parts[0].shape[0] - inner) // rows
    else:
        inner, joined = out_parts[0].shape[0], False
        terms = in_parts[0].shape[0] // rows
    base = terms * size * rows
    if rest % 128:
        order = behind(z, jnp.arange(size), size)
        if joined:
            out_parts = [p[terms * rows :] for p in in_parts]
            in_parts = [p[: terms * rows] for p in in_parts]
        full = jnp.take(jnp.stack(in_parts), order, axis=0).reshape(size, terms, rows, COLUMNS)
        ins = full.transpose(1, 0, 2, 3).reshape(base, COLUMNS)
        full = jnp.stack([p.reshape(inner, dp, rest) for p in out_parts], axis=2)
        full = jnp.take(full, order, axis=2).reshape(inner, steps, COLUMNS)
        return jnp.concatenate([ins, full.transpose(1, 0, 2).reshape(-1, COLUMNS)])

    def kernel(z, *refs):
        out = refs[-1]
        for k in range(size):
            at = behind(z[0], k, size)
            for t in range(terms):
                first = pl.multiple_of((t * size + at) * rows, rows)
                out[pl.ds(first, rows), :] = refs[k][t * rows : (t + 1) * rows, :]
            place = pl.multiple_of(at * rest, rest)
            ref = refs[k] if joined else refs[size + k]
            top = terms * rows if joined else 0
            for d in range(dp):
                first = base + d * inner
                part = ref[top : top + inner, d * rest : (d + 1) * rest]
                out[first : first + inner, pl.ds(place, rest)] = part

    parts = list(in_parts) if joined else list(in_parts) + list(out_parts)
    out = shape((base + steps * inner, COLUMNS), BF)
    return call(kernel, [out], parts, [z], after=after)[0]


def split_shard(shard, terms, rows, inner, z, after=()):
    size, dp = lax.axis_size("row"), lax.axis_size("dp")
    rest = MODEL_WIDTH // (size * dp)
    steps = MODEL_WIDTH // COLUMNS
    base = terms * size * rows
    if rest % 128:
        ins = shard[:base].reshape(terms, size, rows, COLUMNS).transpose(1, 0, 2, 3)
        ins = jnp.take(ins, behind(z, jnp.arange(size), size), axis=0)
        outs = shard[base:].reshape(steps, inner, COLUMNS).transpose(1, 0, 2)
        outs = outs.reshape(inner, dp, size, rest)
        outs = jnp.take(outs, behind(z, jnp.arange(size), size), axis=2)
        return [
            jnp.concatenate([ins[k].reshape(-1, COLUMNS), outs[:, :, k].reshape(inner, COLUMNS)])
            for k in range(size)
        ]

    def kernel(z, full, *outs):
        for k in range(size):
            at = behind(z[0], k, size)
            for t in range(terms):
                first = pl.multiple_of((t * size + at) * rows, rows)
                outs[k][t * rows : (t + 1) * rows, :] = full[pl.ds(first, rows), :]
            place = pl.multiple_of(at * rest, rest)
            for d in range(dp):
                part = full[base + d * inner : base + (d + 1) * inner, pl.ds(place, rest)]
                outs[k][terms * rows :, d * rest : (d + 1) * rest] = part

    return call(
        kernel,
        [shape((terms * rows + inner, COLUMNS), BF)] * size,
        [shard],
        [z],
        after=after,
    )


def out_pieces(messages, inner, z):
    size = len(messages)
    quarter = quarter_index()
    parts = regroup(
        [m[-inner:] for m in messages],
        lambda k: ahead(z, k, size),
        lambda k: ahead(quarter, k, size),
        [inner],
    )[0]
    return along_quarters(parts, True)


def update(refs, grad, rate):
    weight, moment, second, weight_new, moment_new, second_new = refs
    m, v, w = adamw(weight[...], moment[...], second[...], grad, rate, DECAY)
    moment_new[...] = m
    second_new[...] = v
    weight_new[...] = w


def update_out(state, pieces, rate):
    size = len(pieces)
    rows, width = pieces[0].shape

    def kernel(q, *refs):
        k = pl.program_id(0)
        for i in range(size):

            @pl.when(k == i)
            def _():
                update(refs[size:], refs[i][...].astype(F32), rate)

    spec = blocked((rows, width), lambda k, q: (lax.bitwise_and(q[0] + size - k, size - 1), 0))
    w, m, v = call(
        kernel,
        [shape(state[0].shape, F32)] * 3,
        list(pieces) + list(state),
        [quarter_index()],
        (size,),
        [None] * size + [spec] * 3,
        [spec] * 3,
        hbm=2**19,
    )
    return m, v, w


def place_columns(messages, rows, cuts, z):
    size = len(messages)

    def kernel(z, *refs):
        for out, cut in zip(refs[size:], cuts):
            width = sum(w for _, _, w in cut)
            for k in range(size):
                at = ahead(z[0], k, size) * width
                for t, first, w in cut:
                    place = pl.multiple_of(at, 128)
                    part = refs[k][t * rows : (t + 1) * rows, first : first + w]
                    out[:, pl.ds(place, w)] = part
                    at = at + w

    out = [shape((rows, size * sum(w for _, _, w in cut)), BF) for cut in cuts]
    return call(kernel, out, messages, [z])


def flat(values):
    rows, two, width = values.shape
    return values.reshape(rows, two, width // 128, 128).transpose(0, 2, 1, 3).reshape(-1, 128)


def update_pair(state, grad, rate):
    rows, two, width = state[0].shape
    total = rows * two * width // 128
    steps = 4 if total % 64 == 0 else 1

    def kernel(grad, *refs):
        update(refs, grad[...].astype(F32), rate)

    spec = blocked((total // steps, 128), lambda i: (i, 0))
    news = call(
        kernel,
        [shape((total, 128), F32)] * 3,
        [grad.reshape(-1, 128)] + [flat(s) for s in state],
        (),
        (steps,),
        [spec] * 4,
        [spec] * 3,
        hbm=2**19,
    )
    w, m, v = [
        n.reshape(rows, width // 128, two, 128).transpose(0, 2, 1, 3).reshape(rows, two, width)
        for n in news
    ]
    return (m, v, w), news[0]


def adamw(weight, moment, second, grad, rate, decay):
    moment_new = BETA_ONE * moment + (1.0 - BETA_ONE) * grad
    second_new = BETA_TWO * second + (1.0 - BETA_TWO) * grad * grad
    first_hat = moment_new / (1.0 - BETA_ONE**STEP)
    second_hat = second_new / (1.0 - BETA_TWO**STEP)
    weight_new = weight - rate * (first_hat / (jnp.sqrt(second_hat) + ADAM_EPS) + decay * weight)
    return (moment_new, second_new, weight_new)


def body(
    tokens,
    cotangent,
    seq_lens,
    query_weight,
    query_moment,
    query_second,
    key_value_master_weight,
    key_value_first_moment,
    key_value_second_moment,
    output_weight,
    output_moment,
    output_second,
    gateup_weight,
    gateup_moment,
    gateup_second,
    down_weight,
    down_moment,
    down_second,
    norm_gains,
    norm_moment,
    norm_second,
    head_gains,
    head_moment,
    head_second,
):
    size, dp, cols = lax.axis_size("row"), lax.axis_size("dp"), lax.axis_size("col")
    z, y = lax.axis_index("row"), lax.axis_index("col")
    rows = tokens.shape[0]
    quarter = rows // size
    item_count = rows * cols
    rest = MODEL_WIDTH // (size * dp)
    head_width = query_weight.shape[1] // size
    kv_width = key_value_master_weight.shape[2] // size

    gains = norm_gains.reshape(2, size, dp, rest).transpose(0, 2, 1, 3).reshape(2, MODEL_WIDTH)
    first_gain, second_gain = gains[0:1], gains[1:2]

    segment, position = token_layout(seq_lens[0], item_count)
    first = y * rows
    own_segment = lax.dynamic_slice_in_dim(segment, first, rows, 0)
    cosine, sine = rope_tables(lax.dynamic_slice_in_dim(position, first, rows, 0))
    valid = (own_segment < SEQS).astype(jnp.int32)[:, None]

    hidden_width = gateup_weight.shape[2] // size * cols

    in_rows = query_weight.shape[0]
    output_inner, down_inner = output_weight.shape[0] // size, down_weight.shape[0] // size
    gateup_terms = 2 * hidden_width // (cols * COLUMNS)
    steps = MODEL_WIDTH // COLUMNS
    down_base = gateup_terms * size * in_rows // down_inner
    output_base = size * in_rows // output_inner
    quarter_place = quarter_index()
    input_chunks = gather_pieces(tokens)
    attention_pieces = pack_attention(query_weight, key_value_master_weight, z)
    out_pieces_sent = pack_out([down_weight, output_weight], attention_pieces[:1])
    down_parts, output_parts = regroup(
        along_quarters(out_pieces_sent, True),
        lambda k: behind(quarter_place, k, size),
        lambda k: ahead(z, k, size),
        [down_inner, output_inner],
    )
    feed_pieces = pack_feed(gateup_weight, down_parts, z, output_parts[:1])
    attention_shard = make_shard(
        along_row(attention_pieces, True),
        along_row(output_parts, True),
        z,
        [feed_pieces[0], input_chunks[2]],
    )
    attention_full = gather_shard(attention_shard)
    inputs = assemble(input_chunks, z, False, False, [attention_shard])
    feed_shard = make_shard(along_row(feed_pieces, True), down_inner, z, [inputs])
    feed_full = gather_shard(feed_shard)
    out_own = masked(cotangent, valid, [feed_shard])
    out_chunks = gather_pieces(out_own)

    first_low, first_scale, query_raw, key_raw, query, keys_values = project(
        inputs,
        first_gain,
        attention_full,
        cosine,
        sine,
        head_gains,
        head_width,
        kv_width,
        [out_own],
    )
    before = lax.ppermute(keys_values, "col", [(i, i + 1) for i in range(cols - 1)])
    masks = (
        y.astype(jnp.int32).reshape(1),
        own_segment.reshape(rows, 1),
        own_segment.reshape(1, rows),
        segment[:rows].reshape(1, rows),
    )
    mixed, logsum = attention_forward(*masks, query, keys_values, before, [])
    out_low = assemble(out_chunks, z, True, False, [mixed])
    hidden_pieces = mixed_parts(mixed, attention_full, z, output_base, [out_low])
    hidden_parts, _ = scatter_pieces(hidden_pieces)
    hidden, second_scale, second_low = hidden_norm(hidden_parts, inputs, second_gain, z)

    second_chunks = gather_pieces(second_low)
    active_grad = down_back(out_low, feed_full, down_base, down_inner, second_chunks[3:])
    far_news = gateup_chunk(second_chunks[2:], feed_full, active_grad, 1, hidden_width, None)
    far_parts = gateup_back(far_news[1], feed_full, 1, (BF, BF))
    active, pair_grad = gateup_chunk(
        second_chunks[:2], feed_full, active_grad, 0, hidden_width, far_news
    )
    near_parts = gateup_back(pair_grad, feed_full, 0, (F32, BF))
    second_parts, sent = scatter_pieces(near_parts + far_parts)
    feed_grads = weight_grads(
        second_chunks, pair_grad, active, out_low, cols, [sent, *near_parts]
    )
    feed_grads, second_parts[1], second_parts[2] = lax.optimization_barrier(
        (feed_grads, second_parts[1], second_parts[2])
    )
    feed_total = scatter_shard(feed_grads)
    hidden_grad, hidden_low, second_gain_grad = hidden_back(
        second_parts, hidden, second_scale, second_gain, out_low, [feed_grads]
    )

    layer_part = down_forward(active, hidden, feed_full, down_base, down_inner, [hidden_low])
    hidden_all, mixed_grad = mixed_back(
        gather_pieces(hidden_low), attention_full, z, output_base, output_inner, [layer_part]
    )
    layer_pieces = take_apart(layer_part, z, True, [hidden_all])
    query_grad, key_grad, value_grad, far_sent = attention_backward(
        *masks, query, keys_values, before, mixed_grad, logsum, layer_pieces[:1]
    )
    far = lax.ppermute(far_sent, "col", [(i + 1, i) for i in range(cols - 1)])
    layer_parts, _ = scatter_pieces(layer_pieces)
    layer_output = add_parts(layer_parts, F32)
    raw_grad, head_part = heads_back(
        query_raw,
        key_raw,
        query_grad,
        key_grad,
        value_grad,
        far,
        cosine,
        sine,
        head_gains,
        cols,
        [layer_output],
    )
    attention_grads = weight_grads([first_low], raw_grad, mixed, hidden_all, cols)
    input_part, inner_part, first_gain_grad = input_back(
        raw_grad,
        attention_full,
        inputs,
        first_scale,
        first_gain,
        hidden_grad,
        z,
        [attention_grads],
    )
    input_pieces = take_apart(input_part, z, False)
    input_parts, _ = scatter_pieces(input_pieces)
    norm_part = jnp.concatenate([first_gain_grad, second_gain_grad])
    norm_part = norm_part.reshape(2, dp, size, rest).transpose(0, 2, 1, 3).reshape(2, MODEL_WIDTH)
    small = jnp.concatenate([norm_part.reshape(-1), head_part.reshape(-1), inner_part.reshape(-1)])
    small, input_parts[0] = lax.optimization_barrier((small, input_parts[0]))
    small = add_along(small.reshape(-1, 128), ("row",)).reshape(-1)
    gain_count = norm_part.size + head_part.size
    inner = small[gain_count:][:, None]
    gain_total = add_along(small[:gain_count].reshape(-1, 128), ("dp", "col")).reshape(-1)
    attention_grads, feed_total, input_parts[1], input_parts[2], gain_total = (
        lax.optimization_barrier(
            (attention_grads, feed_total, input_parts[1], input_parts[2], gain_total)
        )
    )
    norm_total = gain_total[: norm_part.size].reshape(norm_part.shape)
    head_total = gain_total[norm_part.size :].reshape(head_part.shape)
    attention_total = scatter_shard(attention_grads)

    feed_messages = along_row(
        split_shard(feed_total, gateup_terms, in_rows, down_inner, z), False
    )
    down_new = update_out(
        (down_weight, down_moment, down_second),
        out_pieces(feed_messages, down_inner, z),
        RATES[4],
    )
    cut = [(t, 0, COLUMNS) for t in range(gateup_terms)]
    (gateup_total,) = place_columns(feed_messages, in_rows, [cut], z)
    gateup_new, gateup_flat = update_pair(
        (gateup_weight, gateup_moment, gateup_second), gateup_total, RATES[3]
    )
    input_grad = add_parts(input_parts, F32) - (
        first_scale * first_scale * first_scale * inner / MODEL_WIDTH
    ) * tokens.astype(F32)
    attention_messages = along_row(
        split_shard(attention_total, 1, in_rows, output_inner, z, [gateup_flat]), False
    )
    output_new = update_out(
        (output_weight, output_moment, output_second),
        out_pieces(attention_messages, output_inner, z),
        RATES[2],
    )
    query_total, keyval_total = place_columns(
        attention_messages,
        in_rows,
        [[(0, 0, head_width)], [(0, head_width, 2 * kv_width)]],
        z,
    )
    query_new = adamw(
        query_weight, query_moment, query_second, query_total.astype(F32), RATES[0], DECAY
    )
    keyval_new, _ = update_pair(
        (key_value_master_weight, key_value_first_moment, key_value_second_moment),
        keyval_total,
        RATES[1],
    )
    norm_new = adamw(norm_gains, norm_moment, norm_second, norm_total, GAIN_RATE, 0.0)
    head_new = adamw(head_gains, head_moment, head_second, head_total, GAIN_RATE, 0.0)
    return (
        layer_output,
        input_grad,
        *query_new,
        *keyval_new,
        *output_new,
        *gateup_new,
        *down_new,
        *norm_new,
        *head_new,
    )


def solution(mesh):
    items = P(("dp", "col"), "row")
    inward = P(("row", "dp"), "col")
    inward_pair = P(("row", "dp"), None, "col")
    outward = P(("col", "dp"), "row")
    weights = (
        (inward,) * 3 + (inward_pair,) * 3 + (outward,) * 3 + (inward_pair,) * 3 + (outward,) * 3
    )
    return jax.shard_map(
        body,
        mesh=mesh,
        in_specs=(items, items, P("dp", None)) + weights + (P(),) * 6,
        out_specs=(items, items) + weights + (P(),) * 6,
        check_vma=False,
    )
```

```python
import functools
import math

import jax
import jax.numpy as jnp
from jax import lax
from jax.experimental import pallas as pl
from jax.experimental.pallas import tpu as pltpu
from jax.sharding import PartitionSpec as P

MODEL_WIDTH = 2048
HEAD_SIZE = 128
SEQS = 4
STEP = 10

EPS = 1e-06
THETA = 1000000.0
NEGATIVE = -1e30
BETA_ONE = 0.9
BETA_TWO = 0.95
ADAM_EPS = 1e-08
DECAY = 0.1
RATES = (0.066, 0.066, 0.5, 0.066, 0.04)
GAIN_RATE = 0.6
BF = jnp.bfloat16
F32 = jnp.float32
SCALE = 1.0 / math.sqrt(HEAD_SIZE)


def dot(a, b, kind="nn"):
    dims = {"nn": ((1,), (0,)), "nt": ((1,), (1,)), "tn": ((0,), (0,))}[kind]
    return lax.dot_general(a, b, (dims, ((), ())), preferred_element_type=F32)


def token_layout(lengths, item_count):
    ends = jnp.cumsum(lengths)
    places = jnp.arange(item_count, dtype=jnp.int32)
    segment = jnp.sum((places[:, None] >= ends[None, :]).astype(jnp.int32), axis=1)
    starts = jnp.concatenate([ends - lengths, ends[-1:]])
    labels = jnp.arange(starts.shape[0], dtype=jnp.int32)
    begin = jnp.sum(jnp.where(segment[:, None] == labels[None, :], starts[None, :], 0), axis=1)
    return (segment, places - begin)


def rope_tables(position):
    half = HEAD_SIZE // 2
    freq = jnp.exp(jnp.arange(half, dtype=F32) * (-2.0 * math.log(THETA) / HEAD_SIZE))
    angle = position.astype(F32)[:, None] * freq[None, :]
    angle = jnp.concatenate([angle, angle], axis=1)
    return (jnp.cos(angle), jnp.sin(angle))


def block_masks(own_col, own_row, prev_row, later):
    rows = own_col.shape[0]
    r = lax.broadcasted_iota(jnp.int32, (rows, rows), 0)
    c = lax.broadcasted_iota(jnp.int32, (rows, rows), 1)
    own = (c <= r) & (own_col == own_row)
    prev = (own_col == prev_row) & (later > 0)
    return own, prev


def forward_kernel(later, own_col, own_row, prev_row, q, k, v, kp, vp, o, lse):
    own, prev = block_masks(own_col[...], own_row[...], prev_row[...], later[0])
    s_own = jnp.where(own, dot(q[...], k[...], "nt") * SCALE, NEGATIVE)
    s_prev = jnp.where(prev, dot(q[...], kp[...], "nt") * SCALE, NEGATIVE)
    top = jnp.maximum(
        jnp.max(s_own, axis=1, keepdims=True), jnp.max(s_prev, axis=1, keepdims=True)
    )
    total = jnp.sum(jnp.exp(s_own - top), axis=1, keepdims=True) + jnp.sum(
        jnp.exp(s_prev - top), axis=1, keepdims=True
    )
    logsum = top + jnp.log(total)
    p_own = jnp.exp(s_own - logsum).astype(BF)
    p_prev = jnp.exp(s_prev - logsum).astype(BF)
    o[...] = (dot(p_own, v[...]) + dot(p_prev, vp[...])).astype(BF)
    lse[0] = logsum


def attention_forward(later, own_col, own_row, prev_row, q, kv, before, after):
    rows, width = q.shape
    heads = width // HEAD_SIZE
    groups = 2 * width // kv.shape[1]
    inputs = (later, own_col, own_row, prev_row, q, kv, kv, before, before)

    def kernel(*refs):
        forward_kernel(*refs[: len(inputs)], *refs[len(inputs) + len(after) :])

    mine = pl.BlockSpec((rows, HEAD_SIZE), lambda h: (0, h))
    key = pl.BlockSpec((rows, HEAD_SIZE), lambda h: (0, 2 * (h // groups)))
    value = pl.BlockSpec((rows, HEAD_SIZE), lambda h: (0, 2 * (h // groups) + 1))
    column = pl.BlockSpec((rows, 1), lambda h: (0, 0))
    line = pl.BlockSpec((1, rows), lambda h: (0, 0))
    return pl.pallas_call(
        kernel,
        grid=(heads,),
        in_specs=[pl.BlockSpec(memory_space=pltpu.SMEM), column, line, line, mine]
        + [key, value] * 2
        + [pl.BlockSpec(memory_space=pl.ANY)] * len(after),
        out_specs=[mine, pl.BlockSpec((1, rows, 1), lambda h: (h, 0, 0))],
        out_shape=[
            jax.ShapeDtypeStruct((rows, width), BF),
            jax.ShapeDtypeStruct((heads, rows, 1), F32),
        ],
        compiler_params=pltpu.CompilerParams(vmem_limit_bytes=32 * 2**20),
    )(*inputs, *after)


def backward_kernel(
    later, own_col, own_row, prev_row, q, k, v, kp, vp, do, lse, dq, dk, dv, far, total
):
    own, prev = block_masks(own_col[...], own_row[...], prev_row[...], later[0])
    logsum = lse[0]
    p_own = jnp.exp(jnp.where(own, dot(q[...], k[...], "nt") * SCALE, NEGATIVE) - logsum)
    p_prev = jnp.exp(jnp.where(prev, dot(q[...], kp[...], "nt") * SCALE, NEGATIVE) - logsum)
    d_own = dot(do[...], v[...], "nt")
    d_prev = dot(do[...], vp[...], "nt")
    delta = jnp.sum(p_own * d_own, axis=1, keepdims=True) + jnp.sum(
        p_prev * d_prev, axis=1, keepdims=True
    )
    g_own = (p_own * (d_own - delta)).astype(BF)
    g_prev = (p_prev * (d_prev - delta)).astype(BF)
    dq[...] = (dot(g_own, k[...]) + dot(g_prev, kp[...])) * SCALE
    near = ((dk, dot(g_own, q[...], "tn") * SCALE), (dv, dot(p_own.astype(BF), do[...], "tn")))
    dkp = dot(g_prev, q[...], "tn") * SCALE
    dvp = dot(p_prev.astype(BF), do[...], "tn")
    group = pl.program_id(1)

    @pl.when(group == 0)
    def _():
        for ref, value in near:
            ref[...] = value
        total[:, :HEAD_SIZE] = dkp
        total[:, HEAD_SIZE:] = dvp

    @pl.when(group > 0)
    def _():
        for ref, value in near:
            ref[...] += value
        total[:, :HEAD_SIZE] += dkp
        total[:, HEAD_SIZE:] += dvp

    @pl.when(group == pl.num_programs(1) - 1)
    def _():
        far[...] = total[...].astype(BF)


def attention_backward(later, own_col, own_row, prev_row, q, kv, before, do, lse, after):
    rows, width = q.shape
    kv_heads = kv.shape[1] // (2 * HEAD_SIZE)
    groups = 2 * width // kv.shape[1]
    inputs = (later, own_col, own_row, prev_row, q, kv, kv, before, before, do, lse)

    def kernel(*refs):
        backward_kernel(*refs[: len(inputs)], *refs[len(inputs) + len(after) :])

    mine = pl.BlockSpec((rows, HEAD_SIZE), lambda h, g: (0, h * groups + g))
    shared = pl.BlockSpec((rows, HEAD_SIZE), lambda h, g: (0, h))
    key = pl.BlockSpec((rows, HEAD_SIZE), lambda h, g: (0, 2 * h))
    value = pl.BlockSpec((rows, HEAD_SIZE), lambda h, g: (0, 2 * h + 1))
    column = pl.BlockSpec((rows, 1), lambda h, g: (0, 0))
    line = pl.BlockSpec((1, rows), lambda h, g: (0, 0))
    near = jax.ShapeDtypeStruct((rows, kv_heads * HEAD_SIZE), F32)
    return pl.pallas_call(
        kernel,
        grid=(kv_heads, groups),
        in_specs=[pl.BlockSpec(memory_space=pltpu.SMEM), column, line, line, mine]
        + [key, value] * 2
        + [mine, pl.BlockSpec((1, rows, 1), lambda h, g: (h * groups + g, 0, 0))]
        + [pl.BlockSpec(memory_space=pl.ANY)] * len(after),
        out_specs=[mine, shared, shared, pl.BlockSpec((rows, 2 * HEAD_SIZE), lambda h, g: (0, h))],
        out_shape=[
            jax.ShapeDtypeStruct((rows, width), F32),
            near,
            near,
            jax.ShapeDtypeStruct((rows, kv.shape[1]), BF),
        ],
        scratch_shapes=[pltpu.VMEM((rows, 2 * HEAD_SIZE), F32)],
        compiler_params=pltpu.CompilerParams(vmem_limit_bytes=32 * 2**20),
    )(*inputs, *after)


def call(
    kernel,
    out,
    inputs,
    scalars=(),
    grid=(1,),
    in_specs=None,
    out_specs=None,
    scratch=(),
    vmem=20,
    after=(),
    alias=None,
    hbm=4 * 2**20,
):
    def whole(a):
        return pl.BlockSpec(a.shape, lambda *_: (0,) * len(a.shape))

    in_specs = [s or whole(a) for s, a in zip(in_specs or [None] * len(inputs), inputs)]
    out_specs = [s or whole(a) for s, a in zip(out_specs or [None] * len(out), out)]
    alias = alias or {}

    def held(a, least):
        if a.size * a.dtype.itemsize < least:
            return a
        return pltpu.with_memory_space_constraint(a, pltpu.HBM)

    inputs = [held(a, hbm) for a in inputs]
    after = [held(a, hbm) for a in alias.values()] + [held(a, 2**20) for a in after]
    first = len(scalars) + len(inputs)

    def run(*refs):
        kernel(*refs[:first], *refs[first + len(after) :])

    return pl.pallas_call(
        run,
        grid_spec=pltpu.PrefetchScalarGridSpec(
            num_scalar_prefetch=len(scalars),
            grid=grid,
            in_specs=in_specs + [pl.BlockSpec(memory_space=pl.ANY)] * len(after),
            out_specs=out_specs,
            scratch_shapes=list(scratch),
        ),
        out_shape=list(out),
        compiler_params=pltpu.CompilerParams(vmem_limit_bytes=vmem * 2**20),
        input_output_aliases={first + i: place for i, place in enumerate(alias)},
        cost_estimate=pl.CostEstimate(flops=0, bytes_accessed=0, transcendentals=0),
    )(*[s.astype(jnp.int32).reshape(1) for s in scalars], *inputs, *after)


def in_hbm(dims, dtype):
    return pltpu.HBM(tuple(dims), dtype)


def shape(dims, dtype):
    return jax.ShapeDtypeStruct(tuple(dims), dtype)


def blocked(dims, index):
    return pl.BlockSpec(dims, index)


COLUMNS = 512


def other(index, k):
    return lax.bitwise_xor(index, jnp.int32(k))


def partners(z, size):
    return lax.bitwise_xor(z, jnp.arange(size, dtype=jnp.int32))


def ahead(index, k, size):
    return lax.bitwise_and(index + jnp.int32(k), jnp.int32(size - 1))


def behind(index, k, size):
    return lax.bitwise_and(index + jnp.int32(size) - jnp.int32(k), jnp.int32(size - 1))


def out_rows(ref):
    cols, dp, rows, width = ref.shape
    size = 4
    if dp == size:
        return ref[...].reshape(cols * dp * rows, width)
    per = dp // size
    order = [(c, q * per + r) for c in range(cols) for r in range(per) for q in range(size)]
    return jnp.concatenate([ref[c, d] for c, d in order])


def assemble(pieces, z, rolled, direct, after=()):
    def place_of(z, k):
        return behind(z, k, len(pieces)) if direct else other(z, k)

    size, dp = lax.axis_size("row"), lax.axis_size("dp")
    rows, width = pieces[0].shape
    rest = width // dp
    block = rows // size
    if rest % 128:
        out = jnp.stack([p.reshape(rows, dp, rest) for p in pieces], axis=2)
        order = behind(z, jnp.arange(size), size) if direct else partners(z, size)
        out = jnp.take(out, order, axis=2).reshape(rows, -1)
        if rolled:
            out = jnp.concatenate(
                [
                    lax.dynamic_slice_in_dim(out, other(z, k) * block, block, 0)
                    for k in range(size)
                ]
            )
        return out

    def kernel(z, *refs):
        out = refs[-1]
        for k in range(size):
            piece = refs[k][...]
            for d in range(dp):
                place = pl.multiple_of((d * size + place_of(z[0], k)) * rest, rest)
                out[:, pl.ds(place, rest)] = piece[:, d * rest : (d + 1) * rest]

    def index(i, z):
        return (lax.bitwise_xor(z[0], jnp.int32(i)) if rolled else i, 0)

    return call(
        kernel,
        [shape((rows, size * width), pieces[0].dtype)],
        list(pieces),
        [z],
        (size,),
        [blocked((block, width), index)] * size,
        [blocked((block, size * width), lambda i, z: (i, 0))],
        after=after,
    )[0]


def take_apart(full, z, rolled, after=()):
    size, dp = lax.axis_size("row"), lax.axis_size("dp")
    rows, width = full.shape
    rest = width // (size * dp)
    block = rows // size
    if rest % 128:
        if rolled:
            full = jnp.concatenate(
                [
                    lax.dynamic_slice_in_dim(full, other(z, i) * block, block, 0)
                    for i in range(size)
                ]
            )
        split = full.reshape(rows, dp, size, rest)
        split = jnp.take(split, partners(z, size), axis=2)
        return [split[:, :, k].reshape(rows, dp * rest) for k in range(size)]

    def kernel(z, full, *outs):
        for k in range(size):
            for d in range(dp):
                place = pl.multiple_of((d * size + other(z[0], k)) * rest, rest)
                outs[k][:, d * rest : (d + 1) * rest] = full[:, pl.ds(place, rest)]

    def index(i, z):
        return (lax.bitwise_xor(z[0], jnp.int32(i)) if rolled else i, 0)

    return call(
        kernel,
        [shape((rows, dp * rest), full.dtype)] * size,
        [full],
        [z],
        (size,),
        [blocked((block, width), lambda i, z: (i, 0))],
        [blocked((block, dp * rest), index)] * size,
        after=after,
    )


def project_kernel(x, gain, weight, cosine, sine, head_gain, a, scale, qr, kr, qn, kv):
    rows = x.shape[0]
    heads = qr.shape[1] // HEAD_SIZE
    kv_heads = kr.shape[1] // HEAD_SIZE

    @pl.when(pl.program_id(0) == 0)
    def _():
        for first in range(0, rows, 128):
            s = slice(first, first + 128)
            xf = x[s, :].astype(F32)
            r = lax.rsqrt(jnp.mean(xf * xf, axis=1, keepdims=True) + EPS)
            a[s, :] = (xf * r * gain[...]).astype(BF)
            scale[s, :] = r

    raw = dot(a[...], weight[0].reshape(MODEL_WIDTH, COLUMNS))

    def turn(values, gains):
        normed = (
            values
            * lax.rsqrt(jnp.mean(values * values, axis=-1, keepdims=True) + EPS)
            * gains
        )
        half = HEAD_SIZE // 2
        turned = jnp.concatenate([-normed[:, half:], normed[:, :half]], axis=-1)
        return (normed * cosine[...] + turned * sine[...]).astype(BF)

    for h in range(heads):
        s = slice(h * HEAD_SIZE, (h + 1) * HEAD_SIZE)
        qr[:, s] = raw[:, s]
        qn[:, s] = turn(raw[:, s], head_gain[0:1, :])
    first = heads * HEAD_SIZE
    for h in range(kv_heads):
        s = slice(h * HEAD_SIZE, (h + 1) * HEAD_SIZE)
        values = raw[:, first + h * HEAD_SIZE : first + (h + 1) * HEAD_SIZE]
        kr[:, s] = values
        kv[:, s] = turn(values, head_gain[1:2, :])
    kv[:, kv_heads * HEAD_SIZE :] = raw[:, first + kv_heads * HEAD_SIZE :].astype(BF)


def project(x, gain, weight, cosine, sine, head_gain, head_width, kv_width, after):
    rows = x.shape[0]
    cols, dp, _, width = weight.shape
    q = blocked((rows, head_width), lambda c: (0, c))
    k = blocked((rows, kv_width), lambda c: (0, c))
    return call(
        project_kernel,
        [
            shape(x.shape, BF),
            shape((rows, 1), F32),
            shape((rows, cols * head_width), F32),
            shape((rows, cols * kv_width), F32),
            shape((rows, cols * head_width), BF),
            shape((rows, 2 * cols * kv_width), BF),
        ],
        [x, gain, weight, cosine, sine, head_gain],
        (),
        (cols,),
        [None, None, blocked((1, dp, MODEL_WIDTH // dp, width), lambda c: (c, 0, 0, 0)), None, None, None],
        [None, None, q, k, q, blocked((rows, 2 * kv_width), lambda c: (0, c))],
        after=after,
    )


def mixed_parts(mixed, weight, z, base, after):
    size = lax.axis_size("row")
    cols, dp, total_rows, _ = weight.shape
    rows = mixed.shape[0]
    inner = mixed.shape[1] // (cols * dp)
    part = rows // size
    steps = MODEL_WIDTH // COLUMNS

    def kernel(z, mixed, weight, *refs):
        *outs, total = refs
        total[...] = dot(mixed[...], out_rows(weight))
        for k in range(size):
            first = pl.multiple_of(other(z[0], k) * part, part)
            outs[k][...] = total[pl.ds(first, part), :].astype(outs[k].dtype)

    return call(
        kernel,
        [shape((part, MODEL_WIDTH), BF if k else F32) for k in range(size)],
        [mixed, weight],
        [z],
        (steps,),
        [None, blocked((cols, dp, inner, COLUMNS), lambda c, z: (0, 0, base + c, 0))],
        [blocked((part, COLUMNS), lambda c, z: (0, c))] * size,
        scratch=[pltpu.VMEM((rows, COLUMNS), F32)],
        after=after,
    )


def mixed_back(chunks, weight, z, base, inner, after):
    size = len(chunks)
    cols, dp, _, _ = weight.shape
    part, width = chunks[0].shape
    rows = size * part
    heads = cols * dp * inner
    steps = width // COLUMNS

    def kernel(z, *refs):
        *ins, weight, full, out, total = refs
        for k in range(size):
            first = pl.multiple_of(other(z[0], k) * part, part)
            full[pl.ds(first, part), :] = ins[k][...]
        term = dot(full[...], out_rows(weight), "nt")
        c = pl.program_id(0)

        @pl.when(c == 0)
        def _():
            total[...] = term

        @pl.when(c > 0)
        def _():
            total[...] += term

        @pl.when(c == steps - 1)
        def _():
            out[...] = total[...].astype(BF)

    return call(
        kernel,
        [shape((rows, width), BF), shape((rows, heads), BF)],
        list(chunks) + [weight],
        [z],
        (steps,),
        [blocked((part, COLUMNS), lambda c, z: (0, c))] * size
        + [blocked((cols, dp, inner, COLUMNS), lambda c, z: (0, 0, base + c, 0))],
        [blocked((rows, COLUMNS), lambda c, z: (0, c)), None],
        scratch=[pltpu.VMEM((rows, heads), F32)],
        after=after,
    )


def masked(values, valid, after):
    def kernel(values, valid, out):
        out[...] = jnp.where(valid[...] > 0, values[...], jnp.zeros_like(values))

    return call(kernel, [shape(values.shape, values.dtype)], [values, valid], after=after)[0]


def add_parts(parts, dtype, after=()):
    def kernel(*refs):
        total = refs[0][...].astype(F32)
        for ref in refs[1:-1]:
            total = total + ref[...].astype(F32)
        refs[-1][...] = total.astype(dtype)

    return call(kernel, [shape(parts[0].shape, dtype)], list(parts), after=after)[0]


def hidden_norm(parts, x, gain, z, after=()):
    rows, width = parts[0].shape

    def kernel(z, *refs):
        *ps, x, gain, h, scale, a = refs
        total = x[...].astype(F32)
        for p in ps:
            total = total + p[...].astype(F32)
        r = lax.rsqrt(jnp.mean(total * total, axis=1, keepdims=True) + EPS)
        h[...] = total
        scale[...] = r
        a[...] = (total * r * gain[...]).astype(BF)

    return call(
        kernel,
        [shape((rows, width), F32), shape((rows, 1), F32), shape((rows, width), BF)],
        list(parts) + [x, gain],
        [z],
        (1,),
        [None] * len(parts) + [blocked((rows, width), lambda i, z: (z[0], 0)), None],
        after=after,
    )


def gateup_chunk(parts, weight, grad, hidden):
    part, width = parts[0].shape
    rows = part * len(parts)
    cols, dp, _, _ = weight.shape
    steps = 2 * hidden // (cols * COLUMNS)
    half = COLUMNS // 2

    def kernel(*refs):
        *ins, weight, grad, act, out, a = refs

        @pl.when((pl.program_id(0) == 0) & (pl.program_id(1) == 0))
        def _():
            for i, ref in enumerate(ins):
                a[i * part : (i + 1) * part, :] = ref[...]

        p = dot(a[...], weight[0].reshape(width, COLUMNS))
        for j in range(half // 128):
            gate, up = p[:, j * 256 : j * 256 + 128], p[:, j * 256 + 128 : j * 256 + 256]
            s = slice(j * 128, (j + 1) * 128)
            spread = 1.0 / (1.0 + jnp.exp(-gate))
            silu = gate * spread
            act[:, s] = (silu * up).astype(BF)
            g = grad[:, s]
            out[:, j * 256 : j * 256 + 128] = (g * up * (spread + silu * (1.0 - spread))).astype(BF)
            out[:, j * 256 + 128 : j * 256 + 256] = (g * silu).astype(BF)

    def place(c, t):
        return (0, c * steps + t)

    total = grad.shape[0]
    return call(
        kernel,
        [shape((total, hidden), BF), shape((total, 2 * hidden), BF)],
        list(parts) + [weight, grad],
        (),
        (cols, steps),
        [None] * len(parts)
        + [
            blocked((1, dp, width // dp, COLUMNS), lambda c, t: (c, 0, t, 0)),
            blocked((rows, half), place),
        ],
        [blocked((rows, half), place), blocked((rows, COLUMNS), place)],
        scratch=[pltpu.VMEM((rows, width), BF)],
        vmem=24,
    )


def gateup_back(grad, weight, kinds):
    cols, dp, _, _ = weight.shape
    both = grad.shape[1]
    block = MODEL_WIDTH // dp
    terms = both // COLUMNS
    per = terms // cols
    rows = grad.shape[0]
    part = rows // len(kinds)

    def kernel(grad, weight, *outs):
        total = None
        for t in range(terms):
            right = weight[t // per, 0, (t % per) * block : (t % per + 1) * block, :]
            term = dot(grad[:, t * COLUMNS : (t + 1) * COLUMNS], right, "nt")
            total = term if total is None else total + term
        for i, (out, kind) in enumerate(zip(outs, kinds)):
            out[...] = total[i * part : (i + 1) * part, :].astype(kind)

    return call(
        kernel,
        [shape((part, MODEL_WIDTH), kind) for kind in kinds],
        [grad, weight],
        (),
        (dp,),
        [
            None,
            blocked((cols, 1, per * block, COLUMNS), lambda n: (0, n, 0, 0)),
        ],
        [blocked((part, block), lambda n: (0, n))] * len(kinds),
        vmem=24,
    )


def down_back(out_low, weight, base, inner, after):
    cols, dp, _, _ = weight.shape
    rows, width = out_low.shape
    hidden = cols * dp * inner

    def kernel(low, weight, out):
        term = dot(low[...], out_rows(weight), "nt")

        @pl.when(pl.program_id(0) == 0)
        def _():
            out[...] = term

        @pl.when(pl.program_id(0) > 0)
        def _():
            out[...] += term

    return call(
        kernel,
        [shape((rows, hidden), F32)],
        [out_low, weight],
        (),
        (width // COLUMNS,),
        [
            blocked((rows, COLUMNS), lambda c: (0, c)),
            blocked((cols, dp, inner, COLUMNS), lambda c: (0, 0, base + c, 0)),
        ],
        [None],
        vmem=24,
        after=after,
    )[0]


def down_forward(active, hidden, weight, base, inner, after):
    cols, dp, _, _ = weight.shape
    rows, width = active.shape
    part = hidden.shape[0]

    def kernel(active, hidden, weight, out):
        p = dot(active[...], out_rows(weight))
        out[:part, :] = (p[:part, :] + hidden[...]).astype(BF)
        out[part:, :] = p[part:, :].astype(BF)

    return call(
        kernel,
        [shape((rows, MODEL_WIDTH), BF)],
        [active, hidden, weight],
        (),
        (MODEL_WIDTH // COLUMNS,),
        [
            None,
            blocked((part, COLUMNS), lambda c: (0, c)),
            blocked((cols, dp, inner, COLUMNS), lambda c: (0, 0, base + c, 0)),
        ],
        [blocked((rows, COLUMNS), lambda c: (0, c))],
        after=after,
    )[0]


def hidden_back(parts, h, scale, gain, out_low, after):
    rows, width = h.shape

    def kernel(*refs):
        *ps, h, scale, gain, dy, dh, low, gain_grad = refs
        grad = ps[0][...].astype(F32)
        for p in ps[1:]:
            grad = grad + p[...].astype(F32)
        hidden, r = h[...], scale[...]
        weighted = grad * gain[...]
        inner = jnp.sum(weighted * hidden, axis=1, keepdims=True)
        total = dy[...].astype(F32) + r * weighted - (r * r * r * inner / MODEL_WIDTH) * hidden
        dh[...] = total
        low[...] = total.astype(BF)
        gain_grad[...] = jnp.sum(grad * hidden * r, axis=0, keepdims=True)

    return call(
        kernel,
        [shape((rows, width), F32), shape((rows, width), BF), shape((1, width), F32)],
        list(parts) + [h, scale, gain, out_low],
        (),
        (1,),
        [None] * (len(parts) + 3) + [blocked((rows, width), lambda i: (0, 0))],
        after=after,
        hbm=2**17,
    )


def heads_back_kernel(
    qr, kr, dqn, dkn, dv, far, cosine, sine, head_gain, out, gain_grad
):
    heads = qr.shape[1] // HEAD_SIZE
    kv_heads = kr.shape[1] // HEAD_SIZE
    half = HEAD_SIZE // 2

    def back(raw, grad, gains):
        turned = grad * sine[...]
        turned = jnp.concatenate([turned[:, half:], -turned[:, :half]], axis=-1)
        g = grad * cosine[...] + turned
        r = lax.rsqrt(jnp.mean(raw * raw, axis=-1, keepdims=True) + EPS)
        weighted = g * gains
        inner = jnp.sum(weighted * raw, axis=-1, keepdims=True)
        low = (r * weighted - (r * r * r * inner / HEAD_SIZE) * raw).astype(BF)
        return low, jnp.sum(g * raw * r, axis=0, keepdims=True)

    @pl.when(pl.program_id(0) == 0)
    def _():
        gain_grad[...] = jnp.zeros_like(gain_grad)

    for h in range(heads):
        s = slice(h * HEAD_SIZE, (h + 1) * HEAD_SIZE)
        low, total = back(qr[:, s], dqn[:, s], head_gain[0:1, :])
        out[:, s] = low
        gain_grad[0:1, :] += total
    first = heads * HEAD_SIZE
    for h in range(kv_heads):
        s = slice(h * HEAD_SIZE, (h + 1) * HEAD_SIZE)
        low, total = back(kr[:, s], dkn[:, s] + far[:, s].astype(F32), head_gain[1:2, :])
        out[:, first + h * HEAD_SIZE : first + (h + 1) * HEAD_SIZE] = low
        gain_grad[1:2, :] += total
    first += kv_heads * HEAD_SIZE
    out[:, first:] = (dv[...] + far[:, kv_heads * HEAD_SIZE :].astype(F32)).astype(BF)


def heads_back(qr, kr, dqn, dkn, dv, far, cosine, sine, head_gain, cols, after):
    rows = qr.shape[0]
    head_width, kv_width = qr.shape[1] // cols, kr.shape[1] // cols
    q = blocked((rows, head_width), lambda c: (0, c))
    k = blocked((rows, kv_width), lambda c: (0, c))
    far_kv = blocked((rows, 2 * kv_width), lambda c: (0, c))
    width = head_width + 2 * kv_width
    return call(
        heads_back_kernel,
        [shape((rows, cols * width), BF), shape((2, HEAD_SIZE), F32)],
        [qr, kr, dqn, dkn, dv, far, cosine, sine, head_gain],
        (),
        (cols,),
        [q, k, q, k, k, far_kv, None, None, None],
        [blocked((rows, width), lambda c: (0, c)), None],
        after=after,
    )


def input_back(grads, weight, x, scale, gain, dh, z, after):
    cols, steps, _, width = weight.shape
    rows = grads.shape[0]
    model = MODEL_WIDTH
    part = dh.shape[0]

    def kernel(z, grads, weight, x, scale, gain, dh, out, c1, gain_grad):
        total = dot(grads[:, :width], weight[0, 0], "nt")
        for c in range(1, cols):
            total = total + dot(grads[:, c * width : (c + 1) * width], weight[c, 0], "nt")
        r = scale[...]
        xf = x[...].astype(F32)
        weighted = total * gain[...]
        moved = weighted * xf
        gain_grad[...] = jnp.sum(total * xf * r, axis=0, keepdims=True)
        out[...] = (r * weighted).astype(BF)
        first = pl.multiple_of(z[0] * part, part)
        own = pl.ds(first, part)
        out[own, :] = (out[own, :].astype(F32) + dh[...]).astype(BF)

        @pl.when(pl.program_id(0) == 0)
        def _():
            c1[...] = jnp.zeros_like(c1)

        c1[...] += jnp.sum(moved, axis=1, keepdims=True)

    block = model // steps
    wide = blocked((rows, block), lambda n, z: (0, n))
    return call(
        kernel,
        [shape((rows, model), BF), shape((rows, 1), F32), shape((1, model), F32)],
        [grads, weight, x, scale, gain, dh],
        [z],
        (steps,),
        [
            None,
            blocked((cols, 1, block, width), lambda n, z: (0, n, 0, 0)),
            wide,
            None,
            blocked((1, block), lambda n, z: (0, n)),
            blocked((part, block), lambda n, z: (0, n)),
        ],
        [wide, None, blocked((1, block), lambda n, z: (0, n))],
        after=after,
    )


def weight_grads(lefts, right, out_left, out_right, cols, after=()):
    size, dp = lax.axis_size("row"), lax.axis_size("dp")
    rows = right.shape[0]
    block = MODEL_WIDTH // dp
    n = right.shape[1] // cols
    part = rows // len(lefts)
    m = out_left.shape[1] // cols
    inner = m // dp
    terms = n // COLUMNS
    total = terms * block + MODEL_WIDTH // COLUMNS * inner

    def kernel(*refs):
        *ins, right, out_left, out_right, out = refs
        left = jnp.concatenate([ref[...] for ref in ins]) if len(ins) > 1 else ins[0][...]
        for t in range(terms):
            term = dot(left, right[:, t * COLUMNS : (t + 1) * COLUMNS], "tn")
            out[0, 0, t * block : (t + 1) * block, :] = term.astype(BF)
        for d in range(dp):
            q, r = d // (dp // size), d % (dp // size)
            first = (r * size + q) * inner

            @pl.when(pl.program_id(1) == d)
            def _():
                term = dot(out_left[:, first : first + inner], out_right[...], "tn").astype(BF)
                for c in range(MODEL_WIDTH // COLUMNS):
                    place = terms * block + c * inner
                    piece = term[:, c * COLUMNS : (c + 1) * COLUMNS]
                    out[0, 0, place : place + inner, :] = piece

    return call(
        kernel,
        [in_hbm((cols, dp, total, COLUMNS), BF)],
        list(lefts) + [right, out_left, out_right],
        (),
        (cols, dp),
        [blocked((part, block), lambda c, d: (0, d))] * len(lefts)
        + [
            blocked((rows, n), lambda c, d: (0, c)),
            blocked((rows, m), lambda c, d: (0, c)),
            None,
        ],
        [blocked((1, 1, total, COLUMNS), lambda c, d: (c, d, 0, 0))],
        after=after,
        vmem=28,
    )[0]


def swap(value, axis, step):
    return lax.ppermute(value, axis, [(i, i ^ step) for i in range(lax.axis_size(axis))])


def gather_pieces(own, beside=None):
    two = swap(own, "row", 2)
    if beside is not None:
        two, beside = lax.optimization_barrier((two, beside))
    pieces = [own, swap(own, "row", 1), two, swap(two, "row", 1)]
    return pieces if beside is None else (pieces, beside)


def gather_direct(own):
    return along_row([own] * lax.axis_size("row"), True)


def scatter_pieces(pieces):
    sent = add_parts([pieces[2], swap(pieces[3], "row", 1)], BF)
    direct, sent = lax.optimization_barrier((pieces[1], sent))
    return [pieces[0], swap(direct, "row", 1), swap(sent, "row", 2)], sent


def add_along(value, axes):
    for axis in axes:
        step = 1
        while step < lax.axis_size(axis):
            value = value + swap(value, axis, step)
            step *= 2
    return value


def along_row(pieces, forward):
    size = len(pieces)
    sign = 1 if forward else -1
    return [pieces[0]] + [
        lax.ppermute(p, "row", [(i, (i + sign * k) % size) for i in range(size)])
        for k, p in enumerate(pieces)
        if k
    ]


def along_quarters(pieces, forward):
    size = len(pieces)
    per = lax.axis_size("dp") // size
    sign = 1 if forward else -1

    def pairs(k):
        places = [(q, r) for q in range(size) for r in range(per)]
        return [(q * per + r, (q + sign * k) % size * per + r) for q, r in places]

    return [pieces[0]] + [lax.ppermute(p, "dp", pairs(k)) for k, p in enumerate(pieces) if k]


def gather_shard(shard):
    full = lax.all_gather(shard, ("col", "dp"), axis=0)
    return full.reshape(lax.axis_size("col"), lax.axis_size("dp"), *shard.shape)


def scatter_shard(full):
    flat_rows = full.reshape(-1, full.shape[-1])
    return lax.psum_scatter(flat_rows, ("col", "dp"), scatter_dimension=0, tiled=True)


def quarter_index():
    return lax.axis_index("dp") // (lax.axis_size("dp") // lax.axis_size("row"))


def pack_attention(query, keyval, z):
    size = lax.axis_size("row")
    rows = query.shape[0]
    hw, kw = query.shape[1] // size, keyval.shape[2] // size

    def kernel(z, query, keyval, *outs):
        for k in range(size):
            at = ahead(z[0], k, size)
            out = outs[k]
            out[:, :hw] = query[:, pl.ds(pl.multiple_of(at * hw, hw), hw)].astype(BF)
            for s in range(2):
                part = keyval[:, s, pl.ds(pl.multiple_of(at * kw, kw), kw)]
                out[:, hw + s * kw : hw + (s + 1) * kw] = part.astype(BF)

    return call(kernel, [shape((rows, hw + 2 * kw), BF)] * size, [query, keyval], [z], hbm=0)


def pack_feed(gateup, downs, z, after):
    size = lax.axis_size("row")
    rows = gateup.shape[0]
    fw = gateup.shape[2] // size
    terms = 2 * fw // COLUMNS
    inner = downs[0].shape[0]

    def kernel(z, gateup, *refs):
        for k in range(size):
            at = ahead(z[0], k, size)
            out = refs[size + k]
            for s in range(2):
                for j in range(fw // 128):
                    first = pl.multiple_of(at * fw + j * 128, 128)
                    place = (2 * j + s) * 128
                    t, lane = place // COLUMNS, place % COLUMNS
                    part = gateup[:, s, pl.ds(first, 128)].astype(BF)
                    out[t * rows : (t + 1) * rows, lane : lane + 128] = part
            out[terms * rows :, :] = refs[k][...]

    return call(
        kernel,
        [shape((terms * rows + inner, COLUMNS), BF)] * size,
        [gateup, *downs],
        [z],
        after=after,
        vmem=32,
    )


def pack_out(blocks, after=()):
    size = lax.axis_size("row")
    rows = [b.shape[0] // size for b in blocks]

    def kernel(q, *refs):
        for k in range(size):
            place = 0
            for ref, n in zip(refs, rows):
                first = pl.multiple_of(ahead(q[0], k, size) * n, n)
                refs[len(rows) + k][place : place + n, :] = ref[pl.ds(first, n), :].astype(BF)
                place += n

    return call(
        kernel,
        [shape((sum(rows), blocks[0].shape[1]), BF)] * size,
        blocks,
        [quarter_index()],
        after=after,
        hbm=0,
    )


def regroup(parts, source, target, cuts, after=()):
    size = len(parts)
    sources = [source(k) for k in range(size)]
    targets = [target(k) for k in range(size)]
    starts = [sum(cuts[:i]) for i in range(len(cuts))]

    def kernel(*refs):
        places, ins = refs[: 2 * size], refs[2 * size : 3 * size]
        outs, held = refs[3 * size : -1], refs[-1]
        for k in range(size):
            held[places[k][0]] = ins[k][...]
        for i, (first, n) in enumerate(zip(starts, cuts)):
            for k in range(size):
                outs[i * size + k][...] = held[places[size + k][0], first : first + n]

    rows, width = parts[0].shape
    outs = call(
        kernel,
        [shape((n, width), BF) for n in cuts for _ in range(size)],
        parts,
        sources + targets,
        scratch=[pltpu.VMEM((size, rows, width), BF)],
        after=after,
    )
    return [outs[i * size : (i + 1) * size] for i in range(len(cuts))]


def make_shard(in_parts, out_parts, z, after=()):
    size, dp = len(in_parts), lax.axis_size("dp")
    rest = MODEL_WIDTH // (size * dp)
    steps = MODEL_WIDTH // COLUMNS
    rows = MODEL_WIDTH // (size * dp)
    if isinstance(out_parts, int):
        inner, joined = out_parts, True
        terms = (in_parts[0].shape[0] - inner) // rows
    else:
        inner, joined = out_parts[0].shape[0], False
        terms = in_parts[0].shape[0] // rows
    base = terms * size * rows
    if rest % 128:
        order = behind(z, jnp.arange(size), size)
        if joined:
            out_parts = [p[terms * rows :] for p in in_parts]
            in_parts = [p[: terms * rows] for p in in_parts]
        full = jnp.take(jnp.stack(in_parts), order, axis=0).reshape(size, terms, rows, COLUMNS)
        ins = full.transpose(1, 0, 2, 3).reshape(base, COLUMNS)
        full = jnp.stack([p.reshape(inner, dp, rest) for p in out_parts], axis=2)
        full = jnp.take(full, order, axis=2).reshape(inner, steps, COLUMNS)
        return jnp.concatenate([ins, full.transpose(1, 0, 2).reshape(-1, COLUMNS)])

    def kernel(z, *refs):
        out = refs[-1]
        for k in range(size):
            at = behind(z[0], k, size)
            for t in range(terms):
                first = pl.multiple_of((t * size + at) * rows, rows)
                out[pl.ds(first, rows), :] = refs[k][t * rows : (t + 1) * rows, :]
            place = pl.multiple_of(at * rest, rest)
            ref = refs[k] if joined else refs[size + k]
            top = terms * rows if joined else 0
            for d in range(dp):
                first = base + d * inner
                part = ref[top : top + inner, d * rest : (d + 1) * rest]
                out[first : first + inner, pl.ds(place, rest)] = part

    parts = list(in_parts) if joined else list(in_parts) + list(out_parts)
    out = shape((base + steps * inner, COLUMNS), BF)
    return call(kernel, [out], parts, [z], after=after)[0]


def split_shard(shard, terms, rows, inner, z, after=()):
    size, dp = lax.axis_size("row"), lax.axis_size("dp")
    rest = MODEL_WIDTH // (size * dp)
    steps = MODEL_WIDTH // COLUMNS
    base = terms * size * rows
    if rest % 128:
        ins = shard[:base].reshape(terms, size, rows, COLUMNS).transpose(1, 0, 2, 3)
        ins = jnp.take(ins, behind(z, jnp.arange(size), size), axis=0)
        outs = shard[base:].reshape(steps, inner, COLUMNS).transpose(1, 0, 2)
        outs = outs.reshape(inner, dp, size, rest)
        outs = jnp.take(outs, behind(z, jnp.arange(size), size), axis=2)
        return [
            jnp.concatenate([ins[k].reshape(-1, COLUMNS), outs[:, :, k].reshape(inner, COLUMNS)])
            for k in range(size)
        ]

    def kernel(z, full, *outs):
        for k in range(size):
            at = behind(z[0], k, size)
            for t in range(terms):
                first = pl.multiple_of((t * size + at) * rows, rows)
                outs[k][t * rows : (t + 1) * rows, :] = full[pl.ds(first, rows), :]
            place = pl.multiple_of(at * rest, rest)
            for d in range(dp):
                part = full[base + d * inner : base + (d + 1) * inner, pl.ds(place, rest)]
                outs[k][terms * rows :, d * rest : (d + 1) * rest] = part

    return call(
        kernel,
        [shape((terms * rows + inner, COLUMNS), BF)] * size,
        [shard],
        [z],
        after=after,
    )


def out_pieces(messages, inner, z):
    size = len(messages)
    quarter = quarter_index()
    parts = regroup(
        [m[-inner:] for m in messages],
        lambda k: ahead(z, k, size),
        lambda k: ahead(quarter, k, size),
        [inner],
    )[0]
    return along_quarters(parts, True)


def update(refs, grad, rate):
    weight, moment, second, weight_new, moment_new, second_new = refs
    m, v, w = adamw(weight[...], moment[...], second[...], grad, rate, DECAY)
    moment_new[...] = m
    second_new[...] = v
    weight_new[...] = w


def update_out(state, pieces, rate):
    size = len(pieces)
    rows, width = pieces[0].shape

    def kernel(q, *refs):
        k = pl.program_id(0)
        for i in range(size):

            @pl.when(k == i)
            def _():
                update(refs[size:], refs[i][...].astype(F32), rate)

    spec = blocked((rows, width), lambda k, q: (lax.bitwise_and(q[0] + size - k, size - 1), 0))
    w, m, v = call(
        kernel,
        [shape(state[0].shape, F32)] * 3,
        list(pieces) + list(state),
        [quarter_index()],
        (size,),
        [None] * size + [spec] * 3,
        [spec] * 3,
        hbm=2**19,
    )
    return m, v, w


def place_columns(messages, rows, cuts, z):
    size = len(messages)

    def kernel(z, *refs):
        for out, cut in zip(refs[size:], cuts):
            width = sum(w for _, _, w in cut)
            for k in range(size):
                at = ahead(z[0], k, size) * width
                for t, first, w in cut:
                    place = pl.multiple_of(at, 128)
                    part = refs[k][t * rows : (t + 1) * rows, first : first + w]
                    out[:, pl.ds(place, w)] = part
                    at = at + w

    out = [shape((rows, size * sum(w for _, _, w in cut)), BF) for cut in cuts]
    return call(kernel, out, messages, [z])


def flat(values):
    rows, two, width = values.shape
    return values.reshape(rows, two, width // 128, 128).transpose(0, 2, 1, 3).reshape(-1, 128)


def update_pair(state, grad, rate):
    rows, two, width = state[0].shape
    total = rows * two * width // 128
    steps = 4 if total % 64 == 0 else 1

    def kernel(grad, *refs):
        update(refs, grad[...].astype(F32), rate)

    spec = blocked((total // steps, 128), lambda i: (i, 0))
    news = call(
        kernel,
        [shape((total, 128), F32)] * 3,
        [grad.reshape(-1, 128)] + [flat(s) for s in state],
        (),
        (steps,),
        [spec] * 4,
        [spec] * 3,
        hbm=2**19,
    )
    w, m, v = [
        n.reshape(rows, width // 128, two, 128).transpose(0, 2, 1, 3).reshape(rows, two, width)
        for n in news
    ]
    return (m, v, w), news[0]


def adamw(weight, moment, second, grad, rate, decay):
    moment_new = BETA_ONE * moment + (1.0 - BETA_ONE) * grad
    second_new = BETA_TWO * second + (1.0 - BETA_TWO) * grad * grad
    first_hat = moment_new / (1.0 - BETA_ONE**STEP)
    second_hat = second_new / (1.0 - BETA_TWO**STEP)
    weight_new = weight - rate * (first_hat / (jnp.sqrt(second_hat) + ADAM_EPS) + decay * weight)
    return (moment_new, second_new, weight_new)


def body(
    tokens,
    cotangent,
    seq_lens,
    query_weight,
    query_moment,
    query_second,
    key_value_master_weight,
    key_value_first_moment,
    key_value_second_moment,
    output_weight,
    output_moment,
    output_second,
    gateup_weight,
    gateup_moment,
    gateup_second,
    down_weight,
    down_moment,
    down_second,
    norm_gains,
    norm_moment,
    norm_second,
    head_gains,
    head_moment,
    head_second,
):
    size, dp, cols = lax.axis_size("row"), lax.axis_size("dp"), lax.axis_size("col")
    z, y = lax.axis_index("row"), lax.axis_index("col")
    rows = tokens.shape[0]
    quarter = rows // size
    item_count = rows * cols
    rest = MODEL_WIDTH // (size * dp)
    head_width = query_weight.shape[1] // size
    kv_width = key_value_master_weight.shape[2] // size

    gains = norm_gains.reshape(2, size, dp, rest).transpose(0, 2, 1, 3).reshape(2, MODEL_WIDTH)
    first_gain, second_gain = gains[0:1], gains[1:2]

    segment, position = token_layout(seq_lens[0], item_count)
    first = y * rows
    own_segment = lax.dynamic_slice_in_dim(segment, first, rows, 0)
    cosine, sine = rope_tables(lax.dynamic_slice_in_dim(position, first, rows, 0))
    valid = (own_segment < SEQS).astype(jnp.int32)[:, None]

    hidden_width = gateup_weight.shape[2] // size * cols

    in_rows = query_weight.shape[0]
    output_inner, down_inner = output_weight.shape[0] // size, down_weight.shape[0] // size
    gateup_terms = 2 * hidden_width // (cols * COLUMNS)
    steps = MODEL_WIDTH // COLUMNS
    down_base = gateup_terms * size * in_rows // down_inner
    output_base = size * in_rows // output_inner
    quarter_place = quarter_index()
    input_chunks = gather_pieces(tokens)
    attention_pieces = pack_attention(query_weight, key_value_master_weight, z)
    out_pieces_sent = pack_out([down_weight, output_weight], attention_pieces[:1])
    down_parts, output_parts = regroup(
        along_quarters(out_pieces_sent, True),
        lambda k: behind(quarter_place, k, size),
        lambda k: ahead(z, k, size),
        [down_inner, output_inner],
    )
    feed_pieces = pack_feed(gateup_weight, down_parts, z, output_parts[:1])
    attention_shard = make_shard(
        along_row(attention_pieces, True),
        along_row(output_parts, True),
        z,
        [feed_pieces[0], input_chunks[2]],
    )
    attention_full = gather_shard(attention_shard)
    inputs = assemble(input_chunks, z, False, False, [attention_shard])
    feed_shard = make_shard(along_row(feed_pieces, True), down_inner, z, [inputs])
    feed_full = gather_shard(feed_shard)
    out_own = masked(cotangent, valid, [feed_shard])
    out_chunks = gather_pieces(out_own)

    first_low, first_scale, query_raw, key_raw, query, keys_values = project(
        inputs,
        first_gain,
        attention_full,
        cosine,
        sine,
        head_gains,
        head_width,
        kv_width,
        [out_own],
    )
    before = lax.ppermute(keys_values, "col", [(i, i + 1) for i in range(cols - 1)])
    masks = (
        y.astype(jnp.int32).reshape(1),
        own_segment.reshape(rows, 1),
        own_segment.reshape(1, rows),
        segment[:rows].reshape(1, rows),
    )
    mixed, logsum = attention_forward(*masks, query, keys_values, before, [])
    hidden_pieces = mixed_parts(mixed, attention_full, z, output_base, out_chunks[1:])
    out_low = assemble(out_chunks, z, True, False, hidden_pieces[1:2])
    hidden_parts, _ = scatter_pieces(hidden_pieces)
    hidden, second_scale, second_low = hidden_norm(hidden_parts, inputs, second_gain, z)

    second_chunks = gather_pieces(second_low)
    active_grad = down_back(out_low, feed_full, down_base, down_inner, second_chunks[2:3])
    active, pair_grad = gateup_chunk(second_chunks, feed_full, active_grad, hidden_width)
    second_parts = gateup_back(pair_grad, feed_full, (F32, BF, BF, BF))
    second_parts, sent = scatter_pieces(second_parts)
    feed_grads = weight_grads(
        second_chunks, pair_grad, active, out_low, cols, [sent]
    )
    feed_grads, second_parts[1], second_parts[2] = lax.optimization_barrier(
        (feed_grads, second_parts[1], second_parts[2])
    )
    feed_total = scatter_shard(feed_grads)
    hidden_grad, hidden_low, second_gain_grad = hidden_back(
        second_parts, hidden, second_scale, second_gain, out_low, [feed_grads]
    )

    layer_part = down_forward(active, hidden, feed_full, down_base, down_inner, [hidden_low])
    hidden_all, mixed_grad = mixed_back(
        gather_pieces(hidden_low), attention_full, z, output_base, output_inner, [layer_part]
    )
    layer_pieces = take_apart(layer_part, z, True, [hidden_all])
    query_grad, key_grad, value_grad, far_sent = attention_backward(
        *masks, query, keys_values, before, mixed_grad, logsum, layer_pieces[:1]
    )
    far = lax.ppermute(far_sent, "col", [(i + 1, i) for i in range(cols - 1)])
    layer_parts, _ = scatter_pieces(layer_pieces)
    layer_output = add_parts(layer_parts, F32)
    raw_grad, head_part = heads_back(
        query_raw,
        key_raw,
        query_grad,
        key_grad,
        value_grad,
        far,
        cosine,
        sine,
        head_gains,
        cols,
        [layer_output],
    )
    attention_grads = weight_grads([first_low], raw_grad, mixed, hidden_all, cols)
    input_part, inner_part, first_gain_grad = input_back(
        raw_grad,
        attention_full,
        inputs,
        first_scale,
        first_gain,
        hidden_grad,
        z,
        [attention_grads],
    )
    input_pieces = take_apart(input_part, z, False)
    input_parts, _ = scatter_pieces(input_pieces)
    norm_part = jnp.concatenate([first_gain_grad, second_gain_grad])
    norm_part = norm_part.reshape(2, dp, size, rest).transpose(0, 2, 1, 3).reshape(2, MODEL_WIDTH)
    small = jnp.concatenate([norm_part.reshape(-1), head_part.reshape(-1), inner_part.reshape(-1)])
    small, input_parts[0] = lax.optimization_barrier((small, input_parts[0]))
    small = add_along(small.reshape(-1, 128), ("row",)).reshape(-1)
    gain_count = norm_part.size + head_part.size
    inner = small[gain_count:][:, None]
    gain_total = add_along(small[:gain_count].reshape(-1, 128), ("dp", "col")).reshape(-1)
    attention_grads, feed_total, input_parts[1], input_parts[2], gain_total = (
        lax.optimization_barrier(
            (attention_grads, feed_total, input_parts[1], input_parts[2], gain_total)
        )
    )
    norm_total = gain_total[: norm_part.size].reshape(norm_part.shape)
    head_total = gain_total[norm_part.size :].reshape(head_part.shape)
    attention_total = scatter_shard(attention_grads)

    feed_messages = along_row(
        split_shard(feed_total, gateup_terms, in_rows, down_inner, z), False
    )
    down_new = update_out(
        (down_weight, down_moment, down_second),
        out_pieces(feed_messages, down_inner, z),
        RATES[4],
    )
    cut = [(t, 0, COLUMNS) for t in range(gateup_terms)]
    (gateup_total,) = place_columns(feed_messages, in_rows, [cut], z)
    gateup_new, _ = update_pair(
        (gateup_weight, gateup_moment, gateup_second), gateup_total, RATES[3]
    )
    input_grad = add_parts(input_parts, F32) - (
        first_scale * first_scale * first_scale * inner / MODEL_WIDTH
    ) * tokens.astype(F32)
    attention_messages = along_row(
        split_shard(attention_total, 1, in_rows, output_inner, z), False
    )
    output_new = update_out(
        (output_weight, output_moment, output_second),
        out_pieces(attention_messages, output_inner, z),
        RATES[2],
    )
    query_total, keyval_total = place_columns(
        attention_messages,
        in_rows,
        [[(0, 0, head_width)], [(0, head_width, 2 * kv_width)]],
        z,
    )
    query_new = adamw(
        query_weight, query_moment, query_second, query_total.astype(F32), RATES[0], DECAY
    )
    keyval_new, _ = update_pair(
        (key_value_master_weight, key_value_first_moment, key_value_second_moment),
        keyval_total,
        RATES[1],
    )
    norm_new = adamw(norm_gains, norm_moment, norm_second, norm_total, GAIN_RATE, 0.0)
    head_new = adamw(head_gains, head_moment, head_second, head_total, GAIN_RATE, 0.0)
    return (
        layer_output,
        input_grad,
        *query_new,
        *keyval_new,
        *output_new,
        *gateup_new,
        *down_new,
        *norm_new,
        *head_new,
    )


def solution(mesh):
    items = P(("dp", "col"), "row")
    inward = P(("row", "dp"), "col")
    inward_pair = P(("row", "dp"), None, "col")
    outward = P(("col", "dp"), "row")
    weights = (
        (inward,) * 3 + (inward_pair,) * 3 + (outward,) * 3 + (inward_pair,) * 3 + (outward,) * 3
    )
    return jax.shard_map(
        body,
        mesh=mesh,
        in_specs=(items, items, P("dp", None)) + weights + (P(),) * 6,
        out_specs=(items, items) + weights + (P(),) * 6,
        check_vma=False,
    )
```

```python
import functools
import math

import jax
import jax.numpy as jnp
from jax import lax
from jax.experimental import pallas as pl
from jax.experimental.pallas import tpu as pltpu
from jax.sharding import PartitionSpec as P

MODEL_WIDTH = 2048
HEAD_SIZE = 128
SEQS = 4
STEP = 10

EPS = 1e-06
THETA = 1000000.0
NEGATIVE = -1e30
BETA_ONE = 0.9
BETA_TWO = 0.95
ADAM_EPS = 1e-08
DECAY = 0.1
RATES = (0.066, 0.066, 0.5, 0.066, 0.04)
GAIN_RATE = 0.6
BF = jnp.bfloat16
F32 = jnp.float32
SCALE = 1.0 / math.sqrt(HEAD_SIZE)


def dot(a, b, kind="nn"):
    dims = {"nn": ((1,), (0,)), "nt": ((1,), (1,)), "tn": ((0,), (0,))}[kind]
    return lax.dot_general(a, b, (dims, ((), ())), preferred_element_type=F32)


def token_layout(lengths, item_count):
    ends = jnp.cumsum(lengths)
    places = jnp.arange(item_count, dtype=jnp.int32)
    segment = jnp.sum((places[:, None] >= ends[None, :]).astype(jnp.int32), axis=1)
    starts = jnp.concatenate([ends - lengths, ends[-1:]])
    labels = jnp.arange(starts.shape[0], dtype=jnp.int32)
    begin = jnp.sum(jnp.where(segment[:, None] == labels[None, :], starts[None, :], 0), axis=1)
    return (segment, places - begin)


def rope_tables(position):
    half = HEAD_SIZE // 2
    freq = jnp.exp(jnp.arange(half, dtype=F32) * (-2.0 * math.log(THETA) / HEAD_SIZE))
    angle = position.astype(F32)[:, None] * freq[None, :]
    angle = jnp.concatenate([angle, angle], axis=1)
    return (jnp.cos(angle), jnp.sin(angle))


def block_masks(own_col, own_row, prev_row, later):
    rows = own_col.shape[0]
    r = lax.broadcasted_iota(jnp.int32, (rows, rows), 0)
    c = lax.broadcasted_iota(jnp.int32, (rows, rows), 1)
    own = (c <= r) & (own_col == own_row)
    prev = (own_col == prev_row) & (later > 0)
    return own, prev


def forward_kernel(later, own_col, own_row, prev_row, q, k, v, kp, vp, o, lse):
    own, prev = block_masks(own_col[...], own_row[...], prev_row[...], later[0])
    s_own = jnp.where(own, dot(q[...], k[...], "nt") * SCALE, NEGATIVE)
    s_prev = jnp.where(prev, dot(q[...], kp[...], "nt") * SCALE, NEGATIVE)
    top = jnp.maximum(
        jnp.max(s_own, axis=1, keepdims=True), jnp.max(s_prev, axis=1, keepdims=True)
    )
    total = jnp.sum(jnp.exp(s_own - top), axis=1, keepdims=True) + jnp.sum(
        jnp.exp(s_prev - top), axis=1, keepdims=True
    )
    logsum = top + jnp.log(total)
    p_own = jnp.exp(s_own - logsum).astype(BF)
    p_prev = jnp.exp(s_prev - logsum).astype(BF)
    o[...] = (dot(p_own, v[...]) + dot(p_prev, vp[...])).astype(BF)
    lse[0] = logsum


def attention_forward(later, own_col, own_row, prev_row, q, kv, before, after):
    rows, width = q.shape
    heads = width // HEAD_SIZE
    groups = 2 * width // kv.shape[1]
    inputs = (later, own_col, own_row, prev_row, q, kv, kv, before, before)

    def kernel(*refs):
        forward_kernel(*refs[: len(inputs)], *refs[len(inputs) + len(after) :])

    mine = pl.BlockSpec((rows, HEAD_SIZE), lambda h: (0, h))
    key = pl.BlockSpec((rows, HEAD_SIZE), lambda h: (0, 2 * (h // groups)))
    value = pl.BlockSpec((rows, HEAD_SIZE), lambda h: (0, 2 * (h // groups) + 1))
    column = pl.BlockSpec((rows, 1), lambda h: (0, 0))
    line = pl.BlockSpec((1, rows), lambda h: (0, 0))
    return pl.pallas_call(
        kernel,
        grid=(heads,),
        in_specs=[pl.BlockSpec(memory_space=pltpu.SMEM), column, line, line, mine]
        + [key, value] * 2
        + [pl.BlockSpec(memory_space=pl.ANY)] * len(after),
        out_specs=[mine, pl.BlockSpec((1, rows, 1), lambda h: (h, 0, 0))],
        out_shape=[
            jax.ShapeDtypeStruct((rows, width), BF),
            jax.ShapeDtypeStruct((heads, rows, 1), F32),
        ],
        compiler_params=pltpu.CompilerParams(vmem_limit_bytes=32 * 2**20),
    )(*inputs, *after)


def backward_kernel(
    later, own_col, own_row, prev_row, q, k, v, kp, vp, do, lse, dq, dk, dv, far, total
):
    own, prev = block_masks(own_col[...], own_row[...], prev_row[...], later[0])
    logsum = lse[0]
    p_own = jnp.exp(jnp.where(own, dot(q[...], k[...], "nt") * SCALE, NEGATIVE) - logsum)
    p_prev = jnp.exp(jnp.where(prev, dot(q[...], kp[...], "nt") * SCALE, NEGATIVE) - logsum)
    d_own = dot(do[...], v[...], "nt")
    d_prev = dot(do[...], vp[...], "nt")
    delta = jnp.sum(p_own * d_own, axis=1, keepdims=True) + jnp.sum(
        p_prev * d_prev, axis=1, keepdims=True
    )
    g_own = (p_own * (d_own - delta)).astype(BF)
    g_prev = (p_prev * (d_prev - delta)).astype(BF)
    dq[...] = (dot(g_own, k[...]) + dot(g_prev, kp[...])) * SCALE
    near = ((dk, dot(g_own, q[...], "tn") * SCALE), (dv, dot(p_own.astype(BF), do[...], "tn")))
    dkp = dot(g_prev, q[...], "tn") * SCALE
    dvp = dot(p_prev.astype(BF), do[...], "tn")
    group = pl.program_id(1)

    @pl.when(group == 0)
    def _():
        for ref, value in near:
            ref[...] = value
        total[:, :HEAD_SIZE] = dkp
        total[:, HEAD_SIZE:] = dvp

    @pl.when(group > 0)
    def _():
        for ref, value in near:
            ref[...] += value
        total[:, :HEAD_SIZE] += dkp
        total[:, HEAD_SIZE:] += dvp

    @pl.when(group == pl.num_programs(1) - 1)
    def _():
        far[...] = total[...].astype(BF)


def attention_backward(later, own_col, own_row, prev_row, q, kv, before, do, lse, after):
    rows, width = q.shape
    kv_heads = kv.shape[1] // (2 * HEAD_SIZE)
    groups = 2 * width // kv.shape[1]
    inputs = (later, own_col, own_row, prev_row, q, kv, kv, before, before, do, lse)

    def kernel(*refs):
        backward_kernel(*refs[: len(inputs)], *refs[len(inputs) + len(after) :])

    mine = pl.BlockSpec((rows, HEAD_SIZE), lambda h, g: (0, h * groups + g))
    shared = pl.BlockSpec((rows, HEAD_SIZE), lambda h, g: (0, h))
    key = pl.BlockSpec((rows, HEAD_SIZE), lambda h, g: (0, 2 * h))
    value = pl.BlockSpec((rows, HEAD_SIZE), lambda h, g: (0, 2 * h + 1))
    column = pl.BlockSpec((rows, 1), lambda h, g: (0, 0))
    line = pl.BlockSpec((1, rows), lambda h, g: (0, 0))
    near = jax.ShapeDtypeStruct((rows, kv_heads * HEAD_SIZE), F32)
    return pl.pallas_call(
        kernel,
        grid=(kv_heads, groups),
        in_specs=[pl.BlockSpec(memory_space=pltpu.SMEM), column, line, line, mine]
        + [key, value] * 2
        + [mine, pl.BlockSpec((1, rows, 1), lambda h, g: (h * groups + g, 0, 0))]
        + [pl.BlockSpec(memory_space=pl.ANY)] * len(after),
        out_specs=[mine, shared, shared, pl.BlockSpec((rows, 2 * HEAD_SIZE), lambda h, g: (0, h))],
        out_shape=[
            jax.ShapeDtypeStruct((rows, width), F32),
            near,
            near,
            jax.ShapeDtypeStruct((rows, kv.shape[1]), BF),
        ],
        scratch_shapes=[pltpu.VMEM((rows, 2 * HEAD_SIZE), F32)],
        compiler_params=pltpu.CompilerParams(vmem_limit_bytes=32 * 2**20),
    )(*inputs, *after)


def call(
    kernel,
    out,
    inputs,
    scalars=(),
    grid=(1,),
    in_specs=None,
    out_specs=None,
    scratch=(),
    vmem=20,
    after=(),
    alias=None,
    hbm=4 * 2**20,
):
    def whole(a):
        return pl.BlockSpec(a.shape, lambda *_: (0,) * len(a.shape))

    in_specs = [s or whole(a) for s, a in zip(in_specs or [None] * len(inputs), inputs)]
    out_specs = [s or whole(a) for s, a in zip(out_specs or [None] * len(out), out)]
    alias = alias or {}

    def held(a, least):
        if a.size * a.dtype.itemsize < least:
            return a
        return pltpu.with_memory_space_constraint(a, pltpu.HBM)

    inputs = [held(a, hbm) for a in inputs]
    after = [held(a, hbm) for a in alias.values()] + [held(a, 2**20) for a in after]
    first = len(scalars) + len(inputs)

    def run(*refs):
        kernel(*refs[:first], *refs[first + len(after) :])

    return pl.pallas_call(
        run,
        grid_spec=pltpu.PrefetchScalarGridSpec(
            num_scalar_prefetch=len(scalars),
            grid=grid,
            in_specs=in_specs + [pl.BlockSpec(memory_space=pl.ANY)] * len(after),
            out_specs=out_specs,
            scratch_shapes=list(scratch),
        ),
        out_shape=list(out),
        compiler_params=pltpu.CompilerParams(vmem_limit_bytes=vmem * 2**20),
        input_output_aliases={first + i: place for i, place in enumerate(alias)},
        cost_estimate=pl.CostEstimate(flops=0, bytes_accessed=0, transcendentals=0),
    )(*[s.astype(jnp.int32).reshape(1) for s in scalars], *inputs, *after)


def in_hbm(dims, dtype):
    return pltpu.HBM(tuple(dims), dtype)


def shape(dims, dtype):
    return jax.ShapeDtypeStruct(tuple(dims), dtype)


def blocked(dims, index):
    return pl.BlockSpec(dims, index)


COLUMNS = 512


def other(index, k):
    return lax.bitwise_xor(index, jnp.int32(k))


def partners(z, size):
    return lax.bitwise_xor(z, jnp.arange(size, dtype=jnp.int32))


def ahead(index, k, size):
    return lax.bitwise_and(index + jnp.int32(k), jnp.int32(size - 1))


def behind(index, k, size):
    return lax.bitwise_and(index + jnp.int32(size) - jnp.int32(k), jnp.int32(size - 1))


def out_rows(ref):
    cols, dp, rows, width = ref.shape
    size = 4
    if dp == size:
        return ref[...].reshape(cols * dp * rows, width)
    per = dp // size
    order = [(c, q * per + r) for c in range(cols) for r in range(per) for q in range(size)]
    return jnp.concatenate([ref[c, d] for c, d in order])


def assemble(pieces, z, rolled, direct, after=()):
    def place_of(z, k):
        return behind(z, k, len(pieces)) if direct else other(z, k)

    size, dp = lax.axis_size("row"), lax.axis_size("dp")
    rows, width = pieces[0].shape
    rest = width // dp
    block = rows // size
    if rest % 128:
        out = jnp.stack([p.reshape(rows, dp, rest) for p in pieces], axis=2)
        order = behind(z, jnp.arange(size), size) if direct else partners(z, size)
        out = jnp.take(out, order, axis=2).reshape(rows, -1)
        if rolled:
            out = jnp.concatenate(
                [
                    lax.dynamic_slice_in_dim(out, other(z, k) * block, block, 0)
                    for k in range(size)
                ]
            )
        return out

    def kernel(z, *refs):
        out = refs[-1]
        for k in range(size):
            piece = refs[k][...]
            for d in range(dp):
                place = pl.multiple_of((d * size + place_of(z[0], k)) * rest, rest)
                out[:, pl.ds(place, rest)] = piece[:, d * rest : (d + 1) * rest]

    def index(i, z):
        return (lax.bitwise_xor(z[0], jnp.int32(i)) if rolled else i, 0)

    return call(
        kernel,
        [shape((rows, size * width), pieces[0].dtype)],
        list(pieces),
        [z],
        (size,),
        [blocked((block, width), index)] * size,
        [blocked((block, size * width), lambda i, z: (i, 0))],
        after=after,
    )[0]


def take_apart(full, z, rolled, after=()):
    size, dp = lax.axis_size("row"), lax.axis_size("dp")
    rows, width = full.shape
    rest = width // (size * dp)
    block = rows // size
    if rest % 128:
        if rolled:
            full = jnp.concatenate(
                [
                    lax.dynamic_slice_in_dim(full, other(z, i) * block, block, 0)
                    for i in range(size)
                ]
            )
        split = full.reshape(rows, dp, size, rest)
        split = jnp.take(split, partners(z, size), axis=2)
        return [split[:, :, k].reshape(rows, dp * rest) for k in range(size)]

    def kernel(z, full, *outs):
        for k in range(size):
            for d in range(dp):
                place = pl.multiple_of((d * size + other(z[0], k)) * rest, rest)
                outs[k][:, d * rest : (d + 1) * rest] = full[:, pl.ds(place, rest)]

    def index(i, z):
        return (lax.bitwise_xor(z[0], jnp.int32(i)) if rolled else i, 0)

    return call(
        kernel,
        [shape((rows, dp * rest), full.dtype)] * size,
        [full],
        [z],
        (size,),
        [blocked((block, width), lambda i, z: (i, 0))],
        [blocked((block, dp * rest), index)] * size,
        after=after,
    )


def project_kernel(x, gain, weight, cosine, sine, head_gain, a, scale, qr, kr, qn, kv):
    rows = x.shape[0]
    heads = qr.shape[1] // HEAD_SIZE
    kv_heads = kr.shape[1] // HEAD_SIZE

    @pl.when(pl.program_id(0) == 0)
    def _():
        for first in range(0, rows, 128):
            s = slice(first, first + 128)
            xf = x[s, :].astype(F32)
            r = lax.rsqrt(jnp.mean(xf * xf, axis=1, keepdims=True) + EPS)
            a[s, :] = (xf * r * gain[...]).astype(BF)
            scale[s, :] = r

    raw = dot(a[...], weight[0].reshape(MODEL_WIDTH, COLUMNS))

    def turn(values, gains):
        normed = (
            values
            * lax.rsqrt(jnp.mean(values * values, axis=-1, keepdims=True) + EPS)
            * gains
        )
        half = HEAD_SIZE // 2
        turned = jnp.concatenate([-normed[:, half:], normed[:, :half]], axis=-1)
        return (normed * cosine[...] + turned * sine[...]).astype(BF)

    for h in range(heads):
        s = slice(h * HEAD_SIZE, (h + 1) * HEAD_SIZE)
        qr[:, s] = raw[:, s]
        qn[:, s] = turn(raw[:, s], head_gain[0:1, :])
    first = heads * HEAD_SIZE
    for h in range(kv_heads):
        s = slice(h * HEAD_SIZE, (h + 1) * HEAD_SIZE)
        values = raw[:, first + h * HEAD_SIZE : first + (h + 1) * HEAD_SIZE]
        kr[:, s] = values
        kv[:, s] = turn(values, head_gain[1:2, :])
    kv[:, kv_heads * HEAD_SIZE :] = raw[:, first + kv_heads * HEAD_SIZE :].astype(BF)


def project(x, gain, weight, cosine, sine, head_gain, head_width, kv_width, after):
    rows = x.shape[0]
    cols, dp, _, width = weight.shape
    q = blocked((rows, head_width), lambda c: (0, c))
    k = blocked((rows, kv_width), lambda c: (0, c))
    return call(
        project_kernel,
        [
            shape(x.shape, BF),
            shape((rows, 1), F32),
            shape((rows, cols * head_width), F32),
            shape((rows, cols * kv_width), F32),
            shape((rows, cols * head_width), BF),
            shape((rows, 2 * cols * kv_width), BF),
        ],
        [x, gain, weight, cosine, sine, head_gain],
        (),
        (cols,),
        [None, None, blocked((1, dp, MODEL_WIDTH // dp, width), lambda c: (c, 0, 0, 0)), None, None, None],
        [None, None, q, k, q, blocked((rows, 2 * kv_width), lambda c: (0, c))],
        after=after,
    )


def mixed_parts(mixed, weight, z, base, after):
    size = lax.axis_size("row")
    cols, dp, total_rows, _ = weight.shape
    rows = mixed.shape[0]
    inner = mixed.shape[1] // (cols * dp)
    part = rows // size
    steps = MODEL_WIDTH // COLUMNS

    def kernel(z, mixed, weight, *refs):
        *outs, total = refs
        total[...] = dot(mixed[...], out_rows(weight))
        for k in range(size):
            first = pl.multiple_of(other(z[0], k) * part, part)
            outs[k][...] = total[pl.ds(first, part), :].astype(outs[k].dtype)

    return call(
        kernel,
        [shape((part, MODEL_WIDTH), BF if k else F32) for k in range(size)],
        [mixed, weight],
        [z],
        (steps,),
        [None, blocked((cols, dp, inner, COLUMNS), lambda c, z: (0, 0, base + c, 0))],
        [blocked((part, COLUMNS), lambda c, z: (0, c))] * size,
        scratch=[pltpu.VMEM((rows, COLUMNS), F32)],
        after=after,
    )


def mixed_back(chunks, weight, z, base, inner, after):
    size = len(chunks)
    cols, dp, _, _ = weight.shape
    part, width = chunks[0].shape
    rows = size * part
    heads = cols * dp * inner
    steps = width // COLUMNS

    def kernel(z, *refs):
        *ins, weight, full, out, total = refs
        for k in range(size):
            first = pl.multiple_of(other(z[0], k) * part, part)
            full[pl.ds(first, part), :] = ins[k][...]
        term = dot(full[...], out_rows(weight), "nt")
        c = pl.program_id(0)

        @pl.when(c == 0)
        def _():
            total[...] = term

        @pl.when(c > 0)
        def _():
            total[...] += term

        @pl.when(c == steps - 1)
        def _():
            out[...] = total[...].astype(BF)

    return call(
        kernel,
        [shape((rows, width), BF), shape((rows, heads), BF)],
        list(chunks) + [weight],
        [z],
        (steps,),
        [blocked((part, COLUMNS), lambda c, z: (0, c))] * size
        + [blocked((cols, dp, inner, COLUMNS), lambda c, z: (0, 0, base + c, 0))],
        [blocked((rows, COLUMNS), lambda c, z: (0, c)), None],
        scratch=[pltpu.VMEM((rows, heads), F32)],
        after=after,
    )


def masked(values, valid, after):
    def kernel(values, valid, out):
        out[...] = jnp.where(valid[...] > 0, values[...], jnp.zeros_like(values))

    return call(kernel, [shape(values.shape, values.dtype)], [values, valid], after=after)[0]


def add_parts(parts, dtype, after=()):
    def kernel(*refs):
        total = refs[0][...].astype(F32)
        for ref in refs[1:-1]:
            total = total + ref[...].astype(F32)
        refs[-1][...] = total.astype(dtype)

    return call(kernel, [shape(parts[0].shape, dtype)], list(parts), after=after)[0]


def hidden_norm(parts, x, gain, z, after=()):
    rows, width = parts[0].shape

    def kernel(z, *refs):
        *ps, x, gain, h, scale, a = refs
        total = x[...].astype(F32)
        for p in ps:
            total = total + p[...].astype(F32)
        r = lax.rsqrt(jnp.mean(total * total, axis=1, keepdims=True) + EPS)
        h[...] = total
        scale[...] = r
        a[...] = (total * r * gain[...]).astype(BF)

    return call(
        kernel,
        [shape((rows, width), F32), shape((rows, 1), F32), shape((rows, width), BF)],
        list(parts) + [x, gain],
        [z],
        (1,),
        [None] * len(parts) + [blocked((rows, width), lambda i, z: (z[0], 0)), None],
        after=after,
    )


def gateup_chunk(parts, weight, grad, hidden):
    part, width = parts[0].shape
    rows = part * len(parts)
    cols, dp, _, _ = weight.shape
    steps = 2 * hidden // (cols * COLUMNS)
    half = COLUMNS // 2

    def kernel(*refs):
        *ins, weight, grad, act, out, a = refs

        @pl.when((pl.program_id(0) == 0) & (pl.program_id(1) == 0))
        def _():
            for i, ref in enumerate(ins):
                a[i * part : (i + 1) * part, :] = ref[...]

        p = dot(a[...], weight[0].reshape(width, COLUMNS))
        for j in range(half // 128):
            gate, up = p[:, j * 256 : j * 256 + 128], p[:, j * 256 + 128 : j * 256 + 256]
            s = slice(j * 128, (j + 1) * 128)
            spread = 1.0 / (1.0 + jnp.exp(-gate))
            silu = gate * spread
            act[:, s] = (silu * up).astype(BF)
            g = grad[:, s]
            out[:, j * 256 : j * 256 + 128] = (g * up * (spread + silu * (1.0 - spread))).astype(BF)
            out[:, j * 256 + 128 : j * 256 + 256] = (g * silu).astype(BF)

    def place(c, t):
        return (0, c * steps + t)

    total = grad.shape[0]
    return call(
        kernel,
        [shape((total, hidden), BF), shape((total, 2 * hidden), BF)],
        list(parts) + [weight, grad],
        (),
        (cols, steps),
        [None] * len(parts)
        + [
            blocked((1, dp, width // dp, COLUMNS), lambda c, t: (c, 0, t, 0)),
            blocked((rows, half), place),
        ],
        [blocked((rows, half), place), blocked((rows, COLUMNS), place)],
        scratch=[pltpu.VMEM((rows, width), BF)],
        vmem=24,
    )


def gateup_back(grad, weight, kinds):
    cols, dp, _, _ = weight.shape
    both = grad.shape[1]
    block = MODEL_WIDTH // dp
    terms = both // COLUMNS
    per = terms // cols
    rows = grad.shape[0]
    part = rows // len(kinds)

    def kernel(grad, weight, *outs):
        total = None
        for t in range(terms):
            right = weight[t // per, 0, (t % per) * block : (t % per + 1) * block, :]
            term = dot(grad[:, t * COLUMNS : (t + 1) * COLUMNS], right, "nt")
            total = term if total is None else total + term
        for i, (out, kind) in enumerate(zip(outs, kinds)):
            out[...] = total[i * part : (i + 1) * part, :].astype(kind)

    return call(
        kernel,
        [shape((part, MODEL_WIDTH), kind) for kind in kinds],
        [grad, weight],
        (),
        (dp,),
        [
            None,
            blocked((cols, 1, per * block, COLUMNS), lambda n: (0, n, 0, 0)),
        ],
        [blocked((part, block), lambda n: (0, n))] * len(kinds),
        vmem=24,
    )


def down_back(out_low, weight, base, inner, after):
    cols, dp, _, _ = weight.shape
    rows, width = out_low.shape
    hidden = cols * dp * inner

    def kernel(low, weight, out):
        term = dot(low[...], out_rows(weight), "nt")

        @pl.when(pl.program_id(0) == 0)
        def _():
            out[...] = term

        @pl.when(pl.program_id(0) > 0)
        def _():
            out[...] += term

    return call(
        kernel,
        [shape((rows, hidden), F32)],
        [out_low, weight],
        (),
        (width // COLUMNS,),
        [
            blocked((rows, COLUMNS), lambda c: (0, c)),
            blocked((cols, dp, inner, COLUMNS), lambda c: (0, 0, base + c, 0)),
        ],
        [None],
        vmem=24,
        after=after,
    )[0]


def down_forward(active, hidden, weight, base, inner, after):
    cols, dp, _, _ = weight.shape
    rows, width = active.shape
    part = hidden.shape[0]

    def kernel(active, hidden, weight, out):
        p = dot(active[...], out_rows(weight))
        out[:part, :] = (p[:part, :] + hidden[...]).astype(BF)
        out[part:, :] = p[part:, :].astype(BF)

    return call(
        kernel,
        [shape((rows, MODEL_WIDTH), BF)],
        [active, hidden, weight],
        (),
        (MODEL_WIDTH // COLUMNS,),
        [
            None,
            blocked((part, COLUMNS), lambda c: (0, c)),
            blocked((cols, dp, inner, COLUMNS), lambda c: (0, 0, base + c, 0)),
        ],
        [blocked((rows, COLUMNS), lambda c: (0, c))],
        after=after,
    )[0]


def hidden_back(parts, h, scale, gain, out_low, after):
    rows, width = h.shape

    def kernel(*refs):
        *ps, h, scale, gain, dy, dh, low, gain_grad = refs
        grad = ps[0][...].astype(F32)
        for p in ps[1:]:
            grad = grad + p[...].astype(F32)
        hidden, r = h[...], scale[...]
        weighted = grad * gain[...]
        inner = jnp.sum(weighted * hidden, axis=1, keepdims=True)
        total = dy[...].astype(F32) + r * weighted - (r * r * r * inner / MODEL_WIDTH) * hidden
        dh[...] = total
        low[...] = total.astype(BF)
        gain_grad[...] = jnp.sum(grad * hidden * r, axis=0, keepdims=True)

    return call(
        kernel,
        [shape((rows, width), F32), shape((rows, width), BF), shape((1, width), F32)],
        list(parts) + [h, scale, gain, out_low],
        (),
        (1,),
        [None] * (len(parts) + 3) + [blocked((rows, width), lambda i: (0, 0))],
        after=after,
        hbm=2**17,
    )


def heads_back_kernel(
    qr, kr, dqn, dkn, dv, far, cosine, sine, head_gain, out, gain_grad
):
    heads = qr.shape[1] // HEAD_SIZE
    kv_heads = kr.shape[1] // HEAD_SIZE
    half = HEAD_SIZE // 2

    def back(raw, grad, gains):
        turned = grad * sine[...]
        turned = jnp.concatenate([turned[:, half:], -turned[:, :half]], axis=-1)
        g = grad * cosine[...] + turned
        r = lax.rsqrt(jnp.mean(raw * raw, axis=-1, keepdims=True) + EPS)
        weighted = g * gains
        inner = jnp.sum(weighted * raw, axis=-1, keepdims=True)
        low = (r * weighted - (r * r * r * inner / HEAD_SIZE) * raw).astype(BF)
        return low, jnp.sum(g * raw * r, axis=0, keepdims=True)

    @pl.when(pl.program_id(0) == 0)
    def _():
        gain_grad[...] = jnp.zeros_like(gain_grad)

    for h in range(heads):
        s = slice(h * HEAD_SIZE, (h + 1) * HEAD_SIZE)
        low, total = back(qr[:, s], dqn[:, s], head_gain[0:1, :])
        out[:, s] = low
        gain_grad[0:1, :] += total
    first = heads * HEAD_SIZE
    for h in range(kv_heads):
        s = slice(h * HEAD_SIZE, (h + 1) * HEAD_SIZE)
        low, total = back(kr[:, s], dkn[:, s] + far[:, s].astype(F32), head_gain[1:2, :])
        out[:, first + h * HEAD_SIZE : first + (h + 1) * HEAD_SIZE] = low
        gain_grad[1:2, :] += total
    first += kv_heads * HEAD_SIZE
    out[:, first:] = (dv[...] + far[:, kv_heads * HEAD_SIZE :].astype(F32)).astype(BF)


def heads_back(qr, kr, dqn, dkn, dv, far, cosine, sine, head_gain, cols, after):
    rows = qr.shape[0]
    head_width, kv_width = qr.shape[1] // cols, kr.shape[1] // cols
    q = blocked((rows, head_width), lambda c: (0, c))
    k = blocked((rows, kv_width), lambda c: (0, c))
    far_kv = blocked((rows, 2 * kv_width), lambda c: (0, c))
    width = head_width + 2 * kv_width
    return call(
        heads_back_kernel,
        [shape((rows, cols * width), BF), shape((2, HEAD_SIZE), F32)],
        [qr, kr, dqn, dkn, dv, far, cosine, sine, head_gain],
        (),
        (cols,),
        [q, k, q, k, k, far_kv, None, None, None],
        [blocked((rows, width), lambda c: (0, c)), None],
        after=after,
    )


def input_back(grads, weight, x, scale, gain, dh, z, after):
    cols, steps, _, width = weight.shape
    rows = grads.shape[0]
    model = MODEL_WIDTH
    part = dh.shape[0]

    def kernel(z, grads, weight, x, scale, gain, dh, out, c1, gain_grad):
        total = dot(grads[:, :width], weight[0, 0], "nt")
        for c in range(1, cols):
            total = total + dot(grads[:, c * width : (c + 1) * width], weight[c, 0], "nt")
        r = scale[...]
        xf = x[...].astype(F32)
        weighted = total * gain[...]
        moved = weighted * xf
        gain_grad[...] = jnp.sum(total * xf * r, axis=0, keepdims=True)
        out[...] = (r * weighted).astype(BF)
        first = pl.multiple_of(z[0] * part, part)
        own = pl.ds(first, part)
        out[own, :] = (out[own, :].astype(F32) + dh[...]).astype(BF)

        @pl.when(pl.program_id(0) == 0)
        def _():
            c1[...] = jnp.zeros_like(c1)

        c1[...] += jnp.sum(moved, axis=1, keepdims=True)

    block = model // steps
    wide = blocked((rows, block), lambda n, z: (0, n))
    return call(
        kernel,
        [shape((rows, model), BF), shape((rows, 1), F32), shape((1, model), F32)],
        [grads, weight, x, scale, gain, dh],
        [z],
        (steps,),
        [
            None,
            blocked((cols, 1, block, width), lambda n, z: (0, n, 0, 0)),
            wide,
            None,
            blocked((1, block), lambda n, z: (0, n)),
            blocked((part, block), lambda n, z: (0, n)),
        ],
        [wide, None, blocked((1, block), lambda n, z: (0, n))],
        after=after,
    )


def weight_grads(lefts, right, out_left, out_right, cols, after=()):
    size, dp = lax.axis_size("row"), lax.axis_size("dp")
    rows = right.shape[0]
    block = MODEL_WIDTH // dp
    n = right.shape[1] // cols
    part = rows // len(lefts)
    m = out_left.shape[1] // cols
    inner = m // dp
    terms = n // COLUMNS
    total = terms * block + MODEL_WIDTH // COLUMNS * inner

    def kernel(*refs):
        *ins, right, out_left, out_right, out = refs
        left = jnp.concatenate([ref[...] for ref in ins]) if len(ins) > 1 else ins[0][...]
        for t in range(terms):
            term = dot(left, right[:, t * COLUMNS : (t + 1) * COLUMNS], "tn")
            out[0, 0, t * block : (t + 1) * block, :] = term.astype(BF)
        for d in range(dp):
            q, r = d // (dp // size), d % (dp // size)
            first = (r * size + q) * inner

            @pl.when(pl.program_id(1) == d)
            def _():
                term = dot(out_left[:, first : first + inner], out_right[...], "tn").astype(BF)
                for c in range(MODEL_WIDTH // COLUMNS):
                    place = terms * block + c * inner
                    piece = term[:, c * COLUMNS : (c + 1) * COLUMNS]
                    out[0, 0, place : place + inner, :] = piece

    return call(
        kernel,
        [in_hbm((cols, dp, total, COLUMNS), BF)],
        list(lefts) + [right, out_left, out_right],
        (),
        (cols, dp),
        [blocked((part, block), lambda c, d: (0, d))] * len(lefts)
        + [
            blocked((rows, n), lambda c, d: (0, c)),
            blocked((rows, m), lambda c, d: (0, c)),
            None,
        ],
        [blocked((1, 1, total, COLUMNS), lambda c, d: (c, d, 0, 0))],
        after=after,
        vmem=28,
    )[0]


def swap(value, axis, step):
    return lax.ppermute(value, axis, [(i, i ^ step) for i in range(lax.axis_size(axis))])


def gather_pieces(own, beside=None):
    two = swap(own, "row", 2)
    if beside is not None:
        two, beside = lax.optimization_barrier((two, beside))
    pieces = [own, swap(own, "row", 1), two, swap(two, "row", 1)]
    return pieces if beside is None else (pieces, beside)


def gather_direct(own):
    return along_row([own] * lax.axis_size("row"), True)


def scatter_pieces(pieces):
    sent = add_parts([pieces[2], swap(pieces[3], "row", 1)], BF)
    direct, sent = lax.optimization_barrier((pieces[1], sent))
    return [pieces[0], swap(direct, "row", 1), swap(sent, "row", 2)], sent


def add_along(value, axes):
    for axis in axes:
        step = 1
        while step < lax.axis_size(axis):
            value = value + swap(value, axis, step)
            step *= 2
    return value


def along_row(pieces, forward):
    size = len(pieces)
    sign = 1 if forward else -1
    return [pieces[0]] + [
        lax.ppermute(p, "row", [(i, (i + sign * k) % size) for i in range(size)])
        for k, p in enumerate(pieces)
        if k
    ]


def along_quarters(pieces, forward):
    size = len(pieces)
    per = lax.axis_size("dp") // size
    sign = 1 if forward else -1

    def pairs(k):
        places = [(q, r) for q in range(size) for r in range(per)]
        return [(q * per + r, (q + sign * k) % size * per + r) for q, r in places]

    return [pieces[0]] + [lax.ppermute(p, "dp", pairs(k)) for k, p in enumerate(pieces) if k]


def gather_shard(shard):
    full = lax.all_gather(shard, ("col", "dp"), axis=0)
    return full.reshape(lax.axis_size("col"), lax.axis_size("dp"), *shard.shape)


def scatter_shard(full):
    flat_rows = full.reshape(-1, full.shape[-1])
    return lax.psum_scatter(flat_rows, ("col", "dp"), scatter_dimension=0, tiled=True)


def quarter_index():
    return lax.axis_index("dp") // (lax.axis_size("dp") // lax.axis_size("row"))


def pack_attention(query, keyval, z):
    size = lax.axis_size("row")
    rows = query.shape[0]
    hw, kw = query.shape[1] // size, keyval.shape[2] // size

    def kernel(z, query, keyval, *outs):
        for k in range(size):
            at = ahead(z[0], k, size)
            out = outs[k]
            out[:, :hw] = query[:, pl.ds(pl.multiple_of(at * hw, hw), hw)].astype(BF)
            for s in range(2):
                part = keyval[:, s, pl.ds(pl.multiple_of(at * kw, kw), kw)]
                out[:, hw + s * kw : hw + (s + 1) * kw] = part.astype(BF)

    return call(kernel, [shape((rows, hw + 2 * kw), BF)] * size, [query, keyval], [z], hbm=0)


def pack_feed(gateup, downs, z, after):
    size = lax.axis_size("row")
    rows = gateup.shape[0]
    fw = gateup.shape[2] // size
    terms = 2 * fw // COLUMNS
    inner = downs[0].shape[0]

    def kernel(z, gateup, *refs):
        for k in range(size):
            at = ahead(z[0], k, size)
            out = refs[size + k]
            for s in range(2):
                for j in range(fw // 128):
                    first = pl.multiple_of(at * fw + j * 128, 128)
                    place = (2 * j + s) * 128
                    t, lane = place // COLUMNS, place % COLUMNS
                    part = gateup[:, s, pl.ds(first, 128)].astype(BF)
                    out[t * rows : (t + 1) * rows, lane : lane + 128] = part
            out[terms * rows :, :] = refs[k][...]

    return call(
        kernel,
        [shape((terms * rows + inner, COLUMNS), BF)] * size,
        [gateup, *downs],
        [z],
        after=after,
        vmem=32,
    )


def pack_out(blocks, after=()):
    size = lax.axis_size("row")
    rows = [b.shape[0] // size for b in blocks]

    def kernel(q, *refs):
        for k in range(size):
            place = 0
            for ref, n in zip(refs, rows):
                first = pl.multiple_of(ahead(q[0], k, size) * n, n)
                refs[len(rows) + k][place : place + n, :] = ref[pl.ds(first, n), :].astype(BF)
                place += n

    return call(
        kernel,
        [shape((sum(rows), blocks[0].shape[1]), BF)] * size,
        blocks,
        [quarter_index()],
        after=after,
        hbm=0,
    )


def regroup(parts, source, target, cuts, after=()):
    size = len(parts)
    sources = [source(k) for k in range(size)]
    targets = [target(k) for k in range(size)]
    starts = [sum(cuts[:i]) for i in range(len(cuts))]

    def kernel(*refs):
        places, ins = refs[: 2 * size], refs[2 * size : 3 * size]
        outs, held = refs[3 * size : -1], refs[-1]
        for k in range(size):
            held[places[k][0]] = ins[k][...]
        for i, (first, n) in enumerate(zip(starts, cuts)):
            for k in range(size):
                outs[i * size + k][...] = held[places[size + k][0], first : first + n]

    rows, width = parts[0].shape
    outs = call(
        kernel,
        [shape((n, width), BF) for n in cuts for _ in range(size)],
        parts,
        sources + targets,
        scratch=[pltpu.VMEM((size, rows, width), BF)],
        after=after,
    )
    return [outs[i * size : (i + 1) * size] for i in range(len(cuts))]


def make_shard(in_parts, out_parts, z, after=()):
    size, dp = len(in_parts), lax.axis_size("dp")
    rest = MODEL_WIDTH // (size * dp)
    steps = MODEL_WIDTH // COLUMNS
    rows = MODEL_WIDTH // (size * dp)
    if isinstance(out_parts, int):
        inner, joined = out_parts, True
        terms = (in_parts[0].shape[0] - inner) // rows
    else:
        inner, joined = out_parts[0].shape[0], False
        terms = in_parts[0].shape[0] // rows
    base = terms * size * rows
    if rest % 128:
        order = behind(z, jnp.arange(size), size)
        if joined:
            out_parts = [p[terms * rows :] for p in in_parts]
            in_parts = [p[: terms * rows] for p in in_parts]
        full = jnp.take(jnp.stack(in_parts), order, axis=0).reshape(size, terms, rows, COLUMNS)
        ins = full.transpose(1, 0, 2, 3).reshape(base, COLUMNS)
        full = jnp.stack([p.reshape(inner, dp, rest) for p in out_parts], axis=2)
        full = jnp.take(full, order, axis=2).reshape(inner, steps, COLUMNS)
        return jnp.concatenate([ins, full.transpose(1, 0, 2).reshape(-1, COLUMNS)])

    def kernel(z, *refs):
        out = refs[-1]
        for k in range(size):
            at = behind(z[0], k, size)
            for t in range(terms):
                first = pl.multiple_of((t * size + at) * rows, rows)
                out[pl.ds(first, rows), :] = refs[k][t * rows : (t + 1) * rows, :]
            place = pl.multiple_of(at * rest, rest)
            ref = refs[k] if joined else refs[size + k]
            top = terms * rows if joined else 0
            for d in range(dp):
                first = base + d * inner
                part = ref[top : top + inner, d * rest : (d + 1) * rest]
                out[first : first + inner, pl.ds(place, rest)] = part

    parts = list(in_parts) if joined else list(in_parts) + list(out_parts)
    out = shape((base + steps * inner, COLUMNS), BF)
    return call(kernel, [out], parts, [z], after=after)[0]


def split_shard(shard, terms, rows, inner, z, after=()):
    size, dp = lax.axis_size("row"), lax.axis_size("dp")
    rest = MODEL_WIDTH // (size * dp)
    steps = MODEL_WIDTH // COLUMNS
    base = terms * size * rows
    if rest % 128:
        ins = shard[:base].reshape(terms, size, rows, COLUMNS).transpose(1, 0, 2, 3)
        ins = jnp.take(ins, behind(z, jnp.arange(size), size), axis=0)
        outs = shard[base:].reshape(steps, inner, COLUMNS).transpose(1, 0, 2)
        outs = outs.reshape(inner, dp, size, rest)
        outs = jnp.take(outs, behind(z, jnp.arange(size), size), axis=2)
        return [
            jnp.concatenate([ins[k].reshape(-1, COLUMNS), outs[:, :, k].reshape(inner, COLUMNS)])
            for k in range(size)
        ]

    def kernel(z, full, *outs):
        for k in range(size):
            at = behind(z[0], k, size)
            for t in range(terms):
                first = pl.multiple_of((t * size + at) * rows, rows)
                outs[k][t * rows : (t + 1) * rows, :] = full[pl.ds(first, rows), :]
            place = pl.multiple_of(at * rest, rest)
            for d in range(dp):
                part = full[base + d * inner : base + (d + 1) * inner, pl.ds(place, rest)]
                outs[k][terms * rows :, d * rest : (d + 1) * rest] = part

    return call(
        kernel,
        [shape((terms * rows + inner, COLUMNS), BF)] * size,
        [shard],
        [z],
        after=after,
    )


def split_attention(shard, terms, rows, inner, z, after=()):
    size, dp = lax.axis_size("row"), lax.axis_size("dp")
    rest = MODEL_WIDTH // (size * dp)
    steps = MODEL_WIDTH // COLUMNS
    base = terms * size * rows
    quarter = quarter_index()
    if rest % 128:
        ins = shard[:base].reshape(terms, size, rows, COLUMNS).transpose(1, 0, 2, 3)
        ins = jnp.take(ins, behind(z, jnp.arange(size), size), axis=0)
        outs = shard[base:].reshape(steps, inner, COLUMNS).transpose(1, 0, 2)
        outs = outs.reshape(inner, dp, size, rest)
        outs = jnp.take(outs, ahead(quarter, jnp.arange(size), size), axis=2)
        return (
            [ins[k].reshape(-1, COLUMNS) for k in range(size)],
            [outs[:, :, k].reshape(inner, COLUMNS) for k in range(size)],
        )

    def kernel(z, quarter, full, *outs):
        for k in range(size):
            at = behind(z[0], k, size)
            for t in range(terms):
                first = pl.multiple_of((t * size + at) * rows, rows)
                outs[k][t * rows : (t + 1) * rows, :] = full[pl.ds(first, rows), :]
            place = pl.multiple_of(ahead(quarter[0], k, size) * rest, rest)
            for d in range(dp):
                part = full[base + d * inner : base + (d + 1) * inner, pl.ds(place, rest)]
                outs[size + k][:, d * rest : (d + 1) * rest] = part

    pieces = call(
        kernel,
        [shape((terms * rows, COLUMNS), BF)] * size + [shape((inner, COLUMNS), BF)] * size,
        [shard],
        [z, quarter],
        after=after,
    )
    return pieces[:size], pieces[size:]


def turned_back(pieces):
    size = len(pieces)
    per = lax.axis_size("dp") // size
    result = []
    for k, piece in enumerate(pieces):
        pairs = []
        for q in range(size):
            for r in range(per):
                for z in range(size):
                    target = (z * per + r) * size + (q + k) % size
                    pairs.append(((q * per + r) * size + z, target))
        result.append(lax.ppermute(piece, ("dp", "row"), pairs))
    return result


def out_pieces(messages, inner, z):
    size = len(messages)
    quarter = quarter_index()
    parts = regroup(
        [m[-inner:] for m in messages],
        lambda k: ahead(z, k, size),
        lambda k: ahead(quarter, k, size),
        [inner],
    )[0]
    return along_quarters(parts, True)


def update(refs, grad, rate):
    weight, moment, second, weight_new, moment_new, second_new = refs
    m, v, w = adamw(weight[...], moment[...], second[...], grad, rate, DECAY)
    moment_new[...] = m
    second_new[...] = v
    weight_new[...] = w


def update_out(state, pieces, rate, place):
    size = len(pieces)
    rows, width = pieces[0].shape

    def kernel(q, *refs):
        k = pl.program_id(0)
        for i in range(size):

            @pl.when(k == i)
            def _():
                update(refs[size:], refs[i][...].astype(F32), rate)

    spec = blocked((rows, width), lambda k, q: (lax.bitwise_and(q[0] + size - k, size - 1), 0))
    w, m, v = call(
        kernel,
        [shape(state[0].shape, F32)] * 3,
        list(pieces) + list(state),
        [place],
        (size,),
        [None] * size + [spec] * 3,
        [spec] * 3,
        hbm=2**19,
    )
    return m, v, w


def place_columns(messages, rows, cuts, z):
    size = len(messages)

    def kernel(z, *refs):
        for out, cut in zip(refs[size:], cuts):
            width = sum(w for _, _, w in cut)
            for k in range(size):
                at = ahead(z[0], k, size) * width
                for t, first, w in cut:
                    place = pl.multiple_of(at, 128)
                    part = refs[k][t * rows : (t + 1) * rows, first : first + w]
                    out[:, pl.ds(place, w)] = part
                    at = at + w

    out = [shape((rows, size * sum(w for _, _, w in cut)), BF) for cut in cuts]
    return call(kernel, out, messages, [z])


def flat(values):
    rows, two, width = values.shape
    return values.reshape(rows, two, width // 128, 128).transpose(0, 2, 1, 3).reshape(-1, 128)


def update_pair(state, grad, rate):
    rows, two, width = state[0].shape
    total = rows * two * width // 128
    steps = 4 if total % 64 == 0 else 1

    def kernel(grad, *refs):
        update(refs, grad[...].astype(F32), rate)

    spec = blocked((total // steps, 128), lambda i: (i, 0))
    news = call(
        kernel,
        [shape((total, 128), F32)] * 3,
        [grad.reshape(-1, 128)] + [flat(s) for s in state],
        (),
        (steps,),
        [spec] * 4,
        [spec] * 3,
        hbm=2**19,
    )
    w, m, v = [
        n.reshape(rows, width // 128, two, 128).transpose(0, 2, 1, 3).reshape(rows, two, width)
        for n in news
    ]
    return (m, v, w), news[0]


def adamw(weight, moment, second, grad, rate, decay):
    moment_new = BETA_ONE * moment + (1.0 - BETA_ONE) * grad
    second_new = BETA_TWO * second + (1.0 - BETA_TWO) * grad * grad
    first_hat = moment_new / (1.0 - BETA_ONE**STEP)
    second_hat = second_new / (1.0 - BETA_TWO**STEP)
    weight_new = weight - rate * (first_hat / (jnp.sqrt(second_hat) + ADAM_EPS) + decay * weight)
    return (moment_new, second_new, weight_new)


def body(
    tokens,
    cotangent,
    seq_lens,
    query_weight,
    query_moment,
    query_second,
    key_value_master_weight,
    key_value_first_moment,
    key_value_second_moment,
    output_weight,
    output_moment,
    output_second,
    gateup_weight,
    gateup_moment,
    gateup_second,
    down_weight,
    down_moment,
    down_second,
    norm_gains,
    norm_moment,
    norm_second,
    head_gains,
    head_moment,
    head_second,
):
    size, dp, cols = lax.axis_size("row"), lax.axis_size("dp"), lax.axis_size("col")
    z, y = lax.axis_index("row"), lax.axis_index("col")
    rows = tokens.shape[0]
    quarter = rows // size
    item_count = rows * cols
    rest = MODEL_WIDTH // (size * dp)
    head_width = query_weight.shape[1] // size
    kv_width = key_value_master_weight.shape[2] // size

    gains = norm_gains.reshape(2, size, dp, rest).transpose(0, 2, 1, 3).reshape(2, MODEL_WIDTH)
    first_gain, second_gain = gains[0:1], gains[1:2]

    segment, position = token_layout(seq_lens[0], item_count)
    first = y * rows
    own_segment = lax.dynamic_slice_in_dim(segment, first, rows, 0)
    cosine, sine = rope_tables(lax.dynamic_slice_in_dim(position, first, rows, 0))
    valid = (own_segment < SEQS).astype(jnp.int32)[:, None]

    hidden_width = gateup_weight.shape[2] // size * cols

    in_rows = query_weight.shape[0]
    output_inner, down_inner = output_weight.shape[0] // size, down_weight.shape[0] // size
    gateup_terms = 2 * hidden_width // (cols * COLUMNS)
    steps = MODEL_WIDTH // COLUMNS
    down_base = gateup_terms * size * in_rows // down_inner
    output_base = size * in_rows // output_inner
    quarter_place = quarter_index()
    input_chunks = gather_pieces(tokens)
    attention_pieces = pack_attention(query_weight, key_value_master_weight, z)
    out_pieces_sent = pack_out([down_weight, output_weight], attention_pieces[:1])
    down_parts, output_parts = regroup(
        along_quarters(out_pieces_sent, True),
        lambda k: behind(quarter_place, k, size),
        lambda k: ahead(z, k, size),
        [down_inner, output_inner],
    )
    feed_pieces = pack_feed(gateup_weight, down_parts, z, output_parts[:1])
    attention_shard = make_shard(
        along_row(attention_pieces, True),
        along_row(output_parts, True),
        z,
        [feed_pieces[0], input_chunks[2]],
    )
    attention_full = gather_shard(attention_shard)
    inputs = assemble(input_chunks, z, False, False, [attention_shard])
    feed_shard = make_shard(along_row(feed_pieces, True), down_inner, z, [inputs])
    feed_full = gather_shard(feed_shard)
    out_own = masked(cotangent, valid, [feed_shard])
    out_chunks = gather_pieces(out_own)

    first_low, first_scale, query_raw, key_raw, query, keys_values = project(
        inputs,
        first_gain,
        attention_full,
        cosine,
        sine,
        head_gains,
        head_width,
        kv_width,
        [out_own],
    )
    before = lax.ppermute(keys_values, "col", [(i, i + 1) for i in range(cols - 1)])
    masks = (
        y.astype(jnp.int32).reshape(1),
        own_segment.reshape(rows, 1),
        own_segment.reshape(1, rows),
        segment[:rows].reshape(1, rows),
    )
    mixed, logsum = attention_forward(*masks, query, keys_values, before, [])
    hidden_pieces = mixed_parts(mixed, attention_full, z, output_base, out_chunks[1:])
    out_low = assemble(out_chunks, z, True, False, hidden_pieces[1:2])
    hidden_parts, _ = scatter_pieces(hidden_pieces)
    hidden, second_scale, second_low = hidden_norm(hidden_parts, inputs, second_gain, z)

    second_chunks = gather_pieces(second_low)
    active_grad = down_back(out_low, feed_full, down_base, down_inner, second_chunks[2:3])
    active, pair_grad = gateup_chunk(second_chunks, feed_full, active_grad, hidden_width)
    second_parts = gateup_back(pair_grad, feed_full, (F32, BF, BF, BF))
    feed_grads = weight_grads(
        second_chunks, pair_grad, active, out_low, cols, [second_parts[3]]
    )
    passed = swap(second_parts[3], "row", 1)
    feed_grads, passed = lax.optimization_barrier((feed_grads, passed))
    sent = add_parts([second_parts[2], passed], BF)
    direct, sent = lax.optimization_barrier((second_parts[1], sent))
    second_parts = [second_parts[0], swap(direct, "row", 1), swap(sent, "row", 2)]
    feed_total = scatter_shard(feed_grads)
    hidden_grad, hidden_low, second_gain_grad = hidden_back(
        second_parts, hidden, second_scale, second_gain, out_low, []
    )

    layer_part = down_forward(active, hidden, feed_full, down_base, down_inner, [hidden_low])
    hidden_all, mixed_grad = mixed_back(
        gather_pieces(hidden_low), attention_full, z, output_base, output_inner, [layer_part]
    )
    layer_pieces = take_apart(layer_part, z, True, [hidden_all])
    query_grad, key_grad, value_grad, far_sent = attention_backward(
        *masks, query, keys_values, before, mixed_grad, logsum, layer_pieces[:1]
    )
    far = lax.ppermute(far_sent, "col", [(i + 1, i) for i in range(cols - 1)])
    layer_parts, _ = scatter_pieces(layer_pieces)
    layer_output = add_parts(layer_parts, F32)
    raw_grad, head_part = heads_back(
        query_raw,
        key_raw,
        query_grad,
        key_grad,
        value_grad,
        far,
        cosine,
        sine,
        head_gains,
        cols,
        [layer_output],
    )
    attention_grads = weight_grads([first_low], raw_grad, mixed, hidden_all, cols)
    attention_grads, feed_total = lax.optimization_barrier((attention_grads, feed_total))
    attention_total = scatter_shard(attention_grads)
    feed_pieces = split_shard(feed_total, gateup_terms, in_rows, down_inner, z)
    input_part, inner_part, first_gain_grad = input_back(
        raw_grad,
        attention_full,
        inputs,
        first_scale,
        first_gain,
        hidden_grad,
        z,
        feed_pieces[:1],
    )
    input_pieces = take_apart(input_part, z, False)
    input_parts, _ = scatter_pieces(input_pieces)
    feed_messages = along_row(feed_pieces, False)
    norm_part = jnp.concatenate([first_gain_grad, second_gain_grad])
    norm_part = norm_part.reshape(2, dp, size, rest).transpose(0, 2, 1, 3).reshape(2, MODEL_WIDTH)
    gain_part = jnp.concatenate([norm_part.reshape(-1), head_part.reshape(-1)]).reshape(-1, 128)
    gain_part, feed_messages[1] = lax.optimization_barrier((gain_part, feed_messages[1]))
    gain_part = add_along(gain_part, ("dp", "col"))
    small = jnp.concatenate([gain_part, inner_part.reshape(-1, 128)])
    small = add_along(small, ("row",)).reshape(-1)
    inner = small[gain_part.size :][:, None]
    norm_total = small[: norm_part.size].reshape(norm_part.shape)
    head_total = small[norm_part.size : gain_part.size].reshape(head_part.shape)

    down_new = update_out(
        (down_weight, down_moment, down_second),
        out_pieces(feed_messages, down_inner, z),
        RATES[4],
        quarter_place,
    )
    cut = [(t, 0, COLUMNS) for t in range(gateup_terms)]
    (gateup_total,) = place_columns(feed_messages, in_rows, [cut], z)
    gateup_new, gateup_flat = update_pair(
        (gateup_weight, gateup_moment, gateup_second), gateup_total, RATES[3]
    )
    attention_pieces, output_pieces = split_attention(
        attention_total, 1, in_rows, output_inner, z, [gateup_flat]
    )
    output_pieces = turned_back(output_pieces)
    attention_messages = along_row(attention_pieces, False)
    output_new = update_out(
        (output_weight, output_moment, output_second), output_pieces, RATES[2], z
    )
    query_total, keyval_total = place_columns(
        attention_messages,
        in_rows,
        [[(0, 0, head_width)], [(0, head_width, 2 * kv_width)]],
        z,
    )
    input_grad = add_parts(input_parts, F32, [query_total]) - (
        first_scale * first_scale * first_scale * inner / MODEL_WIDTH
    ) * tokens.astype(F32)
    query_new = adamw(
        query_weight, query_moment, query_second, query_total.astype(F32), RATES[0], DECAY
    )
    keyval_new, _ = update_pair(
        (key_value_master_weight, key_value_first_moment, key_value_second_moment),
        keyval_total,
        RATES[1],
    )
    norm_new = adamw(norm_gains, norm_moment, norm_second, norm_total, GAIN_RATE, 0.0)
    head_new = adamw(head_gains, head_moment, head_second, head_total, GAIN_RATE, 0.0)
    return (
        layer_output,
        input_grad,
        *query_new,
        *keyval_new,
        *output_new,
        *gateup_new,
        *down_new,
        *norm_new,
        *head_new,
    )


def solution(mesh):
    items = P(("dp", "col"), "row")
    inward = P(("row", "dp"), "col")
    inward_pair = P(("row", "dp"), None, "col")
    outward = P(("col", "dp"), "row")
    weights = (
        (inward,) * 3 + (inward_pair,) * 3 + (outward,) * 3 + (inward_pair,) * 3 + (outward,) * 3
    )
    return jax.shard_map(
        body,
        mesh=mesh,
        in_specs=(items, items, P("dp", None)) + weights + (P(),) * 6,
        out_specs=(items, items) + weights + (P(),) * 6,
        check_vma=False,
    )
```

```python
import functools
import math

import jax
import jax.numpy as jnp
from jax import lax
from jax.experimental import pallas as pl
from jax.experimental.pallas import tpu as pltpu
from jax.sharding import PartitionSpec as P

MODEL_WIDTH = 2048
HEAD_SIZE = 128
SEQS = 4
STEP = 10

EPS = 1e-06
THETA = 1000000.0
NEGATIVE = -1e30
BETA_ONE = 0.9
BETA_TWO = 0.95
ADAM_EPS = 1e-08
DECAY = 0.1
RATES = (0.066, 0.066, 0.5, 0.066, 0.04)
GAIN_RATE = 0.6
BF = jnp.bfloat16
F32 = jnp.float32
SCALE = 1.0 / math.sqrt(HEAD_SIZE)


def dot(a, b, kind="nn"):
    dims = {"nn": ((1,), (0,)), "nt": ((1,), (1,)), "tn": ((0,), (0,))}[kind]
    return lax.dot_general(a, b, (dims, ((), ())), preferred_element_type=F32)


def token_layout(lengths, item_count):
    ends = jnp.cumsum(lengths)
    places = jnp.arange(item_count, dtype=jnp.int32)
    segment = jnp.sum((places[:, None] >= ends[None, :]).astype(jnp.int32), axis=1)
    starts = jnp.concatenate([ends - lengths, ends[-1:]])
    labels = jnp.arange(starts.shape[0], dtype=jnp.int32)
    begin = jnp.sum(jnp.where(segment[:, None] == labels[None, :], starts[None, :], 0), axis=1)
    return (segment, places - begin)


def rope_tables(position):
    half = HEAD_SIZE // 2
    freq = jnp.exp(jnp.arange(half, dtype=F32) * (-2.0 * math.log(THETA) / HEAD_SIZE))
    angle = position.astype(F32)[:, None] * freq[None, :]
    angle = jnp.concatenate([angle, angle], axis=1)
    return (jnp.cos(angle), jnp.sin(angle))


def block_masks(own_col, own_row, prev_row, later):
    rows = own_col.shape[0]
    r = lax.broadcasted_iota(jnp.int32, (rows, rows), 0)
    c = lax.broadcasted_iota(jnp.int32, (rows, rows), 1)
    own = (c <= r) & (own_col == own_row)
    prev = (own_col == prev_row) & (later > 0)
    return own, prev


def forward_kernel(later, own_col, own_row, prev_row, q, k, v, kp, vp, o, lse):
    own, prev = block_masks(own_col[...], own_row[...], prev_row[...], later[0])
    s_own = jnp.where(own, dot(q[...], k[...], "nt") * SCALE, NEGATIVE)
    s_prev = jnp.where(prev, dot(q[...], kp[...], "nt") * SCALE, NEGATIVE)
    top = jnp.maximum(
        jnp.max(s_own, axis=1, keepdims=True), jnp.max(s_prev, axis=1, keepdims=True)
    )
    total = jnp.sum(jnp.exp(s_own - top), axis=1, keepdims=True) + jnp.sum(
        jnp.exp(s_prev - top), axis=1, keepdims=True
    )
    logsum = top + jnp.log(total)
    p_own = jnp.exp(s_own - logsum).astype(BF)
    p_prev = jnp.exp(s_prev - logsum).astype(BF)
    o[...] = (dot(p_own, v[...]) + dot(p_prev, vp[...])).astype(BF)
    lse[0] = logsum


def attention_forward(later, own_col, own_row, prev_row, q, kv, before, after):
    rows, width = q.shape
    heads = width // HEAD_SIZE
    groups = 2 * width // kv.shape[1]
    inputs = (later, own_col, own_row, prev_row, q, kv, kv, before, before)

    def kernel(*refs):
        forward_kernel(*refs[: len(inputs)], *refs[len(inputs) + len(after) :])

    mine = pl.BlockSpec((rows, HEAD_SIZE), lambda h: (0, h))
    key = pl.BlockSpec((rows, HEAD_SIZE), lambda h: (0, 2 * (h // groups)))
    value = pl.BlockSpec((rows, HEAD_SIZE), lambda h: (0, 2 * (h // groups) + 1))
    column = pl.BlockSpec((rows, 1), lambda h: (0, 0))
    line = pl.BlockSpec((1, rows), lambda h: (0, 0))
    return pl.pallas_call(
        kernel,
        grid=(heads,),
        in_specs=[pl.BlockSpec(memory_space=pltpu.SMEM), column, line, line, mine]
        + [key, value] * 2
        + [pl.BlockSpec(memory_space=pl.ANY)] * len(after),
        out_specs=[mine, pl.BlockSpec((1, rows, 1), lambda h: (h, 0, 0))],
        out_shape=[
            jax.ShapeDtypeStruct((rows, width), BF),
            jax.ShapeDtypeStruct((heads, rows, 1), F32),
        ],
        compiler_params=pltpu.CompilerParams(vmem_limit_bytes=32 * 2**20),
    )(*inputs, *after)


def backward_kernel(
    later, own_col, own_row, prev_row, q, k, v, kp, vp, do, lse, dq, dk, dv, far, total
):
    own, prev = block_masks(own_col[...], own_row[...], prev_row[...], later[0])
    logsum = lse[0]
    p_own = jnp.exp(jnp.where(own, dot(q[...], k[...], "nt") * SCALE, NEGATIVE) - logsum)
    p_prev = jnp.exp(jnp.where(prev, dot(q[...], kp[...], "nt") * SCALE, NEGATIVE) - logsum)
    d_own = dot(do[...], v[...], "nt")
    d_prev = dot(do[...], vp[...], "nt")
    delta = jnp.sum(p_own * d_own, axis=1, keepdims=True) + jnp.sum(
        p_prev * d_prev, axis=1, keepdims=True
    )
    g_own = (p_own * (d_own - delta)).astype(BF)
    g_prev = (p_prev * (d_prev - delta)).astype(BF)
    dq[...] = (dot(g_own, k[...]) + dot(g_prev, kp[...])) * SCALE
    near = ((dk, dot(g_own, q[...], "tn") * SCALE), (dv, dot(p_own.astype(BF), do[...], "tn")))
    dkp = dot(g_prev, q[...], "tn") * SCALE
    dvp = dot(p_prev.astype(BF), do[...], "tn")
    group = pl.program_id(1)

    @pl.when(group == 0)
    def _():
        for ref, value in near:
            ref[...] = value
        total[:, :HEAD_SIZE] = dkp
        total[:, HEAD_SIZE:] = dvp

    @pl.when(group > 0)
    def _():
        for ref, value in near:
            ref[...] += value
        total[:, :HEAD_SIZE] += dkp
        total[:, HEAD_SIZE:] += dvp

    @pl.when(group == pl.num_programs(1) - 1)
    def _():
        far[...] = total[...].astype(BF)


def attention_backward(later, own_col, own_row, prev_row, q, kv, before, do, lse, after):
    rows, width = q.shape
    kv_heads = kv.shape[1] // (2 * HEAD_SIZE)
    groups = 2 * width // kv.shape[1]
    inputs = (later, own_col, own_row, prev_row, q, kv, kv, before, before, do, lse)

    def kernel(*refs):
        backward_kernel(*refs[: len(inputs)], *refs[len(inputs) + len(after) :])

    mine = pl.BlockSpec((rows, HEAD_SIZE), lambda h, g: (0, h * groups + g))
    shared = pl.BlockSpec((rows, HEAD_SIZE), lambda h, g: (0, h))
    key = pl.BlockSpec((rows, HEAD_SIZE), lambda h, g: (0, 2 * h))
    value = pl.BlockSpec((rows, HEAD_SIZE), lambda h, g: (0, 2 * h + 1))
    column = pl.BlockSpec((rows, 1), lambda h, g: (0, 0))
    line = pl.BlockSpec((1, rows), lambda h, g: (0, 0))
    near = jax.ShapeDtypeStruct((rows, kv_heads * HEAD_SIZE), F32)
    return pl.pallas_call(
        kernel,
        grid=(kv_heads, groups),
        in_specs=[pl.BlockSpec(memory_space=pltpu.SMEM), column, line, line, mine]
        + [key, value] * 2
        + [mine, pl.BlockSpec((1, rows, 1), lambda h, g: (h * groups + g, 0, 0))]
        + [pl.BlockSpec(memory_space=pl.ANY)] * len(after),
        out_specs=[mine, shared, shared, pl.BlockSpec((rows, 2 * HEAD_SIZE), lambda h, g: (0, h))],
        out_shape=[
            jax.ShapeDtypeStruct((rows, width), F32),
            near,
            near,
            jax.ShapeDtypeStruct((rows, kv.shape[1]), BF),
        ],
        scratch_shapes=[pltpu.VMEM((rows, 2 * HEAD_SIZE), F32)],
        compiler_params=pltpu.CompilerParams(vmem_limit_bytes=32 * 2**20),
    )(*inputs, *after)


def call(
    kernel,
    out,
    inputs,
    scalars=(),
    grid=(1,),
    in_specs=None,
    out_specs=None,
    scratch=(),
    vmem=20,
    after=(),
    alias=None,
    hbm=4 * 2**20,
):
    def whole(a):
        return pl.BlockSpec(a.shape, lambda *_: (0,) * len(a.shape))

    in_specs = [s or whole(a) for s, a in zip(in_specs or [None] * len(inputs), inputs)]
    out_specs = [s or whole(a) for s, a in zip(out_specs or [None] * len(out), out)]
    alias = alias or {}

    def held(a, least):
        if a.size * a.dtype.itemsize < least:
            return a
        return pltpu.with_memory_space_constraint(a, pltpu.HBM)

    inputs = [held(a, hbm) for a in inputs]
    after = [held(a, hbm) for a in alias.values()] + [held(a, 2**20) for a in after]
    first = len(scalars) + len(inputs)

    def run(*refs):
        kernel(*refs[:first], *refs[first + len(after) :])

    return pl.pallas_call(
        run,
        grid_spec=pltpu.PrefetchScalarGridSpec(
            num_scalar_prefetch=len(scalars),
            grid=grid,
            in_specs=in_specs + [pl.BlockSpec(memory_space=pl.ANY)] * len(after),
            out_specs=out_specs,
            scratch_shapes=list(scratch),
        ),
        out_shape=list(out),
        compiler_params=pltpu.CompilerParams(vmem_limit_bytes=vmem * 2**20),
        input_output_aliases={first + i: place for i, place in enumerate(alias)},
        cost_estimate=pl.CostEstimate(flops=0, bytes_accessed=0, transcendentals=0),
    )(*[s.astype(jnp.int32).reshape(1) for s in scalars], *inputs, *after)


def in_hbm(dims, dtype):
    return pltpu.HBM(tuple(dims), dtype)


def shape(dims, dtype):
    return jax.ShapeDtypeStruct(tuple(dims), dtype)


def blocked(dims, index):
    return pl.BlockSpec(dims, index)


COLUMNS = 512


def other(index, k):
    return lax.bitwise_xor(index, jnp.int32(k))


def partners(z, size):
    return lax.bitwise_xor(z, jnp.arange(size, dtype=jnp.int32))


def ahead(index, k, size):
    return lax.bitwise_and(index + jnp.int32(k), jnp.int32(size - 1))


def behind(index, k, size):
    return lax.bitwise_and(index + jnp.int32(size) - jnp.int32(k), jnp.int32(size - 1))


def out_rows(ref):
    cols, dp, rows, width = ref.shape
    size = 4
    if dp == size:
        return ref[...].reshape(cols * dp * rows, width)
    per = dp // size
    order = [(c, q * per + r) for c in range(cols) for r in range(per) for q in range(size)]
    return jnp.concatenate([ref[c, d] for c, d in order])


def assemble(pieces, z, rolled, direct, after=()):
    def place_of(z, k):
        return behind(z, k, len(pieces)) if direct else other(z, k)

    size, dp = lax.axis_size("row"), lax.axis_size("dp")
    rows, width = pieces[0].shape
    rest = width // dp
    block = rows // size
    if rest % 128:
        out = jnp.stack([p.reshape(rows, dp, rest) for p in pieces], axis=2)
        order = behind(z, jnp.arange(size), size) if direct else partners(z, size)
        out = jnp.take(out, order, axis=2).reshape(rows, -1)
        if rolled:
            out = jnp.concatenate(
                [
                    lax.dynamic_slice_in_dim(out, other(z, k) * block, block, 0)
                    for k in range(size)
                ]
            )
        return out

    def kernel(z, *refs):
        out = refs[-1]
        for k in range(size):
            piece = refs[k][...]
            for d in range(dp):
                place = pl.multiple_of((d * size + place_of(z[0], k)) * rest, rest)
                out[:, pl.ds(place, rest)] = piece[:, d * rest : (d + 1) * rest]

    def index(i, z):
        return (lax.bitwise_xor(z[0], jnp.int32(i)) if rolled else i, 0)

    return call(
        kernel,
        [shape((rows, size * width), pieces[0].dtype)],
        list(pieces),
        [z],
        (size,),
        [blocked((block, width), index)] * size,
        [blocked((block, size * width), lambda i, z: (i, 0))],
        after=after,
    )[0]


def take_apart(full, z, rolled, after=()):
    size, dp = lax.axis_size("row"), lax.axis_size("dp")
    rows, width = full.shape
    rest = width // (size * dp)
    block = rows // size
    if rest % 128:
        if rolled:
            full = jnp.concatenate(
                [
                    lax.dynamic_slice_in_dim(full, other(z, i) * block, block, 0)
                    for i in range(size)
                ]
            )
        split = full.reshape(rows, dp, size, rest)
        split = jnp.take(split, partners(z, size), axis=2)
        return [split[:, :, k].reshape(rows, dp * rest) for k in range(size)]

    def kernel(z, full, *outs):
        for k in range(size):
            for d in range(dp):
                place = pl.multiple_of((d * size + other(z[0], k)) * rest, rest)
                outs[k][:, d * rest : (d + 1) * rest] = full[:, pl.ds(place, rest)]

    def index(i, z):
        return (lax.bitwise_xor(z[0], jnp.int32(i)) if rolled else i, 0)

    return call(
        kernel,
        [shape((rows, dp * rest), full.dtype)] * size,
        [full],
        [z],
        (size,),
        [blocked((block, width), lambda i, z: (i, 0))],
        [blocked((block, dp * rest), index)] * size,
        after=after,
    )


def project_kernel(x, gain, weight, cosine, sine, head_gain, a, scale, qr, kr, qn, kv):
    rows = x.shape[0]
    heads = qr.shape[1] // HEAD_SIZE
    kv_heads = kr.shape[1] // HEAD_SIZE

    @pl.when(pl.program_id(0) == 0)
    def _():
        for first in range(0, rows, 128):
            s = slice(first, first + 128)
            xf = x[s, :].astype(F32)
            r = lax.rsqrt(jnp.mean(xf * xf, axis=1, keepdims=True) + EPS)
            a[s, :] = (xf * r * gain[...]).astype(BF)
            scale[s, :] = r

    raw = dot(a[...], weight[0].reshape(MODEL_WIDTH, COLUMNS))

    def turn(values, gains):
        normed = (
            values
            * lax.rsqrt(jnp.mean(values * values, axis=-1, keepdims=True) + EPS)
            * gains
        )
        half = HEAD_SIZE // 2
        turned = jnp.concatenate([-normed[:, half:], normed[:, :half]], axis=-1)
        return (normed * cosine[...] + turned * sine[...]).astype(BF)

    for h in range(heads):
        s = slice(h * HEAD_SIZE, (h + 1) * HEAD_SIZE)
        qr[:, s] = raw[:, s]
        qn[:, s] = turn(raw[:, s], head_gain[0:1, :])
    first = heads * HEAD_SIZE
    for h in range(kv_heads):
        s = slice(h * HEAD_SIZE, (h + 1) * HEAD_SIZE)
        values = raw[:, first + h * HEAD_SIZE : first + (h + 1) * HEAD_SIZE]
        kr[:, s] = values
        kv[:, s] = turn(values, head_gain[1:2, :])
    kv[:, kv_heads * HEAD_SIZE :] = raw[:, first + kv_heads * HEAD_SIZE :].astype(BF)


def project(x, gain, weight, cosine, sine, head_gain, head_width, kv_width, after):
    rows = x.shape[0]
    cols, dp, _, width = weight.shape
    q = blocked((rows, head_width), lambda c: (0, c))
    k = blocked((rows, kv_width), lambda c: (0, c))
    return call(
        project_kernel,
        [
            shape(x.shape, BF),
            shape((rows, 1), F32),
            shape((rows, cols * head_width), F32),
            shape((rows, cols * kv_width), F32),
            shape((rows, cols * head_width), BF),
            shape((rows, 2 * cols * kv_width), BF),
        ],
        [x, gain, weight, cosine, sine, head_gain],
        (),
        (cols,),
        [None, None, blocked((1, dp, MODEL_WIDTH // dp, width), lambda c: (c, 0, 0, 0)), None, None, None],
        [None, None, q, k, q, blocked((rows, 2 * kv_width), lambda c: (0, c))],
        after=after,
    )


def mixed_parts(mixed, weight, z, base, after):
    size = lax.axis_size("row")
    cols, dp, total_rows, _ = weight.shape
    rows = mixed.shape[0]
    inner = mixed.shape[1] // (cols * dp)
    part = rows // size
    steps = MODEL_WIDTH // COLUMNS

    def kernel(z, mixed, weight, *refs):
        *outs, total = refs
        total[...] = dot(mixed[...], out_rows(weight))
        for k in range(size):
            first = pl.multiple_of(other(z[0], k) * part, part)
            outs[k][...] = total[pl.ds(first, part), :].astype(outs[k].dtype)

    return call(
        kernel,
        [shape((part, MODEL_WIDTH), BF if k else F32) for k in range(size)],
        [mixed, weight],
        [z],
        (steps,),
        [None, blocked((cols, dp, inner, COLUMNS), lambda c, z: (0, 0, base + c, 0))],
        [blocked((part, COLUMNS), lambda c, z: (0, c))] * size,
        scratch=[pltpu.VMEM((rows, COLUMNS), F32)],
        after=after,
    )


def mixed_back(chunks, weight, z, base, inner, after):
    size = len(chunks)
    cols, dp, _, _ = weight.shape
    part, width = chunks[0].shape
    rows = size * part
    heads = cols * dp * inner
    steps = width // COLUMNS

    def kernel(z, *refs):
        *ins, weight, full, out, total = refs
        for k in range(size):
            first = pl.multiple_of(other(z[0], k) * part, part)
            full[pl.ds(first, part), :] = ins[k][...]
        term = dot(full[...], out_rows(weight), "nt")
        c = pl.program_id(0)

        @pl.when(c == 0)
        def _():
            total[...] = term

        @pl.when(c > 0)
        def _():
            total[...] += term

        @pl.when(c == steps - 1)
        def _():
            out[...] = total[...].astype(BF)

    return call(
        kernel,
        [shape((rows, width), BF), shape((rows, heads), BF)],
        list(chunks) + [weight],
        [z],
        (steps,),
        [blocked((part, COLUMNS), lambda c, z: (0, c))] * size
        + [blocked((cols, dp, inner, COLUMNS), lambda c, z: (0, 0, base + c, 0))],
        [blocked((rows, COLUMNS), lambda c, z: (0, c)), None],
        scratch=[pltpu.VMEM((rows, heads), F32)],
        after=after,
    )


def masked(values, valid, after):
    def kernel(values, valid, out):
        out[...] = jnp.where(valid[...] > 0, values[...], jnp.zeros_like(values))

    return call(kernel, [shape(values.shape, values.dtype)], [values, valid], after=after)[0]


def add_parts(parts, dtype, after=()):
    def kernel(*refs):
        total = refs[0][...].astype(F32)
        for ref in refs[1:-1]:
            total = total + ref[...].astype(F32)
        refs[-1][...] = total.astype(dtype)

    return call(kernel, [shape(parts[0].shape, dtype)], list(parts), after=after)[0]


def hidden_norm(parts, x, gain, z, after=()):
    rows, width = parts[0].shape

    def kernel(z, *refs):
        *ps, x, gain, h, scale, a = refs
        total = x[...].astype(F32)
        for p in ps:
            total = total + p[...].astype(F32)
        r = lax.rsqrt(jnp.mean(total * total, axis=1, keepdims=True) + EPS)
        h[...] = total
        scale[...] = r
        a[...] = (total * r * gain[...]).astype(BF)

    return call(
        kernel,
        [shape((rows, width), F32), shape((rows, 1), F32), shape((rows, width), BF)],
        list(parts) + [x, gain],
        [z],
        (1,),
        [None] * len(parts) + [blocked((rows, width), lambda i, z: (z[0], 0)), None],
        after=after,
    )


def gateup_chunk(parts, weight, grad, hidden):
    part, width = parts[0].shape
    rows = part * len(parts)
    cols, dp, _, _ = weight.shape
    steps = 2 * hidden // (cols * COLUMNS)
    half = COLUMNS // 2

    def kernel(*refs):
        *ins, weight, grad, act, out, a = refs

        @pl.when((pl.program_id(0) == 0) & (pl.program_id(1) == 0))
        def _():
            for i, ref in enumerate(ins):
                a[i * part : (i + 1) * part, :] = ref[...]

        p = dot(a[...], weight[0].reshape(width, COLUMNS))
        for j in range(half // 128):
            gate, up = p[:, j * 256 : j * 256 + 128], p[:, j * 256 + 128 : j * 256 + 256]
            s = slice(j * 128, (j + 1) * 128)
            spread = 1.0 / (1.0 + jnp.exp(-gate))
            silu = gate * spread
            act[:, s] = (silu * up).astype(BF)
            g = grad[:, s]
            out[:, j * 256 : j * 256 + 128] = (g * up * (spread + silu * (1.0 - spread))).astype(BF)
            out[:, j * 256 + 128 : j * 256 + 256] = (g * silu).astype(BF)

    def place(c, t):
        return (0, c * steps + t)

    total = grad.shape[0]
    return call(
        kernel,
        [shape((total, hidden), BF), shape((total, 2 * hidden), BF)],
        list(parts) + [weight, grad],
        (),
        (cols, steps),
        [None] * len(parts)
        + [
            blocked((1, dp, width // dp, COLUMNS), lambda c, t: (c, 0, t, 0)),
            blocked((rows, half), place),
        ],
        [blocked((rows, half), place), blocked((rows, COLUMNS), place)],
        scratch=[pltpu.VMEM((rows, width), BF)],
        vmem=24,
    )


def gateup_back(grad, weight, kinds):
    cols, dp, _, _ = weight.shape
    both = grad.shape[1]
    block = MODEL_WIDTH // dp
    terms = both // COLUMNS
    per = terms // cols
    rows = grad.shape[0]
    part = rows // len(kinds)

    def kernel(grad, weight, *outs):
        total = None
        for t in range(terms):
            right = weight[t // per, 0, (t % per) * block : (t % per + 1) * block, :]
            term = dot(grad[:, t * COLUMNS : (t + 1) * COLUMNS], right, "nt")
            total = term if total is None else total + term
        for i, (out, kind) in enumerate(zip(outs, kinds)):
            out[...] = total[i * part : (i + 1) * part, :].astype(kind)

    return call(
        kernel,
        [shape((part, MODEL_WIDTH), kind) for kind in kinds],
        [grad, weight],
        (),
        (dp,),
        [
            None,
            blocked((cols, 1, per * block, COLUMNS), lambda n: (0, n, 0, 0)),
        ],
        [blocked((part, block), lambda n: (0, n))] * len(kinds),
        vmem=24,
    )


def down_back(out_low, weight, base, inner, after):
    cols, dp, _, _ = weight.shape
    rows, width = out_low.shape
    hidden = cols * dp * inner

    def kernel(low, weight, out):
        term = dot(low[...], out_rows(weight), "nt")

        @pl.when(pl.program_id(0) == 0)
        def _():
            out[...] = term

        @pl.when(pl.program_id(0) > 0)
        def _():
            out[...] += term

    return call(
        kernel,
        [shape((rows, hidden), F32)],
        [out_low, weight],
        (),
        (width // COLUMNS,),
        [
            blocked((rows, COLUMNS), lambda c: (0, c)),
            blocked((cols, dp, inner, COLUMNS), lambda c: (0, 0, base + c, 0)),
        ],
        [None],
        vmem=24,
        after=after,
    )[0]


def down_forward(active, hidden, weight, base, inner, after):
    cols, dp, _, _ = weight.shape
    rows, width = active.shape
    part = hidden.shape[0]

    def kernel(active, hidden, weight, out):
        p = dot(active[...], out_rows(weight))
        out[:part, :] = (p[:part, :] + hidden[...]).astype(BF)
        out[part:, :] = p[part:, :].astype(BF)

    return call(
        kernel,
        [shape((rows, MODEL_WIDTH), BF)],
        [active, hidden, weight],
        (),
        (MODEL_WIDTH // COLUMNS,),
        [
            None,
            blocked((part, COLUMNS), lambda c: (0, c)),
            blocked((cols, dp, inner, COLUMNS), lambda c: (0, 0, base + c, 0)),
        ],
        [blocked((rows, COLUMNS), lambda c: (0, c))],
        after=after,
    )[0]


def hidden_back(parts, h, scale, gain, out_low, after):
    rows, width = h.shape

    def kernel(*refs):
        *ps, h, scale, gain, dy, dh, low, gain_grad = refs
        grad = ps[0][...].astype(F32)
        for p in ps[1:]:
            grad = grad + p[...].astype(F32)
        hidden, r = h[...], scale[...]
        weighted = grad * gain[...]
        inner = jnp.sum(weighted * hidden, axis=1, keepdims=True)
        total = dy[...].astype(F32) + r * weighted - (r * r * r * inner / MODEL_WIDTH) * hidden
        dh[...] = total
        low[...] = total.astype(BF)
        gain_grad[...] = jnp.sum(grad * hidden * r, axis=0, keepdims=True)

    return call(
        kernel,
        [shape((rows, width), F32), shape((rows, width), BF), shape((1, width), F32)],
        list(parts) + [h, scale, gain, out_low],
        (),
        (1,),
        [None] * (len(parts) + 3) + [blocked((rows, width), lambda i: (0, 0))],
        after=after,
        hbm=2**17,
    )


def heads_back_kernel(
    qr, kr, dqn, dkn, dv, far, cosine, sine, head_gain, out, gain_grad
):
    heads = qr.shape[1] // HEAD_SIZE
    kv_heads = kr.shape[1] // HEAD_SIZE
    half = HEAD_SIZE // 2

    def back(raw, grad, gains):
        turned = grad * sine[...]
        turned = jnp.concatenate([turned[:, half:], -turned[:, :half]], axis=-1)
        g = grad * cosine[...] + turned
        r = lax.rsqrt(jnp.mean(raw * raw, axis=-1, keepdims=True) + EPS)
        weighted = g * gains
        inner = jnp.sum(weighted * raw, axis=-1, keepdims=True)
        low = (r * weighted - (r * r * r * inner / HEAD_SIZE) * raw).astype(BF)
        return low, jnp.sum(g * raw * r, axis=0, keepdims=True)

    @pl.when(pl.program_id(0) == 0)
    def _():
        gain_grad[...] = jnp.zeros_like(gain_grad)

    for h in range(heads):
        s = slice(h * HEAD_SIZE, (h + 1) * HEAD_SIZE)
        low, total = back(qr[:, s], dqn[:, s], head_gain[0:1, :])
        out[:, s] = low
        gain_grad[0:1, :] += total
    first = heads * HEAD_SIZE
    for h in range(kv_heads):
        s = slice(h * HEAD_SIZE, (h + 1) * HEAD_SIZE)
        low, total = back(kr[:, s], dkn[:, s] + far[:, s].astype(F32), head_gain[1:2, :])
        out[:, first + h * HEAD_SIZE : first + (h + 1) * HEAD_SIZE] = low
        gain_grad[1:2, :] += total
    first += kv_heads * HEAD_SIZE
    out[:, first:] = (dv[...] + far[:, kv_heads * HEAD_SIZE :].astype(F32)).astype(BF)


def heads_back(qr, kr, dqn, dkn, dv, far, cosine, sine, head_gain, cols, after):
    rows = qr.shape[0]
    head_width, kv_width = qr.shape[1] // cols, kr.shape[1] // cols
    q = blocked((rows, head_width), lambda c: (0, c))
    k = blocked((rows, kv_width), lambda c: (0, c))
    far_kv = blocked((rows, 2 * kv_width), lambda c: (0, c))
    width = head_width + 2 * kv_width
    return call(
        heads_back_kernel,
        [shape((rows, cols * width), BF), shape((2, HEAD_SIZE), F32)],
        [qr, kr, dqn, dkn, dv, far, cosine, sine, head_gain],
        (),
        (cols,),
        [q, k, q, k, k, far_kv, None, None, None],
        [blocked((rows, width), lambda c: (0, c)), None],
        after=after,
    )


def input_back(grads, weight, x, scale, gain, dh, z, after):
    cols, steps, _, width = weight.shape
    rows = grads.shape[0]
    model = MODEL_WIDTH
    part = dh.shape[0]

    def kernel(z, grads, weight, x, scale, gain, dh, out, c1, gain_grad):
        total = dot(grads[:, :width], weight[0, 0], "nt")
        for c in range(1, cols):
            total = total + dot(grads[:, c * width : (c + 1) * width], weight[c, 0], "nt")
        r = scale[...]
        xf = x[...].astype(F32)
        weighted = total * gain[...]
        moved = weighted * xf
        gain_grad[...] = jnp.sum(total * xf * r, axis=0, keepdims=True)
        out[...] = (r * weighted).astype(BF)
        first = pl.multiple_of(z[0] * part, part)
        own = pl.ds(first, part)
        out[own, :] = (out[own, :].astype(F32) + dh[...]).astype(BF)

        @pl.when(pl.program_id(0) == 0)
        def _():
            c1[...] = jnp.zeros_like(c1)

        c1[...] += jnp.sum(moved, axis=1, keepdims=True)

    block = model // steps
    wide = blocked((rows, block), lambda n, z: (0, n))
    return call(
        kernel,
        [shape((rows, model), BF), shape((rows, 1), F32), shape((1, model), F32)],
        [grads, weight, x, scale, gain, dh],
        [z],
        (steps,),
        [
            None,
            blocked((cols, 1, block, width), lambda n, z: (0, n, 0, 0)),
            wide,
            None,
            blocked((1, block), lambda n, z: (0, n)),
            blocked((part, block), lambda n, z: (0, n)),
        ],
        [wide, None, blocked((1, block), lambda n, z: (0, n))],
        after=after,
    )


def weight_grads(lefts, right, out_left, out_right, cols, after=()):
    size, dp = lax.axis_size("row"), lax.axis_size("dp")
    rows = right.shape[0]
    block = MODEL_WIDTH // dp
    n = right.shape[1] // cols
    part = rows // len(lefts)
    m = out_left.shape[1] // cols
    inner = m // dp
    terms = n // COLUMNS
    total = terms * block + MODEL_WIDTH // COLUMNS * inner

    def kernel(*refs):
        *ins, right, out_left, out_right, out = refs
        left = jnp.concatenate([ref[...] for ref in ins]) if len(ins) > 1 else ins[0][...]
        for t in range(terms):
            term = dot(left, right[:, t * COLUMNS : (t + 1) * COLUMNS], "tn")
            out[0, 0, t * block : (t + 1) * block, :] = term.astype(BF)
        for d in range(dp):
            q, r = d // (dp // size), d % (dp // size)
            first = (r * size + q) * inner

            @pl.when(pl.program_id(1) == d)
            def _():
                term = dot(out_left[:, first : first + inner], out_right[...], "tn").astype(BF)
                for c in range(MODEL_WIDTH // COLUMNS):
                    place = terms * block + c * inner
                    piece = term[:, c * COLUMNS : (c + 1) * COLUMNS]
                    out[0, 0, place : place + inner, :] = piece

    return call(
        kernel,
        [in_hbm((cols, dp, total, COLUMNS), BF)],
        list(lefts) + [right, out_left, out_right],
        (),
        (cols, dp),
        [blocked((part, block), lambda c, d: (0, d))] * len(lefts)
        + [
            blocked((rows, n), lambda c, d: (0, c)),
            blocked((rows, m), lambda c, d: (0, c)),
            None,
        ],
        [blocked((1, 1, total, COLUMNS), lambda c, d: (c, d, 0, 0))],
        after=after,
        vmem=28,
    )[0]


def swap(value, axis, step):
    return lax.ppermute(value, axis, [(i, i ^ step) for i in range(lax.axis_size(axis))])


def gather_pieces(own, beside=None):
    two = swap(own, "row", 2)
    if beside is not None:
        two, beside = lax.optimization_barrier((two, beside))
    pieces = [own, swap(own, "row", 1), two, swap(two, "row", 1)]
    return pieces if beside is None else (pieces, beside)


def gather_direct(own):
    return along_row([own] * lax.axis_size("row"), True)


def scatter_pieces(pieces):
    sent = add_parts([pieces[2], swap(pieces[3], "row", 1)], BF)
    direct, sent = lax.optimization_barrier((pieces[1], sent))
    return [pieces[0], swap(direct, "row", 1), swap(sent, "row", 2)], sent


def add_along(value, axes):
    for axis in axes:
        step = 1
        while step < lax.axis_size(axis):
            value = value + swap(value, axis, step)
            step *= 2
    return value


def along_row(pieces, forward):
    size = len(pieces)
    sign = 1 if forward else -1
    return [pieces[0]] + [
        lax.ppermute(p, "row", [(i, (i + sign * k) % size) for i in range(size)])
        for k, p in enumerate(pieces)
        if k
    ]


def along_quarters(pieces, forward):
    size = len(pieces)
    per = lax.axis_size("dp") // size
    sign = 1 if forward else -1

    def pairs(k):
        places = [(q, r) for q in range(size) for r in range(per)]
        return [(q * per + r, (q + sign * k) % size * per + r) for q, r in places]

    return [pieces[0]] + [lax.ppermute(p, "dp", pairs(k)) for k, p in enumerate(pieces) if k]


def gather_shard(shard):
    full = lax.all_gather(shard, ("col", "dp"), axis=0)
    return full.reshape(lax.axis_size("col"), lax.axis_size("dp"), *shard.shape)


def scatter_shard(full):
    flat_rows = full.reshape(-1, full.shape[-1])
    return lax.psum_scatter(flat_rows, ("col", "dp"), scatter_dimension=0, tiled=True)


def quarter_index():
    return lax.axis_index("dp") // (lax.axis_size("dp") // lax.axis_size("row"))


def pack_attention(query, keyval, z):
    size = lax.axis_size("row")
    rows = query.shape[0]
    hw, kw = query.shape[1] // size, keyval.shape[2] // size

    def kernel(z, query, keyval, *outs):
        for k in range(size):
            at = ahead(z[0], k, size)
            out = outs[k]
            out[:, :hw] = query[:, pl.ds(pl.multiple_of(at * hw, hw), hw)].astype(BF)
            for s in range(2):
                part = keyval[:, s, pl.ds(pl.multiple_of(at * kw, kw), kw)]
                out[:, hw + s * kw : hw + (s + 1) * kw] = part.astype(BF)

    return call(kernel, [shape((rows, hw + 2 * kw), BF)] * size, [query, keyval], [z], hbm=0)


def pack_feed(gateup, downs, z, after):
    size = lax.axis_size("row")
    rows = gateup.shape[0]
    fw = gateup.shape[2] // size
    terms = 2 * fw // COLUMNS
    inner = downs[0].shape[0]

    def kernel(z, gateup, *refs):
        for k in range(size):
            at = ahead(z[0], k, size)
            out = refs[size + k]
            for s in range(2):
                for j in range(fw // 128):
                    first = pl.multiple_of(at * fw + j * 128, 128)
                    place = (2 * j + s) * 128
                    t, lane = place // COLUMNS, place % COLUMNS
                    part = gateup[:, s, pl.ds(first, 128)].astype(BF)
                    out[t * rows : (t + 1) * rows, lane : lane + 128] = part
            out[terms * rows :, :] = refs[k][...]

    return call(
        kernel,
        [shape((terms * rows + inner, COLUMNS), BF)] * size,
        [gateup, *downs],
        [z],
        after=after,
        vmem=32,
    )


def pack_out(blocks, after=()):
    size = lax.axis_size("row")
    rows = [b.shape[0] // size for b in blocks]

    def kernel(q, *refs):
        for k in range(size):
            place = 0
            for ref, n in zip(refs, rows):
                first = pl.multiple_of(ahead(q[0], k, size) * n, n)
                refs[len(rows) + k][place : place + n, :] = ref[pl.ds(first, n), :].astype(BF)
                place += n

    return call(
        kernel,
        [shape((sum(rows), blocks[0].shape[1]), BF)] * size,
        blocks,
        [quarter_index()],
        after=after,
        hbm=0,
    )


def regroup(parts, source, target, cuts, after=(), top=0):
    size = len(parts)
    sources = [source(k) for k in range(size)]
    targets = [target(k) for k in range(size)]
    starts = [sum(cuts[:i]) for i in range(len(cuts))]

    def kernel(*refs):
        places, ins = refs[: 2 * size], refs[2 * size : 3 * size]
        outs, held = refs[3 * size : -1], refs[-1]
        for k in range(size):
            held[places[k][0]] = ins[k][top:, :]
        for i, (first, n) in enumerate(zip(starts, cuts)):
            for k in range(size):
                outs[i * size + k][...] = held[places[size + k][0], first : first + n]

    rows, width = parts[0].shape
    outs = call(
        kernel,
        [shape((n, width), BF) for n in cuts for _ in range(size)],
        parts,
        sources + targets,
        scratch=[pltpu.VMEM((size, rows - top, width), BF)],
        after=after,
    )
    return [outs[i * size : (i + 1) * size] for i in range(len(cuts))]


def make_shard(in_parts, out_parts, z, after=()):
    size, dp = len(in_parts), lax.axis_size("dp")
    rest = MODEL_WIDTH // (size * dp)
    steps = MODEL_WIDTH // COLUMNS
    rows = MODEL_WIDTH // (size * dp)
    if isinstance(out_parts, int):
        inner, joined = out_parts, True
        terms = (in_parts[0].shape[0] - inner) // rows
    else:
        inner, joined = out_parts[0].shape[0], False
        terms = in_parts[0].shape[0] // rows
    base = terms * size * rows
    if rest % 128:
        order = behind(z, jnp.arange(size), size)
        if joined:
            out_parts = [p[terms * rows :] for p in in_parts]
            in_parts = [p[: terms * rows] for p in in_parts]
        full = jnp.take(jnp.stack(in_parts), order, axis=0).reshape(size, terms, rows, COLUMNS)
        ins = full.transpose(1, 0, 2, 3).reshape(base, COLUMNS)
        full = jnp.stack([p.reshape(inner, dp, rest) for p in out_parts], axis=2)
        full = jnp.take(full, order, axis=2).reshape(inner, steps, COLUMNS)
        return jnp.concatenate([ins, full.transpose(1, 0, 2).reshape(-1, COLUMNS)])

    def kernel(z, *refs):
        out = refs[-1]
        for k in range(size):
            at = behind(z[0], k, size)
            for t in range(terms):
                first = pl.multiple_of((t * size + at) * rows, rows)
                out[pl.ds(first, rows), :] = refs[k][t * rows : (t + 1) * rows, :]
            place = pl.multiple_of(at * rest, rest)
            ref = refs[k] if joined else refs[size + k]
            top = terms * rows if joined else 0
            for d in range(dp):
                first = base + d * inner
                part = ref[top : top + inner, d * rest : (d + 1) * rest]
                out[first : first + inner, pl.ds(place, rest)] = part

    parts = list(in_parts) if joined else list(in_parts) + list(out_parts)
    out = shape((base + steps * inner, COLUMNS), BF)
    return call(kernel, [out], parts, [z], after=after)[0]


def split_shard(shard, terms, rows, inner, z, after=()):
    size, dp = lax.axis_size("row"), lax.axis_size("dp")
    rest = MODEL_WIDTH // (size * dp)
    steps = MODEL_WIDTH // COLUMNS
    base = terms * size * rows
    if rest % 128:
        ins = shard[:base].reshape(terms, size, rows, COLUMNS).transpose(1, 0, 2, 3)
        ins = jnp.take(ins, behind(z, jnp.arange(size), size), axis=0)
        outs = shard[base:].reshape(steps, inner, COLUMNS).transpose(1, 0, 2)
        outs = outs.reshape(inner, dp, size, rest)
        outs = jnp.take(outs, behind(z, jnp.arange(size), size), axis=2)
        return [
            jnp.concatenate([ins[k].reshape(-1, COLUMNS), outs[:, :, k].reshape(inner, COLUMNS)])
            for k in range(size)
        ]

    def kernel(z, full, *outs):
        for k in range(size):
            at = behind(z[0], k, size)
            for t in range(terms):
                first = pl.multiple_of((t * size + at) * rows, rows)
                outs[k][t * rows : (t + 1) * rows, :] = full[pl.ds(first, rows), :]
            place = pl.multiple_of(at * rest, rest)
            for d in range(dp):
                part = full[base + d * inner : base + (d + 1) * inner, pl.ds(place, rest)]
                outs[k][terms * rows :, d * rest : (d + 1) * rest] = part

    return call(
        kernel,
        [shape((terms * rows + inner, COLUMNS), BF)] * size,
        [shard],
        [z],
        after=after,
    )


def split_attention(shard, terms, rows, inner, z, after=()):
    size, dp = lax.axis_size("row"), lax.axis_size("dp")
    rest = MODEL_WIDTH // (size * dp)
    steps = MODEL_WIDTH // COLUMNS
    base = terms * size * rows
    quarter = quarter_index()
    if rest % 128:
        ins = shard[:base].reshape(terms, size, rows, COLUMNS).transpose(1, 0, 2, 3)
        ins = jnp.take(ins, behind(z, jnp.arange(size), size), axis=0)
        outs = shard[base:].reshape(steps, inner, COLUMNS).transpose(1, 0, 2)
        outs = outs.reshape(inner, dp, size, rest)
        outs = jnp.take(outs, ahead(quarter, jnp.arange(size), size), axis=2)
        return (
            [ins[k].reshape(-1, COLUMNS) for k in range(size)],
            [outs[:, :, k].reshape(inner, COLUMNS) for k in range(size)],
        )

    def kernel(z, quarter, full, *outs):
        for k in range(size):
            at = behind(z[0], k, size)
            for t in range(terms):
                first = pl.multiple_of((t * size + at) * rows, rows)
                outs[k][t * rows : (t + 1) * rows, :] = full[pl.ds(first, rows), :]
            place = pl.multiple_of(ahead(quarter[0], k, size) * rest, rest)
            for d in range(dp):
                part = full[base + d * inner : base + (d + 1) * inner, pl.ds(place, rest)]
                outs[size + k][:, d * rest : (d + 1) * rest] = part

    pieces = call(
        kernel,
        [shape((terms * rows, COLUMNS), BF)] * size + [shape((inner, COLUMNS), BF)] * size,
        [shard],
        [z, quarter],
        after=after,
    )
    return pieces[:size], pieces[size:]


def turned_back(pieces):
    size = len(pieces)
    per = lax.axis_size("dp") // size
    result = []
    for k, piece in enumerate(pieces):
        pairs = []
        for q in range(size):
            for r in range(per):
                for z in range(size):
                    target = (z * per + r) * size + (q + k) % size
                    pairs.append(((q * per + r) * size + z, target))
        result.append(lax.ppermute(piece, ("dp", "row"), pairs))
    return result


def out_pieces(messages, inner, z, after=()):
    size = len(messages)
    quarter = quarter_index()
    parts = regroup(
        messages,
        lambda k: ahead(z, k, size),
        lambda k: ahead(quarter, k, size),
        [inner],
        after,
        messages[0].shape[0] - inner,
    )[0]
    return along_quarters(parts, True)


def update(refs, grad, rate):
    weight, moment, second, weight_new, moment_new, second_new = refs
    m, v, w = adamw(weight[...], moment[...], second[...], grad, rate, DECAY)
    moment_new[...] = m
    second_new[...] = v
    weight_new[...] = w


def update_out(state, pieces, rate, place):
    size = len(pieces)
    rows, width = pieces[0].shape

    def kernel(q, *refs):
        k = pl.program_id(0)
        for i in range(size):

            @pl.when(k == i)
            def _():
                update(refs[size:], refs[i][...].astype(F32), rate)

    spec = blocked((rows, width), lambda k, q: (lax.bitwise_and(q[0] + size - k, size - 1), 0))
    w, m, v = call(
        kernel,
        [shape(state[0].shape, F32)] * 3,
        list(pieces) + list(state),
        [place],
        (size,),
        [None] * size + [spec] * 3,
        [spec] * 3,
        hbm=2**19,
    )
    return m, v, w


def place_columns(messages, rows, cuts, z, after=()):
    size = len(messages)

    def kernel(z, *refs):
        for out, cut in zip(refs[size:], cuts):
            width = sum(w for _, _, w in cut)
            for k in range(size):
                at = ahead(z[0], k, size) * width
                for t, first, w in cut:
                    place = pl.multiple_of(at, 128)
                    part = refs[k][t * rows : (t + 1) * rows, first : first + w]
                    out[:, pl.ds(place, w)] = part
                    at = at + w

    out = [shape((rows, size * sum(w for _, _, w in cut)), BF) for cut in cuts]
    return call(kernel, out, messages, [z], after=after)


def flat(values):
    rows, two, width = values.shape
    return values.reshape(rows, two, width // 128, 128).transpose(0, 2, 1, 3).reshape(-1, 128)


def update_pair(state, grad, rate):
    rows, two, width = state[0].shape
    total = rows * two * width // 128
    steps = 4 if total % 64 == 0 else 1

    def kernel(grad, *refs):
        update(refs, grad[...].astype(F32), rate)

    spec = blocked((total // steps, 128), lambda i: (i, 0))
    news = call(
        kernel,
        [shape((total, 128), F32)] * 3,
        [grad.reshape(-1, 128)] + [flat(s) for s in state],
        (),
        (steps,),
        [spec] * 4,
        [spec] * 3,
        hbm=2**19,
    )
    w, m, v = [
        n.reshape(rows, width // 128, two, 128).transpose(0, 2, 1, 3).reshape(rows, two, width)
        for n in news
    ]
    return (m, v, w), news[0]


def adamw(weight, moment, second, grad, rate, decay):
    moment_new = BETA_ONE * moment + (1.0 - BETA_ONE) * grad
    second_new = BETA_TWO * second + (1.0 - BETA_TWO) * grad * grad
    first_hat = moment_new * (1.0 / (1.0 - BETA_ONE**STEP))
    second_hat = second_new * (1.0 / (1.0 - BETA_TWO**STEP))
    weight_new = weight - rate * (first_hat / (jnp.sqrt(second_hat) + ADAM_EPS) + decay * weight)
    return (moment_new, second_new, weight_new)


def body(
    tokens,
    cotangent,
    seq_lens,
    query_weight,
    query_moment,
    query_second,
    key_value_master_weight,
    key_value_first_moment,
    key_value_second_moment,
    output_weight,
    output_moment,
    output_second,
    gateup_weight,
    gateup_moment,
    gateup_second,
    down_weight,
    down_moment,
    down_second,
    norm_gains,
    norm_moment,
    norm_second,
    head_gains,
    head_moment,
    head_second,
):
    size, dp, cols = lax.axis_size("row"), lax.axis_size("dp"), lax.axis_size("col")
    z, y = lax.axis_index("row"), lax.axis_index("col")
    rows = tokens.shape[0]
    quarter = rows // size
    item_count = rows * cols
    rest = MODEL_WIDTH // (size * dp)
    head_width = query_weight.shape[1] // size
    kv_width = key_value_master_weight.shape[2] // size

    gains = norm_gains.reshape(2, size, dp, rest).transpose(0, 2, 1, 3).reshape(2, MODEL_WIDTH)
    first_gain, second_gain = gains[0:1], gains[1:2]

    segment, position = token_layout(seq_lens[0], item_count)
    first = y * rows
    own_segment = lax.dynamic_slice_in_dim(segment, first, rows, 0)
    cosine, sine = rope_tables(lax.dynamic_slice_in_dim(position, first, rows, 0))
    valid = (own_segment < SEQS).astype(jnp.int32)[:, None]

    hidden_width = gateup_weight.shape[2] // size * cols

    in_rows = query_weight.shape[0]
    output_inner, down_inner = output_weight.shape[0] // size, down_weight.shape[0] // size
    gateup_terms = 2 * hidden_width // (cols * COLUMNS)
    steps = MODEL_WIDTH // COLUMNS
    down_base = gateup_terms * size * in_rows // down_inner
    output_base = size * in_rows // output_inner
    quarter_place = quarter_index()
    input_chunks = gather_pieces(tokens)
    attention_pieces = pack_attention(query_weight, key_value_master_weight, z)
    out_pieces_sent = pack_out([down_weight, output_weight], attention_pieces[:1])
    down_parts, output_parts = regroup(
        along_quarters(out_pieces_sent, True),
        lambda k: behind(quarter_place, k, size),
        lambda k: ahead(z, k, size),
        [down_inner, output_inner],
    )
    feed_pieces = pack_feed(gateup_weight, down_parts, z, output_parts[:1])
    attention_shard = make_shard(
        along_row(attention_pieces, True),
        along_row(output_parts, True),
        z,
        [feed_pieces[0], input_chunks[2]],
    )
    attention_full = gather_shard(attention_shard)
    inputs = assemble(input_chunks, z, False, False, [attention_shard])
    feed_shard = make_shard(along_row(feed_pieces, True), down_inner, z, [inputs])
    feed_full = gather_shard(feed_shard)
    out_own = masked(cotangent, valid, [feed_shard])
    out_chunks = gather_pieces(out_own)

    first_low, first_scale, query_raw, key_raw, query, keys_values = project(
        inputs,
        first_gain,
        attention_full,
        cosine,
        sine,
        head_gains,
        head_width,
        kv_width,
        [out_own],
    )
    before = lax.ppermute(keys_values, "col", [(i, i + 1) for i in range(cols - 1)])
    masks = (
        y.astype(jnp.int32).reshape(1),
        own_segment.reshape(rows, 1),
        own_segment.reshape(1, rows),
        segment[:rows].reshape(1, rows),
    )
    mixed, logsum = attention_forward(*masks, query, keys_values, before, [])
    hidden_pieces = mixed_parts(mixed, attention_full, z, output_base, out_chunks[1:])
    out_low = assemble(out_chunks, z, True, False, hidden_pieces[1:2])
    hidden_parts, _ = scatter_pieces(hidden_pieces)
    hidden, second_scale, second_low = hidden_norm(hidden_parts, inputs, second_gain, z)

    second_chunks = gather_pieces(second_low)
    active_grad = down_back(out_low, feed_full, down_base, down_inner, second_chunks[2:3])
    active, pair_grad = gateup_chunk(second_chunks, feed_full, active_grad, hidden_width)
    second_parts = gateup_back(pair_grad, feed_full, (F32, BF, BF, BF))
    feed_grads = weight_grads(
        second_chunks, pair_grad, active, out_low, cols, [second_parts[3]]
    )
    passed = swap(second_parts[3], "row", 1)
    feed_grads, passed = lax.optimization_barrier((feed_grads, passed))
    sent = add_parts([second_parts[2], passed], BF)
    direct, sent = lax.optimization_barrier((second_parts[1], sent))
    second_parts = [second_parts[0], swap(direct, "row", 1), swap(sent, "row", 2)]
    feed_total = scatter_shard(feed_grads)
    hidden_grad, hidden_low, second_gain_grad = hidden_back(
        second_parts, hidden, second_scale, second_gain, out_low, []
    )

    layer_part = down_forward(active, hidden, feed_full, down_base, down_inner, [hidden_low])
    hidden_all, mixed_grad = mixed_back(
        gather_pieces(hidden_low), attention_full, z, output_base, output_inner, [layer_part]
    )
    layer_pieces = take_apart(layer_part, z, True, [hidden_all])
    query_grad, key_grad, value_grad, far_sent = attention_backward(
        *masks, query, keys_values, before, mixed_grad, logsum, layer_pieces[:1]
    )
    far = lax.ppermute(far_sent, "col", [(i + 1, i) for i in range(cols - 1)])
    layer_parts, _ = scatter_pieces(layer_pieces)
    layer_output = add_parts(layer_parts, F32)
    raw_grad, head_part = heads_back(
        query_raw,
        key_raw,
        query_grad,
        key_grad,
        value_grad,
        far,
        cosine,
        sine,
        head_gains,
        cols,
        [layer_output],
    )
    attention_grads = weight_grads([first_low], raw_grad, mixed, hidden_all, cols)
    attention_grads, feed_total = lax.optimization_barrier((attention_grads, feed_total))
    attention_total = scatter_shard(attention_grads)
    feed_pieces = split_shard(feed_total, gateup_terms, in_rows, down_inner, z)
    input_part, inner_part, first_gain_grad = input_back(
        raw_grad,
        attention_full,
        inputs,
        first_scale,
        first_gain,
        hidden_grad,
        z,
        feed_pieces[:1],
    )
    input_pieces = take_apart(input_part, z, False)
    input_parts, _ = scatter_pieces(input_pieces)
    feed_messages = along_row(feed_pieces, False)
    norm_part = jnp.concatenate([first_gain_grad, second_gain_grad])
    norm_part = norm_part.reshape(2, dp, size, rest).transpose(0, 2, 1, 3).reshape(2, MODEL_WIDTH)
    gain_part = jnp.concatenate([norm_part.reshape(-1), head_part.reshape(-1)]).reshape(-1, 128)
    gain_part, feed_messages[1] = lax.optimization_barrier((gain_part, feed_messages[1]))
    gain_part = add_along(gain_part, ("dp", "col"))
    small = jnp.concatenate([gain_part, inner_part.reshape(-1, 128)])
    small = add_along(small, ("row",)).reshape(-1)
    inner = small[gain_part.size :][:, None]
    norm_total = small[: norm_part.size].reshape(norm_part.shape)
    head_total = small[norm_part.size : gain_part.size].reshape(head_part.shape)

    down_new = update_out(
        (down_weight, down_moment, down_second),
        out_pieces(feed_messages, down_inner, z, [gain_part]),
        RATES[4],
        quarter_place,
    )
    attention_pieces, output_pieces = split_attention(
        attention_total, 1, in_rows, output_inner, z
    )
    cut = [(t, 0, COLUMNS) for t in range(gateup_terms)]
    (gateup_total,) = place_columns(
        feed_messages, in_rows, [cut], z, attention_pieces[:1]
    )
    gateup_new, _ = update_pair(
        (gateup_weight, gateup_moment, gateup_second), gateup_total, RATES[3]
    )
    output_pieces = turned_back(output_pieces)
    attention_messages = along_row(attention_pieces, False)
    output_new = update_out(
        (output_weight, output_moment, output_second), output_pieces, RATES[2], z
    )
    query_total, keyval_total = place_columns(
        attention_messages,
        in_rows,
        [[(0, 0, head_width)], [(0, head_width, 2 * kv_width)]],
        z,
    )
    input_grad = add_parts(input_parts, F32, [query_total]) - (
        first_scale * first_scale * first_scale * inner / MODEL_WIDTH
    ) * tokens.astype(F32)
    query_new = adamw(
        query_weight, query_moment, query_second, query_total.astype(F32), RATES[0], DECAY
    )
    keyval_new, _ = update_pair(
        (key_value_master_weight, key_value_first_moment, key_value_second_moment),
        keyval_total,
        RATES[1],
    )
    norm_new = adamw(norm_gains, norm_moment, norm_second, norm_total, GAIN_RATE, 0.0)
    head_new = adamw(head_gains, head_moment, head_second, head_total, GAIN_RATE, 0.0)
    return (
        layer_output,
        input_grad,
        *query_new,
        *keyval_new,
        *output_new,
        *gateup_new,
        *down_new,
        *norm_new,
        *head_new,
    )


def solution(mesh):
    items = P(("dp", "col"), "row")
    inward = P(("row", "dp"), "col")
    inward_pair = P(("row", "dp"), None, "col")
    outward = P(("col", "dp"), "row")
    weights = (
        (inward,) * 3 + (inward_pair,) * 3 + (outward,) * 3 + (inward_pair,) * 3 + (outward,) * 3
    )
    return jax.shard_map(
        body,
        mesh=mesh,
        in_specs=(items, items, P("dp", None)) + weights + (P(),) * 6,
        out_specs=(items, items) + weights + (P(),) * 6,
        check_vma=False,
    )
```

```python
import functools
import math

import jax
import jax.numpy as jnp
from jax import lax
from jax.experimental import pallas as pl
from jax.experimental.pallas import tpu as pltpu
from jax.sharding import PartitionSpec as P

MODEL_WIDTH = 2048
HEAD_SIZE = 128
SEQS = 4
STEP = 10

EPS = 1e-06
THETA = 1000000.0
NEGATIVE = -1e30
BETA_ONE = 0.9
BETA_TWO = 0.95
ADAM_EPS = 1e-08
DECAY = 0.1
RATES = (0.066, 0.066, 0.5, 0.066, 0.04)
GAIN_RATE = 0.6
BF = jnp.bfloat16
F32 = jnp.float32
SCALE = 1.0 / math.sqrt(HEAD_SIZE)


def dot(a, b, kind="nn"):
    dims = {"nn": ((1,), (0,)), "nt": ((1,), (1,)), "tn": ((0,), (0,))}[kind]
    return lax.dot_general(a, b, (dims, ((), ())), preferred_element_type=F32)


def token_layout(lengths, item_count):
    ends = jnp.cumsum(lengths)
    places = jnp.arange(item_count, dtype=jnp.int32)
    segment = jnp.sum((places[:, None] >= ends[None, :]).astype(jnp.int32), axis=1)
    starts = jnp.concatenate([ends - lengths, ends[-1:]])
    labels = jnp.arange(starts.shape[0], dtype=jnp.int32)
    begin = jnp.sum(jnp.where(segment[:, None] == labels[None, :], starts[None, :], 0), axis=1)
    return (segment, places - begin)


def rope_tables(position):
    half = HEAD_SIZE // 2
    freq = jnp.exp(jnp.arange(half, dtype=F32) * (-2.0 * math.log(THETA) / HEAD_SIZE))
    angle = position.astype(F32)[:, None] * freq[None, :]
    angle = jnp.concatenate([angle, angle], axis=1)
    return (jnp.cos(angle), jnp.sin(angle))


def block_masks(own_col, own_row, prev_row, later):
    rows = own_col.shape[0]
    r = lax.broadcasted_iota(jnp.int32, (rows, rows), 0)
    c = lax.broadcasted_iota(jnp.int32, (rows, rows), 1)
    own = (c <= r) & (own_col == own_row)
    prev = (own_col == prev_row) & (later > 0)
    return own, prev


def forward_kernel(later, own_col, own_row, prev_row, q, k, v, kp, vp, o, lse):
    own, prev = block_masks(own_col[...], own_row[...], prev_row[...], later[0])
    s_own = jnp.where(own, dot(q[...], k[...], "nt") * SCALE, NEGATIVE)
    s_prev = jnp.where(prev, dot(q[...], kp[...], "nt") * SCALE, NEGATIVE)
    top = jnp.maximum(
        jnp.max(s_own, axis=1, keepdims=True), jnp.max(s_prev, axis=1, keepdims=True)
    )
    total = jnp.sum(jnp.exp(s_own - top), axis=1, keepdims=True) + jnp.sum(
        jnp.exp(s_prev - top), axis=1, keepdims=True
    )
    logsum = top + jnp.log(total)
    p_own = jnp.exp(s_own - logsum).astype(BF)
    p_prev = jnp.exp(s_prev - logsum).astype(BF)
    o[...] = (dot(p_own, v[...]) + dot(p_prev, vp[...])).astype(BF)
    lse[0] = logsum


def attention_forward(later, own_col, own_row, prev_row, q, kv, before, after):
    rows, width = q.shape
    heads = width // HEAD_SIZE
    groups = 2 * width // kv.shape[1]
    inputs = (later, own_col, own_row, prev_row, q, kv, kv, before, before)

    def kernel(*refs):
        forward_kernel(*refs[: len(inputs)], *refs[len(inputs) + len(after) :])

    mine = pl.BlockSpec((rows, HEAD_SIZE), lambda h: (0, h))
    key = pl.BlockSpec((rows, HEAD_SIZE), lambda h: (0, 2 * (h // groups)))
    value = pl.BlockSpec((rows, HEAD_SIZE), lambda h: (0, 2 * (h // groups) + 1))
    column = pl.BlockSpec((rows, 1), lambda h: (0, 0))
    line = pl.BlockSpec((1, rows), lambda h: (0, 0))
    return pl.pallas_call(
        kernel,
        grid=(heads,),
        in_specs=[pl.BlockSpec(memory_space=pltpu.SMEM), column, line, line, mine]
        + [key, value] * 2
        + [pl.BlockSpec(memory_space=pl.ANY)] * len(after),
        out_specs=[mine, pl.BlockSpec((1, rows, 1), lambda h: (h, 0, 0))],
        out_shape=[
            jax.ShapeDtypeStruct((rows, width), BF),
            jax.ShapeDtypeStruct((heads, rows, 1), F32),
        ],
        compiler_params=pltpu.CompilerParams(vmem_limit_bytes=32 * 2**20),
    )(*inputs, *after)


def backward_kernel(
    later, own_col, own_row, prev_row, q, k, v, kp, vp, do, lse, dq, dk, dv, far, total
):
    own, prev = block_masks(own_col[...], own_row[...], prev_row[...], later[0])
    logsum = lse[0]
    p_own = jnp.exp(jnp.where(own, dot(q[...], k[...], "nt") * SCALE, NEGATIVE) - logsum)
    p_prev = jnp.exp(jnp.where(prev, dot(q[...], kp[...], "nt") * SCALE, NEGATIVE) - logsum)
    d_own = dot(do[...], v[...], "nt")
    d_prev = dot(do[...], vp[...], "nt")
    delta = jnp.sum(p_own * d_own, axis=1, keepdims=True) + jnp.sum(
        p_prev * d_prev, axis=1, keepdims=True
    )
    g_own = (p_own * (d_own - delta)).astype(BF)
    g_prev = (p_prev * (d_prev - delta)).astype(BF)
    dq[...] = (dot(g_own, k[...]) + dot(g_prev, kp[...])) * SCALE
    near = ((dk, dot(g_own, q[...], "tn") * SCALE), (dv, dot(p_own.astype(BF), do[...], "tn")))
    dkp = dot(g_prev, q[...], "tn") * SCALE
    dvp = dot(p_prev.astype(BF), do[...], "tn")
    group = pl.program_id(1)

    @pl.when(group == 0)
    def _():
        for ref, value in near:
            ref[...] = value
        total[:, :HEAD_SIZE] = dkp
        total[:, HEAD_SIZE:] = dvp

    @pl.when(group > 0)
    def _():
        for ref, value in near:
            ref[...] += value
        total[:, :HEAD_SIZE] += dkp
        total[:, HEAD_SIZE:] += dvp

    @pl.when(group == pl.num_programs(1) - 1)
    def _():
        far[...] = total[...].astype(BF)


def attention_backward(later, own_col, own_row, prev_row, q, kv, before, do, lse, after):
    rows, width = q.shape
    kv_heads = kv.shape[1] // (2 * HEAD_SIZE)
    groups = 2 * width // kv.shape[1]
    inputs = (later, own_col, own_row, prev_row, q, kv, kv, before, before, do, lse)

    def kernel(*refs):
        backward_kernel(*refs[: len(inputs)], *refs[len(inputs) + len(after) :])

    mine = pl.BlockSpec((rows, HEAD_SIZE), lambda h, g: (0, h * groups + g))
    shared = pl.BlockSpec((rows, HEAD_SIZE), lambda h, g: (0, h))
    key = pl.BlockSpec((rows, HEAD_SIZE), lambda h, g: (0, 2 * h))
    value = pl.BlockSpec((rows, HEAD_SIZE), lambda h, g: (0, 2 * h + 1))
    column = pl.BlockSpec((rows, 1), lambda h, g: (0, 0))
    line = pl.BlockSpec((1, rows), lambda h, g: (0, 0))
    near = jax.ShapeDtypeStruct((rows, kv_heads * HEAD_SIZE), F32)
    return pl.pallas_call(
        kernel,
        grid=(kv_heads, groups),
        in_specs=[pl.BlockSpec(memory_space=pltpu.SMEM), column, line, line, mine]
        + [key, value] * 2
        + [mine, pl.BlockSpec((1, rows, 1), lambda h, g: (h * groups + g, 0, 0))]
        + [pl.BlockSpec(memory_space=pl.ANY)] * len(after),
        out_specs=[mine, shared, shared, pl.BlockSpec((rows, 2 * HEAD_SIZE), lambda h, g: (0, h))],
        out_shape=[
            jax.ShapeDtypeStruct((rows, width), F32),
            near,
            near,
            jax.ShapeDtypeStruct((rows, kv.shape[1]), BF),
        ],
        scratch_shapes=[pltpu.VMEM((rows, 2 * HEAD_SIZE), F32)],
        compiler_params=pltpu.CompilerParams(vmem_limit_bytes=32 * 2**20),
    )(*inputs, *after)


def call(
    kernel,
    out,
    inputs,
    scalars=(),
    grid=(1,),
    in_specs=None,
    out_specs=None,
    scratch=(),
    vmem=20,
    after=(),
    alias=None,
    hbm=4 * 2**20,
):
    def whole(a):
        return pl.BlockSpec(a.shape, lambda *_: (0,) * len(a.shape))

    in_specs = [s or whole(a) for s, a in zip(in_specs or [None] * len(inputs), inputs)]
    out_specs = [s or whole(a) for s, a in zip(out_specs or [None] * len(out), out)]
    alias = alias or {}

    def held(a, least):
        if a.size * a.dtype.itemsize < least:
            return a
        return pltpu.with_memory_space_constraint(a, pltpu.HBM)

    inputs = [held(a, hbm) for a in inputs]
    after = [held(a, hbm) for a in alias.values()] + [held(a, 2**20) for a in after]
    first = len(scalars) + len(inputs)

    def run(*refs):
        kernel(*refs[:first], *refs[first + len(after) :])

    return pl.pallas_call(
        run,
        grid_spec=pltpu.PrefetchScalarGridSpec(
            num_scalar_prefetch=len(scalars),
            grid=grid,
            in_specs=in_specs + [pl.BlockSpec(memory_space=pl.ANY)] * len(after),
            out_specs=out_specs,
            scratch_shapes=list(scratch),
        ),
        out_shape=list(out),
        compiler_params=pltpu.CompilerParams(vmem_limit_bytes=vmem * 2**20),
        input_output_aliases={first + i: place for i, place in enumerate(alias)},
        cost_estimate=pl.CostEstimate(flops=0, bytes_accessed=0, transcendentals=0),
    )(*[s.astype(jnp.int32).reshape(1) for s in scalars], *inputs, *after)


def in_hbm(dims, dtype):
    return pltpu.HBM(tuple(dims), dtype)


def shape(dims, dtype):
    return jax.ShapeDtypeStruct(tuple(dims), dtype)


def blocked(dims, index):
    return pl.BlockSpec(dims, index)


COLUMNS = 512


def other(index, k):
    return lax.bitwise_xor(index, jnp.int32(k))


def partners(z, size):
    return lax.bitwise_xor(z, jnp.arange(size, dtype=jnp.int32))


def ahead(index, k, size):
    return lax.bitwise_and(index + jnp.int32(k), jnp.int32(size - 1))


def behind(index, k, size):
    return lax.bitwise_and(index + jnp.int32(size) - jnp.int32(k), jnp.int32(size - 1))


def out_rows(ref):
    cols, dp, rows, width = ref.shape
    size = 4
    if dp == size:
        return ref[...].reshape(cols * dp * rows, width)
    per = dp // size
    order = [(c, q * per + r) for c in range(cols) for r in range(per) for q in range(size)]
    return jnp.concatenate([ref[c, d] for c, d in order])


def assemble(pieces, z, rolled, direct, after=()):
    def place_of(z, k):
        return behind(z, k, len(pieces)) if direct else other(z, k)

    size, dp = lax.axis_size("row"), lax.axis_size("dp")
    rows, width = pieces[0].shape
    rest = width // dp
    block = rows // size
    if rest % 128:
        out = jnp.stack([p.reshape(rows, dp, rest) for p in pieces], axis=2)
        order = behind(z, jnp.arange(size), size) if direct else partners(z, size)
        out = jnp.take(out, order, axis=2).reshape(rows, -1)
        if rolled:
            out = jnp.concatenate(
                [
                    lax.dynamic_slice_in_dim(out, other(z, k) * block, block, 0)
                    for k in range(size)
                ]
            )
        return out

    def kernel(z, *refs):
        out = refs[-1]
        for k in range(size):
            piece = refs[k][...]
            for d in range(dp):
                place = pl.multiple_of((d * size + place_of(z[0], k)) * rest, rest)
                out[:, pl.ds(place, rest)] = piece[:, d * rest : (d + 1) * rest]

    def index(i, z):
        return (lax.bitwise_xor(z[0], jnp.int32(i)) if rolled else i, 0)

    return call(
        kernel,
        [shape((rows, size * width), pieces[0].dtype)],
        list(pieces),
        [z],
        (size,),
        [blocked((block, width), index)] * size,
        [blocked((block, size * width), lambda i, z: (i, 0))],
        after=after,
    )[0]


def take_apart(full, z, rolled, after=()):
    size, dp = lax.axis_size("row"), lax.axis_size("dp")
    rows, width = full.shape
    rest = width // (size * dp)
    block = rows // size
    if rest % 128:
        if rolled:
            full = jnp.concatenate(
                [
                    lax.dynamic_slice_in_dim(full, other(z, i) * block, block, 0)
                    for i in range(size)
                ]
            )
        split = full.reshape(rows, dp, size, rest)
        split = jnp.take(split, partners(z, size), axis=2)
        return [split[:, :, k].reshape(rows, dp * rest) for k in range(size)]

    def kernel(z, full, *outs):
        for k in range(size):
            for d in range(dp):
                place = pl.multiple_of((d * size + other(z[0], k)) * rest, rest)
                outs[k][:, d * rest : (d + 1) * rest] = full[:, pl.ds(place, rest)]

    def index(i, z):
        return (lax.bitwise_xor(z[0], jnp.int32(i)) if rolled else i, 0)

    return call(
        kernel,
        [shape((rows, dp * rest), full.dtype)] * size,
        [full],
        [z],
        (size,),
        [blocked((block, width), lambda i, z: (i, 0))],
        [blocked((block, dp * rest), index)] * size,
        after=after,
    )


def project_kernel(x, gain, weight, cosine, sine, head_gain, a, scale, qr, kr, qn, kv):
    rows = x.shape[0]
    heads = qr.shape[1] // HEAD_SIZE
    kv_heads = kr.shape[1] // HEAD_SIZE

    @pl.when(pl.program_id(0) == 0)
    def _():
        for first in range(0, rows, 128):
            s = slice(first, first + 128)
            xf = x[s, :].astype(F32)
            r = lax.rsqrt(jnp.mean(xf * xf, axis=1, keepdims=True) + EPS)
            a[s, :] = (xf * r * gain[...]).astype(BF)
            scale[s, :] = r

    raw = dot(a[...], weight[0].reshape(MODEL_WIDTH, COLUMNS))

    def turn(values, gains):
        normed = (
            values
            * lax.rsqrt(jnp.mean(values * values, axis=-1, keepdims=True) + EPS)
            * gains
        )
        half = HEAD_SIZE // 2
        turned = jnp.concatenate([-normed[:, half:], normed[:, :half]], axis=-1)
        return (normed * cosine[...] + turned * sine[...]).astype(BF)

    for h in range(heads):
        s = slice(h * HEAD_SIZE, (h + 1) * HEAD_SIZE)
        qr[:, s] = raw[:, s]
        qn[:, s] = turn(raw[:, s], head_gain[0:1, :])
    first = heads * HEAD_SIZE
    for h in range(kv_heads):
        s = slice(h * HEAD_SIZE, (h + 1) * HEAD_SIZE)
        values = raw[:, first + h * HEAD_SIZE : first + (h + 1) * HEAD_SIZE]
        kr[:, s] = values
        kv[:, s] = turn(values, head_gain[1:2, :])
    kv[:, kv_heads * HEAD_SIZE :] = raw[:, first + kv_heads * HEAD_SIZE :].astype(BF)


def project(x, gain, weight, cosine, sine, head_gain, head_width, kv_width, after):
    rows = x.shape[0]
    cols, dp, _, width = weight.shape
    q = blocked((rows, head_width), lambda c: (0, c))
    k = blocked((rows, kv_width), lambda c: (0, c))
    return call(
        project_kernel,
        [
            shape(x.shape, BF),
            shape((rows, 1), F32),
            shape((rows, cols * head_width), F32),
            shape((rows, cols * kv_width), F32),
            shape((rows, cols * head_width), BF),
            shape((rows, 2 * cols * kv_width), BF),
        ],
        [x, gain, weight, cosine, sine, head_gain],
        (),
        (cols,),
        [None, None, blocked((1, dp, MODEL_WIDTH // dp, width), lambda c: (c, 0, 0, 0)), None, None, None],
        [None, None, q, k, q, blocked((rows, 2 * kv_width), lambda c: (0, c))],
        after=after,
    )


def mixed_parts(mixed, weight, z, base, after):
    size = lax.axis_size("row")
    cols, dp, total_rows, _ = weight.shape
    rows = mixed.shape[0]
    inner = mixed.shape[1] // (cols * dp)
    part = rows // size
    steps = MODEL_WIDTH // COLUMNS

    def kernel(z, mixed, weight, *refs):
        *outs, total = refs
        total[...] = dot(mixed[...], out_rows(weight))
        for k in range(size):
            first = pl.multiple_of(other(z[0], k) * part, part)
            outs[k][...] = total[pl.ds(first, part), :].astype(outs[k].dtype)

    return call(
        kernel,
        [shape((part, MODEL_WIDTH), BF if k else F32) for k in range(size)],
        [mixed, weight],
        [z],
        (steps,),
        [None, blocked((cols, dp, inner, COLUMNS), lambda c, z: (0, 0, base + c, 0))],
        [blocked((part, COLUMNS), lambda c, z: (0, c))] * size,
        scratch=[pltpu.VMEM((rows, COLUMNS), F32)],
        after=after,
    )


def mixed_back(chunks, weight, z, base, inner, after):
    size = len(chunks)
    cols, dp, _, _ = weight.shape
    part, width = chunks[0].shape
    rows = size * part
    heads = cols * dp * inner
    steps = width // COLUMNS

    def kernel(z, *refs):
        *ins, weight, full, out, total = refs
        for k in range(size):
            first = pl.multiple_of(other(z[0], k) * part, part)
            full[pl.ds(first, part), :] = ins[k][...]
        term = dot(full[...], out_rows(weight), "nt")
        c = pl.program_id(0)

        @pl.when(c == 0)
        def _():
            total[...] = term

        @pl.when(c > 0)
        def _():
            total[...] += term

        @pl.when(c == steps - 1)
        def _():
            out[...] = total[...].astype(BF)

    return call(
        kernel,
        [shape((rows, width), BF), shape((rows, heads), BF)],
        list(chunks) + [weight],
        [z],
        (steps,),
        [blocked((part, COLUMNS), lambda c, z: (0, c))] * size
        + [blocked((cols, dp, inner, COLUMNS), lambda c, z: (0, 0, base + c, 0))],
        [blocked((rows, COLUMNS), lambda c, z: (0, c)), None],
        scratch=[pltpu.VMEM((rows, heads), F32)],
        after=after,
    )


def masked(values, valid, after):
    def kernel(values, valid, out):
        out[...] = jnp.where(valid[...] > 0, values[...], jnp.zeros_like(values))

    return call(kernel, [shape(values.shape, values.dtype)], [values, valid], after=after)[0]


def add_parts(parts, dtype, after=()):
    def kernel(*refs):
        total = refs[0][...].astype(F32)
        for ref in refs[1:-1]:
            total = total + ref[...].astype(F32)
        refs[-1][...] = total.astype(dtype)

    return call(kernel, [shape(parts[0].shape, dtype)], list(parts), after=after)[0]


def hidden_norm(parts, x, gain, z, after=()):
    rows, width = parts[0].shape

    def kernel(z, *refs):
        *ps, x, gain, h, scale, a = refs
        total = x[...].astype(F32)
        for p in ps:
            total = total + p[...].astype(F32)
        r = lax.rsqrt(jnp.mean(total * total, axis=1, keepdims=True) + EPS)
        h[...] = total
        scale[...] = r
        a[...] = (total * r * gain[...]).astype(BF)

    return call(
        kernel,
        [shape((rows, width), F32), shape((rows, 1), F32), shape((rows, width), BF)],
        list(parts) + [x, gain],
        [z],
        (1,),
        [None] * len(parts) + [blocked((rows, width), lambda i, z: (z[0], 0)), None],
        after=after,
    )


def gateup_chunk(parts, weight, grad, hidden):
    part, width = parts[0].shape
    rows = part * len(parts)
    cols, dp, _, _ = weight.shape
    steps = 2 * hidden // (cols * COLUMNS)
    half = COLUMNS // 2

    def kernel(*refs):
        *ins, weight, grad, act, out, a = refs

        @pl.when((pl.program_id(0) == 0) & (pl.program_id(1) == 0))
        def _():
            for i, ref in enumerate(ins):
                a[i * part : (i + 1) * part, :] = ref[...]

        p = dot(a[...], weight[0].reshape(width, COLUMNS))
        for j in range(half // 128):
            gate, up = p[:, j * 256 : j * 256 + 128], p[:, j * 256 + 128 : j * 256 + 256]
            s = slice(j * 128, (j + 1) * 128)
            spread = 1.0 / (1.0 + jnp.exp(-gate))
            silu = gate * spread
            act[:, s] = (silu * up).astype(BF)
            g = grad[:, s]
            out[:, j * 256 : j * 256 + 128] = (g * up * (spread + silu * (1.0 - spread))).astype(BF)
            out[:, j * 256 + 128 : j * 256 + 256] = (g * silu).astype(BF)

    def place(c, t):
        return (0, c * steps + t)

    total = grad.shape[0]
    return call(
        kernel,
        [shape((total, hidden), BF), shape((total, 2 * hidden), BF)],
        list(parts) + [weight, grad],
        (),
        (cols, steps),
        [None] * len(parts)
        + [
            blocked((1, dp, width // dp, COLUMNS), lambda c, t: (c, 0, t, 0)),
            blocked((rows, half), place),
        ],
        [blocked((rows, half), place), blocked((rows, COLUMNS), place)],
        scratch=[pltpu.VMEM((rows, width), BF)],
        vmem=24,
    )


def gateup_back(grad, weight, kinds):
    cols, dp, _, _ = weight.shape
    both = grad.shape[1]
    block = MODEL_WIDTH // dp
    terms = both // COLUMNS
    per = terms // cols
    rows = grad.shape[0]
    part = rows // len(kinds)

    def kernel(grad, weight, *outs):
        total = None
        for t in range(terms):
            right = weight[t // per, 0, (t % per) * block : (t % per + 1) * block, :]
            term = dot(grad[:, t * COLUMNS : (t + 1) * COLUMNS], right, "nt")
            total = term if total is None else total + term
        for i, (out, kind) in enumerate(zip(outs, kinds)):
            out[...] = total[i * part : (i + 1) * part, :].astype(kind)

    return call(
        kernel,
        [shape((part, MODEL_WIDTH), kind) for kind in kinds],
        [grad, weight],
        (),
        (dp,),
        [
            None,
            blocked((cols, 1, per * block, COLUMNS), lambda n: (0, n, 0, 0)),
        ],
        [blocked((part, block), lambda n: (0, n))] * len(kinds),
        vmem=24,
    )


def down_back(out_low, weight, base, inner, after):
    cols, dp, _, _ = weight.shape
    rows, width = out_low.shape
    hidden = cols * dp * inner

    def kernel(low, weight, out):
        term = dot(low[...], out_rows(weight), "nt")

        @pl.when(pl.program_id(0) == 0)
        def _():
            out[...] = term

        @pl.when(pl.program_id(0) > 0)
        def _():
            out[...] += term

    return call(
        kernel,
        [shape((rows, hidden), F32)],
        [out_low, weight],
        (),
        (width // COLUMNS,),
        [
            blocked((rows, COLUMNS), lambda c: (0, c)),
            blocked((cols, dp, inner, COLUMNS), lambda c: (0, 0, base + c, 0)),
        ],
        [None],
        vmem=24,
        after=after,
    )[0]


def down_forward(active, hidden, weight, base, inner, after):
    cols, dp, _, _ = weight.shape
    rows, width = active.shape
    part = hidden.shape[0]

    def kernel(active, hidden, weight, out):
        p = dot(active[...], out_rows(weight))
        out[:part, :] = (p[:part, :] + hidden[...]).astype(BF)
        out[part:, :] = p[part:, :].astype(BF)

    return call(
        kernel,
        [shape((rows, MODEL_WIDTH), BF)],
        [active, hidden, weight],
        (),
        (MODEL_WIDTH // COLUMNS,),
        [
            None,
            blocked((part, COLUMNS), lambda c: (0, c)),
            blocked((cols, dp, inner, COLUMNS), lambda c: (0, 0, base + c, 0)),
        ],
        [blocked((rows, COLUMNS), lambda c: (0, c))],
        after=after,
    )[0]


def hidden_back(parts, h, scale, gain, out_low, after):
    rows, width = h.shape

    def kernel(*refs):
        *ps, h, scale, gain, dy, dh, low, gain_grad = refs
        grad = ps[0][...].astype(F32)
        for p in ps[1:]:
            grad = grad + p[...].astype(F32)
        hidden, r = h[...], scale[...]
        weighted = grad * gain[...]
        inner = jnp.sum(weighted * hidden, axis=1, keepdims=True)
        total = dy[...].astype(F32) + r * weighted - (r * r * r * inner / MODEL_WIDTH) * hidden
        dh[...] = total
        low[...] = total.astype(BF)
        gain_grad[...] = jnp.sum(grad * hidden * r, axis=0, keepdims=True)

    return call(
        kernel,
        [shape((rows, width), F32), shape((rows, width), BF), shape((1, width), F32)],
        list(parts) + [h, scale, gain, out_low],
        (),
        (1,),
        [None] * (len(parts) + 3) + [blocked((rows, width), lambda i: (0, 0))],
        after=after,
        hbm=2**17,
    )


def heads_back_kernel(
    qr, kr, dqn, dkn, dv, far, cosine, sine, head_gain, out, gain_grad
):
    heads = qr.shape[1] // HEAD_SIZE
    kv_heads = kr.shape[1] // HEAD_SIZE
    half = HEAD_SIZE // 2

    def back(raw, grad, gains):
        turned = grad * sine[...]
        turned = jnp.concatenate([turned[:, half:], -turned[:, :half]], axis=-1)
        g = grad * cosine[...] + turned
        r = lax.rsqrt(jnp.mean(raw * raw, axis=-1, keepdims=True) + EPS)
        weighted = g * gains
        inner = jnp.sum(weighted * raw, axis=-1, keepdims=True)
        low = (r * weighted - (r * r * r * inner / HEAD_SIZE) * raw).astype(BF)
        return low, jnp.sum(g * raw * r, axis=0, keepdims=True)

    @pl.when(pl.program_id(0) == 0)
    def _():
        gain_grad[...] = jnp.zeros_like(gain_grad)

    for h in range(heads):
        s = slice(h * HEAD_SIZE, (h + 1) * HEAD_SIZE)
        low, total = back(qr[:, s], dqn[:, s], head_gain[0:1, :])
        out[:, s] = low
        gain_grad[0:1, :] += total
    first = heads * HEAD_SIZE
    for h in range(kv_heads):
        s = slice(h * HEAD_SIZE, (h + 1) * HEAD_SIZE)
        low, total = back(kr[:, s], dkn[:, s] + far[:, s].astype(F32), head_gain[1:2, :])
        out[:, first + h * HEAD_SIZE : first + (h + 1) * HEAD_SIZE] = low
        gain_grad[1:2, :] += total
    first += kv_heads * HEAD_SIZE
    out[:, first:] = (dv[...] + far[:, kv_heads * HEAD_SIZE :].astype(F32)).astype(BF)


def heads_back(qr, kr, dqn, dkn, dv, far, cosine, sine, head_gain, cols, after):
    rows = qr.shape[0]
    head_width, kv_width = qr.shape[1] // cols, kr.shape[1] // cols
    q = blocked((rows, head_width), lambda c: (0, c))
    k = blocked((rows, kv_width), lambda c: (0, c))
    far_kv = blocked((rows, 2 * kv_width), lambda c: (0, c))
    width = head_width + 2 * kv_width
    return call(
        heads_back_kernel,
        [shape((rows, cols * width), BF), shape((2, HEAD_SIZE), F32)],
        [qr, kr, dqn, dkn, dv, far, cosine, sine, head_gain],
        (),
        (cols,),
        [q, k, q, k, k, far_kv, None, None, None],
        [blocked((rows, width), lambda c: (0, c)), None],
        after=after,
    )


def input_back(grads, weight, x, scale, gain, dh, z, after):
    cols, steps, _, width = weight.shape
    rows = grads.shape[0]
    model = MODEL_WIDTH
    part = dh.shape[0]

    def kernel(z, grads, weight, x, scale, gain, dh, out, c1, gain_grad):
        total = dot(grads[:, :width], weight[0, 0], "nt")
        for c in range(1, cols):
            total = total + dot(grads[:, c * width : (c + 1) * width], weight[c, 0], "nt")
        r = scale[...]
        xf = x[...].astype(F32)
        weighted = total * gain[...]
        moved = weighted * xf
        gain_grad[...] = jnp.sum(total * xf * r, axis=0, keepdims=True)
        out[...] = (r * weighted).astype(BF)
        first = pl.multiple_of(z[0] * part, part)
        own = pl.ds(first, part)
        out[own, :] = (out[own, :].astype(F32) + dh[...]).astype(BF)

        @pl.when(pl.program_id(0) == 0)
        def _():
            c1[...] = jnp.zeros_like(c1)

        c1[...] += jnp.sum(moved, axis=1, keepdims=True)

    block = model // steps
    wide = blocked((rows, block), lambda n, z: (0, n))
    return call(
        kernel,
        [shape((rows, model), BF), shape((rows, 1), F32), shape((1, model), F32)],
        [grads, weight, x, scale, gain, dh],
        [z],
        (steps,),
        [
            None,
            blocked((cols, 1, block, width), lambda n, z: (0, n, 0, 0)),
            wide,
            None,
            blocked((1, block), lambda n, z: (0, n)),
            blocked((part, block), lambda n, z: (0, n)),
        ],
        [wide, None, blocked((1, block), lambda n, z: (0, n))],
        after=after,
    )


def weight_grads(lefts, right, out_left, out_right, cols, after=()):
    size, dp = lax.axis_size("row"), lax.axis_size("dp")
    rows = right.shape[0]
    block = MODEL_WIDTH // dp
    n = right.shape[1] // cols
    part = rows // len(lefts)
    m = out_left.shape[1] // cols
    inner = m // dp
    terms = n // COLUMNS
    total = terms * block + MODEL_WIDTH // COLUMNS * inner

    def kernel(*refs):
        *ins, right, out_left, out_right, out = refs
        left = jnp.concatenate([ref[...] for ref in ins]) if len(ins) > 1 else ins[0][...]
        for t in range(terms):
            term = dot(left, right[:, t * COLUMNS : (t + 1) * COLUMNS], "tn")
            out[0, 0, t * block : (t + 1) * block, :] = term.astype(BF)
        for d in range(dp):
            q, r = d // (dp // size), d % (dp // size)
            first = (r * size + q) * inner

            @pl.when(pl.program_id(1) == d)
            def _():
                term = dot(out_left[:, first : first + inner], out_right[...], "tn").astype(BF)
                for c in range(MODEL_WIDTH // COLUMNS):
                    place = terms * block + c * inner
                    piece = term[:, c * COLUMNS : (c + 1) * COLUMNS]
                    out[0, 0, place : place + inner, :] = piece

    return call(
        kernel,
        [in_hbm((cols, dp, total, COLUMNS), BF)],
        list(lefts) + [right, out_left, out_right],
        (),
        (cols, dp),
        [blocked((part, block), lambda c, d: (0, d))] * len(lefts)
        + [
            blocked((rows, n), lambda c, d: (0, c)),
            blocked((rows, m), lambda c, d: (0, c)),
            None,
        ],
        [blocked((1, 1, total, COLUMNS), lambda c, d: (c, d, 0, 0))],
        after=after,
        vmem=28,
    )[0]


def swap(value, axis, step):
    return lax.ppermute(value, axis, [(i, i ^ step) for i in range(lax.axis_size(axis))])


def gather_pieces(own, beside=None):
    two = swap(own, "row", 2)
    if beside is not None:
        two, beside = lax.optimization_barrier((two, beside))
    pieces = [own, swap(own, "row", 1), two, swap(two, "row", 1)]
    return pieces if beside is None else (pieces, beside)


def gather_direct(own):
    return along_row([own] * lax.axis_size("row"), True)


def scatter_pieces(pieces, after=()):
    sent = add_parts([pieces[2], swap(pieces[3], "row", 1)], BF, after)
    direct, sent = lax.optimization_barrier((pieces[1], sent))
    return [pieces[0], swap(direct, "row", 1), swap(sent, "row", 2)], sent


def add_along(value, axes):
    for axis in axes:
        step = 1
        while step < lax.axis_size(axis):
            value = value + swap(value, axis, step)
            step *= 2
    return value


def along_row(pieces, forward):
    size = len(pieces)
    sign = 1 if forward else -1
    return [pieces[0]] + [
        lax.ppermute(p, "row", [(i, (i + sign * k) % size) for i in range(size)])
        for k, p in enumerate(pieces)
        if k
    ]


def along_quarters(pieces, forward):
    size = len(pieces)
    per = lax.axis_size("dp") // size
    sign = 1 if forward else -1

    def pairs(k):
        places = [(q, r) for q in range(size) for r in range(per)]
        return [(q * per + r, (q + sign * k) % size * per + r) for q, r in places]

    return [pieces[0]] + [lax.ppermute(p, "dp", pairs(k)) for k, p in enumerate(pieces) if k]


def gather_shard(shard):
    full = lax.all_gather(shard, ("col", "dp"), axis=0)
    return full.reshape(lax.axis_size("col"), lax.axis_size("dp"), *shard.shape)


def scatter_shard(full):
    flat_rows = full.reshape(-1, full.shape[-1])
    return lax.psum_scatter(flat_rows, ("col", "dp"), scatter_dimension=0, tiled=True)


def quarter_index():
    return lax.axis_index("dp") // (lax.axis_size("dp") // lax.axis_size("row"))


def pack_attention(query, keyval, z):
    size = lax.axis_size("row")
    rows = query.shape[0]
    hw, kw = query.shape[1] // size, keyval.shape[2] // size

    def kernel(z, query, keyval, *outs):
        for k in range(size):
            at = ahead(z[0], k, size)
            out = outs[k]
            out[:, :hw] = query[:, pl.ds(pl.multiple_of(at * hw, hw), hw)].astype(BF)
            for s in range(2):
                part = keyval[:, s, pl.ds(pl.multiple_of(at * kw, kw), kw)]
                out[:, hw + s * kw : hw + (s + 1) * kw] = part.astype(BF)

    return call(kernel, [shape((rows, hw + 2 * kw), BF)] * size, [query, keyval], [z], hbm=0)


def pack_feed(gateup, downs, z, after):
    size = lax.axis_size("row")
    rows = gateup.shape[0]
    fw = gateup.shape[2] // size
    terms = 2 * fw // COLUMNS
    inner = downs[0].shape[0]

    def kernel(z, gateup, *refs):
        for k in range(size):
            at = ahead(z[0], k, size)
            out = refs[size + k]
            for s in range(2):
                for j in range(fw // 128):
                    first = pl.multiple_of(at * fw + j * 128, 128)
                    place = (2 * j + s) * 128
                    t, lane = place // COLUMNS, place % COLUMNS
                    part = gateup[:, s, pl.ds(first, 128)].astype(BF)
                    out[t * rows : (t + 1) * rows, lane : lane + 128] = part
            out[terms * rows :, :] = refs[k][...]

    return call(
        kernel,
        [shape((terms * rows + inner, COLUMNS), BF)] * size,
        [gateup, *downs],
        [z],
        after=after,
        vmem=32,
    )


def pack_out(blocks, after=()):
    size = lax.axis_size("row")
    rows = [b.shape[0] // size for b in blocks]

    def kernel(q, *refs):
        for k in range(size):
            place = 0
            for ref, n in zip(refs, rows):
                first = pl.multiple_of(ahead(q[0], k, size) * n, n)
                refs[len(rows) + k][place : place + n, :] = ref[pl.ds(first, n), :].astype(BF)
                place += n

    return call(
        kernel,
        [shape((sum(rows), blocks[0].shape[1]), BF)] * size,
        blocks,
        [quarter_index()],
        after=after,
        hbm=0,
    )


def regroup(parts, source, target, cuts, after=(), top=0):
    size = len(parts)
    sources = [source(k) for k in range(size)]
    targets = [target(k) for k in range(size)]
    starts = [sum(cuts[:i]) for i in range(len(cuts))]

    def kernel(*refs):
        places, ins = refs[: 2 * size], refs[2 * size : 3 * size]
        outs, held = refs[3 * size : -1], refs[-1]
        for k in range(size):
            held[places[k][0]] = ins[k][top:, :]
        for i, (first, n) in enumerate(zip(starts, cuts)):
            for k in range(size):
                outs[i * size + k][...] = held[places[size + k][0], first : first + n]

    rows, width = parts[0].shape
    outs = call(
        kernel,
        [shape((n, width), BF) for n in cuts for _ in range(size)],
        parts,
        sources + targets,
        scratch=[pltpu.VMEM((size, rows - top, width), BF)],
        after=after,
    )
    return [outs[i * size : (i + 1) * size] for i in range(len(cuts))]


def make_shard(in_parts, out_parts, z, after=()):
    size, dp = len(in_parts), lax.axis_size("dp")
    rest = MODEL_WIDTH // (size * dp)
    steps = MODEL_WIDTH // COLUMNS
    rows = MODEL_WIDTH // (size * dp)
    if isinstance(out_parts, int):
        inner, joined = out_parts, True
        terms = (in_parts[0].shape[0] - inner) // rows
    else:
        inner, joined = out_parts[0].shape[0], False
        terms = in_parts[0].shape[0] // rows
    base = terms * size * rows
    if rest % 128:
        order = behind(z, jnp.arange(size), size)
        if joined:
            out_parts = [p[terms * rows :] for p in in_parts]
            in_parts = [p[: terms * rows] for p in in_parts]
        full = jnp.take(jnp.stack(in_parts), order, axis=0).reshape(size, terms, rows, COLUMNS)
        ins = full.transpose(1, 0, 2, 3).reshape(base, COLUMNS)
        full = jnp.stack([p.reshape(inner, dp, rest) for p in out_parts], axis=2)
        full = jnp.take(full, order, axis=2).reshape(inner, steps, COLUMNS)
        return jnp.concatenate([ins, full.transpose(1, 0, 2).reshape(-1, COLUMNS)])

    def kernel(z, *refs):
        out = refs[-1]
        for k in range(size):
            at = behind(z[0], k, size)
            for t in range(terms):
                first = pl.multiple_of((t * size + at) * rows, rows)
                out[pl.ds(first, rows), :] = refs[k][t * rows : (t + 1) * rows, :]
            place = pl.multiple_of(at * rest, rest)
            ref = refs[k] if joined else refs[size + k]
            top = terms * rows if joined else 0
            for d in range(dp):
                first = base + d * inner
                part = ref[top : top + inner, d * rest : (d + 1) * rest]
                out[first : first + inner, pl.ds(place, rest)] = part

    parts = list(in_parts) if joined else list(in_parts) + list(out_parts)
    out = shape((base + steps * inner, COLUMNS), BF)
    return call(kernel, [out], parts, [z], after=after)[0]


def split_shard(shard, terms, rows, inner, z, after=()):
    size, dp = lax.axis_size("row"), lax.axis_size("dp")
    rest = MODEL_WIDTH // (size * dp)
    steps = MODEL_WIDTH // COLUMNS
    base = terms * size * rows
    if rest % 128:
        ins = shard[:base].reshape(terms, size, rows, COLUMNS).transpose(1, 0, 2, 3)
        ins = jnp.take(ins, behind(z, jnp.arange(size), size), axis=0)
        outs = shard[base:].reshape(steps, inner, COLUMNS).transpose(1, 0, 2)
        outs = outs.reshape(inner, dp, size, rest)
        outs = jnp.take(outs, behind(z, jnp.arange(size), size), axis=2)
        return [
            jnp.concatenate([ins[k].reshape(-1, COLUMNS), outs[:, :, k].reshape(inner, COLUMNS)])
            for k in range(size)
        ]

    def kernel(z, full, *outs):
        for k in range(size):
            at = behind(z[0], k, size)
            for t in range(terms):
                first = pl.multiple_of((t * size + at) * rows, rows)
                outs[k][t * rows : (t + 1) * rows, :] = full[pl.ds(first, rows), :]
            place = pl.multiple_of(at * rest, rest)
            for d in range(dp):
                part = full[base + d * inner : base + (d + 1) * inner, pl.ds(place, rest)]
                outs[k][terms * rows :, d * rest : (d + 1) * rest] = part

    return call(
        kernel,
        [shape((terms * rows + inner, COLUMNS), BF)] * size,
        [shard],
        [z],
        after=after,
    )


def split_attention(shard, terms, rows, inner, z, after=()):
    size, dp = lax.axis_size("row"), lax.axis_size("dp")
    rest = MODEL_WIDTH // (size * dp)
    steps = MODEL_WIDTH // COLUMNS
    base = terms * size * rows
    quarter = quarter_index()
    if rest % 128:
        ins = shard[:base].reshape(terms, size, rows, COLUMNS).transpose(1, 0, 2, 3)
        ins = jnp.take(ins, behind(z, jnp.arange(size), size), axis=0)
        outs = shard[base:].reshape(steps, inner, COLUMNS).transpose(1, 0, 2)
        outs = outs.reshape(inner, dp, size, rest)
        outs = jnp.take(outs, ahead(quarter, jnp.arange(size), size), axis=2)
        return (
            [ins[k].reshape(-1, COLUMNS) for k in range(size)],
            [outs[:, :, k].reshape(inner, COLUMNS) for k in range(size)],
        )

    def kernel(z, quarter, full, *outs):
        for k in range(size):
            at = behind(z[0], k, size)
            for t in range(terms):
                first = pl.multiple_of((t * size + at) * rows, rows)
                outs[k][t * rows : (t + 1) * rows, :] = full[pl.ds(first, rows), :]
            place = pl.multiple_of(ahead(quarter[0], k, size) * rest, rest)
            for d in range(dp):
                part = full[base + d * inner : base + (d + 1) * inner, pl.ds(place, rest)]
                outs[size + k][:, d * rest : (d + 1) * rest] = part

    pieces = call(
        kernel,
        [shape((terms * rows, COLUMNS), BF)] * size + [shape((inner, COLUMNS), BF)] * size,
        [shard],
        [z, quarter],
        after=after,
    )
    return pieces[:size], pieces[size:]


def turned_back(pieces):
    size = len(pieces)
    per = lax.axis_size("dp") // size
    result = []
    for k, piece in enumerate(pieces):
        pairs = []
        for q in range(size):
            for r in range(per):
                for z in range(size):
                    target = (z * per + r) * size + (q + k) % size
                    pairs.append(((q * per + r) * size + z, target))
        result.append(lax.ppermute(piece, ("dp", "row"), pairs))
    return result


def out_pieces(messages, inner, z, after=()):
    size = len(messages)
    quarter = quarter_index()
    parts = regroup(
        messages,
        lambda k: ahead(z, k, size),
        lambda k: ahead(quarter, k, size),
        [inner],
        after,
        messages[0].shape[0] - inner,
    )[0]
    return along_quarters(parts, True)


def update(refs, grad, rate):
    weight, moment, second, weight_new, moment_new, second_new = refs
    m, v, w = adamw(weight[...], moment[...], second[...], grad, rate, DECAY)
    moment_new[...] = m
    second_new[...] = v
    weight_new[...] = w


def update_out(state, pieces, rate, place):
    size = len(pieces)
    rows, width = pieces[0].shape

    def kernel(q, *refs):
        k = pl.program_id(0)
        for i in range(size):

            @pl.when(k == i)
            def _():
                update(refs[size:], refs[i][...].astype(F32), rate)

    spec = blocked((rows, width), lambda k, q: (lax.bitwise_and(q[0] + size - k, size - 1), 0))
    w, m, v = call(
        kernel,
        [shape(state[0].shape, F32)] * 3,
        list(pieces) + list(state),
        [place],
        (size,),
        [None] * size + [spec] * 3,
        [spec] * 3,
        hbm=2**19,
    )
    return m, v, w


def place_columns(messages, rows, cuts, z, after=()):
    size = len(messages)

    def kernel(z, *refs):
        for out, cut in zip(refs[size:], cuts):
            width = sum(w for _, _, w in cut)
            for k in range(size):
                at = ahead(z[0], k, size) * width
                for t, first, w in cut:
                    place = pl.multiple_of(at, 128)
                    part = refs[k][t * rows : (t + 1) * rows, first : first + w]
                    out[:, pl.ds(place, w)] = part
                    at = at + w

    out = [shape((rows, size * sum(w for _, _, w in cut)), BF) for cut in cuts]
    return call(kernel, out, messages, [z], after=after)


def flat(values):
    rows, two, width = values.shape
    return values.reshape(rows, two, width // 128, 128).transpose(0, 2, 1, 3).reshape(-1, 128)


def update_pair(state, grad, rate):
    rows, two, width = state[0].shape
    total = rows * two * width // 128
    steps = 4 if total % 64 == 0 else 1

    def kernel(grad, *refs):
        update(refs, grad[...].astype(F32), rate)

    spec = blocked((total // steps, 128), lambda i: (i, 0))
    news = call(
        kernel,
        [shape((total, 128), F32)] * 3,
        [grad.reshape(-1, 128)] + [flat(s) for s in state],
        (),
        (steps,),
        [spec] * 4,
        [spec] * 3,
        hbm=2**19,
    )
    w, m, v = [
        n.reshape(rows, width // 128, two, 128).transpose(0, 2, 1, 3).reshape(rows, two, width)
        for n in news
    ]
    return (m, v, w), news[0]


def adamw(weight, moment, second, grad, rate, decay):
    moment_new = BETA_ONE * moment + (1.0 - BETA_ONE) * grad
    second_new = BETA_TWO * second + (1.0 - BETA_TWO) * grad * grad
    first_hat = moment_new * (1.0 / (1.0 - BETA_ONE**STEP))
    second_hat = second_new * (1.0 / (1.0 - BETA_TWO**STEP))
    weight_new = weight - rate * (first_hat / (jnp.sqrt(second_hat) + ADAM_EPS) + decay * weight)
    return (moment_new, second_new, weight_new)


def body(
    tokens,
    cotangent,
    seq_lens,
    query_weight,
    query_moment,
    query_second,
    key_value_master_weight,
    key_value_first_moment,
    key_value_second_moment,
    output_weight,
    output_moment,
    output_second,
    gateup_weight,
    gateup_moment,
    gateup_second,
    down_weight,
    down_moment,
    down_second,
    norm_gains,
    norm_moment,
    norm_second,
    head_gains,
    head_moment,
    head_second,
):
    size, dp, cols = lax.axis_size("row"), lax.axis_size("dp"), lax.axis_size("col")
    z, y = lax.axis_index("row"), lax.axis_index("col")
    rows = tokens.shape[0]
    quarter = rows // size
    item_count = rows * cols
    rest = MODEL_WIDTH // (size * dp)
    head_width = query_weight.shape[1] // size
    kv_width = key_value_master_weight.shape[2] // size

    gains = norm_gains.reshape(2, size, dp, rest).transpose(0, 2, 1, 3).reshape(2, MODEL_WIDTH)
    first_gain, second_gain = gains[0:1], gains[1:2]

    segment, position = token_layout(seq_lens[0], item_count)
    first = y * rows
    own_segment = lax.dynamic_slice_in_dim(segment, first, rows, 0)
    cosine, sine = rope_tables(lax.dynamic_slice_in_dim(position, first, rows, 0))
    valid = (own_segment < SEQS).astype(jnp.int32)[:, None]

    hidden_width = gateup_weight.shape[2] // size * cols

    in_rows = query_weight.shape[0]
    output_inner, down_inner = output_weight.shape[0] // size, down_weight.shape[0] // size
    gateup_terms = 2 * hidden_width // (cols * COLUMNS)
    steps = MODEL_WIDTH // COLUMNS
    down_base = gateup_terms * size * in_rows // down_inner
    output_base = size * in_rows // output_inner
    quarter_place = quarter_index()
    input_chunks = gather_pieces(tokens)
    attention_pieces = pack_attention(query_weight, key_value_master_weight, z)
    out_pieces_sent = pack_out([down_weight, output_weight], attention_pieces[:1])
    down_parts, output_parts = regroup(
        along_quarters(out_pieces_sent, True),
        lambda k: behind(quarter_place, k, size),
        lambda k: ahead(z, k, size),
        [down_inner, output_inner],
    )
    feed_pieces = pack_feed(gateup_weight, down_parts, z, output_parts[:1])
    attention_shard = make_shard(
        along_row(attention_pieces, True),
        along_row(output_parts, True),
        z,
        [feed_pieces[0], input_chunks[2]],
    )
    attention_full = gather_shard(attention_shard)
    inputs = assemble(input_chunks, z, False, False, [attention_shard])
    feed_shard = make_shard(along_row(feed_pieces, True), down_inner, z, [inputs])
    feed_full = gather_shard(feed_shard)
    out_own = masked(cotangent, valid, [feed_shard])
    out_chunks = gather_pieces(out_own)

    first_low, first_scale, query_raw, key_raw, query, keys_values = project(
        inputs,
        first_gain,
        attention_full,
        cosine,
        sine,
        head_gains,
        head_width,
        kv_width,
        [out_own],
    )
    before = lax.ppermute(keys_values, "col", [(i, i + 1) for i in range(cols - 1)])
    masks = (
        y.astype(jnp.int32).reshape(1),
        own_segment.reshape(rows, 1),
        own_segment.reshape(1, rows),
        segment[:rows].reshape(1, rows),
    )
    mixed, logsum = attention_forward(*masks, query, keys_values, before, [])
    hidden_pieces = mixed_parts(mixed, attention_full, z, output_base, out_chunks[1:])
    out_low = assemble(out_chunks, z, True, False, hidden_pieces[1:2])
    hidden_parts, _ = scatter_pieces(hidden_pieces)
    hidden, second_scale, second_low = hidden_norm(hidden_parts, inputs, second_gain, z)

    second_chunks = gather_pieces(second_low)
    active_grad = down_back(out_low, feed_full, down_base, down_inner, second_chunks[2:3])
    active, pair_grad = gateup_chunk(second_chunks, feed_full, active_grad, hidden_width)
    second_parts = gateup_back(pair_grad, feed_full, (F32, BF, BF, BF))
    feed_grads = weight_grads(
        second_chunks, pair_grad, active, out_low, cols, [second_parts[3]]
    )
    passed = swap(second_parts[3], "row", 1)
    feed_grads, passed = lax.optimization_barrier((feed_grads, passed))
    sent = add_parts([second_parts[2], passed], BF)
    direct, sent = lax.optimization_barrier((second_parts[1], sent))
    second_parts = [second_parts[0], swap(direct, "row", 1), swap(sent, "row", 2)]
    feed_total = scatter_shard(feed_grads)
    hidden_grad, hidden_low, second_gain_grad = hidden_back(
        second_parts, hidden, second_scale, second_gain, out_low, []
    )

    layer_part = down_forward(active, hidden, feed_full, down_base, down_inner, [hidden_low])
    hidden_all, mixed_grad = mixed_back(
        gather_pieces(hidden_low), attention_full, z, output_base, output_inner, [layer_part]
    )
    layer_pieces = take_apart(layer_part, z, True, [hidden_all])
    query_grad, key_grad, value_grad, far_sent = attention_backward(
        *masks, query, keys_values, before, mixed_grad, logsum, layer_pieces[:1]
    )
    far = lax.ppermute(far_sent, "col", [(i + 1, i) for i in range(cols - 1)])
    layer_parts, _ = scatter_pieces(layer_pieces)
    layer_output = add_parts(layer_parts, F32)
    raw_grad, head_part = heads_back(
        query_raw,
        key_raw,
        query_grad,
        key_grad,
        value_grad,
        far,
        cosine,
        sine,
        head_gains,
        cols,
        [layer_output],
    )
    attention_grads = weight_grads([first_low], raw_grad, mixed, hidden_all, cols)
    attention_grads, feed_total = lax.optimization_barrier((attention_grads, feed_total))
    attention_total = scatter_shard(attention_grads)
    feed_pieces = split_shard(feed_total, gateup_terms, in_rows, down_inner, z)
    input_part, inner_part, first_gain_grad = input_back(
        raw_grad,
        attention_full,
        inputs,
        first_scale,
        first_gain,
        hidden_grad,
        z,
        feed_pieces[:1],
    )
    input_pieces = take_apart(input_part, z, False)
    attention_pieces = split_shard(attention_total, 1, in_rows, output_inner, z)
    attention_messages = along_row(attention_pieces, False)
    input_parts, _ = scatter_pieces(input_pieces, attention_messages[1:2])
    feed_messages = along_row(feed_pieces, False)
    norm_part = jnp.concatenate([first_gain_grad, second_gain_grad])
    norm_part = norm_part.reshape(2, dp, size, rest).transpose(0, 2, 1, 3).reshape(2, MODEL_WIDTH)
    gain_part = jnp.concatenate([norm_part.reshape(-1), head_part.reshape(-1)]).reshape(-1, 128)
    gain_part, feed_messages[1], input_parts[0] = lax.optimization_barrier(
        (gain_part, feed_messages[1], input_parts[0])
    )
    gain_part = add_along(gain_part, ("dp", "col"))
    small = jnp.concatenate([gain_part, inner_part.reshape(-1, 128)])
    small, feed_messages[2] = lax.optimization_barrier((small, feed_messages[2]))
    small = add_along(small, ("row",)).reshape(-1)
    inner = small[gain_part.size :][:, None]
    norm_total = small[: norm_part.size].reshape(norm_part.shape)
    head_total = small[norm_part.size : gain_part.size].reshape(head_part.shape)

    down_new = update_out(
        (down_weight, down_moment, down_second),
        out_pieces(feed_messages, down_inner, z, [gain_part]),
        RATES[4],
        quarter_place,
    )
    cut = [(t, 0, COLUMNS) for t in range(gateup_terms)]
    (gateup_total,) = place_columns(
        feed_messages, in_rows, [cut], z, attention_pieces[:1]
    )
    gateup_new, _ = update_pair(
        (gateup_weight, gateup_moment, gateup_second), gateup_total, RATES[3]
    )
    output_new = update_out(
        (output_weight, output_moment, output_second),
        out_pieces(attention_messages, output_inner, z),
        RATES[2],
        quarter_place,
    )
    query_total, keyval_total = place_columns(
        attention_messages,
        in_rows,
        [[(0, 0, head_width)], [(0, head_width, 2 * kv_width)]],
        z,
    )
    input_grad = add_parts(input_parts, F32, [query_total]) - (
        first_scale * first_scale * first_scale * inner / MODEL_WIDTH
    ) * tokens.astype(F32)
    query_new = adamw(
        query_weight, query_moment, query_second, query_total.astype(F32), RATES[0], DECAY
    )
    keyval_new, _ = update_pair(
        (key_value_master_weight, key_value_first_moment, key_value_second_moment),
        keyval_total,
        RATES[1],
    )
    norm_new = adamw(norm_gains, norm_moment, norm_second, norm_total, GAIN_RATE, 0.0)
    head_new = adamw(head_gains, head_moment, head_second, head_total, GAIN_RATE, 0.0)
    return (
        layer_output,
        input_grad,
        *query_new,
        *keyval_new,
        *output_new,
        *gateup_new,
        *down_new,
        *norm_new,
        *head_new,
    )


def solution(mesh):
    items = P(("dp", "col"), "row")
    inward = P(("row", "dp"), "col")
    inward_pair = P(("row", "dp"), None, "col")
    outward = P(("col", "dp"), "row")
    weights = (
        (inward,) * 3 + (inward_pair,) * 3 + (outward,) * 3 + (inward_pair,) * 3 + (outward,) * 3
    )
    return jax.shard_map(
        body,
        mesh=mesh,
        in_specs=(items, items, P("dp", None)) + weights + (P(),) * 6,
        out_specs=(items, items) + weights + (P(),) * 6,
        check_vma=False,
    )
```

```python
import functools
import math

import jax
import jax.numpy as jnp
from jax import lax
from jax.experimental import pallas as pl
from jax.experimental.pallas import tpu as pltpu
from jax.sharding import PartitionSpec as P

MODEL_WIDTH = 2048
HEAD_SIZE = 128
SEQS = 4
STEP = 10

EPS = 1e-06
THETA = 1000000.0
NEGATIVE = -1e30
BETA_ONE = 0.9
BETA_TWO = 0.95
ADAM_EPS = 1e-08
DECAY = 0.1
RATES = (0.066, 0.066, 0.5, 0.066, 0.04)
GAIN_RATE = 0.6
BF = jnp.bfloat16
F32 = jnp.float32
SCALE = 1.0 / math.sqrt(HEAD_SIZE)


def dot(a, b, kind="nn"):
    dims = {"nn": ((1,), (0,)), "nt": ((1,), (1,)), "tn": ((0,), (0,))}[kind]
    return lax.dot_general(a, b, (dims, ((), ())), preferred_element_type=F32)


def token_layout(lengths, item_count):
    ends = jnp.cumsum(lengths)
    places = jnp.arange(item_count, dtype=jnp.int32)
    segment = jnp.sum((places[:, None] >= ends[None, :]).astype(jnp.int32), axis=1)
    starts = jnp.concatenate([ends - lengths, ends[-1:]])
    labels = jnp.arange(starts.shape[0], dtype=jnp.int32)
    begin = jnp.sum(jnp.where(segment[:, None] == labels[None, :], starts[None, :], 0), axis=1)
    return (segment, places - begin)


def rope_tables(position):
    half = HEAD_SIZE // 2
    freq = jnp.exp(jnp.arange(half, dtype=F32) * (-2.0 * math.log(THETA) / HEAD_SIZE))
    angle = position.astype(F32)[:, None] * freq[None, :]
    angle = jnp.concatenate([angle, angle], axis=1)
    return (jnp.cos(angle), jnp.sin(angle))


def block_masks(own_col, own_row, prev_row, later):
    rows = own_col.shape[0]
    r = lax.broadcasted_iota(jnp.int32, (rows, rows), 0)
    c = lax.broadcasted_iota(jnp.int32, (rows, rows), 1)
    own = (c <= r) & (own_col == own_row)
    prev = (own_col == prev_row) & (later > 0)
    return own, prev


def forward_kernel(later, own_col, own_row, prev_row, q, k, v, kp, vp, o, lse):
    own, prev = block_masks(own_col[...], own_row[...], prev_row[...], later[0])
    s_own = jnp.where(own, dot(q[...], k[...], "nt") * SCALE, NEGATIVE)
    s_prev = jnp.where(prev, dot(q[...], kp[...], "nt") * SCALE, NEGATIVE)
    top = jnp.maximum(
        jnp.max(s_own, axis=1, keepdims=True), jnp.max(s_prev, axis=1, keepdims=True)
    )
    total = jnp.sum(jnp.exp(s_own - top), axis=1, keepdims=True) + jnp.sum(
        jnp.exp(s_prev - top), axis=1, keepdims=True
    )
    logsum = top + jnp.log(total)
    p_own = jnp.exp(s_own - logsum).astype(BF)
    p_prev = jnp.exp(s_prev - logsum).astype(BF)
    o[...] = (dot(p_own, v[...]) + dot(p_prev, vp[...])).astype(BF)
    lse[0] = logsum


def attention_forward(later, own_col, own_row, prev_row, q, kv, before, after):
    rows, width = q.shape
    heads = width // HEAD_SIZE
    groups = 2 * width // kv.shape[1]
    inputs = (later, own_col, own_row, prev_row, q, kv, kv, before, before)

    def kernel(*refs):
        forward_kernel(*refs[: len(inputs)], *refs[len(inputs) + len(after) :])

    mine = pl.BlockSpec((rows, HEAD_SIZE), lambda h: (0, h))
    key = pl.BlockSpec((rows, HEAD_SIZE), lambda h: (0, 2 * (h // groups)))
    value = pl.BlockSpec((rows, HEAD_SIZE), lambda h: (0, 2 * (h // groups) + 1))
    column = pl.BlockSpec((rows, 1), lambda h: (0, 0))
    line = pl.BlockSpec((1, rows), lambda h: (0, 0))
    return pl.pallas_call(
        kernel,
        grid=(heads,),
        in_specs=[pl.BlockSpec(memory_space=pltpu.SMEM), column, line, line, mine]
        + [key, value] * 2
        + [pl.BlockSpec(memory_space=pl.ANY)] * len(after),
        out_specs=[mine, pl.BlockSpec((1, rows, 1), lambda h: (h, 0, 0))],
        out_shape=[
            jax.ShapeDtypeStruct((rows, width), BF),
            jax.ShapeDtypeStruct((heads, rows, 1), F32),
        ],
        compiler_params=pltpu.CompilerParams(vmem_limit_bytes=32 * 2**20),
    )(*inputs, *after)


def backward_kernel(
    later, own_col, own_row, prev_row, q, k, v, kp, vp, do, lse, dq, dk, dv, far, total
):
    own, prev = block_masks(own_col[...], own_row[...], prev_row[...], later[0])
    logsum = lse[0]
    p_own = jnp.exp(jnp.where(own, dot(q[...], k[...], "nt") * SCALE, NEGATIVE) - logsum)
    p_prev = jnp.exp(jnp.where(prev, dot(q[...], kp[...], "nt") * SCALE, NEGATIVE) - logsum)
    d_own = dot(do[...], v[...], "nt")
    d_prev = dot(do[...], vp[...], "nt")
    delta = jnp.sum(p_own * d_own, axis=1, keepdims=True) + jnp.sum(
        p_prev * d_prev, axis=1, keepdims=True
    )
    g_own = (p_own * (d_own - delta)).astype(BF)
    g_prev = (p_prev * (d_prev - delta)).astype(BF)
    dq[...] = (dot(g_own, k[...]) + dot(g_prev, kp[...])) * SCALE
    near = ((dk, dot(g_own, q[...], "tn") * SCALE), (dv, dot(p_own.astype(BF), do[...], "tn")))
    dkp = dot(g_prev, q[...], "tn") * SCALE
    dvp = dot(p_prev.astype(BF), do[...], "tn")
    group = pl.program_id(1)

    @pl.when(group == 0)
    def _():
        for ref, value in near:
            ref[...] = value
        total[:, :HEAD_SIZE] = dkp
        total[:, HEAD_SIZE:] = dvp

    @pl.when(group > 0)
    def _():
        for ref, value in near:
            ref[...] += value
        total[:, :HEAD_SIZE] += dkp
        total[:, HEAD_SIZE:] += dvp

    @pl.when(group == pl.num_programs(1) - 1)
    def _():
        far[...] = total[...].astype(BF)


def attention_backward(later, own_col, own_row, prev_row, q, kv, before, do, lse, after):
    rows, width = q.shape
    kv_heads = kv.shape[1] // (2 * HEAD_SIZE)
    groups = 2 * width // kv.shape[1]
    inputs = (later, own_col, own_row, prev_row, q, kv, kv, before, before, do, lse)

    def kernel(*refs):
        backward_kernel(*refs[: len(inputs)], *refs[len(inputs) + len(after) :])

    mine = pl.BlockSpec((rows, HEAD_SIZE), lambda h, g: (0, h * groups + g))
    shared = pl.BlockSpec((rows, HEAD_SIZE), lambda h, g: (0, h))
    key = pl.BlockSpec((rows, HEAD_SIZE), lambda h, g: (0, 2 * h))
    value = pl.BlockSpec((rows, HEAD_SIZE), lambda h, g: (0, 2 * h + 1))
    column = pl.BlockSpec((rows, 1), lambda h, g: (0, 0))
    line = pl.BlockSpec((1, rows), lambda h, g: (0, 0))
    near = jax.ShapeDtypeStruct((rows, kv_heads * HEAD_SIZE), F32)
    return pl.pallas_call(
        kernel,
        grid=(kv_heads, groups),
        in_specs=[pl.BlockSpec(memory_space=pltpu.SMEM), column, line, line, mine]
        + [key, value] * 2
        + [mine, pl.BlockSpec((1, rows, 1), lambda h, g: (h * groups + g, 0, 0))]
        + [pl.BlockSpec(memory_space=pl.ANY)] * len(after),
        out_specs=[mine, shared, shared, pl.BlockSpec((rows, 2 * HEAD_SIZE), lambda h, g: (0, h))],
        out_shape=[
            jax.ShapeDtypeStruct((rows, width), F32),
            near,
            near,
            jax.ShapeDtypeStruct((rows, kv.shape[1]), BF),
        ],
        scratch_shapes=[pltpu.VMEM((rows, 2 * HEAD_SIZE), F32)],
        compiler_params=pltpu.CompilerParams(vmem_limit_bytes=32 * 2**20),
    )(*inputs, *after)


def call(
    kernel,
    out,
    inputs,
    scalars=(),
    grid=(1,),
    in_specs=None,
    out_specs=None,
    scratch=(),
    vmem=20,
    after=(),
    alias=None,
    hbm=4 * 2**20,
):
    def whole(a):
        return pl.BlockSpec(a.shape, lambda *_: (0,) * len(a.shape))

    in_specs = [s or whole(a) for s, a in zip(in_specs or [None] * len(inputs), inputs)]
    out_specs = [s or whole(a) for s, a in zip(out_specs or [None] * len(out), out)]
    alias = alias or {}

    def held(a, least):
        if a.size * a.dtype.itemsize < least:
            return a
        return pltpu.with_memory_space_constraint(a, pltpu.HBM)

    inputs = [held(a, hbm) for a in inputs]
    after = [held(a, hbm) for a in alias.values()] + [held(a, 2**20) for a in after]
    first = len(scalars) + len(inputs)

    def run(*refs):
        kernel(*refs[:first], *refs[first + len(after) :])

    return pl.pallas_call(
        run,
        grid_spec=pltpu.PrefetchScalarGridSpec(
            num_scalar_prefetch=len(scalars),
            grid=grid,
            in_specs=in_specs + [pl.BlockSpec(memory_space=pl.ANY)] * len(after),
            out_specs=out_specs,
            scratch_shapes=list(scratch),
        ),
        out_shape=list(out),
        compiler_params=pltpu.CompilerParams(vmem_limit_bytes=vmem * 2**20),
        input_output_aliases={first + i: place for i, place in enumerate(alias)},
        cost_estimate=pl.CostEstimate(flops=0, bytes_accessed=0, transcendentals=0),
    )(*[s.astype(jnp.int32).reshape(1) for s in scalars], *inputs, *after)


def in_hbm(dims, dtype):
    return pltpu.HBM(tuple(dims), dtype)


def shape(dims, dtype):
    return jax.ShapeDtypeStruct(tuple(dims), dtype)


def blocked(dims, index):
    return pl.BlockSpec(dims, index)


COLUMNS = 512


def other(index, k):
    return lax.bitwise_xor(index, jnp.int32(k))


def partners(z, size):
    return lax.bitwise_xor(z, jnp.arange(size, dtype=jnp.int32))


def ahead(index, k, size):
    return lax.bitwise_and(index + jnp.int32(k), jnp.int32(size - 1))


def behind(index, k, size):
    return lax.bitwise_and(index + jnp.int32(size) - jnp.int32(k), jnp.int32(size - 1))


def out_rows(ref):
    cols, dp, rows, width = ref.shape
    size = 4
    if dp == size:
        return ref[...].reshape(cols * dp * rows, width)
    per = dp // size
    order = [(c, q * per + r) for c in range(cols) for r in range(per) for q in range(size)]
    return jnp.concatenate([ref[c, d] for c, d in order])


def assemble(pieces, z, rolled, direct, after=()):
    def place_of(z, k):
        return behind(z, k, len(pieces)) if direct else other(z, k)

    size, dp = lax.axis_size("row"), lax.axis_size("dp")
    rows, width = pieces[0].shape
    rest = width // dp
    block = rows // size
    if rest % 128:
        out = jnp.stack([p.reshape(rows, dp, rest) for p in pieces], axis=2)
        order = behind(z, jnp.arange(size), size) if direct else partners(z, size)
        out = jnp.take(out, order, axis=2).reshape(rows, -1)
        if rolled:
            out = jnp.concatenate(
                [
                    lax.dynamic_slice_in_dim(out, other(z, k) * block, block, 0)
                    for k in range(size)
                ]
            )
        return out

    def kernel(z, *refs):
        out = refs[-1]
        for k in range(size):
            piece = refs[k][...]
            for d in range(dp):
                place = pl.multiple_of((d * size + place_of(z[0], k)) * rest, rest)
                out[:, pl.ds(place, rest)] = piece[:, d * rest : (d + 1) * rest]

    def index(i, z):
        return (lax.bitwise_xor(z[0], jnp.int32(i)) if rolled else i, 0)

    return call(
        kernel,
        [shape((rows, size * width), pieces[0].dtype)],
        list(pieces),
        [z],
        (size,),
        [blocked((block, width), index)] * size,
        [blocked((block, size * width), lambda i, z: (i, 0))],
        after=after,
    )[0]


def take_apart(full, z, rolled, after=()):
    size, dp = lax.axis_size("row"), lax.axis_size("dp")
    rows, width = full.shape
    rest = width // (size * dp)
    block = rows // size
    if rest % 128:
        if rolled:
            full = jnp.concatenate(
                [
                    lax.dynamic_slice_in_dim(full, other(z, i) * block, block, 0)
                    for i in range(size)
                ]
            )
        split = full.reshape(rows, dp, size, rest)
        split = jnp.take(split, partners(z, size), axis=2)
        return [split[:, :, k].reshape(rows, dp * rest) for k in range(size)]

    def kernel(z, full, *outs):
        for k in range(size):
            for d in range(dp):
                place = pl.multiple_of((d * size + other(z[0], k)) * rest, rest)
                outs[k][:, d * rest : (d + 1) * rest] = full[:, pl.ds(place, rest)]

    def index(i, z):
        return (lax.bitwise_xor(z[0], jnp.int32(i)) if rolled else i, 0)

    return call(
        kernel,
        [shape((rows, dp * rest), full.dtype)] * size,
        [full],
        [z],
        (size,),
        [blocked((block, width), lambda i, z: (i, 0))],
        [blocked((block, dp * rest), index)] * size,
        after=after,
        hbm=2**20,
    )


def project_kernel(x, gain, weight, cosine, sine, head_gain, a, scale, qr, kr, qn, kv):
    rows = x.shape[0]
    heads = qr.shape[1] // HEAD_SIZE
    kv_heads = kr.shape[1] // HEAD_SIZE

    @pl.when(pl.program_id(0) == 0)
    def _():
        for first in range(0, rows, 128):
            s = slice(first, first + 128)
            xf = x[s, :].astype(F32)
            r = lax.rsqrt(jnp.mean(xf * xf, axis=1, keepdims=True) + EPS)
            a[s, :] = (xf * r * gain[...]).astype(BF)
            scale[s, :] = r

    raw = dot(a[...], weight[0].reshape(MODEL_WIDTH, COLUMNS))

    def turn(values, gains):
        normed = (
            values
            * lax.rsqrt(jnp.mean(values * values, axis=-1, keepdims=True) + EPS)
            * gains
        )
        half = HEAD_SIZE // 2
        turned = jnp.concatenate([-normed[:, half:], normed[:, :half]], axis=-1)
        return (normed * cosine[...] + turned * sine[...]).astype(BF)

    for h in range(heads):
        s = slice(h * HEAD_SIZE, (h + 1) * HEAD_SIZE)
        qr[:, s] = raw[:, s]
        qn[:, s] = turn(raw[:, s], head_gain[0:1, :])
    first = heads * HEAD_SIZE
    for h in range(kv_heads):
        s = slice(h * HEAD_SIZE, (h + 1) * HEAD_SIZE)
        values = raw[:, first + h * HEAD_SIZE : first + (h + 1) * HEAD_SIZE]
        kr[:, s] = values
        kv[:, s] = turn(values, head_gain[1:2, :])
    kv[:, kv_heads * HEAD_SIZE :] = raw[:, first + kv_heads * HEAD_SIZE :].astype(BF)


def project(x, gain, weight, cosine, sine, head_gain, head_width, kv_width, after):
    rows = x.shape[0]
    cols, dp, _, width = weight.shape
    q = blocked((rows, head_width), lambda c: (0, c))
    k = blocked((rows, kv_width), lambda c: (0, c))
    return call(
        project_kernel,
        [
            shape(x.shape, BF),
            shape((rows, 1), F32),
            shape((rows, cols * head_width), F32),
            shape((rows, cols * kv_width), F32),
            shape((rows, cols * head_width), BF),
            shape((rows, 2 * cols * kv_width), BF),
        ],
        [x, gain, weight, cosine, sine, head_gain],
        (),
        (cols,),
        [None, None, blocked((1, dp, MODEL_WIDTH // dp, width), lambda c: (c, 0, 0, 0)), None, None, None],
        [None, None, q, k, q, blocked((rows, 2 * kv_width), lambda c: (0, c))],
        after=after,
    )


def mixed_parts(mixed, weight, z, base, after):
    size = lax.axis_size("row")
    cols, dp, total_rows, _ = weight.shape
    rows = mixed.shape[0]
    inner = mixed.shape[1] // (cols * dp)
    part = rows // size
    steps = MODEL_WIDTH // COLUMNS

    def kernel(z, mixed, weight, *refs):
        *outs, total = refs
        total[...] = dot(mixed[...], out_rows(weight))
        for k in range(size):
            first = pl.multiple_of(other(z[0], k) * part, part)
            outs[k][...] = total[pl.ds(first, part), :].astype(outs[k].dtype)

    return call(
        kernel,
        [shape((part, MODEL_WIDTH), BF if k else F32) for k in range(size)],
        [mixed, weight],
        [z],
        (steps,),
        [None, blocked((cols, dp, inner, COLUMNS), lambda c, z: (0, 0, base + c, 0))],
        [blocked((part, COLUMNS), lambda c, z: (0, c))] * size,
        scratch=[pltpu.VMEM((rows, COLUMNS), F32)],
        after=after,
    )


def mixed_back(chunks, weight, z, base, inner, after):
    size = len(chunks)
    cols, dp, _, _ = weight.shape
    part, width = chunks[0].shape
    rows = size * part
    heads = cols * dp * inner
    steps = width // COLUMNS

    def kernel(z, *refs):
        *ins, weight, full, out, total = refs
        for k in range(size):
            first = pl.multiple_of(other(z[0], k) * part, part)
            full[pl.ds(first, part), :] = ins[k][...]
        term = dot(full[...], out_rows(weight), "nt")
        c = pl.program_id(0)

        @pl.when(c == 0)
        def _():
            total[...] = term

        @pl.when(c > 0)
        def _():
            total[...] += term

        @pl.when(c == steps - 1)
        def _():
            out[...] = total[...].astype(BF)

    return call(
        kernel,
        [shape((rows, width), BF), shape((rows, heads), BF)],
        list(chunks) + [weight],
        [z],
        (steps,),
        [blocked((part, COLUMNS), lambda c, z: (0, c))] * size
        + [blocked((cols, dp, inner, COLUMNS), lambda c, z: (0, 0, base + c, 0))],
        [blocked((rows, COLUMNS), lambda c, z: (0, c)), None],
        scratch=[pltpu.VMEM((rows, heads), F32)],
        after=after,
    )


def masked(values, valid, after):
    def kernel(values, valid, out):
        out[...] = jnp.where(valid[...] > 0, values[...], jnp.zeros_like(values))

    return call(kernel, [shape(values.shape, values.dtype)], [values, valid], after=after)[0]


def add_parts(parts, dtype, after=()):
    def kernel(*refs):
        total = refs[0][...].astype(F32)
        for ref in refs[1:-1]:
            total = total + ref[...].astype(F32)
        refs[-1][...] = total.astype(dtype)

    return call(kernel, [shape(parts[0].shape, dtype)], list(parts), after=after)[0]


def hidden_norm(parts, x, gain, z, after=()):
    rows, width = parts[0].shape

    def kernel(z, *refs):
        *ps, x, gain, h, scale, a = refs
        total = x[...].astype(F32)
        for p in ps:
            total = total + p[...].astype(F32)
        r = lax.rsqrt(jnp.mean(total * total, axis=1, keepdims=True) + EPS)
        h[...] = total
        scale[...] = r
        a[...] = (total * r * gain[...]).astype(BF)

    return call(
        kernel,
        [shape((rows, width), F32), shape((rows, 1), F32), shape((rows, width), BF)],
        list(parts) + [x, gain],
        [z],
        (1,),
        [None] * len(parts) + [blocked((rows, width), lambda i, z: (z[0], 0)), None],
        after=after,
    )


def gateup_chunk(parts, weight, grad, hidden):
    part, width = parts[0].shape
    rows = part * len(parts)
    cols, dp, _, _ = weight.shape
    steps = 2 * hidden // (cols * COLUMNS)
    half = COLUMNS // 2

    def kernel(*refs):
        *ins, weight, grad, act, out, a = refs

        @pl.when((pl.program_id(0) == 0) & (pl.program_id(1) == 0))
        def _():
            for i, ref in enumerate(ins):
                a[i * part : (i + 1) * part, :] = ref[...]

        p = dot(a[...], weight[0].reshape(width, COLUMNS))
        for j in range(half // 128):
            gate, up = p[:, j * 256 : j * 256 + 128], p[:, j * 256 + 128 : j * 256 + 256]
            s = slice(j * 128, (j + 1) * 128)
            spread = 1.0 / (1.0 + jnp.exp(-gate))
            silu = gate * spread
            act[:, s] = (silu * up).astype(BF)
            g = grad[:, s]
            out[:, j * 256 : j * 256 + 128] = (g * up * (spread + silu * (1.0 - spread))).astype(BF)
            out[:, j * 256 + 128 : j * 256 + 256] = (g * silu).astype(BF)

    def place(c, t):
        return (0, c * steps + t)

    total = grad.shape[0]
    return call(
        kernel,
        [shape((total, hidden), BF), shape((total, 2 * hidden), BF)],
        list(parts) + [weight, grad],
        (),
        (cols, steps),
        [None] * len(parts)
        + [
            blocked((1, dp, width // dp, COLUMNS), lambda c, t: (c, 0, t, 0)),
            blocked((rows, half), place),
        ],
        [blocked((rows, half), place), blocked((rows, COLUMNS), place)],
        scratch=[pltpu.VMEM((rows, width), BF)],
        vmem=24,
    )


def gateup_back(grad, weight, kinds):
    cols, dp, _, _ = weight.shape
    both = grad.shape[1]
    block = MODEL_WIDTH // dp
    terms = both // COLUMNS
    per = terms // cols
    rows = grad.shape[0]
    part = rows // len(kinds)

    def kernel(grad, weight, *outs):
        total = None
        for t in range(terms):
            right = weight[t // per, 0, (t % per) * block : (t % per + 1) * block, :]
            term = dot(grad[:, t * COLUMNS : (t + 1) * COLUMNS], right, "nt")
            total = term if total is None else total + term
        for i, (out, kind) in enumerate(zip(outs, kinds)):
            out[...] = total[i * part : (i + 1) * part, :].astype(kind)

    return call(
        kernel,
        [shape((part, MODEL_WIDTH), kind) for kind in kinds],
        [grad, weight],
        (),
        (dp,),
        [
            None,
            blocked((cols, 1, per * block, COLUMNS), lambda n: (0, n, 0, 0)),
        ],
        [blocked((part, block), lambda n: (0, n))] * len(kinds),
        vmem=24,
    )


def down_back(out_low, weight, base, inner, after):
    cols, dp, _, _ = weight.shape
    rows, width = out_low.shape
    hidden = cols * dp * inner

    def kernel(low, weight, out):
        term = dot(low[...], out_rows(weight), "nt")

        @pl.when(pl.program_id(0) == 0)
        def _():
            out[...] = term

        @pl.when(pl.program_id(0) > 0)
        def _():
            out[...] += term

    return call(
        kernel,
        [shape((rows, hidden), F32)],
        [out_low, weight],
        (),
        (width // COLUMNS,),
        [
            blocked((rows, COLUMNS), lambda c: (0, c)),
            blocked((cols, dp, inner, COLUMNS), lambda c: (0, 0, base + c, 0)),
        ],
        [None],
        vmem=24,
        after=after,
    )[0]


def down_forward(active, hidden, weight, base, inner, after):
    cols, dp, _, _ = weight.shape
    rows, width = active.shape
    part = hidden.shape[0]

    def kernel(active, hidden, weight, out):
        p = dot(active[...], out_rows(weight))
        out[:part, :] = (p[:part, :] + hidden[...]).astype(BF)
        out[part:, :] = p[part:, :].astype(BF)

    return call(
        kernel,
        [shape((rows, MODEL_WIDTH), BF)],
        [active, hidden, weight],
        (),
        (MODEL_WIDTH // COLUMNS,),
        [
            None,
            blocked((part, COLUMNS), lambda c: (0, c)),
            blocked((cols, dp, inner, COLUMNS), lambda c: (0, 0, base + c, 0)),
        ],
        [blocked((rows, COLUMNS), lambda c: (0, c))],
        after=after,
    )[0]


def hidden_back(parts, h, scale, gain, out_low, after):
    rows, width = h.shape

    def kernel(*refs):
        *ps, h, scale, gain, dy, dh, low, gain_grad = refs
        grad = ps[0][...].astype(F32)
        for p in ps[1:]:
            grad = grad + p[...].astype(F32)
        hidden, r = h[...], scale[...]
        weighted = grad * gain[...]
        inner = jnp.sum(weighted * hidden, axis=1, keepdims=True)
        total = dy[...].astype(F32) + r * weighted - (r * r * r * inner / MODEL_WIDTH) * hidden
        dh[...] = total
        low[...] = total.astype(BF)
        gain_grad[...] = jnp.sum(grad * hidden * r, axis=0, keepdims=True)

    return call(
        kernel,
        [shape((rows, width), F32), shape((rows, width), BF), shape((1, width), F32)],
        list(parts) + [h, scale, gain, out_low],
        (),
        (1,),
        [None] * (len(parts) + 3) + [blocked((rows, width), lambda i: (0, 0))],
        after=after,
        hbm=2**17,
    )


def heads_back_kernel(
    qr, kr, dqn, dkn, dv, far, cosine, sine, head_gain, out, gain_grad
):
    heads = qr.shape[1] // HEAD_SIZE
    kv_heads = kr.shape[1] // HEAD_SIZE
    half = HEAD_SIZE // 2

    def back(raw, grad, gains):
        turned = grad * sine[...]
        turned = jnp.concatenate([turned[:, half:], -turned[:, :half]], axis=-1)
        g = grad * cosine[...] + turned
        r = lax.rsqrt(jnp.mean(raw * raw, axis=-1, keepdims=True) + EPS)
        weighted = g * gains
        inner = jnp.sum(weighted * raw, axis=-1, keepdims=True)
        low = (r * weighted - (r * r * r * inner / HEAD_SIZE) * raw).astype(BF)
        return low, jnp.sum(g * raw * r, axis=0, keepdims=True)

    @pl.when(pl.program_id(0) == 0)
    def _():
        gain_grad[...] = jnp.zeros_like(gain_grad)

    for h in range(heads):
        s = slice(h * HEAD_SIZE, (h + 1) * HEAD_SIZE)
        low, total = back(qr[:, s], dqn[:, s], head_gain[0:1, :])
        out[:, s] = low
        gain_grad[0:1, :] += total
    first = heads * HEAD_SIZE
    for h in range(kv_heads):
        s = slice(h * HEAD_SIZE, (h + 1) * HEAD_SIZE)
        low, total = back(kr[:, s], dkn[:, s] + far[:, s].astype(F32), head_gain[1:2, :])
        out[:, first + h * HEAD_SIZE : first + (h + 1) * HEAD_SIZE] = low
        gain_grad[1:2, :] += total
    first += kv_heads * HEAD_SIZE
    out[:, first:] = (dv[...] + far[:, kv_heads * HEAD_SIZE :].astype(F32)).astype(BF)


def heads_back(qr, kr, dqn, dkn, dv, far, cosine, sine, head_gain, cols, after):
    rows = qr.shape[0]
    head_width, kv_width = qr.shape[1] // cols, kr.shape[1] // cols
    q = blocked((rows, head_width), lambda c: (0, c))
    k = blocked((rows, kv_width), lambda c: (0, c))
    far_kv = blocked((rows, 2 * kv_width), lambda c: (0, c))
    width = head_width + 2 * kv_width
    return call(
        heads_back_kernel,
        [shape((rows, cols * width), BF), shape((2, HEAD_SIZE), F32)],
        [qr, kr, dqn, dkn, dv, far, cosine, sine, head_gain],
        (),
        (cols,),
        [q, k, q, k, k, far_kv, None, None, None],
        [blocked((rows, width), lambda c: (0, c)), None],
        after=after,
    )


def input_back(grads, weight, x, scale, gain, dh, z, after):
    cols, steps, _, width = weight.shape
    rows = grads.shape[0]
    model = MODEL_WIDTH
    part = dh.shape[0]

    def kernel(z, grads, weight, x, scale, gain, dh, out, c1, gain_grad):
        total = dot(grads[:, :width], weight[0, 0], "nt")
        for c in range(1, cols):
            total = total + dot(grads[:, c * width : (c + 1) * width], weight[c, 0], "nt")
        r = scale[...]
        xf = x[...].astype(F32)
        weighted = total * gain[...]
        moved = weighted * xf
        gain_grad[...] = jnp.sum(total * xf * r, axis=0, keepdims=True)
        out[...] = (r * weighted).astype(BF)
        first = pl.multiple_of(z[0] * part, part)
        own = pl.ds(first, part)
        out[own, :] = (out[own, :].astype(F32) + dh[...]).astype(BF)

        @pl.when(pl.program_id(0) == 0)
        def _():
            c1[...] = jnp.zeros_like(c1)

        c1[...] += jnp.sum(moved, axis=1, keepdims=True)

    block = model // steps
    wide = blocked((rows, block), lambda n, z: (0, n))
    return call(
        kernel,
        [shape((rows, model), BF), shape((rows, 1), F32), shape((1, model), F32)],
        [grads, weight, x, scale, gain, dh],
        [z],
        (steps,),
        [
            None,
            blocked((cols, 1, block, width), lambda n, z: (0, n, 0, 0)),
            wide,
            None,
            blocked((1, block), lambda n, z: (0, n)),
            blocked((part, block), lambda n, z: (0, n)),
        ],
        [wide, None, blocked((1, block), lambda n, z: (0, n))],
        after=after,
    )


def weight_grads(lefts, right, out_left, out_right, cols, after=()):
    size, dp = lax.axis_size("row"), lax.axis_size("dp")
    rows = right.shape[0]
    block = MODEL_WIDTH // dp
    n = right.shape[1] // cols
    part = rows // len(lefts)
    m = out_left.shape[1] // cols
    inner = m // dp
    terms = n // COLUMNS
    total = terms * block + MODEL_WIDTH // COLUMNS * inner

    def kernel(*refs):
        *ins, right, out_left, out_right, out = refs
        left = jnp.concatenate([ref[...] for ref in ins]) if len(ins) > 1 else ins[0][...]
        for t in range(terms):
            term = dot(left, right[:, t * COLUMNS : (t + 1) * COLUMNS], "tn")
            out[0, 0, t * block : (t + 1) * block, :] = term.astype(BF)
        for d in range(dp):
            q, r = d // (dp // size), d % (dp // size)
            first = (r * size + q) * inner

            @pl.when(pl.program_id(1) == d)
            def _():
                term = dot(out_left[:, first : first + inner], out_right[...], "tn").astype(BF)
                for c in range(MODEL_WIDTH // COLUMNS):
                    place = terms * block + c * inner
                    piece = term[:, c * COLUMNS : (c + 1) * COLUMNS]
                    out[0, 0, place : place + inner, :] = piece

    return call(
        kernel,
        [in_hbm((cols, dp, total, COLUMNS), BF)],
        list(lefts) + [right, out_left, out_right],
        (),
        (cols, dp),
        [blocked((part, block), lambda c, d: (0, d))] * len(lefts)
        + [
            blocked((rows, n), lambda c, d: (0, c)),
            blocked((rows, m), lambda c, d: (0, c)),
            None,
        ],
        [blocked((1, 1, total, COLUMNS), lambda c, d: (c, d, 0, 0))],
        after=after,
        vmem=28,
    )[0]


def swap(value, axis, step):
    return lax.ppermute(value, axis, [(i, i ^ step) for i in range(lax.axis_size(axis))])


def gather_pieces(own, beside=None):
    two = swap(own, "row", 2)
    if beside is not None:
        two, beside = lax.optimization_barrier((two, beside))
    pieces = [own, swap(own, "row", 1), two, swap(two, "row", 1)]
    return pieces if beside is None else (pieces, beside)


def gather_direct(own):
    return along_row([own] * lax.axis_size("row"), True)


def scatter_pieces(pieces, after=()):
    sent = add_parts([pieces[2], swap(pieces[3], "row", 1)], BF, after)
    direct, sent = lax.optimization_barrier((pieces[1], sent))
    return [pieces[0], swap(direct, "row", 1), swap(sent, "row", 2)], sent


def add_along(value, axes):
    for axis in axes:
        step = 1
        while step < lax.axis_size(axis):
            value = value + swap(value, axis, step)
            step *= 2
    return value


def along_row(pieces, forward):
    size = len(pieces)
    sign = 1 if forward else -1
    return [pieces[0]] + [
        lax.ppermute(p, "row", [(i, (i + sign * k) % size) for i in range(size)])
        for k, p in enumerate(pieces)
        if k
    ]


def along_quarters(pieces, forward):
    size = len(pieces)
    per = lax.axis_size("dp") // size
    sign = 1 if forward else -1

    def pairs(k):
        places = [(q, r) for q in range(size) for r in range(per)]
        return [(q * per + r, (q + sign * k) % size * per + r) for q, r in places]

    return [pieces[0]] + [lax.ppermute(p, "dp", pairs(k)) for k, p in enumerate(pieces) if k]


def gather_shard(shard):
    full = lax.all_gather(shard, ("col", "dp"), axis=0)
    return full.reshape(lax.axis_size("col"), lax.axis_size("dp"), *shard.shape)


def scatter_shard(full):
    flat_rows = full.reshape(-1, full.shape[-1])
    return lax.psum_scatter(flat_rows, ("col", "dp"), scatter_dimension=0, tiled=True)


def quarter_index():
    return lax.axis_index("dp") // (lax.axis_size("dp") // lax.axis_size("row"))


def pack_attention(query, keyval, z):
    size = lax.axis_size("row")
    rows = query.shape[0]
    hw, kw = query.shape[1] // size, keyval.shape[2] // size

    def kernel(z, query, keyval, *outs):
        for k in range(size):
            at = ahead(z[0], k, size)
            out = outs[k]
            out[:, :hw] = query[:, pl.ds(pl.multiple_of(at * hw, hw), hw)].astype(BF)
            for s in range(2):
                part = keyval[:, s, pl.ds(pl.multiple_of(at * kw, kw), kw)]
                out[:, hw + s * kw : hw + (s + 1) * kw] = part.astype(BF)

    return call(kernel, [shape((rows, hw + 2 * kw), BF)] * size, [query, keyval], [z], hbm=0)


def pack_feed(gateup, downs, z, after):
    size = lax.axis_size("row")
    rows = gateup.shape[0]
    fw = gateup.shape[2] // size
    terms = 2 * fw // COLUMNS
    inner = downs[0].shape[0]

    def kernel(z, gateup, *refs):
        for k in range(size):
            at = ahead(z[0], k, size)
            out = refs[size + k]
            for s in range(2):
                for j in range(fw // 128):
                    first = pl.multiple_of(at * fw + j * 128, 128)
                    place = (2 * j + s) * 128
                    t, lane = place // COLUMNS, place % COLUMNS
                    part = gateup[:, s, pl.ds(first, 128)].astype(BF)
                    out[t * rows : (t + 1) * rows, lane : lane + 128] = part
            out[terms * rows :, :] = refs[k][...]

    return call(
        kernel,
        [shape((terms * rows + inner, COLUMNS), BF)] * size,
        [gateup, *downs],
        [z],
        after=after,
        vmem=32,
    )


def pack_out(blocks, after=()):
    size = lax.axis_size("row")
    rows = [b.shape[0] // size for b in blocks]

    def kernel(q, *refs):
        for k in range(size):
            place = 0
            for ref, n in zip(refs, rows):
                first = pl.multiple_of(ahead(q[0], k, size) * n, n)
                refs[len(rows) + k][place : place + n, :] = ref[pl.ds(first, n), :].astype(BF)
                place += n

    return call(
        kernel,
        [shape((sum(rows), blocks[0].shape[1]), BF)] * size,
        blocks,
        [quarter_index()],
        after=after,
        hbm=0,
    )


def regroup(parts, source, target, cuts, after=(), top=0):
    size = len(parts)
    sources = [source(k) for k in range(size)]
    targets = [target(k) for k in range(size)]
    starts = [sum(cuts[:i]) for i in range(len(cuts))]

    def kernel(*refs):
        places, ins = refs[: 2 * size], refs[2 * size : 3 * size]
        outs, held = refs[3 * size : -1], refs[-1]
        for k in range(size):
            held[places[k][0]] = ins[k][top:, :]
        for i, (first, n) in enumerate(zip(starts, cuts)):
            for k in range(size):
                outs[i * size + k][...] = held[places[size + k][0], first : first + n]

    rows, width = parts[0].shape
    outs = call(
        kernel,
        [shape((n, width), BF) for n in cuts for _ in range(size)],
        parts,
        sources + targets,
        scratch=[pltpu.VMEM((size, rows - top, width), BF)],
        after=after,
    )
    return [outs[i * size : (i + 1) * size] for i in range(len(cuts))]


def make_shard(in_parts, out_parts, z, after=()):
    size, dp = len(in_parts), lax.axis_size("dp")
    rest = MODEL_WIDTH // (size * dp)
    steps = MODEL_WIDTH // COLUMNS
    rows = MODEL_WIDTH // (size * dp)
    if isinstance(out_parts, int):
        inner, joined = out_parts, True
        terms = (in_parts[0].shape[0] - inner) // rows
    else:
        inner, joined = out_parts[0].shape[0], False
        terms = in_parts[0].shape[0] // rows
    base = terms * size * rows
    if rest % 128:
        order = behind(z, jnp.arange(size), size)
        if joined:
            out_parts = [p[terms * rows :] for p in in_parts]
            in_parts = [p[: terms * rows] for p in in_parts]
        full = jnp.take(jnp.stack(in_parts), order, axis=0).reshape(size, terms, rows, COLUMNS)
        ins = full.transpose(1, 0, 2, 3).reshape(base, COLUMNS)
        full = jnp.stack([p.reshape(inner, dp, rest) for p in out_parts], axis=2)
        full = jnp.take(full, order, axis=2).reshape(inner, steps, COLUMNS)
        return jnp.concatenate([ins, full.transpose(1, 0, 2).reshape(-1, COLUMNS)])

    def kernel(z, *refs):
        out = refs[-1]
        for k in range(size):
            at = behind(z[0], k, size)
            for t in range(terms):
                first = pl.multiple_of((t * size + at) * rows, rows)
                out[pl.ds(first, rows), :] = refs[k][t * rows : (t + 1) * rows, :]
            place = pl.multiple_of(at * rest, rest)
            ref = refs[k] if joined else refs[size + k]
            top = terms * rows if joined else 0
            for d in range(dp):
                first = base + d * inner
                part = ref[top : top + inner, d * rest : (d + 1) * rest]
                out[first : first + inner, pl.ds(place, rest)] = part

    parts = list(in_parts) if joined else list(in_parts) + list(out_parts)
    out = shape((base + steps * inner, COLUMNS), BF)
    return call(kernel, [out], parts, [z], after=after)[0]


def split_shard(shard, terms, rows, inner, z, after=()):
    size, dp = lax.axis_size("row"), lax.axis_size("dp")
    rest = MODEL_WIDTH // (size * dp)
    steps = MODEL_WIDTH // COLUMNS
    base = terms * size * rows
    if rest % 128:
        ins = shard[:base].reshape(terms, size, rows, COLUMNS).transpose(1, 0, 2, 3)
        ins = jnp.take(ins, behind(z, jnp.arange(size), size), axis=0)
        outs = shard[base:].reshape(steps, inner, COLUMNS).transpose(1, 0, 2)
        outs = outs.reshape(inner, dp, size, rest)
        outs = jnp.take(outs, behind(z, jnp.arange(size), size), axis=2)
        return [
            jnp.concatenate([ins[k].reshape(-1, COLUMNS), outs[:, :, k].reshape(inner, COLUMNS)])
            for k in range(size)
        ]

    def kernel(z, full, *outs):
        for k in range(size):
            at = behind(z[0], k, size)
            for t in range(terms):
                first = pl.multiple_of((t * size + at) * rows, rows)
                outs[k][t * rows : (t + 1) * rows, :] = full[pl.ds(first, rows), :]
            place = pl.multiple_of(at * rest, rest)
            for d in range(dp):
                part = full[base + d * inner : base + (d + 1) * inner, pl.ds(place, rest)]
                outs[k][terms * rows :, d * rest : (d + 1) * rest] = part

    return call(
        kernel,
        [shape((terms * rows + inner, COLUMNS), BF)] * size,
        [shard],
        [z],
        after=after,
        hbm=2**19,
    )


def out_pieces(messages, inner, z, after=()):
    size = len(messages)
    quarter = quarter_index()
    parts = regroup(
        messages,
        lambda k: ahead(z, k, size),
        lambda k: ahead(quarter, k, size),
        [inner],
        after,
        messages[0].shape[0] - inner,
    )[0]
    return along_quarters(parts, True)


def update(refs, grad, rate):
    weight, moment, second, weight_new, moment_new, second_new = refs
    m, v, w = adamw(weight[...], moment[...], second[...], grad, rate, DECAY)
    moment_new[...] = m
    second_new[...] = v
    weight_new[...] = w


def update_out(state, pieces, rate, place):
    size = len(pieces)
    rows, width = pieces[0].shape
    if rows * width <= 2**15:

        def whole(q, *refs):
            for k in range(size):
                own = pl.ds(pl.multiple_of(behind(q[0], k, size) * rows, rows), rows)
                update([ref.at[own, :] for ref in refs[size:]], refs[k][...].astype(F32), rate)

        w, m, v = call(
            whole, [shape(state[0].shape, F32)] * 3, list(pieces) + list(state), [place]
        )
        return m, v, w

    def kernel(q, *refs):
        k = pl.program_id(0)
        for i in range(size):

            @pl.when(k == i)
            def _():
                update(refs[size:], refs[i][...].astype(F32), rate)

    spec = blocked((rows, width), lambda k, q: (lax.bitwise_and(q[0] + size - k, size - 1), 0))
    w, m, v = call(
        kernel,
        [shape(state[0].shape, F32)] * 3,
        list(pieces) + list(state),
        [place],
        (size,),
        [None] * size + [spec] * 3,
        [spec] * 3,
        hbm=2**19,
    )
    return m, v, w


def place_columns(messages, rows, cuts, z, after=()):
    size = len(messages)

    def kernel(z, *refs):
        for out, cut in zip(refs[size:], cuts):
            width = sum(w for _, _, w in cut)
            for k in range(size):
                at = ahead(z[0], k, size) * width
                for t, first, w in cut:
                    place = pl.multiple_of(at, 128)
                    part = refs[k][t * rows : (t + 1) * rows, first : first + w]
                    out[:, pl.ds(place, w)] = part
                    at = at + w

    out = [shape((rows, size * sum(w for _, _, w in cut)), BF) for cut in cuts]
    return call(kernel, out, messages, [z], after=after)


def flat(values):
    rows, two, width = values.shape
    return values.reshape(rows, two, width // 128, 128).transpose(0, 2, 1, 3).reshape(-1, 128)


def update_pair(state, grad, rate):
    rows, two, width = state[0].shape
    total = rows * two * width // 128
    steps = 4 if total >= 4096 else 2

    def kernel(grad, *refs):
        update(refs, grad[...].astype(F32), rate)

    spec = blocked((total // steps, 128), lambda i: (i, 0))
    news = call(
        kernel,
        [shape((total, 128), F32)] * 3,
        [grad.reshape(-1, 128)] + [flat(s) for s in state],
        (),
        (steps,),
        [spec] * 4,
        [spec] * 3,
        hbm=2**19,
    )
    w, m, v = [
        n.reshape(rows, width // 128, two, 128).transpose(0, 2, 1, 3).reshape(rows, two, width)
        for n in news
    ]
    return (m, v, w), news[0]


def adamw(weight, moment, second, grad, rate, decay):
    moment_new = BETA_ONE * moment + (1.0 - BETA_ONE) * grad
    second_new = BETA_TWO * second + (1.0 - BETA_TWO) * grad * grad
    first_hat = moment_new * (1.0 / (1.0 - BETA_ONE**STEP))
    second_hat = second_new * (1.0 / (1.0 - BETA_TWO**STEP))
    weight_new = weight - rate * (first_hat / (jnp.sqrt(second_hat) + ADAM_EPS) + decay * weight)
    return (moment_new, second_new, weight_new)


def body(
    tokens,
    cotangent,
    seq_lens,
    query_weight,
    query_moment,
    query_second,
    key_value_master_weight,
    key_value_first_moment,
    key_value_second_moment,
    output_weight,
    output_moment,
    output_second,
    gateup_weight,
    gateup_moment,
    gateup_second,
    down_weight,
    down_moment,
    down_second,
    norm_gains,
    norm_moment,
    norm_second,
    head_gains,
    head_moment,
    head_second,
):
    size, dp, cols = lax.axis_size("row"), lax.axis_size("dp"), lax.axis_size("col")
    z, y = lax.axis_index("row"), lax.axis_index("col")
    rows = tokens.shape[0]
    quarter = rows // size
    item_count = rows * cols
    rest = MODEL_WIDTH // (size * dp)
    head_width = query_weight.shape[1] // size
    kv_width = key_value_master_weight.shape[2] // size

    gains = norm_gains.reshape(2, size, dp, rest).transpose(0, 2, 1, 3).reshape(2, MODEL_WIDTH)
    first_gain, second_gain = gains[0:1], gains[1:2]

    segment, position = token_layout(seq_lens[0], item_count)
    first = y * rows
    own_segment = lax.dynamic_slice_in_dim(segment, first, rows, 0)
    cosine, sine = rope_tables(lax.dynamic_slice_in_dim(position, first, rows, 0))
    valid = (own_segment < SEQS).astype(jnp.int32)[:, None]

    hidden_width = gateup_weight.shape[2] // size * cols

    in_rows = query_weight.shape[0]
    output_inner, down_inner = output_weight.shape[0] // size, down_weight.shape[0] // size
    gateup_terms = 2 * hidden_width // (cols * COLUMNS)
    steps = MODEL_WIDTH // COLUMNS
    down_base = gateup_terms * size * in_rows // down_inner
    output_base = size * in_rows // output_inner
    quarter_place = quarter_index()
    input_chunks = gather_pieces(tokens)
    attention_pieces = pack_attention(query_weight, key_value_master_weight, z)
    out_pieces_sent = pack_out([down_weight, output_weight], attention_pieces[:1])
    down_parts, output_parts = regroup(
        along_quarters(out_pieces_sent, True),
        lambda k: behind(quarter_place, k, size),
        lambda k: ahead(z, k, size),
        [down_inner, output_inner],
    )
    feed_pieces = pack_feed(gateup_weight, down_parts, z, output_parts[:1])
    attention_shard = make_shard(
        along_row(attention_pieces, True),
        along_row(output_parts, True),
        z,
        [feed_pieces[0], input_chunks[2]],
    )
    attention_full = gather_shard(attention_shard)
    inputs = assemble(input_chunks, z, False, False, [attention_shard])
    feed_shard = make_shard(along_row(feed_pieces, True), down_inner, z, [inputs])
    feed_full = gather_shard(feed_shard)
    out_own = masked(cotangent, valid, [feed_shard])
    out_chunks = gather_pieces(out_own)

    first_low, first_scale, query_raw, key_raw, query, keys_values = project(
        inputs,
        first_gain,
        attention_full,
        cosine,
        sine,
        head_gains,
        head_width,
        kv_width,
        [out_own],
    )
    before = lax.ppermute(keys_values, "col", [(i, i + 1) for i in range(cols - 1)])
    masks = (
        y.astype(jnp.int32).reshape(1),
        own_segment.reshape(rows, 1),
        own_segment.reshape(1, rows),
        segment[:rows].reshape(1, rows),
    )
    mixed, logsum = attention_forward(*masks, query, keys_values, before, [])
    hidden_pieces = mixed_parts(mixed, attention_full, z, output_base, out_chunks[1:])
    out_low = assemble(out_chunks, z, True, False, hidden_pieces[1:2])
    hidden_parts, _ = scatter_pieces(hidden_pieces)
    hidden, second_scale, second_low = hidden_norm(hidden_parts, inputs, second_gain, z)

    second_chunks = gather_pieces(second_low)
    active_grad = down_back(out_low, feed_full, down_base, down_inner, second_chunks[2:3])
    active, pair_grad = gateup_chunk(second_chunks, feed_full, active_grad, hidden_width)
    second_parts = gateup_back(pair_grad, feed_full, (F32, BF, BF, BF))
    feed_grads = weight_grads(
        second_chunks, pair_grad, active, out_low, cols, [second_parts[3]]
    )
    passed = swap(second_parts[3], "row", 1)
    feed_grads, passed = lax.optimization_barrier((feed_grads, passed))
    sent = add_parts([second_parts[2], passed], BF)
    direct, sent = lax.optimization_barrier((second_parts[1], sent))
    second_parts = [second_parts[0], swap(direct, "row", 1), swap(sent, "row", 2)]
    feed_total = scatter_shard(feed_grads)
    hidden_grad, hidden_low, second_gain_grad = hidden_back(
        second_parts, hidden, second_scale, second_gain, out_low, []
    )

    layer_part = down_forward(active, hidden, feed_full, down_base, down_inner, [hidden_low])
    hidden_all, mixed_grad = mixed_back(
        gather_pieces(hidden_low), attention_full, z, output_base, output_inner, [layer_part]
    )
    layer_pieces = take_apart(layer_part, z, True, [hidden_all])
    query_grad, key_grad, value_grad, far_sent = attention_backward(
        *masks, query, keys_values, before, mixed_grad, logsum, layer_pieces[:1]
    )
    far = lax.ppermute(far_sent, "col", [(i + 1, i) for i in range(cols - 1)])
    layer_parts, _ = scatter_pieces(layer_pieces)
    layer_output = add_parts(layer_parts, F32)
    raw_grad, head_part = heads_back(
        query_raw,
        key_raw,
        query_grad,
        key_grad,
        value_grad,
        far,
        cosine,
        sine,
        head_gains,
        cols,
        [layer_output],
    )
    attention_grads = weight_grads([first_low], raw_grad, mixed, hidden_all, cols)
    attention_grads, feed_total = lax.optimization_barrier((attention_grads, feed_total))
    attention_total = scatter_shard(attention_grads)
    feed_pieces = split_shard(feed_total, gateup_terms, in_rows, down_inner, z)
    input_part, inner_part, first_gain_grad = input_back(
        raw_grad,
        attention_full,
        inputs,
        first_scale,
        first_gain,
        hidden_grad,
        z,
        feed_pieces[:1],
    )
    input_pieces = take_apart(input_part, z, False)
    attention_pieces = split_shard(attention_total, 1, in_rows, output_inner, z)
    attention_messages = along_row(attention_pieces, False)
    input_parts, _ = scatter_pieces(input_pieces, attention_messages[1:2])
    feed_messages = along_row(feed_pieces, False)
    norm_part = jnp.concatenate([first_gain_grad, second_gain_grad])
    norm_part = norm_part.reshape(2, dp, size, rest).transpose(0, 2, 1, 3).reshape(2, MODEL_WIDTH)
    gain_part = jnp.concatenate([norm_part.reshape(-1), head_part.reshape(-1)]).reshape(-1, 128)
    gain_part, feed_messages[1], input_parts[0] = lax.optimization_barrier(
        (gain_part, feed_messages[1], input_parts[0])
    )
    gain_part = add_along(gain_part, ("dp", "col"))
    small = jnp.concatenate([gain_part, inner_part.reshape(-1, 128)])
    small, feed_messages[2] = lax.optimization_barrier((small, feed_messages[2]))
    small = add_along(small, ("row",)).reshape(-1)
    inner = small[gain_part.size :][:, None]
    norm_total = small[: norm_part.size].reshape(norm_part.shape)
    head_total = small[norm_part.size : gain_part.size].reshape(head_part.shape)

    down_new = update_out(
        (down_weight, down_moment, down_second),
        out_pieces(feed_messages, down_inner, z, [gain_part]),
        RATES[4],
        quarter_place,
    )
    cut = [(t, 0, COLUMNS) for t in range(gateup_terms)]
    (gateup_total,) = place_columns(
        feed_messages, in_rows, [cut], z, attention_pieces[:1]
    )
    gateup_new, _ = update_pair(
        (gateup_weight, gateup_moment, gateup_second), gateup_total, RATES[3]
    )
    output_new = update_out(
        (output_weight, output_moment, output_second),
        out_pieces(attention_messages, output_inner, z),
        RATES[2],
        quarter_place,
    )
    query_total, keyval_total = place_columns(
        attention_messages,
        in_rows,
        [[(0, 0, head_width)], [(0, head_width, 2 * kv_width)]],
        z,
    )
    input_grad = add_parts(input_parts, F32, [query_total]) - (
        first_scale * first_scale * first_scale * inner / MODEL_WIDTH
    ) * tokens.astype(F32)
    query_new = adamw(
        query_weight, query_moment, query_second, query_total.astype(F32), RATES[0], DECAY
    )
    keyval_new, _ = update_pair(
        (key_value_master_weight, key_value_first_moment, key_value_second_moment),
        keyval_total,
        RATES[1],
    )
    norm_new = adamw(norm_gains, norm_moment, norm_second, norm_total, GAIN_RATE, 0.0)
    head_new = adamw(head_gains, head_moment, head_second, head_total, GAIN_RATE, 0.0)
    return (
        layer_output,
        input_grad,
        *query_new,
        *keyval_new,
        *output_new,
        *gateup_new,
        *down_new,
        *norm_new,
        *head_new,
    )


def solution(mesh):
    items = P(("dp", "col"), "row")
    inward = P(("row", "dp"), "col")
    inward_pair = P(("row", "dp"), None, "col")
    outward = P(("col", "dp"), "row")
    weights = (
        (inward,) * 3 + (inward_pair,) * 3 + (outward,) * 3 + (inward_pair,) * 3 + (outward,) * 3
    )
    return jax.shard_map(
        body,
        mesh=mesh,
        in_specs=(items, items, P("dp", None)) + weights + (P(),) * 6,
        out_specs=(items, items) + weights + (P(),) * 6,
        check_vma=False,
    )
```

```python
import functools
import math

import jax
import jax.numpy as jnp
from jax import lax
from jax.experimental import pallas as pl
from jax.experimental.pallas import tpu as pltpu
from jax.sharding import PartitionSpec as P

MODEL_WIDTH = 2048
HEAD_SIZE = 128
SEQS = 4
STEP = 10

EPS = 1e-06
THETA = 1000000.0
NEGATIVE = -1e30
BETA_ONE = 0.9
BETA_TWO = 0.95
ADAM_EPS = 1e-08
DECAY = 0.1
RATES = (0.066, 0.066, 0.5, 0.066, 0.04)
GAIN_RATE = 0.6
BF = jnp.bfloat16
F32 = jnp.float32
SCALE = 1.0 / math.sqrt(HEAD_SIZE)


def dot(a, b, kind="nn"):
    dims = {"nn": ((1,), (0,)), "nt": ((1,), (1,)), "tn": ((0,), (0,))}[kind]
    return lax.dot_general(a, b, (dims, ((), ())), preferred_element_type=F32)


def token_layout(lengths, item_count):
    ends = jnp.cumsum(lengths)
    places = jnp.arange(item_count, dtype=jnp.int32)
    segment = jnp.sum((places[:, None] >= ends[None, :]).astype(jnp.int32), axis=1)
    starts = jnp.concatenate([ends - lengths, ends[-1:]])
    labels = jnp.arange(starts.shape[0], dtype=jnp.int32)
    begin = jnp.sum(jnp.where(segment[:, None] == labels[None, :], starts[None, :], 0), axis=1)
    return (segment, places - begin)


def rope_tables(position):
    half = HEAD_SIZE // 2
    freq = jnp.exp(jnp.arange(half, dtype=F32) * (-2.0 * math.log(THETA) / HEAD_SIZE))
    angle = position.astype(F32)[:, None] * freq[None, :]
    angle = jnp.concatenate([angle, angle], axis=1)
    return (jnp.cos(angle), jnp.sin(angle))


def block_masks(own_col, own_row, prev_row, later):
    rows = own_col.shape[0]
    r = lax.broadcasted_iota(jnp.int32, (rows, rows), 0)
    c = lax.broadcasted_iota(jnp.int32, (rows, rows), 1)
    own = (c <= r) & (own_col == own_row)
    prev = (own_col == prev_row) & (later > 0)
    return own, prev


def forward_kernel(later, own_col, own_row, prev_row, q, k, v, kp, vp, o, lse):
    own, prev = block_masks(own_col[...], own_row[...], prev_row[...], later[0])
    s_own = jnp.where(own, dot(q[...], k[...], "nt") * SCALE, NEGATIVE)
    s_prev = jnp.where(prev, dot(q[...], kp[...], "nt") * SCALE, NEGATIVE)
    top = jnp.maximum(
        jnp.max(s_own, axis=1, keepdims=True), jnp.max(s_prev, axis=1, keepdims=True)
    )
    total = jnp.sum(jnp.exp(s_own - top), axis=1, keepdims=True) + jnp.sum(
        jnp.exp(s_prev - top), axis=1, keepdims=True
    )
    logsum = top + jnp.log(total)
    p_own = jnp.exp(s_own - logsum).astype(BF)
    p_prev = jnp.exp(s_prev - logsum).astype(BF)
    o[...] = (dot(p_own, v[...]) + dot(p_prev, vp[...])).astype(BF)
    lse[0] = logsum


def attention_forward(later, own_col, own_row, prev_row, q, kv, before, after):
    rows, width = q.shape
    heads = width // HEAD_SIZE
    groups = 2 * width // kv.shape[1]
    inputs = (later, own_col, own_row, prev_row, q, kv, kv, before, before)

    def kernel(*refs):
        forward_kernel(*refs[: len(inputs)], *refs[len(inputs) + len(after) :])

    mine = pl.BlockSpec((rows, HEAD_SIZE), lambda h: (0, h))
    key = pl.BlockSpec((rows, HEAD_SIZE), lambda h: (0, 2 * (h // groups)))
    value = pl.BlockSpec((rows, HEAD_SIZE), lambda h: (0, 2 * (h // groups) + 1))
    column = pl.BlockSpec((rows, 1), lambda h: (0, 0))
    line = pl.BlockSpec((1, rows), lambda h: (0, 0))
    return pl.pallas_call(
        kernel,
        grid=(heads,),
        in_specs=[pl.BlockSpec(memory_space=pltpu.SMEM), column, line, line, mine]
        + [key, value] * 2
        + [pl.BlockSpec(memory_space=pl.ANY)] * len(after),
        out_specs=[mine, pl.BlockSpec((1, rows, 1), lambda h: (h, 0, 0))],
        out_shape=[
            jax.ShapeDtypeStruct((rows, width), BF),
            jax.ShapeDtypeStruct((heads, rows, 1), F32),
        ],
        compiler_params=pltpu.CompilerParams(vmem_limit_bytes=32 * 2**20),
    )(*inputs, *after)


def backward_kernel(
    later, own_col, own_row, prev_row, q, k, v, kp, vp, do, lse, dq, dk, dv, far, total
):
    own, prev = block_masks(own_col[...], own_row[...], prev_row[...], later[0])
    logsum = lse[0]
    p_own = jnp.exp(jnp.where(own, dot(q[...], k[...], "nt") * SCALE, NEGATIVE) - logsum)
    p_prev = jnp.exp(jnp.where(prev, dot(q[...], kp[...], "nt") * SCALE, NEGATIVE) - logsum)
    d_own = dot(do[...], v[...], "nt")
    d_prev = dot(do[...], vp[...], "nt")
    delta = jnp.sum(p_own * d_own, axis=1, keepdims=True) + jnp.sum(
        p_prev * d_prev, axis=1, keepdims=True
    )
    g_own = (p_own * (d_own - delta)).astype(BF)
    g_prev = (p_prev * (d_prev - delta)).astype(BF)
    dq[...] = (dot(g_own, k[...]) + dot(g_prev, kp[...])) * SCALE
    near = ((dk, dot(g_own, q[...], "tn") * SCALE), (dv, dot(p_own.astype(BF), do[...], "tn")))
    dkp = dot(g_prev, q[...], "tn") * SCALE
    dvp = dot(p_prev.astype(BF), do[...], "tn")
    group = pl.program_id(1)

    @pl.when(group == 0)
    def _():
        for ref, value in near:
            ref[...] = value
        total[:, :HEAD_SIZE] = dkp
        total[:, HEAD_SIZE:] = dvp

    @pl.when(group > 0)
    def _():
        for ref, value in near:
            ref[...] += value
        total[:, :HEAD_SIZE] += dkp
        total[:, HEAD_SIZE:] += dvp

    @pl.when(group == pl.num_programs(1) - 1)
    def _():
        far[...] = total[...].astype(BF)


def attention_backward(later, own_col, own_row, prev_row, q, kv, before, do, lse, after):
    rows, width = q.shape
    kv_heads = kv.shape[1] // (2 * HEAD_SIZE)
    groups = 2 * width // kv.shape[1]
    inputs = (later, own_col, own_row, prev_row, q, kv, kv, before, before, do, lse)

    def kernel(*refs):
        backward_kernel(*refs[: len(inputs)], *refs[len(inputs) + len(after) :])

    mine = pl.BlockSpec((rows, HEAD_SIZE), lambda h, g: (0, h * groups + g))
    shared = pl.BlockSpec((rows, HEAD_SIZE), lambda h, g: (0, h))
    key = pl.BlockSpec((rows, HEAD_SIZE), lambda h, g: (0, 2 * h))
    value = pl.BlockSpec((rows, HEAD_SIZE), lambda h, g: (0, 2 * h + 1))
    column = pl.BlockSpec((rows, 1), lambda h, g: (0, 0))
    line = pl.BlockSpec((1, rows), lambda h, g: (0, 0))
    near = jax.ShapeDtypeStruct((rows, kv_heads * HEAD_SIZE), F32)
    return pl.pallas_call(
        kernel,
        grid=(kv_heads, groups),
        in_specs=[pl.BlockSpec(memory_space=pltpu.SMEM), column, line, line, mine]
        + [key, value] * 2
        + [mine, pl.BlockSpec((1, rows, 1), lambda h, g: (h * groups + g, 0, 0))]
        + [pl.BlockSpec(memory_space=pl.ANY)] * len(after),
        out_specs=[mine, shared, shared, pl.BlockSpec((rows, 2 * HEAD_SIZE), lambda h, g: (0, h))],
        out_shape=[
            jax.ShapeDtypeStruct((rows, width), F32),
            near,
            near,
            jax.ShapeDtypeStruct((rows, kv.shape[1]), BF),
        ],
        scratch_shapes=[pltpu.VMEM((rows, 2 * HEAD_SIZE), F32)],
        compiler_params=pltpu.CompilerParams(vmem_limit_bytes=32 * 2**20),
    )(*inputs, *after)


def call(
    kernel,
    out,
    inputs,
    scalars=(),
    grid=(1,),
    in_specs=None,
    out_specs=None,
    scratch=(),
    vmem=20,
    after=(),
    alias=None,
    hbm=4 * 2**20,
):
    def whole(a):
        return pl.BlockSpec(a.shape, lambda *_: (0,) * len(a.shape))

    in_specs = [s or whole(a) for s, a in zip(in_specs or [None] * len(inputs), inputs)]
    out_specs = [s or whole(a) for s, a in zip(out_specs or [None] * len(out), out)]
    alias = alias or {}

    def held(a, least):
        if a.size * a.dtype.itemsize < least:
            return a
        return pltpu.with_memory_space_constraint(a, pltpu.HBM)

    inputs = [held(a, hbm) for a in inputs]
    after = [held(a, hbm) for a in alias.values()] + [held(a, 2**20) for a in after]
    first = len(scalars) + len(inputs)

    def run(*refs):
        kernel(*refs[:first], *refs[first + len(after) :])

    return pl.pallas_call(
        run,
        grid_spec=pltpu.PrefetchScalarGridSpec(
            num_scalar_prefetch=len(scalars),
            grid=grid,
            in_specs=in_specs + [pl.BlockSpec(memory_space=pl.ANY)] * len(after),
            out_specs=out_specs,
            scratch_shapes=list(scratch),
        ),
        out_shape=list(out),
        compiler_params=pltpu.CompilerParams(vmem_limit_bytes=vmem * 2**20),
        input_output_aliases={first + i: place for i, place in enumerate(alias)},
        cost_estimate=pl.CostEstimate(flops=0, bytes_accessed=0, transcendentals=0),
    )(*[s.astype(jnp.int32).reshape(1) for s in scalars], *inputs, *after)


def in_hbm(dims, dtype):
    return pltpu.HBM(tuple(dims), dtype)


def shape(dims, dtype):
    return jax.ShapeDtypeStruct(tuple(dims), dtype)


def blocked(dims, index):
    return pl.BlockSpec(dims, index)


COLUMNS = 512


def other(index, k):
    return lax.bitwise_xor(index, jnp.int32(k))


def partners(z, size):
    return lax.bitwise_xor(z, jnp.arange(size, dtype=jnp.int32))


def ahead(index, k, size):
    return lax.bitwise_and(index + jnp.int32(k), jnp.int32(size - 1))


def behind(index, k, size):
    return lax.bitwise_and(index + jnp.int32(size) - jnp.int32(k), jnp.int32(size - 1))


def out_rows(ref):
    cols, dp, rows, width = ref.shape
    size = 4
    if dp == size:
        return ref[...].reshape(cols * dp * rows, width)
    per = dp // size
    order = [(c, q * per + r) for c in range(cols) for r in range(per) for q in range(size)]
    return jnp.concatenate([ref[c, d] for c, d in order])


def assemble(pieces, z, rolled, direct, after=()):
    def place_of(z, k):
        return behind(z, k, len(pieces)) if direct else other(z, k)

    size, dp = lax.axis_size("row"), lax.axis_size("dp")
    rows, width = pieces[0].shape
    rest = width // dp
    block = rows // size
    if rest % 128:
        out = jnp.stack([p.reshape(rows, dp, rest) for p in pieces], axis=2)
        order = behind(z, jnp.arange(size), size) if direct else partners(z, size)
        out = jnp.take(out, order, axis=2).reshape(rows, -1)
        if rolled:
            out = jnp.concatenate(
                [
                    lax.dynamic_slice_in_dim(out, other(z, k) * block, block, 0)
                    for k in range(size)
                ]
            )
        return out

    def kernel(z, *refs):
        out = refs[-1]
        for k in range(size):
            piece = refs[k][...]
            for d in range(dp):
                place = pl.multiple_of((d * size + place_of(z[0], k)) * rest, rest)
                out[:, pl.ds(place, rest)] = piece[:, d * rest : (d + 1) * rest]

    def index(i, z):
        return (lax.bitwise_xor(z[0], jnp.int32(i)) if rolled else i, 0)

    return call(
        kernel,
        [shape((rows, size * width), pieces[0].dtype)],
        list(pieces),
        [z],
        (size,),
        [blocked((block, width), index)] * size,
        [blocked((block, size * width), lambda i, z: (i, 0))],
        after=after,
    )[0]


def take_apart(full, z, rolled, after=()):
    size, dp = lax.axis_size("row"), lax.axis_size("dp")
    rows, width = full.shape
    rest = width // (size * dp)
    block = rows // size
    if rest % 128:
        if rolled:
            full = jnp.concatenate(
                [
                    lax.dynamic_slice_in_dim(full, other(z, i) * block, block, 0)
                    for i in range(size)
                ]
            )
        split = full.reshape(rows, dp, size, rest)
        split = jnp.take(split, partners(z, size), axis=2)
        return [split[:, :, k].reshape(rows, dp * rest) for k in range(size)]

    def kernel(z, full, *outs):
        for k in range(size):
            for d in range(dp):
                place = pl.multiple_of((d * size + other(z[0], k)) * rest, rest)
                outs[k][:, d * rest : (d + 1) * rest] = full[:, pl.ds(place, rest)]

    def index(i, z):
        return (lax.bitwise_xor(z[0], jnp.int32(i)) if rolled else i, 0)

    return call(
        kernel,
        [shape((rows, dp * rest), full.dtype)] * size,
        [full],
        [z],
        (size,),
        [blocked((block, width), lambda i, z: (i, 0))],
        [blocked((block, dp * rest), index)] * size,
        after=after,
        hbm=2**20,
    )


def project_kernel(x, gain, weight, cosine, sine, head_gain, a, scale, qr, kr, qn, kv):
    rows = x.shape[0]
    heads = qr.shape[1] // HEAD_SIZE
    kv_heads = kr.shape[1] // HEAD_SIZE

    @pl.when(pl.program_id(0) == 0)
    def _():
        for first in range(0, rows, 128):
            s = slice(first, first + 128)
            xf = x[s, :].astype(F32)
            r = lax.rsqrt(jnp.mean(xf * xf, axis=1, keepdims=True) + EPS)
            a[s, :] = (xf * r * gain[...]).astype(BF)
            scale[s, :] = r

    raw = dot(a[...], weight[0].reshape(MODEL_WIDTH, COLUMNS))

    def turn(values, gains):
        normed = (
            values
            * lax.rsqrt(jnp.mean(values * values, axis=-1, keepdims=True) + EPS)
            * gains
        )
        half = HEAD_SIZE // 2
        turned = jnp.concatenate([-normed[:, half:], normed[:, :half]], axis=-1)
        return (normed * cosine[...] + turned * sine[...]).astype(BF)

    for h in range(heads):
        s = slice(h * HEAD_SIZE, (h + 1) * HEAD_SIZE)
        qr[:, s] = raw[:, s]
        qn[:, s] = turn(raw[:, s], head_gain[0:1, :])
    first = heads * HEAD_SIZE
    for h in range(kv_heads):
        s = slice(h * HEAD_SIZE, (h + 1) * HEAD_SIZE)
        values = raw[:, first + h * HEAD_SIZE : first + (h + 1) * HEAD_SIZE]
        kr[:, s] = values
        kv[:, s] = turn(values, head_gain[1:2, :])
    kv[:, kv_heads * HEAD_SIZE :] = raw[:, first + kv_heads * HEAD_SIZE :].astype(BF)


def project(x, gain, weight, cosine, sine, head_gain, head_width, kv_width, after):
    rows = x.shape[0]
    cols, dp, _, width = weight.shape
    q = blocked((rows, head_width), lambda c: (0, c))
    k = blocked((rows, kv_width), lambda c: (0, c))
    return call(
        project_kernel,
        [
            shape(x.shape, BF),
            shape((rows, 1), F32),
            shape((rows, cols * head_width), F32),
            shape((rows, cols * kv_width), F32),
            shape((rows, cols * head_width), BF),
            shape((rows, 2 * cols * kv_width), BF),
        ],
        [x, gain, weight, cosine, sine, head_gain],
        (),
        (cols,),
        [None, None, blocked((1, dp, MODEL_WIDTH // dp, width), lambda c: (c, 0, 0, 0)), None, None, None],
        [None, None, q, k, q, blocked((rows, 2 * kv_width), lambda c: (0, c))],
        after=after,
    )


def mixed_parts(mixed, weight, z, base, after):
    size = lax.axis_size("row")
    cols, dp, total_rows, _ = weight.shape
    rows = mixed.shape[0]
    inner = mixed.shape[1] // (cols * dp)
    part = rows // size
    steps = MODEL_WIDTH // COLUMNS

    def kernel(z, mixed, weight, *refs):
        *outs, total = refs
        total[...] = dot(mixed[...], out_rows(weight))
        for k in range(size):
            first = pl.multiple_of(other(z[0], k) * part, part)
            outs[k][...] = total[pl.ds(first, part), :].astype(outs[k].dtype)

    return call(
        kernel,
        [shape((part, MODEL_WIDTH), BF if k else F32) for k in range(size)],
        [mixed, weight],
        [z],
        (steps,),
        [None, blocked((cols, dp, inner, COLUMNS), lambda c, z: (0, 0, base + c, 0))],
        [blocked((part, COLUMNS), lambda c, z: (0, c))] * size,
        scratch=[pltpu.VMEM((rows, COLUMNS), F32)],
        after=after,
    )


def mixed_back(chunks, weight, z, base, inner, after):
    size = len(chunks)
    cols, dp, _, _ = weight.shape
    part, width = chunks[0].shape
    rows = size * part
    heads = cols * dp * inner
    steps = width // COLUMNS

    def kernel(z, *refs):
        *ins, weight, full, out, total = refs
        for k in range(size):
            first = pl.multiple_of(other(z[0], k) * part, part)
            full[pl.ds(first, part), :] = ins[k][...]
        term = dot(full[...], out_rows(weight), "nt")
        c = pl.program_id(0)

        @pl.when(c == 0)
        def _():
            total[...] = term

        @pl.when(c > 0)
        def _():
            total[...] += term

        @pl.when(c == steps - 1)
        def _():
            out[...] = total[...].astype(BF)

    return call(
        kernel,
        [shape((rows, width), BF), shape((rows, heads), BF)],
        list(chunks) + [weight],
        [z],
        (steps,),
        [blocked((part, COLUMNS), lambda c, z: (0, c))] * size
        + [blocked((cols, dp, inner, COLUMNS), lambda c, z: (0, 0, base + c, 0))],
        [blocked((rows, COLUMNS), lambda c, z: (0, c)), None],
        scratch=[pltpu.VMEM((rows, heads), F32)],
        after=after,
    )


def masked(values, valid, after):
    def kernel(values, valid, out):
        out[...] = jnp.where(valid[...] > 0, values[...], jnp.zeros_like(values))

    return call(kernel, [shape(values.shape, values.dtype)], [values, valid], after=after)[0]


def add_parts(parts, dtype, after=()):
    def kernel(*refs):
        total = refs[0][...].astype(F32)
        for ref in refs[1:-1]:
            total = total + ref[...].astype(F32)
        refs[-1][...] = total.astype(dtype)

    return call(kernel, [shape(parts[0].shape, dtype)], list(parts), after=after)[0]


def hidden_norm(parts, x, gain, z, after=()):
    rows, width = parts[0].shape

    def kernel(z, *refs):
        *ps, x, gain, h, scale, a = refs
        total = x[...].astype(F32)
        for p in ps:
            total = total + p[...].astype(F32)
        r = lax.rsqrt(jnp.mean(total * total, axis=1, keepdims=True) + EPS)
        h[...] = total
        scale[...] = r
        a[...] = (total * r * gain[...]).astype(BF)

    return call(
        kernel,
        [shape((rows, width), F32), shape((rows, 1), F32), shape((rows, width), BF)],
        list(parts) + [x, gain],
        [z],
        (1,),
        [None] * len(parts) + [blocked((rows, width), lambda i, z: (z[0], 0)), None],
        after=after,
    )


def gateup_chunk(parts, weight, grad, hidden):
    part, width = parts[0].shape
    rows = part * len(parts)
    cols, dp, _, _ = weight.shape
    steps = 2 * hidden // (cols * COLUMNS)
    half = COLUMNS // 2

    def kernel(*refs):
        *ins, weight, grad, act, out, a = refs

        @pl.when((pl.program_id(0) == 0) & (pl.program_id(1) == 0))
        def _():
            for i, ref in enumerate(ins):
                a[i * part : (i + 1) * part, :] = ref[...]

        p = dot(a[...], weight[0].reshape(width, COLUMNS))
        for j in range(half // 128):
            gate, up = p[:, j * 256 : j * 256 + 128], p[:, j * 256 + 128 : j * 256 + 256]
            s = slice(j * 128, (j + 1) * 128)
            spread = 1.0 / (1.0 + jnp.exp(-gate))
            silu = gate * spread
            act[:, s] = (silu * up).astype(BF)
            g = grad[:, s]
            out[:, j * 256 : j * 256 + 128] = (g * up * (spread + silu * (1.0 - spread))).astype(BF)
            out[:, j * 256 + 128 : j * 256 + 256] = (g * silu).astype(BF)

    def place(c, t):
        return (0, c * steps + t)

    total = grad.shape[0]
    return call(
        kernel,
        [shape((total, hidden), BF), shape((total, 2 * hidden), BF)],
        list(parts) + [weight, grad],
        (),
        (cols, steps),
        [None] * len(parts)
        + [
            blocked((1, dp, width // dp, COLUMNS), lambda c, t: (c, 0, t, 0)),
            blocked((rows, half), place),
        ],
        [blocked((rows, half), place), blocked((rows, COLUMNS), place)],
        scratch=[pltpu.VMEM((rows, width), BF)],
        vmem=24,
    )


def gateup_back(grad, weight, kinds):
    cols, dp, _, _ = weight.shape
    both = grad.shape[1]
    block = MODEL_WIDTH // dp
    terms = both // COLUMNS
    per = terms // cols
    rows = grad.shape[0]
    part = rows // len(kinds)

    def kernel(grad, weight, *outs):
        total = None
        for t in range(terms):
            right = weight[t // per, 0, (t % per) * block : (t % per + 1) * block, :]
            term = dot(grad[:, t * COLUMNS : (t + 1) * COLUMNS], right, "nt")
            total = term if total is None else total + term
        for i, (out, kind) in enumerate(zip(outs, kinds)):
            out[...] = total[i * part : (i + 1) * part, :].astype(kind)

    return call(
        kernel,
        [shape((part, MODEL_WIDTH), kind) for kind in kinds],
        [grad, weight],
        (),
        (dp,),
        [
            None,
            blocked((cols, 1, per * block, COLUMNS), lambda n: (0, n, 0, 0)),
        ],
        [blocked((part, block), lambda n: (0, n))] * len(kinds),
        vmem=24,
    )


def down_back(out_low, weight, base, inner, after):
    cols, dp, _, _ = weight.shape
    rows, width = out_low.shape
    hidden = cols * dp * inner

    def kernel(low, weight, out):
        term = dot(low[...], out_rows(weight), "nt")

        @pl.when(pl.program_id(0) == 0)
        def _():
            out[...] = term

        @pl.when(pl.program_id(0) > 0)
        def _():
            out[...] += term

    return call(
        kernel,
        [shape((rows, hidden), F32)],
        [out_low, weight],
        (),
        (width // COLUMNS,),
        [
            blocked((rows, COLUMNS), lambda c: (0, c)),
            blocked((cols, dp, inner, COLUMNS), lambda c: (0, 0, base + c, 0)),
        ],
        [None],
        vmem=24,
        after=after,
    )[0]


def down_forward(active, hidden, weight, base, inner, after):
    cols, dp, _, _ = weight.shape
    rows, width = active.shape
    part = hidden.shape[0]

    def kernel(active, hidden, weight, out):
        p = dot(active[...], out_rows(weight))
        out[:part, :] = (p[:part, :] + hidden[...]).astype(BF)
        out[part:, :] = p[part:, :].astype(BF)

    return call(
        kernel,
        [shape((rows, MODEL_WIDTH), BF)],
        [active, hidden, weight],
        (),
        (MODEL_WIDTH // COLUMNS,),
        [
            None,
            blocked((part, COLUMNS), lambda c: (0, c)),
            blocked((cols, dp, inner, COLUMNS), lambda c: (0, 0, base + c, 0)),
        ],
        [blocked((rows, COLUMNS), lambda c: (0, c))],
        after=after,
    )[0]


def hidden_back(parts, h, scale, gain, out_low, after):
    rows, width = h.shape

    def kernel(*refs):
        *ps, h, scale, gain, dy, dh, low, gain_grad = refs
        grad = ps[0][...].astype(F32)
        for p in ps[1:]:
            grad = grad + p[...].astype(F32)
        hidden, r = h[...], scale[...]
        weighted = grad * gain[...]
        inner = jnp.sum(weighted * hidden, axis=1, keepdims=True)
        total = dy[...].astype(F32) + r * weighted - (r * r * r * inner / MODEL_WIDTH) * hidden
        dh[...] = total
        low[...] = total.astype(BF)
        gain_grad[...] = jnp.sum(grad * hidden * r, axis=0, keepdims=True)

    return call(
        kernel,
        [shape((rows, width), F32), shape((rows, width), BF), shape((1, width), F32)],
        list(parts) + [h, scale, gain, out_low],
        (),
        (1,),
        [None] * (len(parts) + 3) + [blocked((rows, width), lambda i: (0, 0))],
        after=after,
        hbm=2**17,
    )


def heads_back_kernel(
    qr, kr, dqn, dkn, dv, far, cosine, sine, head_gain, out, gain_grad
):
    heads = qr.shape[1] // HEAD_SIZE
    kv_heads = kr.shape[1] // HEAD_SIZE
    half = HEAD_SIZE // 2

    def back(raw, grad, gains):
        turned = grad * sine[...]
        turned = jnp.concatenate([turned[:, half:], -turned[:, :half]], axis=-1)
        g = grad * cosine[...] + turned
        r = lax.rsqrt(jnp.mean(raw * raw, axis=-1, keepdims=True) + EPS)
        weighted = g * gains
        inner = jnp.sum(weighted * raw, axis=-1, keepdims=True)
        low = (r * weighted - (r * r * r * inner / HEAD_SIZE) * raw).astype(BF)
        return low, jnp.sum(g * raw * r, axis=0, keepdims=True)

    @pl.when(pl.program_id(0) == 0)
    def _():
        gain_grad[...] = jnp.zeros_like(gain_grad)

    for h in range(heads):
        s = slice(h * HEAD_SIZE, (h + 1) * HEAD_SIZE)
        low, total = back(qr[:, s], dqn[:, s], head_gain[0:1, :])
        out[:, s] = low
        gain_grad[0:1, :] += total
    first = heads * HEAD_SIZE
    for h in range(kv_heads):
        s = slice(h * HEAD_SIZE, (h + 1) * HEAD_SIZE)
        low, total = back(kr[:, s], dkn[:, s] + far[:, s].astype(F32), head_gain[1:2, :])
        out[:, first + h * HEAD_SIZE : first + (h + 1) * HEAD_SIZE] = low
        gain_grad[1:2, :] += total
    first += kv_heads * HEAD_SIZE
    out[:, first:] = (dv[...] + far[:, kv_heads * HEAD_SIZE :].astype(F32)).astype(BF)


def heads_back(qr, kr, dqn, dkn, dv, far, cosine, sine, head_gain, cols, after):
    rows = qr.shape[0]
    head_width, kv_width = qr.shape[1] // cols, kr.shape[1] // cols
    q = blocked((rows, head_width), lambda c: (0, c))
    k = blocked((rows, kv_width), lambda c: (0, c))
    far_kv = blocked((rows, 2 * kv_width), lambda c: (0, c))
    width = head_width + 2 * kv_width
    return call(
        heads_back_kernel,
        [shape((rows, cols * width), BF), shape((2, HEAD_SIZE), F32)],
        [qr, kr, dqn, dkn, dv, far, cosine, sine, head_gain],
        (),
        (cols,),
        [q, k, q, k, k, far_kv, None, None, None],
        [blocked((rows, width), lambda c: (0, c)), None],
        after=after,
    )


def input_back(grads, weight, x, scale, gain, dh, z, after):
    cols, steps, _, width = weight.shape
    rows = grads.shape[0]
    model = MODEL_WIDTH
    part = dh.shape[0]

    def kernel(z, grads, weight, x, scale, gain, dh, out, c1, gain_grad):
        total = dot(grads[:, :width], weight[0, 0], "nt")
        for c in range(1, cols):
            total = total + dot(grads[:, c * width : (c + 1) * width], weight[c, 0], "nt")
        r = scale[...]
        xf = x[...].astype(F32)
        weighted = total * gain[...]
        moved = weighted * xf
        gain_grad[...] = jnp.sum(total * xf * r, axis=0, keepdims=True)
        out[...] = (r * weighted).astype(BF)
        first = pl.multiple_of(z[0] * part, part)
        own = pl.ds(first, part)
        out[own, :] = (out[own, :].astype(F32) + dh[...]).astype(BF)

        @pl.when(pl.program_id(0) == 0)
        def _():
            c1[...] = jnp.zeros_like(c1)

        c1[...] += jnp.sum(moved, axis=1, keepdims=True)

    block = model // steps
    wide = blocked((rows, block), lambda n, z: (0, n))
    return call(
        kernel,
        [shape((rows, model), BF), shape((rows, 1), F32), shape((1, model), F32)],
        [grads, weight, x, scale, gain, dh],
        [z],
        (steps,),
        [
            None,
            blocked((cols, 1, block, width), lambda n, z: (0, n, 0, 0)),
            wide,
            None,
            blocked((1, block), lambda n, z: (0, n)),
            blocked((part, block), lambda n, z: (0, n)),
        ],
        [wide, None, blocked((1, block), lambda n, z: (0, n))],
        after=after,
    )


def weight_grads(lefts, right, out_left, out_right, cols, after=()):
    size, dp = lax.axis_size("row"), lax.axis_size("dp")
    rows = right.shape[0]
    block = MODEL_WIDTH // dp
    n = right.shape[1] // cols
    part = rows // len(lefts)
    m = out_left.shape[1] // cols
    inner = m // dp
    terms = n // COLUMNS
    total = terms * block + MODEL_WIDTH // COLUMNS * inner

    def kernel(*refs):
        *ins, right, out_left, out_right, out = refs
        left = jnp.concatenate([ref[...] for ref in ins]) if len(ins) > 1 else ins[0][...]
        for t in range(terms):
            term = dot(left, right[:, t * COLUMNS : (t + 1) * COLUMNS], "tn")
            out[0, 0, t * block : (t + 1) * block, :] = term.astype(BF)
        for d in range(dp):
            q, r = d // (dp // size), d % (dp // size)
            first = (r * size + q) * inner

            @pl.when(pl.program_id(1) == d)
            def _():
                term = dot(out_left[:, first : first + inner], out_right[...], "tn").astype(BF)
                for c in range(MODEL_WIDTH // COLUMNS):
                    place = terms * block + c * inner
                    piece = term[:, c * COLUMNS : (c + 1) * COLUMNS]
                    out[0, 0, place : place + inner, :] = piece

    return call(
        kernel,
        [in_hbm((cols, dp, total, COLUMNS), BF)],
        list(lefts) + [right, out_left, out_right],
        (),
        (cols, dp),
        [blocked((part, block), lambda c, d: (0, d))] * len(lefts)
        + [
            blocked((rows, n), lambda c, d: (0, c)),
            blocked((rows, m), lambda c, d: (0, c)),
            None,
        ],
        [blocked((1, 1, total, COLUMNS), lambda c, d: (c, d, 0, 0))],
        after=after,
        vmem=28,
    )[0]


def swap(value, axis, step):
    return lax.ppermute(value, axis, [(i, i ^ step) for i in range(lax.axis_size(axis))])


def gather_pieces(own, beside=None):
    two = swap(own, "row", 2)
    if beside is not None:
        two, beside = lax.optimization_barrier((two, beside))
    pieces = [own, swap(own, "row", 1), two, swap(two, "row", 1)]
    return pieces if beside is None else (pieces, beside)


def gather_direct(own):
    return along_row([own] * lax.axis_size("row"), True)


def scatter_pieces(pieces, after=()):
    sent = add_parts([pieces[2], swap(pieces[3], "row", 1)], BF, after)
    direct, sent = lax.optimization_barrier((pieces[1], sent))
    return [pieces[0], swap(direct, "row", 1), swap(sent, "row", 2)], sent


def add_along(value, axes):
    for axis in axes:
        step = 1
        while step < lax.axis_size(axis):
            value = value + swap(value, axis, step)
            step *= 2
    return value


def along_row(pieces, forward):
    size = len(pieces)
    sign = 1 if forward else -1
    return [pieces[0]] + [
        lax.ppermute(p, "row", [(i, (i + sign * k) % size) for i in range(size)])
        for k, p in enumerate(pieces)
        if k
    ]


def along_quarters(pieces, forward):
    size = len(pieces)
    per = lax.axis_size("dp") // size
    sign = 1 if forward else -1

    def pairs(k):
        places = [(q, r) for q in range(size) for r in range(per)]
        return [(q * per + r, (q + sign * k) % size * per + r) for q, r in places]

    return [pieces[0]] + [lax.ppermute(p, "dp", pairs(k)) for k, p in enumerate(pieces) if k]


def gather_shard(shard):
    full = lax.all_gather(shard, ("col", "dp"), axis=0)
    return full.reshape(lax.axis_size("col"), lax.axis_size("dp"), *shard.shape)


def scatter_shard(full):
    flat_rows = full.reshape(-1, full.shape[-1])
    return lax.psum_scatter(flat_rows, ("col", "dp"), scatter_dimension=0, tiled=True)


def quarter_index():
    return lax.axis_index("dp") // (lax.axis_size("dp") // lax.axis_size("row"))


def pack_attention(query, keyval, z):
    size = lax.axis_size("row")
    rows = query.shape[0]
    hw, kw = query.shape[1] // size, keyval.shape[2] // size

    def kernel(z, query, keyval, *outs):
        for k in range(size):
            at = ahead(z[0], k, size)
            out = outs[k]
            out[:, :hw] = query[:, pl.ds(pl.multiple_of(at * hw, hw), hw)].astype(BF)
            for s in range(2):
                part = keyval[:, s, pl.ds(pl.multiple_of(at * kw, kw), kw)]
                out[:, hw + s * kw : hw + (s + 1) * kw] = part.astype(BF)

    return call(kernel, [shape((rows, hw + 2 * kw), BF)] * size, [query, keyval], [z], hbm=0)


def pack_feed(gateup, downs, z, after):
    size = lax.axis_size("row")
    rows = gateup.shape[0]
    fw = gateup.shape[2] // size
    terms = 2 * fw // COLUMNS
    inner = downs[0].shape[0]

    def kernel(z, gateup, *refs):
        for k in range(size):
            at = ahead(z[0], k, size)
            out = refs[size + k]
            for s in range(2):
                for j in range(fw // 128):
                    first = pl.multiple_of(at * fw + j * 128, 128)
                    place = (2 * j + s) * 128
                    t, lane = place // COLUMNS, place % COLUMNS
                    part = gateup[:, s, pl.ds(first, 128)].astype(BF)
                    out[t * rows : (t + 1) * rows, lane : lane + 128] = part
            out[terms * rows :, :] = refs[k][...]

    return call(
        kernel,
        [shape((terms * rows + inner, COLUMNS), BF)] * size,
        [gateup, *downs],
        [z],
        after=after,
        vmem=32,
    )


def pack_out(blocks, after=()):
    size = lax.axis_size("row")
    rows = [b.shape[0] // size for b in blocks]

    def kernel(q, *refs):
        for k in range(size):
            place = 0
            for ref, n in zip(refs, rows):
                first = pl.multiple_of(ahead(q[0], k, size) * n, n)
                refs[len(rows) + k][place : place + n, :] = ref[pl.ds(first, n), :].astype(BF)
                place += n

    return call(
        kernel,
        [shape((sum(rows), blocks[0].shape[1]), BF)] * size,
        blocks,
        [quarter_index()],
        after=after,
        hbm=0,
    )


def regroup(parts, source, target, cuts, after=(), top=0):
    size = len(parts)
    sources = [source(k) for k in range(size)]
    targets = [target(k) for k in range(size)]
    starts = [sum(cuts[:i]) for i in range(len(cuts))]

    def kernel(*refs):
        places, ins = refs[: 2 * size], refs[2 * size : 3 * size]
        outs, held = refs[3 * size : -1], refs[-1]
        for k in range(size):
            held[places[k][0]] = ins[k][top:, :]
        for i, (first, n) in enumerate(zip(starts, cuts)):
            for k in range(size):
                outs[i * size + k][...] = held[places[size + k][0], first : first + n]

    rows, width = parts[0].shape
    outs = call(
        kernel,
        [shape((n, width), BF) for n in cuts for _ in range(size)],
        parts,
        sources + targets,
        scratch=[pltpu.VMEM((size, rows - top, width), BF)],
        after=after,
    )
    return [outs[i * size : (i + 1) * size] for i in range(len(cuts))]


def make_shard(in_parts, out_parts, z, after=()):
    size, dp = len(in_parts), lax.axis_size("dp")
    rest = MODEL_WIDTH // (size * dp)
    steps = MODEL_WIDTH // COLUMNS
    rows = MODEL_WIDTH // (size * dp)
    if isinstance(out_parts, int):
        inner, joined = out_parts, True
        terms = (in_parts[0].shape[0] - inner) // rows
    else:
        inner, joined = out_parts[0].shape[0], False
        terms = in_parts[0].shape[0] // rows
    base = terms * size * rows
    if rest % 128:
        order = behind(z, jnp.arange(size), size)
        if joined:
            out_parts = [p[terms * rows :] for p in in_parts]
            in_parts = [p[: terms * rows] for p in in_parts]
        full = jnp.take(jnp.stack(in_parts), order, axis=0).reshape(size, terms, rows, COLUMNS)
        ins = full.transpose(1, 0, 2, 3).reshape(base, COLUMNS)
        full = jnp.stack([p.reshape(inner, dp, rest) for p in out_parts], axis=2)
        full = jnp.take(full, order, axis=2).reshape(inner, steps, COLUMNS)
        return jnp.concatenate([ins, full.transpose(1, 0, 2).reshape(-1, COLUMNS)])

    def kernel(z, *refs):
        out = refs[-1]
        for k in range(size):
            at = behind(z[0], k, size)
            for t in range(terms):
                first = pl.multiple_of((t * size + at) * rows, rows)
                out[pl.ds(first, rows), :] = refs[k][t * rows : (t + 1) * rows, :]
            place = pl.multiple_of(at * rest, rest)
            ref = refs[k] if joined else refs[size + k]
            top = terms * rows if joined else 0
            for d in range(dp):
                first = base + d * inner
                part = ref[top : top + inner, d * rest : (d + 1) * rest]
                out[first : first + inner, pl.ds(place, rest)] = part

    parts = list(in_parts) if joined else list(in_parts) + list(out_parts)
    out = shape((base + steps * inner, COLUMNS), BF)
    return call(kernel, [out], parts, [z], after=after)[0]


def split_shard(shard, terms, rows, inner, z, after=()):
    size, dp = lax.axis_size("row"), lax.axis_size("dp")
    rest = MODEL_WIDTH // (size * dp)
    steps = MODEL_WIDTH // COLUMNS
    base = terms * size * rows
    if rest % 128:
        ins = shard[:base].reshape(terms, size, rows, COLUMNS).transpose(1, 0, 2, 3)
        ins = jnp.take(ins, behind(z, jnp.arange(size), size), axis=0)
        outs = shard[base:].reshape(steps, inner, COLUMNS).transpose(1, 0, 2)
        outs = outs.reshape(inner, dp, size, rest)
        outs = jnp.take(outs, behind(z, jnp.arange(size), size), axis=2)
        return [
            jnp.concatenate([ins[k].reshape(-1, COLUMNS), outs[:, :, k].reshape(inner, COLUMNS)])
            for k in range(size)
        ]

    def kernel(z, full, *outs):
        for k in range(size):
            at = behind(z[0], k, size)
            for t in range(terms):
                first = pl.multiple_of((t * size + at) * rows, rows)
                outs[k][t * rows : (t + 1) * rows, :] = full[pl.ds(first, rows), :]
            place = pl.multiple_of(at * rest, rest)
            for d in range(dp):
                part = full[base + d * inner : base + (d + 1) * inner, pl.ds(place, rest)]
                outs[k][terms * rows :, d * rest : (d + 1) * rest] = part

    return call(
        kernel,
        [shape((terms * rows + inner, COLUMNS), BF)] * size,
        [shard],
        [z],
        after=after,
        hbm=2**19,
    )


def out_pieces(messages, inner, z, after=()):
    size = len(messages)
    quarter = quarter_index()
    parts = regroup(
        messages,
        lambda k: ahead(z, k, size),
        lambda k: ahead(quarter, k, size),
        [inner],
        after,
        messages[0].shape[0] - inner,
    )[0]
    return along_quarters(parts, True)


def update(refs, grad, rate):
    weight, moment, second, weight_new, moment_new, second_new = refs
    m, v, w = adamw(weight[...], moment[...], second[...], grad, rate, DECAY)
    moment_new[...] = m
    second_new[...] = v
    weight_new[...] = w


def update_out(state, pieces, rate, place):
    size = len(pieces)
    rows, width = pieces[0].shape
    if rows * width <= 2**17:

        def whole(q, *refs):
            for k in range(size):
                own = pl.ds(pl.multiple_of(behind(q[0], k, size) * rows, rows), rows)
                update([ref.at[own, :] for ref in refs[size:]], refs[k][...].astype(F32), rate)

        w, m, v = call(
            whole, [shape(state[0].shape, F32)] * 3, list(pieces) + list(state), [place], vmem=32
        )
        return m, v, w

    def kernel(q, *refs):
        k = pl.program_id(0)
        for i in range(size):

            @pl.when(k == i)
            def _():
                update(refs[size:], refs[i][...].astype(F32), rate)

    spec = blocked((rows, width), lambda k, q: (lax.bitwise_and(q[0] + size - k, size - 1), 0))
    w, m, v = call(
        kernel,
        [shape(state[0].shape, F32)] * 3,
        list(pieces) + list(state),
        [place],
        (size,),
        [None] * size + [spec] * 3,
        [spec] * 3,
        hbm=2**19,
    )
    return m, v, w


def place_columns(messages, rows, cuts, z, after=()):
    size = len(messages)

    def kernel(z, *refs):
        for out, cut in zip(refs[size:], cuts):
            width = sum(w for _, _, w in cut)
            for k in range(size):
                at = ahead(z[0], k, size) * width
                for t, first, w in cut:
                    place = pl.multiple_of(at, 128)
                    part = refs[k][t * rows : (t + 1) * rows, first : first + w]
                    out[:, pl.ds(place, w)] = part
                    at = at + w

    out = [shape((rows, size * sum(w for _, _, w in cut)), BF) for cut in cuts]
    return call(kernel, out, messages, [z], after=after)


def flat(values):
    rows, two, width = values.shape
    return values.reshape(rows, two, width // 128, 128).transpose(0, 2, 1, 3).reshape(-1, 128)


def update_pair(state, grad, rate):
    rows, two, width = state[0].shape
    total = rows * two * width // 128
    steps = 2

    def kernel(grad, *refs):
        update(refs, grad[...].astype(F32), rate)

    spec = blocked((total // steps, 128), lambda i: (i, 0))
    news = call(
        kernel,
        [shape((total, 128), F32)] * 3,
        [grad.reshape(-1, 128)] + [flat(s) for s in state],
        (),
        (steps,),
        [spec] * 4,
        [spec] * 3,
        hbm=2**19,
        vmem=32,
    )
    w, m, v = [
        n.reshape(rows, width // 128, two, 128).transpose(0, 2, 1, 3).reshape(rows, two, width)
        for n in news
    ]
    return (m, v, w), news[0]


def adamw(weight, moment, second, grad, rate, decay):
    moment_new = BETA_ONE * moment + (1.0 - BETA_ONE) * grad
    second_new = BETA_TWO * second + (1.0 - BETA_TWO) * grad * grad
    first_hat = moment_new * (1.0 / (1.0 - BETA_ONE**STEP))
    second_hat = second_new * (1.0 / (1.0 - BETA_TWO**STEP))
    weight_new = weight - rate * (first_hat / (jnp.sqrt(second_hat) + ADAM_EPS) + decay * weight)
    return (moment_new, second_new, weight_new)


def body(
    tokens,
    cotangent,
    seq_lens,
    query_weight,
    query_moment,
    query_second,
    key_value_master_weight,
    key_value_first_moment,
    key_value_second_moment,
    output_weight,
    output_moment,
    output_second,
    gateup_weight,
    gateup_moment,
    gateup_second,
    down_weight,
    down_moment,
    down_second,
    norm_gains,
    norm_moment,
    norm_second,
    head_gains,
    head_moment,
    head_second,
):
    size, dp, cols = lax.axis_size("row"), lax.axis_size("dp"), lax.axis_size("col")
    z, y = lax.axis_index("row"), lax.axis_index("col")
    rows = tokens.shape[0]
    quarter = rows // size
    item_count = rows * cols
    rest = MODEL_WIDTH // (size * dp)
    head_width = query_weight.shape[1] // size
    kv_width = key_value_master_weight.shape[2] // size

    gains = norm_gains.reshape(2, size, dp, rest).transpose(0, 2, 1, 3).reshape(2, MODEL_WIDTH)
    first_gain, second_gain = gains[0:1], gains[1:2]

    segment, position = token_layout(seq_lens[0], item_count)
    first = y * rows
    own_segment = lax.dynamic_slice_in_dim(segment, first, rows, 0)
    cosine, sine = rope_tables(lax.dynamic_slice_in_dim(position, first, rows, 0))
    valid = (own_segment < SEQS).astype(jnp.int32)[:, None]

    hidden_width = gateup_weight.shape[2] // size * cols

    in_rows = query_weight.shape[0]
    output_inner, down_inner = output_weight.shape[0] // size, down_weight.shape[0] // size
    gateup_terms = 2 * hidden_width // (cols * COLUMNS)
    steps = MODEL_WIDTH // COLUMNS
    down_base = gateup_terms * size * in_rows // down_inner
    output_base = size * in_rows // output_inner
    quarter_place = quarter_index()
    input_chunks = gather_pieces(tokens)
    attention_pieces = pack_attention(query_weight, key_value_master_weight, z)
    out_pieces_sent = pack_out([down_weight, output_weight], attention_pieces[:1])
    down_parts, output_parts = regroup(
        along_quarters(out_pieces_sent, True),
        lambda k: behind(quarter_place, k, size),
        lambda k: ahead(z, k, size),
        [down_inner, output_inner],
    )
    feed_pieces = pack_feed(gateup_weight, down_parts, z, output_parts[:1])
    attention_shard = make_shard(
        along_row(attention_pieces, True),
        along_row(output_parts, True),
        z,
        [feed_pieces[0], input_chunks[2]],
    )
    attention_full = gather_shard(attention_shard)
    inputs = assemble(input_chunks, z, False, False, [attention_shard])
    feed_shard = make_shard(along_row(feed_pieces, True), down_inner, z, [inputs])
    feed_full = gather_shard(feed_shard)
    out_own = masked(cotangent, valid, [feed_shard])
    out_chunks = gather_pieces(out_own)

    first_low, first_scale, query_raw, key_raw, query, keys_values = project(
        inputs,
        first_gain,
        attention_full,
        cosine,
        sine,
        head_gains,
        head_width,
        kv_width,
        [out_own],
    )
    before = lax.ppermute(keys_values, "col", [(i, i + 1) for i in range(cols - 1)])
    masks = (
        y.astype(jnp.int32).reshape(1),
        own_segment.reshape(rows, 1),
        own_segment.reshape(1, rows),
        segment[:rows].reshape(1, rows),
    )
    mixed, logsum = attention_forward(*masks, query, keys_values, before, [])
    hidden_pieces = mixed_parts(mixed, attention_full, z, output_base, out_chunks[1:])
    out_low = assemble(out_chunks, z, True, False, hidden_pieces[1:2])
    hidden_parts, _ = scatter_pieces(hidden_pieces)
    hidden, second_scale, second_low = hidden_norm(hidden_parts, inputs, second_gain, z)

    second_chunks = gather_pieces(second_low)
    active_grad = down_back(out_low, feed_full, down_base, down_inner, second_chunks[2:3])
    active, pair_grad = gateup_chunk(second_chunks, feed_full, active_grad, hidden_width)
    second_parts = gateup_back(pair_grad, feed_full, (F32, BF, BF, BF))
    feed_grads = weight_grads(
        second_chunks, pair_grad, active, out_low, cols, [second_parts[3]]
    )
    passed = swap(second_parts[3], "row", 1)
    feed_grads, passed = lax.optimization_barrier((feed_grads, passed))
    sent = add_parts([second_parts[2], passed], BF)
    direct, sent = lax.optimization_barrier((second_parts[1], sent))
    second_parts = [second_parts[0], swap(direct, "row", 1), swap(sent, "row", 2)]
    feed_total = scatter_shard(feed_grads)
    hidden_grad, hidden_low, second_gain_grad = hidden_back(
        second_parts, hidden, second_scale, second_gain, out_low, []
    )

    layer_part = down_forward(active, hidden, feed_full, down_base, down_inner, [hidden_low])
    hidden_all, mixed_grad = mixed_back(
        gather_pieces(hidden_low), attention_full, z, output_base, output_inner, [layer_part]
    )
    layer_pieces = take_apart(layer_part, z, True, [hidden_all])
    query_grad, key_grad, value_grad, far_sent = attention_backward(
        *masks, query, keys_values, before, mixed_grad, logsum, layer_pieces[:1]
    )
    far = lax.ppermute(far_sent, "col", [(i + 1, i) for i in range(cols - 1)])
    layer_parts, _ = scatter_pieces(layer_pieces)
    layer_output = add_parts(layer_parts, F32)
    raw_grad, head_part = heads_back(
        query_raw,
        key_raw,
        query_grad,
        key_grad,
        value_grad,
        far,
        cosine,
        sine,
        head_gains,
        cols,
        [layer_output],
    )
    attention_grads = weight_grads([first_low], raw_grad, mixed, hidden_all, cols)
    attention_grads, feed_total = lax.optimization_barrier((attention_grads, feed_total))
    attention_total = scatter_shard(attention_grads)
    feed_pieces = split_shard(feed_total, gateup_terms, in_rows, down_inner, z)
    input_part, inner_part, first_gain_grad = input_back(
        raw_grad,
        attention_full,
        inputs,
        first_scale,
        first_gain,
        hidden_grad,
        z,
        feed_pieces[:1],
    )
    input_pieces = take_apart(input_part, z, False)
    attention_pieces = split_shard(attention_total, 1, in_rows, output_inner, z)
    attention_messages = along_row(attention_pieces, False)
    input_parts, _ = scatter_pieces(input_pieces, attention_messages[1:2])
    feed_messages = along_row(feed_pieces, False)
    norm_part = jnp.concatenate([first_gain_grad, second_gain_grad])
    norm_part = norm_part.reshape(2, dp, size, rest).transpose(0, 2, 1, 3).reshape(2, MODEL_WIDTH)
    gain_part = jnp.concatenate([norm_part.reshape(-1), head_part.reshape(-1)]).reshape(-1, 128)
    gain_part, feed_messages[1], input_parts[0] = lax.optimization_barrier(
        (gain_part, feed_messages[1], input_parts[0])
    )
    gain_part = add_along(gain_part, ("dp", "col"))
    small = jnp.concatenate([gain_part, inner_part.reshape(-1, 128)])
    small, feed_messages[2] = lax.optimization_barrier((small, feed_messages[2]))
    small = add_along(small, ("row",)).reshape(-1)
    inner = small[gain_part.size :][:, None]
    norm_total = small[: norm_part.size].reshape(norm_part.shape)
    head_total = small[norm_part.size : gain_part.size].reshape(head_part.shape)

    down_new = update_out(
        (down_weight, down_moment, down_second),
        out_pieces(feed_messages, down_inner, z, [gain_part]),
        RATES[4],
        quarter_place,
    )
    cut = [(t, 0, COLUMNS) for t in range(gateup_terms)]
    (gateup_total,) = place_columns(
        feed_messages, in_rows, [cut], z, attention_pieces[:1]
    )
    gateup_new, _ = update_pair(
        (gateup_weight, gateup_moment, gateup_second), gateup_total, RATES[3]
    )
    output_new = update_out(
        (output_weight, output_moment, output_second),
        out_pieces(attention_messages, output_inner, z),
        RATES[2],
        quarter_place,
    )
    query_total, keyval_total = place_columns(
        attention_messages,
        in_rows,
        [[(0, 0, head_width)], [(0, head_width, 2 * kv_width)]],
        z,
    )
    input_grad = add_parts(input_parts, F32, [query_total]) - (
        first_scale * first_scale * first_scale * inner / MODEL_WIDTH
    ) * tokens.astype(F32)
    query_new = adamw(
        query_weight, query_moment, query_second, query_total.astype(F32), RATES[0], DECAY
    )
    keyval_new, _ = update_pair(
        (key_value_master_weight, key_value_first_moment, key_value_second_moment),
        keyval_total,
        RATES[1],
    )
    norm_new = adamw(norm_gains, norm_moment, norm_second, norm_total, GAIN_RATE, 0.0)
    head_new = adamw(head_gains, head_moment, head_second, head_total, GAIN_RATE, 0.0)
    return (
        layer_output,
        input_grad,
        *query_new,
        *keyval_new,
        *output_new,
        *gateup_new,
        *down_new,
        *norm_new,
        *head_new,
    )


def solution(mesh):
    items = P(("dp", "col"), "row")
    inward = P(("row", "dp"), "col")
    inward_pair = P(("row", "dp"), None, "col")
    outward = P(("col", "dp"), "row")
    weights = (
        (inward,) * 3 + (inward_pair,) * 3 + (outward,) * 3 + (inward_pair,) * 3 + (outward,) * 3
    )
    return jax.shard_map(
        body,
        mesh=mesh,
        in_specs=(items, items, P("dp", None)) + weights + (P(),) * 6,
        out_specs=(items, items) + weights + (P(),) * 6,
        check_vma=False,
    )
```
